32 devices in a mesh: pipe: 2 (over x), tensor: 4 (over z), dp: 4 (over y, core).
Axes of the slice: x: 2, y: 2, z: 4, core: 2. Of those that a mesh axis runs over, the one named last changes fastest.
Arguments:
- new_coeffs: bfloat16 [1024, 256], P('dp'), may hold values from -6 to 6
- loss_grad: bfloat16 [1024, 256], P('dp'), may hold values from -6 to 6
- sent_forward: bfloat16 [2, 1024, 256], P('pipe', 'dp'), may hold values from -6 to 6
- sent_backward: bfloat16 [2, 1024, 256], P('pipe', 'dp'), may hold values from -6 to 6
- stashed: bfloat16 [2, 1024, 256], P('pipe', 'dp'), may hold values from -6 to 6
- subspace: bfloat16 [4096, 256], replicated, may hold values from -0.09375 to 0.09375
- norm_gain: float32 [2, 4096], P('pipe'), may hold values from 0.5 to 1.5
- w_query: bfloat16 [2, 4096, 4096], P('pipe', None, 'tensor'), may hold values from -3 to 3
- w_key: bfloat16 [2, 4096, 512], P('pipe', None, 'tensor'), may hold values from -3 to 3
- w_value: bfloat16 [2, 4096, 512], P('pipe', None, 'tensor'), may hold values from -0.09375 to 0.09375
- w_output: bfloat16 [2, 4096, 4096], P('pipe', 'tensor'), may hold values from -0.09375 to 0.09375
Outputs:
- forward_out: bfloat16 [2, 1024, 256], P('pipe', 'dp')
- backward_out: bfloat16 [2, 1024, 256], P('pipe', 'dp')
- grad_query: bfloat16 [2, 4096, 4096], P('pipe', 'dp', 'tensor')
- grad_key: bfloat16 [2, 4096, 512], P('pipe', 'dp', 'tensor')
- grad_value: bfloat16 [2, 4096, 512], P('pipe', 'dp', 'tensor')
- grad_output: bfloat16 [2, 4096, 4096], P('pipe', 'tensor', 'dp')
- grad_gain: float32 [2, 4096], P('pipe')
The draws below stay inside these ranges and needn't reach their ends.
All inputs are finite; a program needn't handle non-finite values.
Results may differ from the reference program's by a relative error of at most 0.015.
Values may be sent and summed in bfloat16 or wider, within the bound.
No kernel may reach another device: no remote copies, remote signals or barrier semaphores. Data moves between devices by JAX's collectives and lax.ppermute only.
A program may use at most 192 MiB of HBM per device.

```python
import math
import jax
import jax.numpy as jnp
from jax import lax

D = 4096
QH = 32
KVH = 4
HD = 128
R = 256
SEQ = 256
SECTIONS = 2
TOKENS = 1024
N_DP = 4


def shared_keys(key):
    base_keys = jax.random.normal(key, (SECTIONS, D, KVH * HD), jnp.float32)
    return jnp.clip(base_keys, -6.0, 6.0) / math.sqrt(D)


def draw_w_key(key, part):
    base_keys = shared_keys(key)
    return jnp.clip(base_keys, -3.0, 3.0).astype(jnp.bfloat16)


def draw_w_query(key, part):
    key = jax.random.fold_in(key, 5)
    own_part = jnp.clip(jax.random.normal(key, (SECTIONS, D, QH * HD), jnp.float32), -6.0, 6.0) / math.sqrt(D)
    return jnp.clip(own_part, -3.0, 3.0).astype(jnp.bfloat16)


def block_levels(stream_key, extent, pieces, low, top_value):
    loudness, own = 1.0, jax.random.fold_in(stream_key, 6)
    for axis_at, shards_of in pieces:
        draws = jnp.exp(jax.random.uniform(jax.random.fold_in(own, axis_at), (shards_of,), jnp.float32, low / len(pieces), top_value / len(pieces)))
        loudness = loudness * jnp.repeat(draws, extent[axis_at] // shards_of).reshape([-1 if axis == axis_at else 1 for axis in range(len(extent))])
    return loudness


def bell_draw(key, shape, spread, bound, pieces=(), held_as=jnp.bfloat16):
    entries = spread * jax.random.normal(key, shape, jnp.float32)
    if pieces:
        entries = entries * block_levels(key, shape, pieces, -0.22, 0.18)
    return jnp.clip(entries, -bound, bound).astype(held_as)


def setup_inputs(seed: int = 0) -> dict:
    key_of = jax.random.split(jax.random.key(seed), 12)
    return {
        "new_coeffs": bell_draw(key_of[0], (TOKENS, R), 1.0, 6.0, ((0, 4),)),
        "loss_grad": bell_draw(key_of[1], (TOKENS, R), 1.0, 6.0, ((0, 4),)),
        "sent_forward": bell_draw(key_of[2], (SECTIONS, TOKENS, R), 1.0, 6.0, ((0, 2), (1, 4))),
        "sent_backward": bell_draw(key_of[3], (SECTIONS, TOKENS, R), 1.0, 6.0, ((0, 2), (1, 4))),
        "stashed": bell_draw(key_of[4], (SECTIONS, TOKENS, R), 1.0, 6.0, ((0, 2), (1, 4))),
        "subspace": bell_draw(key_of[5], (D, R), D ** -0.5, 0.09375),
        "norm_gain": jnp.clip(1.0 + 0.1 * jax.random.normal(key_of[6], (SECTIONS, D), jnp.float32), 0.5, 1.5),
        "w_query": draw_w_query(jax.random.fold_in(key_of[11], 71), 0),
        "w_key": draw_w_key(jax.random.fold_in(key_of[11], 71), 0),
        "w_value": bell_draw(key_of[9], (SECTIONS, D, KVH * HD), D ** -0.5, 0.09375, ((0, 2), (2, 4))),
        "w_output": bell_draw(key_of[10], (SECTIONS, QH * HD, D), (QH * HD) ** -0.5, 0.09375, ((0, 2), (1, 4))),
    }


EPSILON = 1e-05
ROPE_BASE = 500000.0

def rope_tables(length, head_width):
    half_width = head_width // 2
    frequency = ROPE_BASE ** (-2.0 * jnp.arange(half_width, dtype=jnp.float32) / head_width)
    angles = jnp.arange(length, dtype=jnp.float32)[:, None] * frequency[None, :]
    angles = jnp.concatenate([angles, angles], axis=1)
    return (jnp.cos(angles), jnp.sin(angles))

def rotate_half(values):
    half_width = values.shape[-1] // 2
    return jnp.concatenate([-values[..., half_width:], values[..., :half_width]], axis=-1)

def apply_rope(values, cosine, sine_table):
    return values * cosine[:, None, :] + rotate_half(values) * sine_table[:, None, :]

def undo_rope(values, cosine, sine_table):
    return values * cosine[:, None, :] - rotate_half(values) * sine_table[:, None, :]

def forward_cache(coeffs, basis_wide, gain_row, query_w, key_w, value_w, cosine, sine_table):
    seq_count = coeffs.shape[0]
    length = coeffs.shape[1]
    decoded = jnp.einsum('ntr,dr->ntd', coeffs.astype(jnp.float32), basis_wide)
    root_mean = jnp.sqrt(lax.optimization_barrier(jnp.mean(decoded * decoded, axis=-1, keepdims=True)) + EPSILON)
    unit_rows = decoded / root_mean
    normed = (unit_rows * gain_row).astype(jnp.bfloat16)
    normed_wide = normed.astype(jnp.float32)
    query_rows = jnp.einsum('ntd,de->nte', normed_wide, query_w.astype(jnp.float32)).reshape(seq_count, length, QH, HD)
    query_rows = apply_rope(query_rows, cosine, sine_table).astype(jnp.bfloat16)
    key_rows = jnp.einsum('ntd,de->nte', normed_wide, key_w.astype(jnp.float32)).reshape(seq_count, length, KVH, HD)
    key_rows = apply_rope(key_rows, cosine, sine_table).astype(jnp.bfloat16)
    value_rows = jnp.einsum('ntd,de->nte', normed_wide, value_w.astype(jnp.float32)).reshape(seq_count, length, KVH, HD).astype(jnp.bfloat16)
    grouped = query_rows.reshape(seq_count, length, KVH, QH // KVH, HD)
    scores = jnp.einsum('ntkgd,nukd->nkgtu', grouped.astype(jnp.float32), key_rows.astype(jnp.float32)) / math.sqrt(HD)
    causal = jnp.arange(length)[:, None] >= jnp.arange(length)[None, :]
    scores = jnp.where(causal, scores, -jnp.inf)
    row_max = lax.optimization_barrier(jnp.max(scores, axis=-1, keepdims=True))
    exps = jnp.exp(scores - row_max)
    probs_full = exps / lax.optimization_barrier(jnp.sum(exps, axis=-1, keepdims=True))
    probs_low = probs_full.astype(jnp.bfloat16)
    mixed_heads = jnp.einsum('nkgtu,nukd->ntkgd', probs_low.astype(jnp.float32), value_rows.astype(jnp.float32))
    head_out = mixed_heads.astype(jnp.bfloat16).reshape(seq_count, length, QH * HD)
    return (decoded, root_mean, unit_rows, normed, grouped, key_rows, value_rows, probs_full, probs_low, head_out)

def reduce_parts(per_seq):
    rounded = lax.optimization_barrier(per_seq.astype(jnp.bfloat16))
    return lax.optimization_barrier(jnp.sum(rounded.astype(jnp.float32), axis=0)).astype(jnp.bfloat16)

def backward_section(coeffs, upstream, basis_wide, gain_row, query_w, key_w, value_w, output_w, cosine, sine_table):
    decoded, root_mean, unit_rows, normed, grouped, key_rows, value_rows, probs_full, probs_low, head_out = forward_cache(coeffs, basis_wide, gain_row, query_w, key_w, value_w, cosine, sine_table)
    seq_count = coeffs.shape[0]
    length = coeffs.shape[1]
    up_wide = jnp.einsum('ntr,dr->ntd', upstream.astype(jnp.float32), basis_wide)
    up_low = up_wide.astype(jnp.bfloat16)
    output_parts = jnp.einsum('nte,ntd->ned', head_out.astype(jnp.float32), up_low.astype(jnp.float32))
    grad_heads = jnp.einsum('ntd,ed->nte', up_low.astype(jnp.float32), output_w.astype(jnp.float32))
    grad_heads = grad_heads.astype(jnp.bfloat16).reshape(seq_count, length, KVH, QH // KVH, HD)
    grad_values = jnp.einsum('nkgtu,ntkgd->nukd', probs_low.astype(jnp.float32), grad_heads.astype(jnp.float32))
    grad_probs = jnp.einsum('ntkgd,nukd->nkgtu', grad_heads.astype(jnp.float32), value_rows.astype(jnp.float32))
    grad_scores = probs_full * (grad_probs - lax.optimization_barrier(jnp.sum(probs_full * grad_probs, axis=-1, keepdims=True))) / math.sqrt(HD)
    scores_low = grad_scores.astype(jnp.bfloat16).astype(jnp.float32)
    grad_query = jnp.einsum('nkgtu,nukd->ntkgd', scores_low, key_rows.astype(jnp.float32)).reshape(seq_count, length, QH, HD)
    grad_keys = jnp.einsum('nkgtu,ntkgd->nukd', scores_low, grouped.astype(jnp.float32))
    grad_query = undo_rope(grad_query, cosine, sine_table).astype(jnp.bfloat16).reshape(seq_count, length, QH * HD)
    grad_keys = undo_rope(grad_keys, cosine, sine_table).astype(jnp.bfloat16).reshape(seq_count, length, KVH * HD)
    grad_values = grad_values.astype(jnp.bfloat16).reshape(seq_count, length, KVH * HD)
    normed_wide = normed.astype(jnp.float32)
    query_parts = jnp.einsum('ntd,nte->nde', normed_wide, grad_query.astype(jnp.float32))
    key_parts = jnp.einsum('ntd,nte->nde', normed_wide, grad_keys.astype(jnp.float32))
    value_parts = jnp.einsum('ntd,nte->nde', normed_wide, grad_values.astype(jnp.float32))
    grad_normed = jnp.einsum('nte,de->ntd', grad_query.astype(jnp.float32), query_w.astype(jnp.float32))
    grad_normed = grad_normed + jnp.einsum('nte,de->ntd', grad_keys.astype(jnp.float32), key_w.astype(jnp.float32))
    grad_normed = grad_normed + jnp.einsum('nte,de->ntd', grad_values.astype(jnp.float32), value_w.astype(jnp.float32))
    grad_gain = lax.optimization_barrier(jnp.sum(grad_normed * unit_rows, axis=(0, 1)))
    scaled = grad_normed * gain_row
    middle = lax.optimization_barrier(jnp.mean(scaled * unit_rows, axis=-1, keepdims=True))
    grad_decoded = (scaled - unit_rows * middle) / root_mean
    back_coeffs = jnp.einsum('ntd,dr->ntr', up_wide + grad_decoded, basis_wide, precision=lax.Precision.HIGHEST).astype(jnp.bfloat16)
    return (back_coeffs, reduce_parts(query_parts), reduce_parts(key_parts), reduce_parts(value_parts), reduce_parts(output_parts), grad_gain)

def reference(new_coeffs, loss_grad, sent_forward, sent_backward, stashed, subspace, norm_gain, w_query, w_key, w_value, w_output):
    cosine, sine_table = rope_tables(SEQ, HD)
    basis_wide = subspace.astype(jnp.float32)
    forward_list = []
    backward_list = []
    query_list = []
    key_list = []
    value_list = []
    output_list = []
    gain_list = []
    for section_index in range(SECTIONS):
        if section_index == 0:
            inputs = new_coeffs
        else:
            inputs = sent_forward[section_index - 1]
        if section_index == SECTIONS - 1:
            upstream = loss_grad
        else:
            upstream = sent_backward[section_index + 1]
        inputs = inputs.reshape(N_DP, SEQ, R)
        upstream = upstream.reshape(N_DP, SEQ, R)
        gain_row = norm_gain[section_index]
        cache = forward_cache(inputs, basis_wide, gain_row, w_query[section_index], w_key[section_index], w_value[section_index], cosine, sine_table)
        attention = jnp.einsum('nte,ed->ntd', cache[9].astype(jnp.float32), w_output[section_index].astype(jnp.float32))
        forward_coeffs = jnp.einsum('ntd,dr->ntr', cache[0] + attention, basis_wide, precision=lax.Precision.HIGHEST).astype(jnp.bfloat16)
        forward_list.append(forward_coeffs.reshape(TOKENS, R))
        result = backward_section(stashed[section_index].reshape(N_DP, SEQ, R), upstream, basis_wide, gain_row, w_query[section_index], w_key[section_index], w_value[section_index], w_output[section_index], cosine, sine_table)
        backward_list.append(result[0].reshape(TOKENS, R))
        query_list.append(result[1])
        key_list.append(result[2])
        value_list.append(result[3])
        output_list.append(result[4])
        gain_list.append(result[5])
    return (jnp.stack(forward_list), jnp.stack(backward_list), jnp.stack(query_list), jnp.stack(key_list), jnp.stack(value_list), jnp.stack(output_list), jnp.stack(gain_list))
```

```python
import functools
import math

import jax
import jax.numpy as jnp
import numpy as np
from jax import lax
from jax.experimental import pallas as pl
from jax.experimental.pallas import tpu as pltpu
from jax.sharding import PartitionSpec as P

HD = 128
EPSILON = 1e-05
ROPE_BASE = 500000.0
BF = jnp.bfloat16
F32 = jnp.float32
VMEM_BYTES = 28 * 1024 * 1024
LOG2E = 1.4426950408889634


def shifted(x, axis, by):
    devices = lax.axis_size(axis)
    pairs = [(i, i + by) for i in range(devices) if 0 <= i + by < devices]
    return lax.ppermute(x, axis, pairs)


def swap(x, axis, bit):
    devices = lax.axis_size(axis)
    return lax.ppermute(x, axis, [(i, i ^ bit) for i in range(devices)])


def cross_pipe(sent_forward, sent_backward):
    if lax.axis_size("pipe") != 2:
        return shifted(sent_forward, "pipe", 1), shifted(sent_backward, "pipe", -1)
    first = lax.axis_index("pipe") == 0
    got = swap(jnp.where(first, sent_forward, sent_backward), "pipe", 1)
    return got, got


def add_wide(a, b):
    return a.astype(F32) + b.astype(F32)


def nt(a, b):
    return lax.dot_general(a, b, (((1,), (1,)), ((), ())), preferred_element_type=F32)


def nn(a, b):
    return jnp.dot(a, b, preferred_element_type=F32)


def split(x, parts):
    out = []
    for _ in range(parts):
        piece = x.astype(BF)
        out.append(piece)
        x = x - piece.astype(F32)
    return out


def rope_tables(length):
    half = HD // 2
    frequency = np.float32(ROPE_BASE) ** (-2.0 * np.arange(half, dtype=np.float32) / HD)
    angles = np.arange(length, dtype=np.float32)[:, None] * frequency.astype(np.float32)
    cosine, sine = np.cos(angles), np.sin(angles)
    tables = (np.concatenate([cosine, cosine], 1), np.concatenate([-sine, sine], 1))
    return tuple(jnp.asarray(t, dtype=F32) for t in tables)


def rope(x, cosine, sine):
    return x * cosine + pltpu.roll(x, HD // 2, 1) * sine


def unrope(x, cosine, sine):
    return x * cosine - pltpu.roll(x, HD // 2, 1) * sine


def inverse_root(square_sum, width):
    return 1.0 / jnp.sqrt(square_sum / width + EPSILON)


def vmem(count):
    return [pl.BlockSpec(memory_space=pltpu.VMEM)] * count


def cost(flops, num_bytes, exps=0):
    return pl.CostEstimate(flops=flops, bytes_accessed=num_bytes, transcendentals=exps)


def project_kernel(
    wide, back_ref, u_ref, gain_ref, wq_ref, wk_ref, wv_ref, wo_ref,
    m_ref, o_ref, g_ref, inv_ref,
    m_acc, o_acc, g_acc, sq_acc,
):
    step = pl.program_id(0)
    rank = u_ref.shape[1]
    nq, nk = wq_ref.shape[1], wk_ref.shape[1]

    @pl.when(step == 0)
    def _():
        m_acc[...] = jnp.zeros_like(m_acc)
        o_acc[...] = jnp.zeros_like(o_acc)
        g_acc[...] = jnp.zeros_like(g_acc)
        sq_acc[...] = jnp.zeros_like(sq_acc)

    u = u_ref[...]
    ut = u.T
    scaled = (ut.astype(F32) * gain_ref[...]).astype(BF)
    for ref, at in ((wq_ref, 0), (wk_ref, nq), (wv_ref, nq + nk)):
        size = ref.shape[1]
        m_acc[:, at : at + size] += nn(scaled, ref[...])
    o_acc[...] += nn(wo_ref[...], u)
    g_acc[...] += nn(ut, u)
    decoded = nn(back_ref[...], ut)
    square = decoded * decoded
    sq_acc[...] += jnp.broadcast_to(jnp.sum(square, axis=1, keepdims=True), sq_acc.shape)

    @pl.when(step == pl.num_programs(0) - 1)
    def _():
        for i, piece in enumerate(split(m_acc[...], 2)):
            m_ref[i * rank : (i + 1) * rank, :] = piece
        o_ref[...] = o_acc[...].astype(BF)
        for i, piece in enumerate(split(g_acc[...], 3)):
            g_ref[i * rank : (i + 1) * rank, :] = piece
        inv_ref[...] = inverse_root(sq_acc[...], wide)


def project(back, basis, gain, wq, wk, wv, wo):
    wide, rank = basis.shape
    length = back.shape[0]
    nq, nk, nv, ne = wq.shape[1], wk.shape[1], wv.shape[1], wo.shape[0]
    block = 512
    rows = lambda i: (i, 0)
    cols = lambda i: (0, i)
    fixed = lambda i: (0, 0)
    total = nq + nk + nv
    return pl.pallas_call(
        functools.partial(project_kernel, wide),
        grid=(wide // block,),
        in_specs=[
            pl.BlockSpec((length, rank), fixed),
            pl.BlockSpec((block, rank), rows),
            pl.BlockSpec((1, block), cols),
            pl.BlockSpec((block, nq), rows),
            pl.BlockSpec((block, nk), rows),
            pl.BlockSpec((block, nv), rows),
            pl.BlockSpec((ne, block), cols),
        ],
        out_specs=[
            pl.BlockSpec((2 * rank, total), fixed),
            pl.BlockSpec((ne, rank), fixed),
            pl.BlockSpec((3 * rank, rank), fixed),
            pl.BlockSpec((length, HD), fixed),
        ],
        out_shape=[
            jax.ShapeDtypeStruct((2 * rank, total), BF),
            jax.ShapeDtypeStruct((ne, rank), BF),
            jax.ShapeDtypeStruct((3 * rank, rank), BF),
            jax.ShapeDtypeStruct((length, HD), F32),
        ],
        scratch_shapes=[
            pltpu.VMEM((rank, total), F32),
            pltpu.VMEM((ne, rank), F32),
            pltpu.VMEM((rank, rank), F32),
            pltpu.VMEM((length, HD), F32),
        ],
        compiler_params=pltpu.CompilerParams(vmem_limit_bytes=VMEM_BYTES),
        cost_estimate=cost(2 * wide * rank * (total + ne + 2 * rank), 2 * wide * (total + ne + rank)),
        name="project_weights",
    )(back, basis, gain, wq, wk, wv, wo)


def project_heads(coeffs, inv, m_ref, cosine, sine, q, k, v1):
    length = coeffs.shape[0]
    heads = q.shape[0] // length
    twice = jnp.concatenate([coeffs, coeffs], axis=1)
    for h in range(heads):
        part = nn(twice, m_ref[:, h * HD : (h + 1) * HD]) * inv
        q[h * length : (h + 1) * length, :] = rope(part, cosine, sine).astype(BF)
    part = nn(twice, m_ref[:, heads * HD :]) * inv
    k[...] = rope(part[:, :HD], cosine, sine).astype(BF)
    v1[:, :HD] = part[:, HD:].astype(BF)
    v1[:, HD:] = jnp.ones_like(v1[:, HD:])


def exps_of(scores, exps, low, length):
    row = lax.broadcasted_iota(jnp.int32, (length, length), 0)
    column = lax.broadcasted_iota(jnp.int32, (length, length), 1)
    causal = row >= column

    def one(h, _):
        at = pl.ds(pl.multiple_of(h * length, length), length)
        s = jnp.where(causal, scores[at, :], -jnp.inf)
        top = jnp.max(s, axis=1, keepdims=True)
        e = jnp.exp2((s - top) * (LOG2E / math.sqrt(HD)))
        if exps is not None:
            exps[at, :] = e
        low[at, :] = e.astype(BF)
        return 0

    lax.fori_loop(0, scores.shape[0] // length, one, 0, unroll=2)


def backward_kernel(
    back_ref, loss_ref, sent_ref, m_ref, o_ref, g_ref, inv_ref, cos_ref, sin_ref,
    inner_ref, give_ref, keep_ref, x_ref, base_ref, unit_ref,
    q, k, v1, gh, ghs, scores, low, mixed, gp, ds, dq, heads, grads,
):
    length, rank = back_ref.shape
    ne = o_ref.shape[0]
    count = ne // HD
    scale = 1.0 / math.sqrt(HD)
    last = lax.axis_size("pipe") - 1
    is_last = lax.axis_index("pipe") == last
    back = back_ref[...]
    up = jnp.where(is_last, loss_ref[...], sent_ref[...])
    cosine, sine = cos_ref[...], sin_ref[...]
    inv = inv_ref[...]
    project_heads(back, inv[:, :1], m_ref, cosine, sine, q, k, v1)
    scores[...] = nt(q[...], k[...])
    for h in range(count):
        gh[h * length : (h + 1) * length, :] = nt(up, o_ref[h * HD : (h + 1) * HD, :]).astype(BF)
    exps_of(scores, scores, low, length)
    mixed[...] = nn(low[...], v1[...])
    gp[...] = nt(gh[...], v1[:, :HD])

    for h in range(count):
        at = slice(h * length, (h + 1) * length)
        inverse = 1.0 / mixed[at, HD:]
        out = mixed[at, :HD] * inverse
        heads[:, h * HD : (h + 1) * HD] = out.astype(BF)
        grad = gh[at, :].astype(F32)
        ghs[at, :] = (grad * inverse).astype(BF)
        delta = jnp.sum(grad * out, axis=1, keepdims=True)
        factor = inverse * scale
        for side in range(0, length, HD):
            part = scores[at, side : side + HD] * factor
            ds[at, side : side + HD] = (part * (gp[at, side : side + HD] - delta)).astype(BF)

    dq[...] = nn(ds[...], k[...])
    for h in range(count):
        part = dq[h * length : (h + 1) * length, :]
        grads[:, h * HD : (h + 1) * HD] = unrope(part, cosine, sine).astype(BF)
    dk = nn(q[...].T, ds[...]).T
    grads[:, ne : ne + HD] = unrope(dk, cosine, sine).astype(BF)
    grads[:, ne + HD :] = nn(ghs[...].T, low[...]).T.astype(BF)
    total = grads.shape[1]
    unit = (back.astype(F32) * inv[:, :1]).astype(BF)
    inner_ref[:, :total] = nn(unit.T, grads[...]).astype(BF)
    inner_ref[:, total:] = nn(up.T, heads[...]).astype(BF)
    half = rank // 2
    core = lax.axis_index("dp") % 2
    give_ref[...] = inner_ref[pl.ds(pl.multiple_of((1 - core) * half, half), half), :]
    keep_ref[...] = inner_ref[pl.ds(pl.multiple_of(core * half, half), half), :]
    x_ref[...] = nt(grads[...], m_ref[:rank, :]).astype(BF)
    base_ref[...] = nn(jnp.concatenate([up] * 3, axis=1), g_ref[...])
    unit_ref[...] = nn(jnp.concatenate([back] * 3, axis=1), g_ref[...]) * inv[:, :1]


def backward(back, loss, sent, m2, o2, g3, inv, cosine, sine):
    length, rank = back.shape
    total = m2.shape[1]
    ne = o2.shape[0]
    assert total == ne + 2 * HD
    width = total + ne
    stack = ne // HD * length
    return pl.pallas_call(
        backward_kernel,
        in_specs=vmem(9),
        out_specs=vmem(6),
        out_shape=[
            jax.ShapeDtypeStruct((rank, width), BF),
            jax.ShapeDtypeStruct((rank // 2, width), BF),
            jax.ShapeDtypeStruct((rank // 2, width), BF),
            jax.ShapeDtypeStruct((length, rank), BF),
            jax.ShapeDtypeStruct((length, rank), F32),
            jax.ShapeDtypeStruct((length, rank), F32),
        ],
        scratch_shapes=[
            pltpu.VMEM((stack, HD), BF),
            pltpu.VMEM((length, HD), BF),
            pltpu.VMEM((length, 2 * HD), BF),
            pltpu.VMEM((stack, HD), BF),
            pltpu.VMEM((stack, HD), BF),
            pltpu.VMEM((stack, length), F32),
            pltpu.VMEM((stack, length), BF),
            pltpu.VMEM((stack, 2 * HD), F32),
            pltpu.VMEM((stack, length), F32),
            pltpu.VMEM((stack, length), BF),
            pltpu.VMEM((stack, HD), F32),
            pltpu.VMEM((length, ne), BF),
            pltpu.VMEM((length, total), BF),
        ],
        compiler_params=pltpu.CompilerParams(vmem_limit_bytes=VMEM_BYTES),
        cost_estimate=cost(2 * 1200 * 10**6, 8 * 10**6, 8 * 65536),
        name="attention_backward",
    )(back, loss, sent, m2, o2, g3, inv, cosine, sine)


def forward_kernel(
    new_ref, sent_ref, u_ref, m_ref, o_ref, g_ref, cos_ref, sin_ref,
    y_ref, base_ref,
    q, k, v1, scores, low, mixed, heads,
):
    length, rank = new_ref.shape
    wide = u_ref.shape[0]
    is_first = lax.axis_index("pipe") == 0
    coeffs = jnp.where(is_first, new_ref[...], sent_ref[...])
    square = jnp.zeros((length, HD), F32)
    block = 512
    for at in range(0, wide, block):
        decoded = nt(coeffs, u_ref[at : at + block, :])
        for side in range(0, block, HD):
            part = decoded[:, side : side + HD]
            square = square + part * part
    inv = inverse_root(jnp.sum(square, axis=1, keepdims=True), wide)
    project_heads(coeffs, inv, m_ref, cos_ref[...], sin_ref[...], q, k, v1)
    scores[...] = nt(q[...], k[...])
    exps_of(scores, None, low, length)
    mixed[...] = nn(low[...], v1[...])
    for h in range(heads.shape[1] // HD):
        at = slice(h * length, (h + 1) * length)
        heads[:, h * HD : (h + 1) * HD] = (mixed[at, :HD] / mixed[at, HD:]).astype(BF)
    y_ref[...] = nn(heads[...], o_ref[...]).astype(BF)
    base_ref[...] = nn(jnp.concatenate([coeffs] * 3, axis=1), g_ref[...])


def forward(new, sent, basis, m2, o2, g3, cosine, sine):
    length, rank = new.shape
    ne = o2.shape[0]
    stack = ne // HD * length
    return pl.pallas_call(
        forward_kernel,
        in_specs=vmem(8),
        out_specs=vmem(2),
        out_shape=[
            jax.ShapeDtypeStruct((length, rank), BF),
            jax.ShapeDtypeStruct((length, rank), F32),
        ],
        scratch_shapes=[
            pltpu.VMEM((stack, HD), BF),
            pltpu.VMEM((length, HD), BF),
            pltpu.VMEM((length, 2 * HD), BF),
            pltpu.VMEM((stack, length), F32),
            pltpu.VMEM((stack, length), BF),
            pltpu.VMEM((stack, 2 * HD), F32),
            pltpu.VMEM((length, ne), BF),
        ],
        compiler_params=pltpu.CompilerParams(vmem_limit_bytes=VMEM_BYTES),
        cost_estimate=cost(2 * 900 * 10**6, 6 * 10**6, 8 * 65536),
        name="attention_forward",
    )(new, sent, basis, m2, o2, g3, cosine, sine)


def gain_kernel(u_ref, wq_ref, wk_ref, wv_ref, inner_ref, out_ref, turned):
    nq, nk, nv = wq_ref.shape[1], wk_ref.shape[1], wv_ref.shape[1]

    @pl.when(pl.program_id(0) == 0)
    def _():
        turned[...] = inner_ref[:, : nq + nk + nv].T

    against = nn(wq_ref[...], turned[:nq, :])
    against += nn(wk_ref[...], turned[nq : nq + nk, :])
    against += nn(wv_ref[...], turned[nq + nk :, :])
    terms = against * u_ref[...].astype(F32)
    folded = sum(terms[:, at : at + HD] for at in range(0, terms.shape[1], HD))
    out_ref[...] = jnp.sum(folded.T, axis=0, keepdims=True)


def gain_part(basis, wq, wk, wv, inner):
    wide, rank = basis.shape
    nq, nk, nv = wq.shape[1], wk.shape[1], wv.shape[1]
    block = 512
    rows = lambda i: (i, 0)
    return pl.pallas_call(
        gain_kernel,
        grid=(wide // block,),
        in_specs=[
            pl.BlockSpec((block, rank), rows),
            pl.BlockSpec((block, nq), rows),
            pl.BlockSpec((block, nk), rows),
            pl.BlockSpec((block, nv), rows),
            pl.BlockSpec(inner.shape, lambda i: (0, 0)),
        ],
        out_specs=pl.BlockSpec((1, block), lambda i: (0, i)),
        scratch_shapes=[pltpu.VMEM((nq + nk + nv, rank), BF)],
        out_shape=jax.ShapeDtypeStruct((1, wide), F32),
        compiler_params=pltpu.CompilerParams(vmem_limit_bytes=VMEM_BYTES),
        cost_estimate=cost(2 * wide * rank * (nq + nk + nv), 2 * wide * (nq + nk + nv + rank)),
        name="gain_gradient",
    )(basis, wq, wk, wv, inner)


def gather_halves(own_ref, other_ref, whole):
    half = own_ref.shape[0]
    core = lax.axis_index("dp") % 2
    whole[pl.ds(pl.multiple_of(core * half, half), half), :] = own_ref[...]
    whole[pl.ds(pl.multiple_of((1 - core) * half, half), half), :] = other_ref[...]


def inward_kernel(me_ref, u_ref, gain_ref, own_ref, other_ref, q_ref, k_ref, v_ref, inner):
    nq, nk = q_ref.shape[1], k_ref.shape[1]
    block = q_ref.shape[0]

    @pl.when(pl.program_id(0) == 0)
    def _():
        gather_halves(own_ref, other_ref, inner)

    gain = jnp.broadcast_to(gain_ref[...], (HD, block)).T[:, :1]
    grad = nn(u_ref[...], inner[...]) * gain
    q_ref[...] = grad[:, :nq].astype(BF)
    k_ref[...] = grad[:, nq : nq + nk].astype(BF)
    v_ref[...] = grad[:, nq + nk :].astype(BF)


def outward_kernel(me_ref, u_ref, own_ref, other_ref, o_ref, inner):
    @pl.when(pl.program_id(0) == 0)
    def _():
        gather_halves(own_ref, other_ref, inner)

    block = o_ref.shape[0]
    at = pl.multiple_of(pl.program_id(0) * block, block)
    o_ref[...] = nt(inner[:, pl.ds(at, block)].T, u_ref[...]).astype(BF)


STEPS = 4


def my_part():
    return lax.axis_index("dp").astype(jnp.int32).reshape(1)


def inward_grads(basis, gain, own, other, sizes):
    wide, rank = basis.shape
    rows = wide // lax.axis_size("dp")
    block = rows // STEPS
    fixed = lambda i, me: (0, 0)
    step_rows = lambda i, me: (i, 0)
    return pl.pallas_call(
        inward_kernel,
        grid_spec=pltpu.PrefetchScalarGridSpec(
            num_scalar_prefetch=1,
            grid=(STEPS,),
            in_specs=[
                pl.BlockSpec((block, rank), lambda i, me: (me[0] * STEPS + i, 0)),
                pl.BlockSpec((1, block), lambda i, me: (0, me[0] * STEPS + i)),
                pl.BlockSpec(own.shape, fixed),
                pl.BlockSpec(other.shape, fixed),
            ],
            out_specs=[pl.BlockSpec((block, n), step_rows) for n in sizes],
            scratch_shapes=[pltpu.VMEM((rank, sum(sizes)), BF)],
        ),
        out_shape=[jax.ShapeDtypeStruct((rows, n), BF) for n in sizes],
        compiler_params=pltpu.CompilerParams(vmem_limit_bytes=VMEM_BYTES),
        cost_estimate=cost(2 * rows * rank * sum(sizes), 4 * 10**6),
        name="inward_weight_gradients",
    )(my_part(), basis, gain, own, other)


def outward_grad(basis, own, other):
    wide, rank = basis.shape
    rows = wide // lax.axis_size("dp")
    ne = own.shape[1]
    fixed = lambda i, me: (0, 0)
    return pl.pallas_call(
        outward_kernel,
        grid_spec=pltpu.PrefetchScalarGridSpec(
            num_scalar_prefetch=1,
            grid=(STEPS,),
            in_specs=[
                pl.BlockSpec((rows, rank), lambda i, me: (me[0], 0)),
                pl.BlockSpec(own.shape, fixed),
                pl.BlockSpec(other.shape, fixed),
            ],
            out_specs=pl.BlockSpec((ne // STEPS, rows), lambda i, me: (i, 0)),
            scratch_shapes=[pltpu.VMEM((rank, ne), BF)],
        ),
        out_shape=jax.ShapeDtypeStruct((ne, rows), BF),
        compiler_params=pltpu.CompilerParams(vmem_limit_bytes=VMEM_BYTES),
        cost_estimate=cost(2 * rows * rank * ne, 3 * 10**6),
        name="output_weight_gradient",
    )(my_part(), basis, own, other)


def results_kernel(
    wide, fbase_ref, y_ref, ygot_ref, base_ref, unit_ref, x_ref, xgot_ref, back_ref, inv_ref,
    f_ref, b_ref,
):
    f_ref[...] = (fbase_ref[...] + add_wide(y_ref[...], ygot_ref[...])).astype(BF)
    x = add_wide(x_ref[...], xgot_ref[...])
    inv = inv_ref[:, :1]
    along = jnp.sum(x * back_ref[...].astype(F32), axis=1, keepdims=True)
    middle = along * inv * (1.0 / wide)
    b_ref[...] = (base_ref[...] + (x - unit_ref[...] * middle) * inv).astype(BF)


def results(wide, *operands):
    shape = operands[0].shape
    return pl.pallas_call(
        functools.partial(results_kernel, wide),
        in_specs=vmem(len(operands)),
        out_specs=vmem(2),
        out_shape=[jax.ShapeDtypeStruct(shape, BF)] * 2,
        compiler_params=pltpu.CompilerParams(vmem_limit_bytes=VMEM_BYTES),
        cost_estimate=cost(10**6, 2 * 10**6),
        name="section_results",
    )(*operands)


def body(
    new_coeffs,
    loss_grad,
    sent_forward,
    sent_backward,
    stashed,
    subspace,
    norm_gain,
    w_query,
    w_key,
    w_value,
    w_output,
):
    wide = subspace.shape[0]
    wq, wk, wv, wo = w_query[0], w_key[0], w_value[0], w_output[0]
    nq, nk, nv = wq.shape[1], wk.shape[1], wv.shape[1]
    back = stashed[0]
    arrived, returned = cross_pipe(sent_forward[0], sent_backward[0])
    cosine, sine = rope_tables(back.shape[0])

    m2, o2, g3, inv = project(back, subspace, norm_gain, wq, wk, wv, wo)
    inner, give, keep, x, base, unit = backward(
        back, loss_grad, returned, m2, o2, g3, inv, cosine, sine
    )
    total = nq + nk + nv
    got = swap(give, "dp", 1)
    x_got = swap(x, "tensor", 1)
    y, fbase = forward(new_coeffs, arrived, subspace, m2, o2, g3, cosine, sine)
    pair_out = add_wide(keep[:, total:], got[:, total:]).astype(BF)
    pair_in = add_wide(keep[:, :total], got[:, :total]).astype(BF)
    got_out = swap(pair_out, "dp", 2)
    got_in = swap(pair_in, "dp", 2)
    y_got = swap(y, "tensor", 1)
    x = add_wide(x, x_got).astype(BF)
    x_got = swap(x, "tensor", 2)
    gain = gain_part(subspace, wq, wk, wv, inner)
    y = add_wide(y, y_got).astype(BF)
    y_got = swap(y, "tensor", 2)
    gain = gain + swap(gain, "tensor", 1)
    gain = gain + swap(gain, "tensor", 2)
    gain = gain + swap(gain, "dp", 1)
    gain = gain + swap(gain, "dp", 2)

    own = add_wide(pair_out, got_out).astype(BF)
    grad_o = outward_grad(subspace, own, swap(own, "dp", 1))
    forward_out, backward_out = results(
        wide, fbase, y, y_got, base, unit, x, x_got, back, inv
    )
    own = add_wide(pair_in, got_in).astype(BF)
    grad_q, grad_k, grad_v = inward_grads(
        subspace, norm_gain, own, swap(own, "dp", 1), (nq, nk, nv)
    )
    return (
        forward_out[None],
        backward_out[None],
        grad_q[None],
        grad_k[None],
        grad_v[None],
        grad_o[None],
        gain,
    )


def solution(mesh):
    return jax.shard_map(
        body,
        mesh=mesh,
        in_specs=(
            P("dp", None),
            P("dp", None),
            P("pipe", "dp", None),
            P("pipe", "dp", None),
            P("pipe", "dp", None),
            P(),
            P("pipe", None),
            P("pipe", None, "tensor"),
            P("pipe", None, "tensor"),
            P("pipe", None, "tensor"),
            P("pipe", "tensor", None),
        ),
        out_specs=(
            P("pipe", "dp", None),
            P("pipe", "dp", None),
            P("pipe", "dp", "tensor"),
            P("pipe", "dp", "tensor"),
            P("pipe", "dp", "tensor"),
            P("pipe", "tensor", "dp"),
            P("pipe", None),
        ),
        check_vma=False,
    )
```

```python
import functools
import math

import jax
import jax.numpy as jnp
import numpy as np
from jax import lax
from jax.experimental import pallas as pl
from jax.experimental.pallas import tpu as pltpu
from jax.sharding import PartitionSpec as P

HD = 128
EPSILON = 1e-05
ROPE_BASE = 500000.0
BF = jnp.bfloat16
F32 = jnp.float32
VMEM_BYTES = 24 * 1024 * 1024
PIECE = 512
LOG2E = 1.4426950408889634


def shifted(x, axis, by):
    devices = lax.axis_size(axis)
    pairs = [(i, i + by) for i in range(devices) if 0 <= i + by < devices]
    return lax.ppermute(x, axis, pairs)


def swap(x, axis, bit):
    devices = lax.axis_size(axis)
    return lax.ppermute(x, axis, [(i, i ^ bit) for i in range(devices)])


def cross_pipe(sent_forward, sent_backward):
    if lax.axis_size("pipe") != 2:
        return shifted(sent_forward, "pipe", 1), shifted(sent_backward, "pipe", -1)
    first = lax.axis_index("pipe") == 0
    got = swap(jnp.where(first, sent_forward, sent_backward), "pipe", 1)
    return got, got


def add_wide(a, b):
    return a.astype(F32) + b.astype(F32)


def nt(a, b):
    return lax.dot_general(a, b, (((1,), (1,)), ((), ())), preferred_element_type=F32)


def nn(a, b):
    return jnp.dot(a, b, preferred_element_type=F32)


def split(x, parts):
    out = []
    for _ in range(parts):
        piece = x.astype(BF)
        out.append(piece)
        x = x - piece.astype(F32)
    return out


def rope_tables(length):
    half = HD // 2
    frequency = np.float32(ROPE_BASE) ** (-2.0 * np.arange(half, dtype=np.float32) / HD)
    angles = np.arange(length, dtype=np.float32)[:, None] * frequency.astype(np.float32)
    cosine, sine = np.cos(angles), np.sin(angles)
    tables = (np.concatenate([cosine, cosine], 1), np.concatenate([-sine, sine], 1))
    return tuple(jnp.asarray(t, dtype=F32) for t in tables)


def rope(x, cosine, sine):
    return x * cosine + pltpu.roll(x, HD // 2, 1) * sine


def unrope(x, cosine, sine):
    return x * cosine - pltpu.roll(x, HD // 2, 1) * sine


def inverse_root(square_sum, width):
    return 1.0 / jnp.sqrt(square_sum / width + EPSILON)


def vmem(count):
    return [pl.BlockSpec(memory_space=pltpu.VMEM)] * count


def in_hbm(arrays):
    return tuple(pltpu.with_memory_space_constraint(a, pltpu.HBM) for a in arrays)


def cost(flops, num_bytes, exps=0):
    return pl.CostEstimate(flops=flops, bytes_accessed=num_bytes, transcendentals=exps)


def streamed(pairs, sems, steps, ahead, work):
    def copies(i):
        out = []
        for n, (source, target, axis) in enumerate(pairs):
            size = source.shape[axis] // steps
            at = pl.ds(pl.multiple_of(i * size, size), size)
            index = (at, slice(None)) if axis == 0 else (slice(None), at)
            out.append(pltpu.make_async_copy(source.at[index], target.at[index], sems.at[n, i]))
        return out

    for i in range(ahead):
        for copy in copies(i):
            copy.start()

    def one(i, _):
        @pl.when(i + ahead < steps)
        def _():
            for copy in copies(i + ahead):
                copy.start()

        for copy in copies(i):
            copy.wait()
        work(i)
        return 0

    lax.fori_loop(0, steps, one, 0)


def project(
    wide, back, u_ref, gain_ref, wq_ref, wk_ref, wv_ref, wo_ref, sems,
    m_ref, o_ref, g_ref, u, wq, wk, wv, wo, m_acc, o_acc, g_acc, square,
):
    rank = u.shape[1]
    nq, nk = wq.shape[1], wk.shape[1]
    steps = wide // 1024
    block = wide // steps
    m_acc[...] = jnp.zeros_like(m_acc)
    o_acc[...] = jnp.zeros_like(o_acc)
    g_acc[...] = jnp.zeros_like(g_acc)
    square[...] = jnp.zeros_like(square)

    def work(i):
        rows = pl.ds(pl.multiple_of(i * block, block), block)
        basis = u[rows, :]
        turned = basis.T
        scaled = (turned.astype(F32) * gain_ref[:, rows]).astype(BF)
        for ref, at in ((wq, 0), (wk, nq), (wv, nq + nk)):
            size = ref.shape[1]
            m_acc[:, at : at + size] += nn(scaled, ref[rows, :])
        o_acc[...] += nn(wo[:, rows], basis)
        g_acc[...] += nn(turned, basis)
        decoded = nn(back, turned)
        total = square[...]
        for side in range(0, block, HD):
            part = decoded[:, side : side + HD]
            total = total + part * part
        square[...] = total

    pairs = ((u_ref, u, 0), (wq_ref, wq, 0), (wk_ref, wk, 0), (wv_ref, wv, 0), (wo_ref, wo, 1))
    streamed(pairs, sems, steps, 2, work)
    for i, piece in enumerate(split(m_acc[...], 2)):
        m_ref[i * rank : (i + 1) * rank, :] = piece
    o_ref[...] = o_acc[...].astype(BF)
    for i, piece in enumerate(split(g_acc[...], 3)):
        g_ref[i * rank : (i + 1) * rank, :] = piece


def project_heads(coeffs, inv, m_ref, cosine, sine, q, k, v1):
    length = coeffs.shape[0]
    heads = q.shape[0] // length
    twice = jnp.concatenate([coeffs, coeffs], axis=1)
    for h in range(heads):
        part = nn(twice, m_ref[:, h * HD : (h + 1) * HD]) * inv
        q[h * length : (h + 1) * length, :] = rope(part, cosine, sine).astype(BF)
    part = nn(twice, m_ref[:, heads * HD :]) * inv
    k[...] = rope(part[:, :HD], cosine, sine).astype(BF)
    v1[:, :HD] = part[:, HD:].astype(BF)
    v1[:, HD:] = jnp.ones_like(v1[:, HD:])


def exps_of(scores, exps, low, length):
    row = lax.broadcasted_iota(jnp.int32, (length, length), 0)
    column = lax.broadcasted_iota(jnp.int32, (length, length), 1)
    causal = row >= column

    def one(h, _):
        at = pl.ds(pl.multiple_of(h * length, length), length)
        s = jnp.where(causal, scores[at, :], -jnp.inf)
        top = jnp.max(s, axis=1, keepdims=True)
        e = jnp.exp2((s - top) * (LOG2E / math.sqrt(HD)))
        if exps is not None:
            exps[at, :] = e
        low[at, :] = e.astype(BF)
        return 0

    lax.fori_loop(0, scores.shape[0] // length, one, 0, unroll=2)


def backward_kernel(
    sent_ref, back_hbm, loss_hbm, gain_hbm, cos_hbm, sin_hbm,
    u_ref, wq_ref, wk_ref, wv_ref, wo_ref,
    inner_ref, give_ref, keep_ref, x_ref, base_ref, unit_ref, inv_ref, m_ref, o_ref, g_ref,
    back_ref, loss_ref, gain_ref, cos_ref, sin_ref, small_sems,
    u, wq, wk, wv, wo, m_acc, o_acc, g_acc, square, sems,
    q, k, v1, gh, ghs, scores, low, mixed, gp, ds, dq, heads, grads,
):
    length, rank = back_ref.shape
    wide = u_ref.shape[0]
    sources = (back_hbm, gain_hbm, loss_hbm, cos_hbm, sin_hbm)
    targets = (back_ref, gain_ref, loss_ref, cos_ref, sin_ref)
    small = [
        pltpu.make_async_copy(source, target, small_sems.at[n])
        for n, (source, target) in enumerate(zip(sources, targets))
    ]
    for copy in small:
        copy.start()
    for copy in small[:2]:
        copy.wait()
    project(
        wide, back_ref[...], u_ref, gain_ref, wq_ref, wk_ref, wv_ref, wo_ref, sems,
        m_ref, o_ref, g_ref, u, wq, wk, wv, wo, m_acc, o_acc, g_acc, square,
    )
    for copy in small[2:]:
        copy.wait()
    inv_ref[...] = jnp.broadcast_to(
        inverse_root(jnp.sum(square[...], axis=1, keepdims=True), wide), inv_ref.shape
    )
    ne = o_ref.shape[0]
    count = ne // HD
    scale = 1.0 / math.sqrt(HD)
    last = lax.axis_size("pipe") - 1
    is_last = lax.axis_index("pipe") == last
    back = back_ref[...]
    up = jnp.where(is_last, loss_ref[...], sent_ref[...])
    cosine, sine = cos_ref[...], sin_ref[...]
    inv = inv_ref[...]
    project_heads(back, inv[:, :1], m_ref, cosine, sine, q, k, v1)
    scores[...] = nt(q[...], k[...])
    for h in range(count):
        gh[h * length : (h + 1) * length, :] = nt(up, o_ref[h * HD : (h + 1) * HD, :]).astype(BF)
    exps_of(scores, scores, low, length)
    mixed[...] = nn(low[...], v1[...])
    gp[...] = nt(gh[...], v1[:, :HD])

    for h in range(count):
        at = slice(h * length, (h + 1) * length)
        inverse = 1.0 / mixed[at, HD:]
        out = mixed[at, :HD] * inverse
        heads[:, h * HD : (h + 1) * HD] = out.astype(BF)
        grad = gh[at, :].astype(F32)
        ghs[at, :] = (grad * inverse).astype(BF)
        delta = jnp.sum(grad * out, axis=1, keepdims=True)
        factor = inverse * scale
        for side in range(0, length, HD):
            part = scores[at, side : side + HD] * factor
            ds[at, side : side + HD] = (part * (gp[at, side : side + HD] - delta)).astype(BF)

    dq[...] = nn(ds[...], k[...])
    for h in range(count):
        part = dq[h * length : (h + 1) * length, :]
        grads[:, h * HD : (h + 1) * HD] = unrope(part, cosine, sine).astype(BF)
    dk = nn(q[...].T, ds[...]).T
    grads[:, ne : ne + HD] = unrope(dk, cosine, sine).astype(BF)
    grads[:, ne + HD :] = nn(ghs[...].T, low[...]).T.astype(BF)
    total = grads.shape[1]
    unit = (back.astype(F32) * inv[:, :1]).astype(BF)
    inner_ref[:, :total] = nn(unit.T, grads[...]).astype(BF)
    inner_ref[:, total:] = nn(up.T, heads[...]).astype(BF)
    half = rank // 2
    core = lax.axis_index("dp") % 2
    give_ref[...] = inner_ref[pl.ds(pl.multiple_of((1 - core) * half, half), half), :]
    keep_ref[...] = inner_ref[pl.ds(pl.multiple_of(core * half, half), half), :]
    x_ref[...] = nt(grads[...], m_ref[:rank, :]).astype(BF)
    base_ref[...] = nn(jnp.concatenate([up] * 3, axis=1), g_ref[...])
    unit_ref[...] = nn(jnp.concatenate([back] * 3, axis=1), g_ref[...]) * inv[:, :1]


def backward(back, loss, sent, gain, cosine, sine, basis, wq, wk, wv, wo):
    length, rank = back.shape
    wide = basis.shape[0]
    ne = wo.shape[0]
    total = wq.shape[1] + wk.shape[1] + wv.shape[1]
    assert total == ne + 2 * HD
    width = total + ne
    stack = ne // HD * length
    weights = in_hbm((basis, wq, wk, wv, wo))
    small = in_hbm((back, loss, gain, cosine, sine))
    return pl.pallas_call(
        backward_kernel,
        in_specs=vmem(1) + [pl.BlockSpec(memory_space=pltpu.HBM)] * len(small + weights),
        out_specs=vmem(10),
        out_shape=[
            jax.ShapeDtypeStruct((rank, width), BF),
            jax.ShapeDtypeStruct((rank // 2, width), BF),
            jax.ShapeDtypeStruct((rank // 2, width), BF),
            jax.ShapeDtypeStruct((length, rank), BF),
            jax.ShapeDtypeStruct((length, rank), F32),
            jax.ShapeDtypeStruct((length, rank), F32),
            jax.ShapeDtypeStruct((length, HD), F32),
            jax.ShapeDtypeStruct((2 * rank, total), BF),
            jax.ShapeDtypeStruct((ne, rank), BF),
            jax.ShapeDtypeStruct((3 * rank, rank), BF),
        ],
        scratch_shapes=[pltpu.VMEM(a.shape, a.dtype) for a in small]
        + [pltpu.SemaphoreType.DMA((len(small),))]
        + [pltpu.VMEM(w.shape, BF) for w in weights]
        + [
            pltpu.VMEM((rank, total), F32),
            pltpu.VMEM((ne, rank), F32),
            pltpu.VMEM((rank, rank), F32),
            pltpu.VMEM((length, HD), F32),
            pltpu.SemaphoreType.DMA((len(weights), wide // 1024)),
            pltpu.VMEM((stack, HD), BF),
            pltpu.VMEM((length, HD), BF),
            pltpu.VMEM((length, 2 * HD), BF),
            pltpu.VMEM((stack, HD), BF),
            pltpu.VMEM((stack, HD), BF),
            pltpu.VMEM((stack, length), F32),
            pltpu.VMEM((stack, length), BF),
            pltpu.VMEM((stack, 2 * HD), F32),
            pltpu.VMEM((stack, length), F32),
            pltpu.VMEM((stack, length), BF),
            pltpu.VMEM((stack, HD), F32),
            pltpu.VMEM((length, ne), BF),
            pltpu.VMEM((length, total), BF),
        ],
        compiler_params=pltpu.CompilerParams(vmem_limit_bytes=2 * VMEM_BYTES),
        cost_estimate=cost(8 * 10**9, 30 * 10**6, 8 * 65536),
        name="project_and_backward",
    )(sent, *small, *weights)


def forward_kernel(
    new_ref, sent_ref, u_ref, m_ref, o_ref, g_ref, cos_ref, sin_ref, *rest,
):
    y_ref, base_ref, q, k, v1, scores, low, mixed, heads = rest[-9:]
    length, rank = new_ref.shape
    wide = u_ref.shape[0]
    is_first = lax.axis_index("pipe") == 0
    coeffs = jnp.where(is_first, new_ref[...], sent_ref[...])
    square = jnp.zeros((length, HD), F32)
    block = 512
    for at in range(0, wide, block):
        decoded = nt(coeffs, u_ref[at : at + block, :])
        for side in range(0, block, HD):
            part = decoded[:, side : side + HD]
            square = square + part * part
    inv = inverse_root(jnp.sum(square, axis=1, keepdims=True), wide)
    project_heads(coeffs, inv, m_ref, cos_ref[...], sin_ref[...], q, k, v1)
    scores[...] = nt(q[...], k[...])
    exps_of(scores, None, low, length)
    mixed[...] = nn(low[...], v1[...])
    for h in range(heads.shape[1] // HD):
        at = slice(h * length, (h + 1) * length)
        heads[:, h * HD : (h + 1) * HD] = (mixed[at, :HD] / mixed[at, HD:]).astype(BF)
    y_ref[...] = nn(heads[...], o_ref[...]).astype(BF)
    base_ref[...] = nn(jnp.concatenate([coeffs] * 3, axis=1), g_ref[...])


def forward(new, sent, basis, m2, o2, g3, cosine, sine, *after):
    length, rank = new.shape
    ne = o2.shape[0]
    stack = ne // HD * length
    return pl.pallas_call(
        forward_kernel,
        in_specs=vmem(8) + [pl.BlockSpec(memory_space=pl.ANY)] * len(after),
        out_specs=vmem(2),
        out_shape=[
            jax.ShapeDtypeStruct((length, rank), BF),
            jax.ShapeDtypeStruct((length, rank), F32),
        ],
        scratch_shapes=[
            pltpu.VMEM((stack, HD), BF),
            pltpu.VMEM((length, HD), BF),
            pltpu.VMEM((length, 2 * HD), BF),
            pltpu.VMEM((stack, length), F32),
            pltpu.VMEM((stack, length), BF),
            pltpu.VMEM((stack, 2 * HD), F32),
            pltpu.VMEM((length, ne), BF),
        ],
        compiler_params=pltpu.CompilerParams(vmem_limit_bytes=VMEM_BYTES),
        cost_estimate=cost(10**8, 10**6),
        name="attention_forward",
    )(new, sent, basis, m2, o2, g3, cosine, sine, *after)


def gain_kernel(u_ref, wq_ref, wk_ref, wv_ref, inner_ref, out_ref, u, wq, wk, wv, turned, sems):
    nq, nk, nv = wq.shape[1], wk.shape[1], wv.shape[1]
    wide = u.shape[0]
    steps = wide // PIECE

    def work(i):
        @pl.when(i == 0)
        def _():
            turned[...] = inner_ref[:, : nq + nk + nv].T

        rows = pl.ds(pl.multiple_of(i * PIECE, PIECE), PIECE)
        against = nn(wq[rows, :], turned[:nq, :])
        against += nn(wk[rows, :], turned[nq : nq + nk, :])
        against += nn(wv[rows, :], turned[nq + nk :, :])
        terms = against * u[rows, :].astype(F32)
        folded = sum(terms[:, at : at + HD] for at in range(0, terms.shape[1], HD))
        out_ref[:, rows] = jnp.sum(folded.T, axis=0, keepdims=True)

    pairs = ((u_ref, u, 0), (wq_ref, wq, 0), (wk_ref, wk, 0), (wv_ref, wv, 0))
    streamed(pairs, sems, steps, 3, work)


def gain_part(basis, wq, wk, wv, inner):
    wide, rank = basis.shape
    weights = in_hbm((basis, wq, wk, wv))
    total = wq.shape[1] + wk.shape[1] + wv.shape[1]
    return pl.pallas_call(
        gain_kernel,
        in_specs=[pl.BlockSpec(memory_space=pltpu.HBM)] * len(weights) + vmem(1),
        out_specs=pl.BlockSpec(memory_space=pltpu.VMEM),
        out_shape=jax.ShapeDtypeStruct((1, wide), F32),
        scratch_shapes=[pltpu.VMEM(w.shape, BF) for w in weights]
        + [
            pltpu.VMEM((total, rank), BF),
            pltpu.SemaphoreType.DMA((len(weights), wide // PIECE)),
        ],
        compiler_params=pltpu.CompilerParams(vmem_limit_bytes=VMEM_BYTES),
        cost_estimate=cost(10**8, 10**6),
        name="gain_gradient",
    )(*weights, inner)


def gather_halves(own_ref, other_ref, whole):
    half = own_ref.shape[0]
    core = lax.axis_index("dp") % 2
    whole[pl.ds(pl.multiple_of(core * half, half), half), :] = own_ref[...]
    whole[pl.ds(pl.multiple_of((1 - core) * half, half), half), :] = other_ref[...]


def inward_kernel(me_ref, u_ref, gain_ref, own_ref, other_ref, after, q_ref, k_ref, v_ref, inner):
    nq, nk = q_ref.shape[1], k_ref.shape[1]
    block = q_ref.shape[0]

    @pl.when(pl.program_id(0) == 0)
    def _():
        gather_halves(own_ref, other_ref, inner)

    gain = jnp.broadcast_to(gain_ref[...], (HD, block)).T[:, :1]
    grad = nn(u_ref[...], inner[...]) * gain
    q_ref[...] = grad[:, :nq].astype(BF)
    k_ref[...] = grad[:, nq : nq + nk].astype(BF)
    v_ref[...] = grad[:, nq + nk :].astype(BF)


def outward_kernel(me_ref, u_ref, own_ref, other_ref, after, o_ref, inner):
    @pl.when(pl.program_id(0) == 0)
    def _():
        gather_halves(own_ref, other_ref, inner)

    block = o_ref.shape[0]
    at = pl.multiple_of(pl.program_id(0) * block, block)
    o_ref[...] = nt(inner[:, pl.ds(at, block)].T, u_ref[...]).astype(BF)


STEPS = 4


def my_part():
    return lax.axis_index("dp").astype(jnp.int32).reshape(1)


def inward_grads(basis, gain, own, other, sizes, after):
    wide, rank = basis.shape
    rows = wide // lax.axis_size("dp")
    block = rows // STEPS
    fixed = lambda i, me: (0, 0)
    step_rows = lambda i, me: (i, 0)
    return pl.pallas_call(
        inward_kernel,
        grid_spec=pltpu.PrefetchScalarGridSpec(
            num_scalar_prefetch=1,
            grid=(STEPS,),
            in_specs=[
                pl.BlockSpec((block, rank), lambda i, me: (me[0] * STEPS + i, 0)),
                pl.BlockSpec((1, block), lambda i, me: (0, me[0] * STEPS + i)),
                pl.BlockSpec(own.shape, fixed),
                pl.BlockSpec(other.shape, fixed),
                pl.BlockSpec(memory_space=pl.ANY),
            ],
            out_specs=[pl.BlockSpec((block, n), step_rows) for n in sizes],
            scratch_shapes=[pltpu.VMEM((rank, sum(sizes)), BF)],
        ),
        out_shape=[jax.ShapeDtypeStruct((rows, n), BF) for n in sizes],
        compiler_params=pltpu.CompilerParams(vmem_limit_bytes=VMEM_BYTES),
        cost_estimate=cost(10**8, 10**6),
        name="inward_weight_gradients",
    )(my_part(), basis, gain, own, other, after)


def outward_grad(basis, own, other, after):
    wide, rank = basis.shape
    rows = wide // lax.axis_size("dp")
    ne = own.shape[1]
    fixed = lambda i, me: (0, 0)
    return pl.pallas_call(
        outward_kernel,
        grid_spec=pltpu.PrefetchScalarGridSpec(
            num_scalar_prefetch=1,
            grid=(STEPS,),
            in_specs=[
                pl.BlockSpec((rows, rank), lambda i, me: (me[0], 0)),
                pl.BlockSpec(own.shape, fixed),
                pl.BlockSpec(other.shape, fixed),
                pl.BlockSpec(memory_space=pl.ANY),
            ],
            out_specs=pl.BlockSpec((ne // STEPS, rows), lambda i, me: (i, 0)),
            scratch_shapes=[pltpu.VMEM((rank, ne), BF)],
        ),
        out_shape=jax.ShapeDtypeStruct((ne, rows), BF),
        compiler_params=pltpu.CompilerParams(vmem_limit_bytes=VMEM_BYTES),
        cost_estimate=cost(10**8, 10**6),
        name="output_weight_gradient",
    )(my_part(), basis, own, other, after)


def results_kernel(
    wide, fbase_ref, y_ref, ygot_ref, base_ref, unit_ref, x_ref, xgot_ref, back_ref, inv_ref,
    f_ref, b_ref,
):
    f_ref[...] = (fbase_ref[...] + add_wide(y_ref[...], ygot_ref[...])).astype(BF)
    x = add_wide(x_ref[...], xgot_ref[...])
    inv = inv_ref[:, :1]
    along = jnp.sum(x * back_ref[...].astype(F32), axis=1, keepdims=True)
    middle = along * inv * (1.0 / wide)
    b_ref[...] = (base_ref[...] + (x - unit_ref[...] * middle) * inv).astype(BF)


def results(wide, *operands):
    shape = operands[0].shape
    return pl.pallas_call(
        functools.partial(results_kernel, wide),
        in_specs=vmem(len(operands)),
        out_specs=vmem(2),
        out_shape=[jax.ShapeDtypeStruct(shape, BF)] * 2,
        compiler_params=pltpu.CompilerParams(vmem_limit_bytes=VMEM_BYTES),
        cost_estimate=cost(10**8, 10**6),
        name="section_results",
    )(*operands)


def body(
    new_coeffs,
    loss_grad,
    sent_forward,
    sent_backward,
    stashed,
    subspace,
    norm_gain,
    w_query,
    w_key,
    w_value,
    w_output,
):
    wide = subspace.shape[0]
    wq, wk, wv, wo = w_query[0], w_key[0], w_value[0], w_output[0]
    nq, nk, nv = wq.shape[1], wk.shape[1], wv.shape[1]
    back = stashed[0]
    arrived, returned = cross_pipe(sent_forward[0], sent_backward[0])
    cosine, sine = rope_tables(back.shape[0])

    inner, give, keep, x, base, unit, inv, m2, o2, g3 = backward(
        back, loss_grad, returned, norm_gain, cosine, sine, subspace, wq, wk, wv, wo
    )
    total = nq + nk + nv
    got = swap(give, "dp", 1)
    x_got = swap(x, "tensor", 1)
    gain = gain_part(subspace, wq, wk, wv, inner)
    pair_out = add_wide(keep[:, total:], got[:, total:]).astype(BF)
    pair_in = add_wide(keep[:, :total], got[:, :total]).astype(BF)
    got_out = swap(pair_out, "dp", 2)
    got_in = swap(pair_in, "dp", 2)
    x = add_wide(x, x_got).astype(BF)
    x_got = swap(x, "tensor", 2)
    y, fbase = forward(
        new_coeffs, arrived, subspace, m2, o2, g3, cosine, sine, gain, pair_out, pair_in, x
    )
    gain = gain + swap(gain, "tensor", 1)
    gain_two = gain + swap(gain, "tensor", 2)
    gain_three = gain_two + swap(gain_two, "dp", 1)
    gain_sum = gain_three + swap(gain_three, "dp", 2)
    y = add_wide(y, swap(y, "tensor", 1)).astype(BF)
    y_got = swap(y, "tensor", 2)

    own = add_wide(pair_out, got_out).astype(BF)
    grad_o = outward_grad(subspace, own, swap(own, "dp", 1), gain)
    forward_out, backward_out = results(
        wide, fbase, y, y_got, base, unit, x, x_got, back, inv
    )
    own = add_wide(pair_in, got_in).astype(BF)
    grad_q, grad_k, grad_v = inward_grads(
        subspace, norm_gain, own, swap(own, "dp", 1), (nq, nk, nv), gain_three
    )
    return (
        forward_out[None],
        backward_out[None],
        grad_q[None],
        grad_k[None],
        grad_v[None],
        grad_o[None],
        gain_sum,
    )


def solution(mesh):
    return jax.shard_map(
        body,
        mesh=mesh,
        in_specs=(
            P("dp", None),
            P("dp", None),
            P("pipe", "dp", None),
            P("pipe", "dp", None),
            P("pipe", "dp", None),
            P(),
            P("pipe", None),
            P("pipe", None, "tensor"),
            P("pipe", None, "tensor"),
            P("pipe", None, "tensor"),
            P("pipe", "tensor", None),
        ),
        out_specs=(
            P("pipe", "dp", None),
            P("pipe", "dp", None),
            P("pipe", "dp", "tensor"),
            P("pipe", "dp", "tensor"),
            P("pipe", "dp", "tensor"),
            P("pipe", "tensor", "dp"),
            P("pipe", None),
        ),
        check_vma=False,
    )
```

```python
import functools
import math

import jax
import jax.numpy as jnp
import numpy as np
from jax import lax
from jax.experimental import pallas as pl
from jax.experimental.pallas import tpu as pltpu
from jax.sharding import PartitionSpec as P

HD = 128
EPSILON = 1e-05
ROPE_BASE = 500000.0
BF = jnp.bfloat16
F32 = jnp.float32
VMEM_BYTES = 24 * 1024 * 1024
CHUNK = 512
LOG2E = 1.4426950408889634


def shifted(x, axis, by):
    devices = lax.axis_size(axis)
    pairs = [(i, i + by) for i in range(devices) if 0 <= i + by < devices]
    return lax.ppermute(x, axis, pairs)


def swap(x, axis, bit):
    devices = lax.axis_size(axis)
    return lax.ppermute(x, axis, [(i, i ^ bit) for i in range(devices)])


def cross_pipe(sent_forward, sent_backward):
    if lax.axis_size("pipe") != 2:
        return shifted(sent_forward, "pipe", 1), shifted(sent_backward, "pipe", -1)
    first = lax.axis_index("pipe") == 0
    got = swap(jnp.where(first, sent_forward, sent_backward), "pipe", 1)
    return got, got


def sum_over_tensor(x):
    if lax.axis_size("tensor") != 4:
        return lax.psum(x, "tensor")
    one, two, three = (swap(x, "tensor", bit) for bit in (1, 2, 3))
    return (x + one) + (two + three)


def add_wide(a, b):
    return a.astype(F32) + b.astype(F32)


def nt(a, b):
    return lax.dot_general(a, b, (((1,), (1,)), ((), ())), preferred_element_type=F32)


def nn(a, b):
    return jnp.dot(a, b, preferred_element_type=F32)


def split(x, parts):
    out = []
    for _ in range(parts):
        piece = x.astype(BF)
        out.append(piece)
        x = x - piece.astype(F32)
    return out


def rope_tables(length):
    half = HD // 2
    frequency = np.float32(ROPE_BASE) ** (-2.0 * np.arange(half, dtype=np.float32) / HD)
    angles = np.arange(length, dtype=np.float32)[:, None] * frequency.astype(np.float32)
    cosine, sine = np.cos(angles), np.sin(angles)
    tables = (np.concatenate([cosine, cosine], 1), np.concatenate([-sine, sine], 1))
    return tuple(jnp.asarray(t, dtype=F32) for t in tables)


def rope(x, cosine, sine):
    return x * cosine + pltpu.roll(x, HD // 2, 1) * sine


def unrope(x, cosine, sine):
    return x * cosine - pltpu.roll(x, HD // 2, 1) * sine


def inverse_root(square_sum, width):
    return 1.0 / jnp.sqrt(square_sum / width + EPSILON)


def vmem(count):
    return [pl.BlockSpec(memory_space=pltpu.VMEM)] * count


def in_hbm(arrays):
    return tuple(pltpu.with_memory_space_constraint(a, pltpu.HBM) for a in arrays)


def cost(flops, num_bytes, exps=0):
    return pl.CostEstimate(flops=flops, bytes_accessed=num_bytes, transcendentals=exps)


def streamed(pairs, sems, first, steps, ahead, work):
    def copies(i):
        out = []
        for n, (source, target, axis) in enumerate(pairs):
            size = target.shape[axis] // steps
            to = pl.ds(pl.multiple_of(i * size, size), size)
            at = pl.ds(pl.multiple_of(first + i * size, size), size)
            if axis == 0:
                piece, place = source.at[at, :], target.at[to, :]
            else:
                piece, place = source.at[:, at], target.at[:, to]
            out.append(pltpu.make_async_copy(piece, place, sems.at[n, i]))
        return out

    for i in range(ahead):
        for copy in copies(i):
            copy.start()

    def one(i, _):
        @pl.when(i + ahead < steps)
        def _():
            for copy in copies(i + ahead):
                copy.start()

        for copy in copies(i):
            copy.wait()
        work(i)
        return 0

    lax.fori_loop(0, steps, one, 0)


def project_kernel(
    back_hbm, gain_hbm, u_ref, wq_ref, wk_ref, wv_ref, wo_ref,
    m_ref, o_ref, g_ref, inv_ref,
    back, gain, small_sems, u, wq, wk, wv, wo, m_acc, o_acc, g_acc, square, sems,
):
    wide, rank = u.shape
    nq, nk = wq.shape[1], wk.shape[1]
    steps = wide // CHUNK
    block = CHUNK
    small = (
        pltpu.make_async_copy(back_hbm, back, small_sems.at[0]),
        pltpu.make_async_copy(gain_hbm, gain, small_sems.at[1]),
    )
    for copy in small:
        copy.start()
    m_acc[...] = jnp.zeros_like(m_acc)
    o_acc[...] = jnp.zeros_like(o_acc)
    g_acc[...] = jnp.zeros_like(g_acc)
    square[...] = jnp.zeros_like(square)

    def work(i):
        @pl.when(i == 0)
        def _():
            for copy in small:
                copy.wait()

        rows = pl.ds(pl.multiple_of(i * block, block), block)
        basis = u[rows, :]
        turned = basis.T
        scaled = (turned.astype(F32) * gain[:, rows]).astype(BF)
        for ref, at in ((wq, 0), (wk, nq), (wv, nq + nk)):
            size = ref.shape[1]
            m_acc[:, at : at + size] += nn(scaled, ref[rows, :])
        o_acc[...] += nn(wo[:, rows], basis)
        g_acc[...] += nn(turned, basis)
        decoded = nn(back[...], turned)
        total = square[...]
        for side in range(0, block, HD):
            part = decoded[:, side : side + HD]
            total = total + part * part
        square[...] = total

    pairs = ((u_ref, u, 0), (wq_ref, wq, 0), (wk_ref, wk, 0), (wv_ref, wv, 0), (wo_ref, wo, 1))
    streamed(pairs, sems, 0, steps, 2, work)
    for i, piece in enumerate(split(m_acc[...], 2)):
        m_ref[i * rank : (i + 1) * rank, :] = piece
    o_ref[...] = o_acc[...].astype(BF)
    for i, piece in enumerate(split(g_acc[...], 3)):
        g_ref[i * rank : (i + 1) * rank, :] = piece
    inv_ref[...] = jnp.broadcast_to(
        inverse_root(jnp.sum(square[...], axis=1, keepdims=True), wide), inv_ref.shape
    )


def project(back, gain, basis, wq, wk, wv, wo):
    wide, rank = basis.shape
    length = back.shape[0]
    ne = wo.shape[0]
    total = wq.shape[1] + wk.shape[1] + wv.shape[1]
    small = in_hbm((back, gain))
    weights = in_hbm((basis, wq, wk, wv, wo))
    return pl.pallas_call(
        project_kernel,
        in_specs=[pl.BlockSpec(memory_space=pltpu.HBM)] * len(small + weights),
        out_specs=vmem(4),
        out_shape=[
            jax.ShapeDtypeStruct((2 * rank, total), BF),
            jax.ShapeDtypeStruct((ne, rank), BF),
            jax.ShapeDtypeStruct((3 * rank, rank), BF),
            jax.ShapeDtypeStruct((length, HD), F32),
        ],
        scratch_shapes=[pltpu.VMEM(a.shape, a.dtype) for a in small]
        + [pltpu.SemaphoreType.DMA((len(small),))]
        + [pltpu.VMEM(w.shape, BF) for w in weights]
        + [
            pltpu.VMEM((rank, total), F32),
            pltpu.VMEM((ne, rank), F32),
            pltpu.VMEM((rank, rank), F32),
            pltpu.VMEM((length, HD), F32),
            pltpu.SemaphoreType.DMA((len(weights), wide // CHUNK)),
        ],
        compiler_params=pltpu.CompilerParams(vmem_limit_bytes=2 * VMEM_BYTES),
        cost_estimate=cost(6 * 10**9, 20 * 10**6),
        name="project_weights",
    )(*small, *weights)


def project_heads(coeffs, inv, m_ref, cosine, sine, q, k, v1):
    length = coeffs.shape[0]
    heads = q.shape[0] // length
    twice = jnp.concatenate([coeffs, coeffs], axis=1)
    for h in range(heads):
        part = nn(twice, m_ref[:, h * HD : (h + 1) * HD]) * inv
        q[h * length : (h + 1) * length, :] = rope(part, cosine, sine).astype(BF)
    part = nn(twice, m_ref[:, heads * HD :]) * inv
    k[...] = rope(part[:, :HD], cosine, sine).astype(BF)
    v1[:, :HD] = part[:, HD:].astype(BF)
    v1[:, HD:] = jnp.ones_like(v1[:, HD:])


def exps_of(scores, exps, low, length):
    row = lax.broadcasted_iota(jnp.int32, (length, length), 0)
    column = lax.broadcasted_iota(jnp.int32, (length, length), 1)
    causal = row >= column

    def one(h, _):
        at = pl.ds(pl.multiple_of(h * length, length), length)
        s = jnp.where(causal, scores[at, :], -jnp.inf)
        top = jnp.max(s, axis=1, keepdims=True)
        e = jnp.exp2((s - top) * (LOG2E / math.sqrt(HD)))
        if exps is not None:
            exps[at, :] = e
        low[at, :] = e.astype(BF)
        return 0

    lax.fori_loop(0, scores.shape[0] // length, one, 0, unroll=2)


def backward_kernel(
    back_ref, loss_ref, sent_ref, m_ref, o_ref, g_ref, inv_ref, cos_ref, sin_ref,
    inner_ref, out_give_ref, out_keep_ref, x_ref, base_ref, unit_ref,
    q, k, v1, gh, ghs, scores, low, mixed, gp, ds, dq, heads, grads, inner, out_inner,
):
    length, rank = back_ref.shape
    ne = o_ref.shape[0]
    count = ne // HD
    scale = 1.0 / math.sqrt(HD)
    last = lax.axis_size("pipe") - 1
    is_last = lax.axis_index("pipe") == last
    back = back_ref[...]
    up = jnp.where(is_last, loss_ref[...], sent_ref[...])
    cosine, sine = cos_ref[...], sin_ref[...]
    inv = inv_ref[...]
    project_heads(back, inv[:, :1], m_ref, cosine, sine, q, k, v1)
    scores[...] = nt(q[...], k[...])
    for h in range(count):
        gh[h * length : (h + 1) * length, :] = nt(up, o_ref[h * HD : (h + 1) * HD, :]).astype(BF)
    exps_of(scores, scores, low, length)
    mixed[...] = nn(low[...], v1[...])
    gp[...] = nt(gh[...], v1[:, :HD])

    for h in range(count):
        at = slice(h * length, (h + 1) * length)
        inverse = 1.0 / mixed[at, HD:]
        out = mixed[at, :HD] * inverse
        heads[:, h * HD : (h + 1) * HD] = out.astype(BF)
        grad = gh[at, :].astype(F32)
        ghs[at, :] = (grad * inverse).astype(BF)
        delta = jnp.sum(grad * out, axis=1, keepdims=True)
        factor = inverse * scale
        for side in range(0, length, HD):
            part = scores[at, side : side + HD] * factor
            ds[at, side : side + HD] = (part * (gp[at, side : side + HD] - delta)).astype(BF)

    dq[...] = nn(ds[...], k[...])
    for h in range(count):
        part = dq[h * length : (h + 1) * length, :]
        grads[:, h * HD : (h + 1) * HD] = unrope(part, cosine, sine).astype(BF)
    dk = nn(q[...].T, ds[...]).T
    grads[:, ne : ne + HD] = unrope(dk, cosine, sine).astype(BF)
    grads[:, ne + HD :] = nn(ghs[...].T, low[...]).T.astype(BF)
    unit = (back.astype(F32) * inv[:, :1]).astype(BF)
    half = rank // 2
    core = lax.axis_index("dp") & 1
    mine = pl.ds(pl.multiple_of(core * half, half), half)
    theirs = pl.ds(pl.multiple_of((1 - core) * half, half), half)
    inner[...] = nn(unit.T, grads[...]).astype(BF)
    inner_ref[:half, :] = inner[mine, :]
    inner_ref[half:, :] = inner[theirs, :]
    out_inner[...] = nn(up.T, heads[...]).astype(BF)
    out_keep_ref[...] = out_inner[mine, :]
    out_give_ref[...] = out_inner[theirs, :]
    x_ref[...] = nt(grads[...], m_ref[:rank, :]).astype(BF)
    base_ref[...] = nn(jnp.concatenate([up] * 3, axis=1), g_ref[...])
    unit_ref[...] = nn(jnp.concatenate([back] * 3, axis=1), g_ref[...]) * inv[:, :1]


def backward(back, loss, sent, m2, o2, g3, inv, cosine, sine):
    length, rank = back.shape
    ne = o2.shape[0]
    total = m2.shape[1]
    assert total == ne + 2 * HD
    stack = ne // HD * length
    return pl.pallas_call(
        backward_kernel,
        in_specs=vmem(9),
        out_specs=vmem(6),
        out_shape=[
            jax.ShapeDtypeStruct((rank, total), BF),
            jax.ShapeDtypeStruct((rank // 2, ne), BF),
            jax.ShapeDtypeStruct((rank // 2, ne), BF),
            jax.ShapeDtypeStruct((length, rank), BF),
            jax.ShapeDtypeStruct((length, rank), F32),
            jax.ShapeDtypeStruct((length, rank), F32),
        ],
        scratch_shapes=[
            pltpu.VMEM((stack, HD), BF),
            pltpu.VMEM((length, HD), BF),
            pltpu.VMEM((length, 2 * HD), BF),
            pltpu.VMEM((stack, HD), BF),
            pltpu.VMEM((stack, HD), BF),
            pltpu.VMEM((stack, length), F32),
            pltpu.VMEM((stack, length), BF),
            pltpu.VMEM((stack, 2 * HD), F32),
            pltpu.VMEM((stack, length), F32),
            pltpu.VMEM((stack, length), BF),
            pltpu.VMEM((stack, HD), F32),
            pltpu.VMEM((length, ne), BF),
            pltpu.VMEM((length, total), BF),
            pltpu.VMEM((rank, total), BF),
            pltpu.VMEM((rank, ne), BF),
        ],
        compiler_params=pltpu.CompilerParams(vmem_limit_bytes=VMEM_BYTES),
        cost_estimate=cost(10**8, 10**6),
        name="attention_backward",
    )(back, loss, sent, m2, o2, g3, inv, cosine, sine)


def forward_kernel(
    new_ref, sent_ref, u_ref, m_ref, o_ref, g_ref, cos_ref, sin_ref, *rest,
):
    y_ref, base_ref, q, k, v1, scores, low, mixed, heads = rest[-9:]
    length, rank = new_ref.shape
    wide = u_ref.shape[0]
    is_first = lax.axis_index("pipe") == 0
    coeffs = jnp.where(is_first, new_ref[...], sent_ref[...])
    square = jnp.zeros((length, HD), F32)
    block = 512
    for at in range(0, wide, block):
        decoded = nt(coeffs, u_ref[at : at + block, :])
        for side in range(0, block, HD):
            part = decoded[:, side : side + HD]
            square = square + part * part
    inv = inverse_root(jnp.sum(square, axis=1, keepdims=True), wide)
    project_heads(coeffs, inv, m_ref, cos_ref[...], sin_ref[...], q, k, v1)
    scores[...] = nt(q[...], k[...])
    exps_of(scores, None, low, length)
    mixed[...] = nn(low[...], v1[...])
    for h in range(heads.shape[1] // HD):
        at = slice(h * length, (h + 1) * length)
        heads[:, h * HD : (h + 1) * HD] = (mixed[at, :HD] / mixed[at, HD:]).astype(BF)
    y_ref[...] = nn(heads[...], o_ref[...]).astype(BF)
    base_ref[...] = nn(jnp.concatenate([coeffs] * 3, axis=1), g_ref[...])


def forward(new, sent, basis, m2, o2, g3, cosine, sine, *after):
    length, rank = new.shape
    ne = o2.shape[0]
    stack = ne // HD * length
    return pl.pallas_call(
        forward_kernel,
        in_specs=vmem(8) + [pl.BlockSpec(memory_space=pl.ANY)] * len(after),
        out_specs=vmem(2),
        out_shape=[
            jax.ShapeDtypeStruct((length, rank), BF),
            jax.ShapeDtypeStruct((length, rank), F32),
        ],
        scratch_shapes=[
            pltpu.VMEM((stack, HD), BF),
            pltpu.VMEM((length, HD), BF),
            pltpu.VMEM((length, 2 * HD), BF),
            pltpu.VMEM((stack, length), F32),
            pltpu.VMEM((stack, length), BF),
            pltpu.VMEM((stack, 2 * HD), F32),
            pltpu.VMEM((length, ne), BF),
        ],
        compiler_params=pltpu.CompilerParams(vmem_limit_bytes=VMEM_BYTES),
        cost_estimate=cost(10**8, 10**6),
        name="attention_forward",
    )(new, sent, basis, m2, o2, g3, cosine, sine, *after)


def gain_kernel(u_ref, wq_ref, wk_ref, wv_ref, inner_ref, got_ref, after, out_ref, turned):
    nq, nk = wq_ref.shape[1], wk_ref.shape[1]
    rows = out_ref.shape[1]
    half = inner_ref.shape[0] // 2
    core = lax.axis_index("dp") & 1
    mine = add_wide(inner_ref[:half, :], got_ref[half:, :]).astype(BF)
    theirs = add_wide(inner_ref[half:, :], got_ref[:half, :]).astype(BF)
    turned[:, pl.ds(pl.multiple_of(core * half, half), half)] = mine.T
    turned[:, pl.ds(pl.multiple_of((1 - core) * half, half), half)] = theirs.T
    for at in range(0, rows, CHUNK):
        place = pl.ds(pl.multiple_of(core * rows + at, CHUNK), CHUNK)
        against = nn(wq_ref[place, :], turned[:nq, :])
        narrow = jnp.concatenate([wk_ref[place, :], wv_ref[place, :]], axis=1)
        against += nn(narrow, turned[nq:, :])
        terms = against * u_ref[place, :].astype(F32)
        folded = sum(terms[:, side : side + HD] for side in range(0, terms.shape[1], HD))
        out_ref[:, at : at + CHUNK] = jnp.sum(folded.T, axis=0, keepdims=True)


def gain_part(basis, wq, wk, wv, inner, got, after):
    wide, rank = basis.shape
    rows = wide // 2
    return pl.pallas_call(
        gain_kernel,
        in_specs=vmem(6) + [pl.BlockSpec(memory_space=pl.ANY)],
        out_specs=pl.BlockSpec(memory_space=pltpu.VMEM),
        out_shape=jax.ShapeDtypeStruct((1, rows), F32),
        scratch_shapes=[pltpu.VMEM((inner.shape[1], rank), BF)],
        compiler_params=pltpu.CompilerParams(vmem_limit_bytes=VMEM_BYTES),
        cost_estimate=cost(10**8, 10**6),
        name="gain_gradient",
    )(basis, wq, wk, wv, inner, got, after)


def add_kernel(a_ref, b_ref, after, out_ref):
    out_ref[...] = add_wide(a_ref[...], b_ref[...]).astype(BF)


def add_after(a, b, after):
    return pl.pallas_call(
        add_kernel,
        in_specs=vmem(2) + [pl.BlockSpec(memory_space=pl.ANY)],
        out_specs=pl.BlockSpec(memory_space=pltpu.VMEM),
        out_shape=jax.ShapeDtypeStruct(a.shape, BF),
        compiler_params=pltpu.CompilerParams(vmem_limit_bytes=VMEM_BYTES // 2),
        cost_estimate=cost(10**6, 10**5),
        name="pair_sum",
    )(a, b, after)


def gather_halves(own_ref, other_ref, whole):
    half = own_ref.shape[0]
    core = lax.axis_index("dp") & 1
    whole[pl.ds(pl.multiple_of(core * half, half), half), :] = own_ref[...]
    whole[pl.ds(pl.multiple_of((1 - core) * half, half), half), :] = other_ref[...]


def inward_kernel(u_ref, gain_ref, own_ref, other_ref, after, q_ref, k_ref, v_ref, inner):
    nq, nk = q_ref.shape[1], k_ref.shape[1]
    block = q_ref.shape[0]

    @pl.when(pl.program_id(0) == 0)
    def _():
        gather_halves(own_ref, other_ref, inner)

    step = lax.axis_index("dp") * pl.num_programs(0) + pl.program_id(0)
    rows = pl.ds(pl.multiple_of(step * block, block), block)
    gain = jnp.broadcast_to(gain_ref[:, rows], (HD, block)).T[:, :1]
    grad = nn(u_ref[rows, :], inner[...]) * gain
    q_ref[...] = grad[:, :nq].astype(BF)
    k_ref[...] = grad[:, nq : nq + nk].astype(BF)
    v_ref[...] = grad[:, nq + nk :].astype(BF)


def outward_kernel(u_ref, own_ref, other_ref, after, o_ref, inner):
    @pl.when(pl.program_id(0) == 0)
    def _():
        gather_halves(own_ref, other_ref, inner)

    block, rows = o_ref.shape
    at = pl.multiple_of(pl.program_id(0) * block, block)
    basis = u_ref[pl.ds(pl.multiple_of(lax.axis_index("dp") * rows, rows), rows), :]
    o_ref[...] = nt(inner[:, pl.ds(at, block)].T, basis).astype(BF)


STEPS = 2


def inward_grads(basis, gain, own, other, sizes, after):
    wide, rank = basis.shape
    rows = wide // lax.axis_size("dp")
    block = rows // STEPS
    return pl.pallas_call(
        inward_kernel,
        grid=(STEPS,),
        in_specs=vmem(4) + [pl.BlockSpec(memory_space=pl.ANY)],
        out_specs=[pl.BlockSpec((block, n), lambda i: (i, 0)) for n in sizes],
        scratch_shapes=[pltpu.VMEM((rank, sum(sizes)), BF)],
        out_shape=[jax.ShapeDtypeStruct((rows, n), BF) for n in sizes],
        compiler_params=pltpu.CompilerParams(vmem_limit_bytes=VMEM_BYTES),
        cost_estimate=cost(10**8, 10**6),
        name="inward_weight_gradients",
    )(basis, gain, own, other, after)


def outward_grad(basis, own, other, after):
    wide, rank = basis.shape
    rows = wide // lax.axis_size("dp")
    ne = own.shape[1]
    return pl.pallas_call(
        outward_kernel,
        grid=(STEPS,),
        in_specs=vmem(3) + [pl.BlockSpec(memory_space=pl.ANY)],
        out_specs=pl.BlockSpec((ne // STEPS, rows), lambda i: (i, 0)),
        scratch_shapes=[pltpu.VMEM((rank, ne), BF)],
        out_shape=jax.ShapeDtypeStruct((ne, rows), BF),
        compiler_params=pltpu.CompilerParams(vmem_limit_bytes=VMEM_BYTES),
        cost_estimate=cost(10**8, 10**6),
        name="output_weight_gradient",
    )(basis, own, other, after)


def results_kernel(
    wide, fbase_ref, y_ref, ygot_ref, base_ref, unit_ref, x_ref, xgot_ref, back_ref, inv_ref,
    gain_ref, gain_one_ref, gain_two_ref, gain_three_ref, after,
    f_ref, b_ref, gain_out_ref,
):
    f_ref[...] = (fbase_ref[...] + add_wide(y_ref[...], ygot_ref[...])).astype(BF)
    x = add_wide(x_ref[...], xgot_ref[...])
    inv = inv_ref[:, :1]
    along = jnp.sum(x * back_ref[...].astype(F32), axis=1, keepdims=True)
    middle = along * inv * (1.0 / wide)
    b_ref[...] = (base_ref[...] + (x - unit_ref[...] * middle) * inv).astype(BF)
    core = lax.axis_index("dp") & 1
    half = gain_ref.shape[1]
    mine = pl.ds(pl.multiple_of(core * half, half), half)
    theirs = pl.ds(pl.multiple_of((1 - core) * half, half), half)
    gain_out_ref[:, mine] = gain_ref[...] + gain_two_ref[...]
    gain_out_ref[:, theirs] = gain_one_ref[...] + gain_three_ref[...]


def results(wide, after, *operands):
    shape = operands[0].shape
    held = tuple(pltpu.with_memory_space_constraint(a, pltpu.VMEM) for a in operands)
    return pl.pallas_call(
        functools.partial(results_kernel, wide),
        in_specs=vmem(len(operands)) + [pl.BlockSpec(memory_space=pl.ANY)],
        out_specs=vmem(3),
        out_shape=[jax.ShapeDtypeStruct(shape, BF)] * 2 + [jax.ShapeDtypeStruct((1, wide), F32)],
        compiler_params=pltpu.CompilerParams(vmem_limit_bytes=VMEM_BYTES // 2),
        cost_estimate=cost(10**8, 10**6),
        name="section_results",
    )(*held, *in_hbm((after,)))


def body(
    new_coeffs,
    loss_grad,
    sent_forward,
    sent_backward,
    stashed,
    subspace,
    norm_gain,
    w_query,
    w_key,
    w_value,
    w_output,
):
    wide = subspace.shape[0]
    wq, wk, wv, wo = w_query[0], w_key[0], w_value[0], w_output[0]
    nq, nk, nv = wq.shape[1], wk.shape[1], wv.shape[1]
    back = stashed[0]
    arrived, returned = cross_pipe(sent_forward[0], sent_backward[0])
    cosine, sine = rope_tables(back.shape[0])

    m2, o2, g3, inv = project(back, norm_gain, subspace, wq, wk, wv, wo)
    inner, out_give, out_keep, x, base, unit = backward(
        back, loss_grad, returned, m2, o2, g3, inv, cosine, sine
    )
    half = inner.shape[0] // 2
    out_got = swap(out_give, "dp", 1)
    inner_got = swap(inner, "dp", 1)
    x_got = swap(x, "tensor", 1)
    out_pair = add_wide(out_keep, out_got).astype(BF)
    pair = add_wide(inner[:half], inner_got[half:]).astype(BF)
    out_got = swap(out_pair, "dp", 2)
    pair_got = swap(pair, "dp", 2)
    x = add_after(x, x_got, pair)
    x_got = swap(x, "tensor", 2)
    y, fbase = forward(
        new_coeffs, arrived, subspace, m2, o2, g3, cosine, sine, out_pair, x
    )
    y_got = swap(y, "tensor", 1)
    gain = gain_part(subspace, wq, wk, wv, inner, inner_got, y)
    y = add_wide(y, y_got).astype(BF)
    y_got = swap(y, "tensor", 2)
    gain = sum_over_tensor(gain)
    gains = [gain] + [swap(gain, "dp", bit) for bit in (1, 2, 3)]

    own = add_wide(out_pair, out_got).astype(BF)
    grad_o = outward_grad(subspace, own, swap(own, "dp", 1), y)
    own = add_wide(pair, pair_got).astype(BF)
    grad_q, grad_k, grad_v = inward_grads(
        subspace, norm_gain, own, swap(own, "dp", 1), (nq, nk, nv), gain
    )
    forward_out, backward_out, grad_gain = results(
        wide, grad_v, fbase, y, y_got, base, unit, x, x_got, back, inv, *gains
    )
    return (
        forward_out[None],
        backward_out[None],
        grad_q[None],
        grad_k[None],
        grad_v[None],
        grad_o[None],
        grad_gain,
    )


def solution(mesh):
    return jax.shard_map(
        body,
        mesh=mesh,
        in_specs=(
            P("dp", None),
            P("dp", None),
            P("pipe", "dp", None),
            P("pipe", "dp", None),
            P("pipe", "dp", None),
            P(),
            P("pipe", None),
            P("pipe", None, "tensor"),
            P("pipe", None, "tensor"),
            P("pipe", None, "tensor"),
            P("pipe", "tensor", None),
        ),
        out_specs=(
            P("pipe", "dp", None),
            P("pipe", "dp", None),
            P("pipe", "dp", "tensor"),
            P("pipe", "dp", "tensor"),
            P("pipe", "dp", "tensor"),
            P("pipe", "tensor", "dp"),
            P("pipe", None),
        ),
        check_vma=False,
    )
```

```python
import functools
import math

import jax
import jax.numpy as jnp
import numpy as np
from jax import lax
from jax.experimental import pallas as pl
from jax.experimental.pallas import tpu as pltpu
from jax.sharding import PartitionSpec as P

HD = 128
EPSILON = 1e-05
ROPE_BASE = 500000.0
BF = jnp.bfloat16
F32 = jnp.float32
VMEM_BYTES = 24 * 1024 * 1024
CHUNK = 512
PIECE = 1024
AHEAD = 3
LOG2E = 1.4426950408889634


def shifted(x, axis, by):
    devices = lax.axis_size(axis)
    pairs = [(i, i + by) for i in range(devices) if 0 <= i + by < devices]
    return lax.ppermute(x, axis, pairs)


def swap(x, axis, bit):
    devices = lax.axis_size(axis)
    return lax.ppermute(x, axis, [(i, i ^ bit) for i in range(devices)])


def cross_pipe(sent_forward, sent_backward):
    if lax.axis_size("pipe") != 2:
        return shifted(sent_forward, "pipe", 1), shifted(sent_backward, "pipe", -1)
    first = lax.axis_index("pipe") == 0
    got = swap(jnp.where(first, sent_forward, sent_backward), "pipe", 1)
    return got, got


def add_wide(a, b):
    return a.astype(F32) + b.astype(F32)


def nt(a, b):
    return lax.dot_general(a, b, (((1,), (1,)), ((), ())), preferred_element_type=F32)


def nn(a, b):
    return jnp.dot(a, b, preferred_element_type=F32)


def split(x, parts):
    out = []
    for _ in range(parts):
        piece = x.astype(BF)
        out.append(piece)
        x = x - piece.astype(F32)
    return out


def rope_tables(length):
    half = HD // 2
    frequency = np.float32(ROPE_BASE) ** (-2.0 * np.arange(half, dtype=np.float32) / HD)
    angles = np.arange(length, dtype=np.float32)[:, None] * frequency.astype(np.float32)
    cosine, sine = np.cos(angles), np.sin(angles)
    tables = (np.concatenate([cosine, cosine], 1), np.concatenate([-sine, sine], 1))
    return tuple(jnp.asarray(t, dtype=F32) for t in tables)


def rope(x, cosine, sine):
    return x * cosine + pltpu.roll(x, HD // 2, 1) * sine


def unrope(x, cosine, sine):
    return x * cosine - pltpu.roll(x, HD // 2, 1) * sine


def inverse_root(square_sum, width):
    return 1.0 / jnp.sqrt(square_sum / width + EPSILON)


def vmem(count):
    return [pl.BlockSpec(memory_space=pltpu.VMEM)] * count


def in_hbm(arrays):
    return tuple(pltpu.with_memory_space_constraint(a, pltpu.HBM) for a in arrays)


def cost(flops, num_bytes, exps=0):
    return pl.CostEstimate(flops=flops, bytes_accessed=num_bytes, transcendentals=exps)


def project_kernel(
    back_hbm, gain_hbm, u_hbm, wq_hbm, wk_hbm, wv_hbm, wo_hbm,
    m_ref, o_ref, g_ref, inv_ref,
    back, gain, u, wq, narrow, wo, turned, scaled, m_acc, o_acc, sems,
):
    wide, rank = u.shape
    nq = wq.shape[1]
    nk = wk_hbm.shape[1]
    parts = wide // PIECE
    pieces = [pl.ds(i * PIECE, PIECE) for i in range(parts)]
    pairs = [(back_hbm, back), (gain_hbm, gain), (u_hbm, u)]
    pairs += [(wq_hbm.at[at, :], wq.at[at, :]) for at in pieces[:2]]
    pairs += [(wk_hbm, narrow.at[:, pl.ds(0, nk)])]
    pairs += [(wv_hbm, narrow.at[:, pl.ds(nk, narrow.shape[1] - nk)])]
    pairs += [(wq_hbm.at[at, :], wq.at[at, :]) for at in pieces[2:]]
    pairs += [(wo_hbm.at[:, at], wo.at[:, at]) for at in pieces]
    copies = [
        pltpu.make_async_copy(source, target, sems.at[n])
        for n, (source, target) in enumerate(pairs)
    ]
    started = 0

    def start_to(count):
        nonlocal started
        for copy in copies[started:count]:
            copy.start()
        started = max(started, min(count, len(copies)))

    def wait(n):
        start_to(n + 1 + AHEAD)
        copies[n].wait()

    start_to(3 + AHEAD)
    for n in range(3):
        copies[n].wait()
    turned[...] = u[...].T
    scaled[...] = (turned[...].astype(F32) * gain[...]).astype(BF)
    gram = nn(turned[...], u[...])
    for i, piece in enumerate(split(gram, 3)):
        g_ref[i * rank : (i + 1) * rank, :] = piece
    square = jnp.zeros((back.shape[0], HD), F32)
    for at in range(0, wide, PIECE):
        decoded = nn(back[...], turned[:, at : at + PIECE])
        for side in range(0, PIECE, HD):
            part = decoded[:, side : side + HD]
            square = square + part * part
    inv_ref[...] = jnp.broadcast_to(
        inverse_root(jnp.sum(square, axis=1, keepdims=True), wide), inv_ref.shape
    )
    place = 3
    for i, at in enumerate(pieces):
        if i == 2:
            wait(place)
            wait(place + 1)
            place += 2
            for p, piece in enumerate(split(nn(scaled[...], narrow[...]), 2)):
                m_ref[p * rank : (p + 1) * rank, nq:] = piece
        wait(place)
        place += 1
        part = nn(scaled[:, at], wq[at, :])
        if i == 0:
            m_acc[...] = part
        else:
            m_acc[...] += part
    for p, piece in enumerate(split(m_acc[...], 2)):
        m_ref[p * rank : (p + 1) * rank, :nq] = piece
    for i, at in enumerate(pieces):
        wait(place)
        place += 1
        part = nn(wo[:, at], u[at, :])
        if i == 0:
            o_acc[...] = part
        else:
            o_acc[...] += part
    o_ref[...] = o_acc[...].astype(BF)


def project(back, gain, basis, wq, wk, wv, wo):
    wide, rank = basis.shape
    length = back.shape[0]
    ne = wo.shape[0]
    nq = wq.shape[1]
    rest = wk.shape[1] + wv.shape[1]
    operands = in_hbm((back, gain, basis, wq, wk, wv, wo))
    return pl.pallas_call(
        project_kernel,
        in_specs=[pl.BlockSpec(memory_space=pltpu.HBM)] * len(operands),
        out_specs=vmem(4),
        out_shape=[
            jax.ShapeDtypeStruct((2 * rank, nq + rest), BF),
            jax.ShapeDtypeStruct((ne, rank), BF),
            jax.ShapeDtypeStruct((3 * rank, rank), BF),
            jax.ShapeDtypeStruct((length, HD), F32),
        ],
        scratch_shapes=[
            pltpu.VMEM(back.shape, BF),
            pltpu.VMEM(gain.shape, F32),
            pltpu.VMEM(basis.shape, BF),
            pltpu.VMEM(wq.shape, BF),
            pltpu.VMEM((wide, rest), BF),
            pltpu.VMEM(wo.shape, BF),
            pltpu.VMEM((rank, wide), BF),
            pltpu.VMEM((rank, wide), BF),
            pltpu.VMEM((rank, nq), F32),
            pltpu.VMEM((ne, rank), F32),
            pltpu.SemaphoreType.DMA((5 + 2 * (wide // PIECE),)),
        ],
        compiler_params=pltpu.CompilerParams(vmem_limit_bytes=2 * VMEM_BYTES),
        cost_estimate=cost(6 * 10**9, 20 * 10**6),
        name="project_weights",
    )(*operands)


def project_heads(coeffs, inv, m_ref, cosine, sine, q, k, v1):
    length = coeffs.shape[0]
    heads = q.shape[0] // length
    twice = jnp.concatenate([coeffs, coeffs], axis=1)
    for h in range(heads):
        part = nn(twice, m_ref[:, h * HD : (h + 1) * HD]) * inv
        q[h * length : (h + 1) * length, :] = rope(part, cosine, sine).astype(BF)
    part = nn(twice, m_ref[:, heads * HD :]) * inv
    k[...] = rope(part[:, :HD], cosine, sine).astype(BF)
    v1[:, :HD] = part[:, HD:].astype(BF)
    v1[:, HD:] = jnp.ones_like(v1[:, HD:])


def exps_of(scores, exps, low, length):
    row = lax.broadcasted_iota(jnp.int32, (length, length), 0)
    column = lax.broadcasted_iota(jnp.int32, (length, length), 1)
    causal = row >= column

    def one(h, _):
        at = pl.ds(pl.multiple_of(h * length, length), length)
        s = jnp.where(causal, scores[at, :], -jnp.inf)
        top = jnp.max(s, axis=1, keepdims=True)
        e = jnp.exp2((s - top) * (LOG2E / math.sqrt(HD)))
        if exps is not None:
            exps[at, :] = e
        low[at, :] = e.astype(BF)
        return 0

    lax.fori_loop(0, scores.shape[0] // length, one, 0, unroll=2)


def backward_kernel(
    back_ref, loss_ref, sent_ref, m_ref, o_ref, g_ref, inv_ref, cos_ref, sin_ref,
    inner_ref, out_give_ref, out_keep_ref, x_ref, base_ref, unit_ref,
    q, k, v1, gh, ghs, scores, low, mixed, gp, ds, dq, heads, grads, inner, out_inner,
):
    length, rank = back_ref.shape
    ne = o_ref.shape[0]
    count = ne // HD
    scale = 1.0 / math.sqrt(HD)
    last = lax.axis_size("pipe") - 1
    is_last = lax.axis_index("pipe") == last
    back = back_ref[...]
    up = jnp.where(is_last, loss_ref[...], sent_ref[...])
    cosine, sine = cos_ref[...], sin_ref[...]
    inv = inv_ref[...]
    project_heads(back, inv[:, :1], m_ref, cosine, sine, q, k, v1)
    scores[...] = nt(q[...], k[...])
    for h in range(count):
        gh[h * length : (h + 1) * length, :] = nt(up, o_ref[h * HD : (h + 1) * HD, :]).astype(BF)
    exps_of(scores, scores, low, length)
    mixed[...] = nn(low[...], v1[...])
    gp[...] = nt(gh[...], v1[:, :HD])

    for h in range(count):
        at = slice(h * length, (h + 1) * length)
        inverse = 1.0 / mixed[at, HD:]
        out = mixed[at, :HD] * inverse
        heads[:, h * HD : (h + 1) * HD] = out.astype(BF)
        grad = gh[at, :].astype(F32)
        ghs[at, :] = (grad * inverse).astype(BF)
        delta = jnp.sum(grad * out, axis=1, keepdims=True)
        factor = inverse * scale
        for side in range(0, length, HD):
            part = scores[at, side : side + HD] * factor
            ds[at, side : side + HD] = (part * (gp[at, side : side + HD] - delta)).astype(BF)

    dq[...] = nn(ds[...], k[...])
    for h in range(count):
        part = dq[h * length : (h + 1) * length, :]
        grads[:, h * HD : (h + 1) * HD] = unrope(part, cosine, sine).astype(BF)
    dk = nn(q[...].T, ds[...]).T
    grads[:, ne : ne + HD] = unrope(dk, cosine, sine).astype(BF)
    grads[:, ne + HD :] = nn(ghs[...].T, low[...]).T.astype(BF)
    unit = (back.astype(F32) * inv[:, :1]).astype(BF)
    half = rank // 2
    core = lax.axis_index("dp") & 1
    mine = pl.ds(pl.multiple_of(core * half, half), half)
    theirs = pl.ds(pl.multiple_of((1 - core) * half, half), half)
    inner[...] = nn(unit.T, grads[...]).astype(BF)
    inner_ref[:half, :] = inner[mine, :]
    inner_ref[half:, :] = inner[theirs, :]
    out_inner[...] = nn(up.T, heads[...]).astype(BF)
    out_keep_ref[...] = out_inner[mine, :]
    out_give_ref[...] = out_inner[theirs, :]
    x_ref[...] = nt(grads[...], m_ref[:rank, :]).astype(BF)
    base_ref[...] = nn(jnp.concatenate([up] * 3, axis=1), g_ref[...])
    unit_ref[...] = nn(jnp.concatenate([back] * 3, axis=1), g_ref[...]) * inv[:, :1]


def backward(back, loss, sent, m2, o2, g3, inv, cosine, sine):
    length, rank = back.shape
    ne = o2.shape[0]
    total = m2.shape[1]
    assert total == ne + 2 * HD
    stack = ne // HD * length
    return pl.pallas_call(
        backward_kernel,
        in_specs=vmem(9),
        out_specs=vmem(6),
        out_shape=[
            jax.ShapeDtypeStruct((rank, total), BF),
            jax.ShapeDtypeStruct((rank // 2, ne), BF),
            jax.ShapeDtypeStruct((rank // 2, ne), BF),
            jax.ShapeDtypeStruct((length, rank), BF),
            jax.ShapeDtypeStruct((length, rank), F32),
            jax.ShapeDtypeStruct((length, rank), F32),
        ],
        scratch_shapes=[
            pltpu.VMEM((stack, HD), BF),
            pltpu.VMEM((length, HD), BF),
            pltpu.VMEM((length, 2 * HD), BF),
            pltpu.VMEM((stack, HD), BF),
            pltpu.VMEM((stack, HD), BF),
            pltpu.VMEM((stack, length), F32),
            pltpu.VMEM((stack, length), BF),
            pltpu.VMEM((stack, 2 * HD), F32),
            pltpu.VMEM((stack, length), F32),
            pltpu.VMEM((stack, length), BF),
            pltpu.VMEM((stack, HD), F32),
            pltpu.VMEM((length, ne), BF),
            pltpu.VMEM((length, total), BF),
            pltpu.VMEM((rank, total), BF),
            pltpu.VMEM((rank, ne), BF),
        ],
        compiler_params=pltpu.CompilerParams(vmem_limit_bytes=VMEM_BYTES),
        cost_estimate=cost(10**4, 10**3),
        name="attention_backward",
    )(back, loss, sent, m2, o2, g3, inv, cosine, sine)


def forward_kernel(
    new_ref, sent_ref, u_ref, m_ref, o_ref, g_ref, cos_ref, sin_ref, *rest,
):
    y_ref, base_ref, q, k, v1, scores, low, mixed, heads = rest[-9:]
    length, rank = new_ref.shape
    wide = u_ref.shape[0]
    is_first = lax.axis_index("pipe") == 0
    coeffs = jnp.where(is_first, new_ref[...], sent_ref[...])
    square = jnp.zeros((length, HD), F32)
    block = 512
    for at in range(0, wide, block):
        decoded = nt(coeffs, u_ref[at : at + block, :])
        for side in range(0, block, HD):
            part = decoded[:, side : side + HD]
            square = square + part * part
    inv = inverse_root(jnp.sum(square, axis=1, keepdims=True), wide)
    project_heads(coeffs, inv, m_ref, cos_ref[...], sin_ref[...], q, k, v1)
    scores[...] = nt(q[...], k[...])
    exps_of(scores, None, low, length)
    mixed[...] = nn(low[...], v1[...])
    for h in range(heads.shape[1] // HD):
        at = slice(h * length, (h + 1) * length)
        heads[:, h * HD : (h + 1) * HD] = (mixed[at, :HD] / mixed[at, HD:]).astype(BF)
    y_ref[...] = nn(heads[...], o_ref[...]).astype(BF)
    base_ref[...] = nn(jnp.concatenate([coeffs] * 3, axis=1), g_ref[...])


def forward(new, sent, basis, m2, o2, g3, cosine, sine, *after):
    length, rank = new.shape
    ne = o2.shape[0]
    stack = ne // HD * length
    return pl.pallas_call(
        forward_kernel,
        in_specs=vmem(8) + [pl.BlockSpec(memory_space=pl.ANY)] * len(after),
        out_specs=vmem(2),
        out_shape=[
            jax.ShapeDtypeStruct((length, rank), BF),
            jax.ShapeDtypeStruct((length, rank), F32),
        ],
        scratch_shapes=[
            pltpu.VMEM((stack, HD), BF),
            pltpu.VMEM((length, HD), BF),
            pltpu.VMEM((length, 2 * HD), BF),
            pltpu.VMEM((stack, length), F32),
            pltpu.VMEM((stack, length), BF),
            pltpu.VMEM((stack, 2 * HD), F32),
            pltpu.VMEM((length, ne), BF),
        ],
        compiler_params=pltpu.CompilerParams(vmem_limit_bytes=VMEM_BYTES),
        cost_estimate=cost(10**4, 10**3),
        name="attention_forward",
    )(new, sent, basis, m2, o2, g3, cosine, sine, *after)


def write_split(ref, first, value):
    high, low = split(value, 2)
    both = jnp.concatenate([high.astype(F32), low.astype(F32)], axis=0)
    ref[first:, : value.shape[1]] = both.astype(BF)


def read_split(ref, first):
    both = ref[first:, :CHUNK].astype(F32)
    return both[:8] + both[8:]


def gain_kernel(
    u_ref, wq_ref, wk_ref, wv_ref, inner_ref, got_ref, after, out_ref, turned, rows_f32
):
    nq = wq_ref.shape[1]
    rows = u_ref.shape[0] // 2
    half = inner_ref.shape[0] // 2
    core = lax.axis_index("dp") & 1
    mine = add_wide(inner_ref[:half, :], got_ref[half:, :]).astype(BF)
    theirs = add_wide(inner_ref[half:, :], got_ref[:half, :]).astype(BF)
    out_ref[:half, :] = mine
    out_ref[half:, :] = jnp.zeros_like(out_ref[half:, :])
    turned[:, pl.ds(pl.multiple_of(core * half, half), half)] = mine.T
    turned[:, pl.ds(pl.multiple_of((1 - core) * half, half), half)] = theirs.T
    rows_f32[...] = jnp.zeros_like(rows_f32)
    for at in range(0, rows, CHUNK):
        place = pl.ds(pl.multiple_of(core * rows + at, CHUNK), CHUNK)
        against = nn(wq_ref[place, :], turned[:nq, :])
        narrow = jnp.concatenate([wk_ref[place, :], wv_ref[place, :]], axis=1)
        against += nn(narrow, turned[nq:, :])
        terms = against * u_ref[place, :].astype(F32)
        folded = sum(terms[:, side : side + HD] for side in range(0, terms.shape[1], HD))
        rows_f32[at // CHUNK : at // CHUNK + 1, :] = jnp.sum(folded.T, axis=0, keepdims=True)
    write_split(out_ref, half, rows_f32[...])


def gain_part(basis, wq, wk, wv, inner, got, after):
    wide, rank = basis.shape
    assert wide // 2 // CHUNK <= 8
    return pl.pallas_call(
        gain_kernel,
        in_specs=vmem(6) + [pl.BlockSpec(memory_space=pl.ANY)],
        out_specs=pl.BlockSpec(memory_space=pltpu.VMEM),
        out_shape=jax.ShapeDtypeStruct((rank // 2 + 16, inner.shape[1]), BF),
        scratch_shapes=[
            pltpu.VMEM((inner.shape[1], rank), BF),
            pltpu.VMEM((8, CHUNK), F32),
        ],
        compiler_params=pltpu.CompilerParams(vmem_limit_bytes=VMEM_BYTES),
        cost_estimate=cost(10**4, 10**3),
        name="pair_sum_and_gain_gradient",
    )(basis, wq, wk, wv, inner, got, after)


def merge_kernel(a_ref, b_ref, after, out_ref):
    half = out_ref.shape[0] - 16
    out_ref[:half, :] = add_wide(a_ref[:half, :], b_ref[:half, :]).astype(BF)
    out_ref[half:, :] = jnp.zeros_like(out_ref[half:, :])
    write_split(out_ref, half, read_split(a_ref, half) + read_split(b_ref, half))


def merge(a, b, after):
    return pl.pallas_call(
        merge_kernel,
        in_specs=vmem(2) + [pl.BlockSpec(memory_space=pl.ANY)],
        out_specs=pl.BlockSpec(memory_space=pltpu.VMEM),
        out_shape=jax.ShapeDtypeStruct(a.shape, BF),
        compiler_params=pltpu.CompilerParams(vmem_limit_bytes=VMEM_BYTES // 2),
        cost_estimate=cost(10**4, 10**3),
        name="sum_over_y",
    )(a, b, after)


def gather_kernel(own_ref, other_ref, out_ref):
    half = own_ref.shape[0] - 16
    out_ref[:8, :] = read_split(own_ref, half)
    out_ref[8:, :] = read_split(other_ref, half)


def gather_gain(own, other):
    return pl.pallas_call(
        gather_kernel,
        in_specs=vmem(2),
        out_specs=pl.BlockSpec(memory_space=pltpu.VMEM),
        out_shape=jax.ShapeDtypeStruct((16, CHUNK), F32),
        compiler_params=pltpu.CompilerParams(vmem_limit_bytes=VMEM_BYTES // 2),
        cost_estimate=cost(10**4, 10**3),
        name="gather_gain",
    )(own, other)


def add_kernel(a_ref, b_ref, after, out_ref):
    out_ref[...] = add_wide(a_ref[...], b_ref[...]).astype(out_ref.dtype)


def add_after(a, b, after):
    return pl.pallas_call(
        add_kernel,
        in_specs=vmem(2) + [pl.BlockSpec(memory_space=pl.ANY)],
        out_specs=pl.BlockSpec(memory_space=pltpu.VMEM),
        out_shape=jax.ShapeDtypeStruct(a.shape, a.dtype),
        compiler_params=pltpu.CompilerParams(vmem_limit_bytes=VMEM_BYTES // 2),
        cost_estimate=cost(10**4, 10**3),
        name="pair_sum",
    )(a, b, after)


def gather_halves(own_ref, other_ref, whole):
    half = whole.shape[0] // 2
    core = lax.axis_index("dp") & 1
    whole[pl.ds(pl.multiple_of(core * half, half), half), :] = own_ref[:half, :]
    whole[pl.ds(pl.multiple_of((1 - core) * half, half), half), :] = other_ref[:half, :]


def inward_kernel(u_ref, gain_ref, own_ref, other_ref, after, q_ref, k_ref, v_ref, inner):
    nq, nk = q_ref.shape[1], k_ref.shape[1]
    block = q_ref.shape[0]

    @pl.when(pl.program_id(0) == 0)
    def _():
        gather_halves(own_ref, other_ref, inner)

    step = lax.axis_index("dp") * pl.num_programs(0) + pl.program_id(0)
    rows = pl.ds(pl.multiple_of(step * block, block), block)
    gain = jnp.broadcast_to(gain_ref[:, rows], (HD, block)).T[:, :1]
    grad = nn(u_ref[rows, :], inner[...]) * gain
    q_ref[...] = grad[:, :nq].astype(BF)
    k_ref[...] = grad[:, nq : nq + nk].astype(BF)
    v_ref[...] = grad[:, nq + nk :].astype(BF)


def outward_kernel(u_ref, own_ref, other_ref, after, o_ref, inner):
    @pl.when(pl.program_id(0) == 0)
    def _():
        gather_halves(own_ref, other_ref, inner)

    block, rows = o_ref.shape
    at = pl.multiple_of(pl.program_id(0) * block, block)
    basis = u_ref[pl.ds(pl.multiple_of(lax.axis_index("dp") * rows, rows), rows), :]
    o_ref[...] = nt(inner[:, pl.ds(at, block)].T, basis).astype(BF)


STEPS = 2


def inward_grads(basis, gain, own, other, sizes, after):
    wide, rank = basis.shape
    rows = wide // lax.axis_size("dp")
    block = rows // STEPS
    return pl.pallas_call(
        inward_kernel,
        grid=(STEPS,),
        in_specs=vmem(4) + [pl.BlockSpec(memory_space=pl.ANY)],
        out_specs=[pl.BlockSpec((block, n), lambda i: (i, 0)) for n in sizes],
        scratch_shapes=[pltpu.VMEM((rank, sum(sizes)), BF)],
        out_shape=[jax.ShapeDtypeStruct((rows, n), BF) for n in sizes],
        compiler_params=pltpu.CompilerParams(vmem_limit_bytes=VMEM_BYTES),
        cost_estimate=cost(10**4, 10**3),
        name="inward_weight_gradients",
    )(basis, gain, own, other, after)


def outward_grad(basis, own, other, after):
    wide, rank = basis.shape
    rows = wide // lax.axis_size("dp")
    ne = own.shape[1]
    return pl.pallas_call(
        outward_kernel,
        grid=(STEPS,),
        in_specs=vmem(3) + [pl.BlockSpec(memory_space=pl.ANY)],
        out_specs=pl.BlockSpec((ne // STEPS, rows), lambda i: (i, 0)),
        scratch_shapes=[pltpu.VMEM((rank, ne), BF)],
        out_shape=jax.ShapeDtypeStruct((ne, rows), BF),
        compiler_params=pltpu.CompilerParams(vmem_limit_bytes=VMEM_BYTES),
        cost_estimate=cost(10**4, 10**3),
        name="output_weight_gradient",
    )(basis, own, other, after)


def results_kernel(
    wide, fbase_ref, y_ref, ygot_ref, base_ref, unit_ref, x_ref, xgot_ref, back_ref, inv_ref,
    gain_ref, gain_got_ref, after,
    f_ref, b_ref, gain_out_ref,
):
    f_ref[...] = (fbase_ref[...] + add_wide(y_ref[...], ygot_ref[...])).astype(BF)
    x = add_wide(x_ref[...], xgot_ref[...])
    inv = inv_ref[:, :1]
    along = jnp.sum(x * back_ref[...].astype(F32), axis=1, keepdims=True)
    middle = along * inv * (1.0 / wide)
    b_ref[...] = (base_ref[...] + (x - unit_ref[...] * middle) * inv).astype(BF)
    core = lax.axis_index("dp") & 1
    gain = gain_ref[...] + gain_got_ref[...]
    half = wide // 2
    for at in range(0, half, CHUNK):
        row = at // CHUNK
        mine = pl.ds(pl.multiple_of(core * half + at, CHUNK), CHUNK)
        theirs = pl.ds(pl.multiple_of((1 - core) * half + at, CHUNK), CHUNK)
        gain_out_ref[:, mine] = gain[row : row + 1, :]
        gain_out_ref[:, theirs] = gain[8 + row : 9 + row, :]


def results(wide, after, *operands):
    shape = operands[0].shape
    held = tuple(pltpu.with_memory_space_constraint(a, pltpu.VMEM) for a in operands)
    return pl.pallas_call(
        functools.partial(results_kernel, wide),
        in_specs=vmem(len(operands)) + [pl.BlockSpec(memory_space=pl.ANY)],
        out_specs=vmem(3),
        out_shape=[jax.ShapeDtypeStruct(shape, BF)] * 2 + [jax.ShapeDtypeStruct((1, wide), F32)],
        compiler_params=pltpu.CompilerParams(vmem_limit_bytes=VMEM_BYTES // 2),
        cost_estimate=cost(10**4, 10**3),
        name="section_results",
    )(*held, *in_hbm((after,)))


def body(
    new_coeffs,
    loss_grad,
    sent_forward,
    sent_backward,
    stashed,
    subspace,
    norm_gain,
    w_query,
    w_key,
    w_value,
    w_output,
):
    wide = subspace.shape[0]
    wq, wk, wv, wo = w_query[0], w_key[0], w_value[0], w_output[0]
    nq, nk, nv = wq.shape[1], wk.shape[1], wv.shape[1]
    back = stashed[0]
    arrived, returned = cross_pipe(sent_forward[0], sent_backward[0])
    cosine, sine = rope_tables(back.shape[0])

    m2, o2, g3, inv = project(back, norm_gain, subspace, wq, wk, wv, wo)
    inner, out_give, out_keep, x, base, unit = backward(
        back, loss_grad, returned, m2, o2, g3, inv, cosine, sine
    )
    out_got = swap(out_give, "dp", 1)
    inner_got = swap(inner, "dp", 1)
    x_got = swap(x, "tensor", 2)
    out_pair = add_wide(out_keep, out_got).astype(BF)
    out_got = swap(out_pair, "dp", 2)
    pair = gain_part(subspace, wq, wk, wv, inner, inner_got, out_pair)
    pair_got = swap(pair, "dp", 2)
    y, fbase = forward(new_coeffs, arrived, subspace, m2, o2, g3, cosine, sine, pair)
    y_got = swap(y, "tensor", 1)
    x = add_after(x, x_got, y)
    x_got = swap(x, "tensor", 1)
    out_own = add_after(out_pair, out_got, x)
    grad_o = outward_grad(subspace, out_own, swap(out_own, "dp", 1), x)
    y = add_after(y, y_got, *in_hbm((grad_o,)))
    y_got = swap(y, "tensor", 2)
    own = merge(pair, pair_got, y)
    other = swap(own, "dp", 1)
    gain = gather_gain(own, other)
    gain_got = swap(gain, "tensor", 1)
    grad_q, grad_k, grad_v = inward_grads(
        subspace, norm_gain, own, other, (nq, nk, nv), gain
    )
    gain = add_after(gain, gain_got, *in_hbm((grad_v,)))
    gain_got = swap(gain, "tensor", 2)
    forward_out, backward_out, grad_gain = results(
        wide, grad_v, fbase, y, y_got, base, unit, x, x_got, back, inv, gain, gain_got
    )
    return (
        forward_out[None],
        backward_out[None],
        grad_q[None],
        grad_k[None],
        grad_v[None],
        grad_o[None],
        grad_gain,
    )


def solution(mesh):
    return jax.shard_map(
        body,
        mesh=mesh,
        in_specs=(
            P("dp", None),
            P("dp", None),
            P("pipe", "dp", None),
            P("pipe", "dp", None),
            P("pipe", "dp", None),
            P(),
            P("pipe", None),
            P("pipe", None, "tensor"),
            P("pipe", None, "tensor"),
            P("pipe", None, "tensor"),
            P("pipe", "tensor", None),
        ),
        out_specs=(
            P("pipe", "dp", None),
            P("pipe", "dp", None),
            P("pipe", "dp", "tensor"),
            P("pipe", "dp", "tensor"),
            P("pipe", "dp", "tensor"),
            P("pipe", "tensor", "dp"),
            P("pipe", None),
        ),
        check_vma=False,
    )
```

```python
import functools
import math

import jax
import jax.numpy as jnp
import numpy as np
from jax import lax
from jax.experimental import pallas as pl
from jax.experimental.pallas import tpu as pltpu
from jax.sharding import PartitionSpec as P

HD = 128
EPSILON = 1e-05
ROPE_BASE = 500000.0
BF = jnp.bfloat16
F32 = jnp.float32
VMEM_BYTES = 24 * 1024 * 1024
CHUNK = 512
PIECE = 1024
AHEAD = 3
LOG2E = 1.4426950408889634


def shifted(x, axis, by):
    devices = lax.axis_size(axis)
    pairs = [(i, i + by) for i in range(devices) if 0 <= i + by < devices]
    return lax.ppermute(x, axis, pairs)


def swap(x, axis, bit):
    devices = lax.axis_size(axis)
    return lax.ppermute(x, axis, [(i, i ^ bit) for i in range(devices)])


def cross_pipe(sent_forward, sent_backward):
    if lax.axis_size("pipe") != 2:
        return shifted(sent_forward, "pipe", 1), shifted(sent_backward, "pipe", -1)
    first = lax.axis_index("pipe") == 0
    got = swap(jnp.where(first, sent_forward, sent_backward), "pipe", 1)
    return got, got


def add_wide(a, b):
    return a.astype(F32) + b.astype(F32)


def nt(a, b):
    return lax.dot_general(a, b, (((1,), (1,)), ((), ())), preferred_element_type=F32)


def nn(a, b):
    return jnp.dot(a, b, preferred_element_type=F32)


def split(x, parts):
    out = []
    for _ in range(parts):
        piece = x.astype(BF)
        out.append(piece)
        x = x - piece.astype(F32)
    return out


def rope_tables(length):
    half = HD // 2
    frequency = np.float32(ROPE_BASE) ** (-2.0 * np.arange(half, dtype=np.float32) / HD)
    angles = np.arange(length, dtype=np.float32)[:, None] * frequency.astype(np.float32)
    cosine, sine = np.cos(angles), np.sin(angles)
    tables = (np.concatenate([cosine, cosine], 1), np.concatenate([-sine, sine], 1))
    return tuple(jnp.asarray(t, dtype=F32) for t in tables)


def rope(x, cosine, sine):
    return x * cosine + pltpu.roll(x, HD // 2, 1) * sine


def unrope(x, cosine, sine):
    return x * cosine - pltpu.roll(x, HD // 2, 1) * sine


def inverse_root(square_sum, width):
    return 1.0 / jnp.sqrt(square_sum / width + EPSILON)


def vmem(count):
    return [pl.BlockSpec(memory_space=pltpu.VMEM)] * count


def in_hbm(arrays):
    return tuple(pltpu.with_memory_space_constraint(a, pltpu.HBM) for a in arrays)


def cost(flops, num_bytes, exps=0):
    return pl.CostEstimate(flops=flops, bytes_accessed=num_bytes, transcendentals=exps)


def project_kernel(
    back_hbm, gain_hbm, u_hbm, wq_hbm, wk_hbm, wv_hbm, wo_hbm,
    m_ref, o_ref, g_ref, inv_ref, u, wq, narrow,
    back, gain, wo, turned, scaled, m_acc, o_acc, sems,
):
    wide, rank = u.shape
    nq = wq.shape[1]
    nk = wk_hbm.shape[1]
    parts = wide // PIECE
    pieces = [pl.ds(i * PIECE, PIECE) for i in range(parts)]
    pairs = [(back_hbm, back), (gain_hbm, gain), (u_hbm, u)]
    pairs += [(wq_hbm.at[at, :], wq.at[at, :]) for at in pieces[:2]]
    pairs += [(wk_hbm, narrow.at[:, pl.ds(0, nk)])]
    pairs += [(wv_hbm, narrow.at[:, pl.ds(nk, narrow.shape[1] - nk)])]
    pairs += [(wq_hbm.at[at, :], wq.at[at, :]) for at in pieces[2:]]
    pairs += [(wo_hbm.at[:, at], wo.at[:, at]) for at in pieces]
    copies = [
        pltpu.make_async_copy(source, target, sems.at[n])
        for n, (source, target) in enumerate(pairs)
    ]
    started = 0

    def start_to(count):
        nonlocal started
        for copy in copies[started:count]:
            copy.start()
        started = max(started, min(count, len(copies)))

    def wait(n):
        start_to(n + 1 + AHEAD)
        copies[n].wait()

    start_to(3 + AHEAD)
    for n in range(3):
        copies[n].wait()
    turned[...] = u[...].T
    scaled[...] = (turned[...].astype(F32) * gain[...]).astype(BF)
    gram = nn(turned[...], u[...])
    for i, piece in enumerate(split(gram, 3)):
        g_ref[i * rank : (i + 1) * rank, :] = piece
    square = jnp.zeros((back.shape[0], HD), F32)
    for at in range(0, wide, PIECE):
        decoded = nn(back[...], turned[:, at : at + PIECE])
        for side in range(0, PIECE, HD):
            part = decoded[:, side : side + HD]
            square = square + part * part
    inv_ref[...] = jnp.broadcast_to(
        inverse_root(jnp.sum(square, axis=1, keepdims=True), wide), inv_ref.shape
    )
    place = 3
    for i, at in enumerate(pieces):
        if i == 2:
            wait(place)
            wait(place + 1)
            place += 2
            for p, piece in enumerate(split(nn(scaled[...], narrow[...]), 2)):
                m_ref[p * rank : (p + 1) * rank, nq:] = piece
        wait(place)
        place += 1
        part = nn(scaled[:, at], wq[at, :])
        if i == 0:
            m_acc[...] = part
        else:
            m_acc[...] += part
    for p, piece in enumerate(split(m_acc[...], 2)):
        m_ref[p * rank : (p + 1) * rank, :nq] = piece
    for i, at in enumerate(pieces):
        wait(place)
        place += 1
        part = nn(wo[:, at], u[at, :])
        if i == 0:
            o_acc[...] = part
        else:
            o_acc[...] += part
    o_ref[...] = o_acc[...].astype(BF)


def project(back, gain, basis, wq, wk, wv, wo):
    wide, rank = basis.shape
    length = back.shape[0]
    ne = wo.shape[0]
    nq = wq.shape[1]
    rest = wk.shape[1] + wv.shape[1]
    operands = in_hbm((back, gain, basis, wq, wk, wv, wo))
    return pl.pallas_call(
        project_kernel,
        in_specs=[pl.BlockSpec(memory_space=pltpu.HBM)] * len(operands),
        out_specs=vmem(7),
        out_shape=[
            jax.ShapeDtypeStruct((2 * rank, nq + rest), BF),
            jax.ShapeDtypeStruct((ne, rank), BF),
            jax.ShapeDtypeStruct((3 * rank, rank), BF),
            jax.ShapeDtypeStruct((length, HD), F32),
            jax.ShapeDtypeStruct(basis.shape, BF),
            jax.ShapeDtypeStruct(wq.shape, BF),
            jax.ShapeDtypeStruct((wide, rest), BF),
        ],
        scratch_shapes=[
            pltpu.VMEM(back.shape, BF),
            pltpu.VMEM(gain.shape, F32),
            pltpu.VMEM(wo.shape, BF),
            pltpu.VMEM((rank, wide), BF),
            pltpu.VMEM((rank, wide), BF),
            pltpu.VMEM((rank, nq), F32),
            pltpu.VMEM((ne, rank), F32),
            pltpu.SemaphoreType.DMA((5 + 2 * (wide // PIECE),)),
        ],
        compiler_params=pltpu.CompilerParams(vmem_limit_bytes=VMEM_BYTES * 3 // 2),
        cost_estimate=cost(6 * 10**9, 20 * 10**6),
        name="project_weights",
    )(*operands)


def project_heads(coeffs, inv, m_ref, cosine, sine, q, k, v1):
    length = coeffs.shape[0]
    heads = q.shape[0] // length
    twice = jnp.concatenate([coeffs, coeffs], axis=1)
    for h in range(heads):
        part = nn(twice, m_ref[:, h * HD : (h + 1) * HD]) * inv
        q[h * length : (h + 1) * length, :] = rope(part, cosine, sine).astype(BF)
    part = nn(twice, m_ref[:, heads * HD :]) * inv
    k[...] = rope(part[:, :HD], cosine, sine).astype(BF)
    v1[:, :HD] = part[:, HD:].astype(BF)
    v1[:, HD:] = jnp.ones_like(v1[:, HD:])


def exps_of(scores, exps, low, length):
    row = lax.broadcasted_iota(jnp.int32, (length, length), 0)
    column = lax.broadcasted_iota(jnp.int32, (length, length), 1)
    causal = row >= column

    def one(h, _):
        at = pl.ds(pl.multiple_of(h * length, length), length)
        s = jnp.where(causal, scores[at, :], -jnp.inf)
        top = jnp.max(s, axis=1, keepdims=True)
        e = jnp.exp2((s - top) * (LOG2E / math.sqrt(HD)))
        if exps is not None:
            exps[at, :] = e
        low[at, :] = e.astype(BF)
        return 0

    lax.fori_loop(0, scores.shape[0] // length, one, 0, unroll=2)


def backward_kernel(
    back_ref, loss_ref, sent_ref, m_ref, o_ref, g_ref, inv_ref, cos_ref, sin_ref,
    inner_ref, out_give_ref, out_keep_ref, x_ref, base_ref, unit_ref,
    q, k, v1, gh, ghs, scores, low, mixed, gp, ds, dq, heads, grads, inner, out_inner,
):
    length, rank = back_ref.shape
    ne = o_ref.shape[0]
    count = ne // HD
    scale = 1.0 / math.sqrt(HD)
    last = lax.axis_size("pipe") - 1
    is_last = lax.axis_index("pipe") == last
    back = back_ref[...]
    up = jnp.where(is_last, loss_ref[...], sent_ref[...])
    cosine, sine = cos_ref[...], sin_ref[...]
    inv = inv_ref[...]
    project_heads(back, inv[:, :1], m_ref, cosine, sine, q, k, v1)
    scores[...] = nt(q[...], k[...])
    for h in range(count):
        gh[h * length : (h + 1) * length, :] = nt(up, o_ref[h * HD : (h + 1) * HD, :]).astype(BF)
    exps_of(scores, scores, low, length)
    mixed[...] = nn(low[...], v1[...])
    gp[...] = nt(gh[...], v1[:, :HD])

    for h in range(count):
        at = slice(h * length, (h + 1) * length)
        inverse = 1.0 / mixed[at, HD:]
        out = mixed[at, :HD] * inverse
        heads[:, h * HD : (h + 1) * HD] = out.astype(BF)
        grad = gh[at, :].astype(F32)
        ghs[at, :] = (grad * inverse).astype(BF)
        delta = jnp.sum(grad * out, axis=1, keepdims=True)
        factor = inverse * scale
        for side in range(0, length, HD):
            part = scores[at, side : side + HD] * factor
            ds[at, side : side + HD] = (part * (gp[at, side : side + HD] - delta)).astype(BF)

    dq[...] = nn(ds[...], k[...])
    for h in range(count):
        part = dq[h * length : (h + 1) * length, :]
        grads[:, h * HD : (h + 1) * HD] = unrope(part, cosine, sine).astype(BF)
    dk = nn(q[...].T, ds[...]).T
    grads[:, ne : ne + HD] = unrope(dk, cosine, sine).astype(BF)
    grads[:, ne + HD :] = nn(ghs[...].T, low[...]).T.astype(BF)
    unit = (back.astype(F32) * inv[:, :1]).astype(BF)
    half = rank // 2
    core = lax.axis_index("dp") & 1
    mine = pl.ds(pl.multiple_of(core * half, half), half)
    theirs = pl.ds(pl.multiple_of((1 - core) * half, half), half)
    inner[...] = nn(unit.T, grads[...]).astype(BF)
    inner_ref[:half, :] = inner[mine, :]
    inner_ref[half:, :] = inner[theirs, :]
    out_inner[...] = nn(up.T, heads[...]).astype(BF)
    out_keep_ref[...] = out_inner[mine, :]
    out_give_ref[...] = out_inner[theirs, :]
    x_ref[...] = nt(grads[...], m_ref[:rank, :]).astype(BF)
    base_ref[...] = nn(jnp.concatenate([up] * 3, axis=1), g_ref[...])
    unit_ref[...] = nn(jnp.concatenate([back] * 3, axis=1), g_ref[...]) * inv[:, :1]


def backward(back, loss, sent, m2, o2, g3, inv, cosine, sine):
    length, rank = back.shape
    ne = o2.shape[0]
    total = m2.shape[1]
    assert total == ne + 2 * HD
    stack = ne // HD * length
    return pl.pallas_call(
        backward_kernel,
        in_specs=vmem(9),
        out_specs=vmem(6),
        out_shape=[
            jax.ShapeDtypeStruct((rank, total), BF),
            jax.ShapeDtypeStruct((rank // 2, ne), BF),
            jax.ShapeDtypeStruct((rank // 2, ne), BF),
            jax.ShapeDtypeStruct((length, rank), BF),
            jax.ShapeDtypeStruct((length, rank), F32),
            jax.ShapeDtypeStruct((length, rank), F32),
        ],
        scratch_shapes=[
            pltpu.VMEM((stack, HD), BF),
            pltpu.VMEM((length, HD), BF),
            pltpu.VMEM((length, 2 * HD), BF),
            pltpu.VMEM((stack, HD), BF),
            pltpu.VMEM((stack, HD), BF),
            pltpu.VMEM((stack, length), F32),
            pltpu.VMEM((stack, length), BF),
            pltpu.VMEM((stack, 2 * HD), F32),
            pltpu.VMEM((stack, length), F32),
            pltpu.VMEM((stack, length), BF),
            pltpu.VMEM((stack, HD), F32),
            pltpu.VMEM((length, ne), BF),
            pltpu.VMEM((length, total), BF),
            pltpu.VMEM((rank, total), BF),
            pltpu.VMEM((rank, ne), BF),
        ],
        compiler_params=pltpu.CompilerParams(vmem_limit_bytes=VMEM_BYTES),
        cost_estimate=cost(10**4, 10**3),
        name="attention_backward",
    )(back, loss, sent, m2, o2, g3, inv, cosine, sine)


def forward_kernel(
    new_ref, sent_ref, u_ref, m_ref, o_ref, g_ref, cos_ref, sin_ref, *rest,
):
    y_ref, base_ref, q, k, v1, scores, low, mixed, heads = rest[-9:]
    length, rank = new_ref.shape
    wide = u_ref.shape[0]
    is_first = lax.axis_index("pipe") == 0
    coeffs = jnp.where(is_first, new_ref[...], sent_ref[...])
    square = jnp.zeros((length, HD), F32)
    block = 512
    for at in range(0, wide, block):
        decoded = nt(coeffs, u_ref[at : at + block, :])
        for side in range(0, block, HD):
            part = decoded[:, side : side + HD]
            square = square + part * part
    inv = inverse_root(jnp.sum(square, axis=1, keepdims=True), wide)
    project_heads(coeffs, inv, m_ref, cos_ref[...], sin_ref[...], q, k, v1)
    scores[...] = nt(q[...], k[...])
    exps_of(scores, None, low, length)
    mixed[...] = nn(low[...], v1[...])
    for h in range(heads.shape[1] // HD):
        at = slice(h * length, (h + 1) * length)
        heads[:, h * HD : (h + 1) * HD] = (mixed[at, :HD] / mixed[at, HD:]).astype(BF)
    y_ref[...] = nn(heads[...], o_ref[...]).astype(BF)
    base_ref[...] = nn(jnp.concatenate([coeffs] * 3, axis=1), g_ref[...])


def forward(new, sent, basis, m2, o2, g3, cosine, sine, *after):
    length, rank = new.shape
    ne = o2.shape[0]
    stack = ne // HD * length
    return pl.pallas_call(
        forward_kernel,
        in_specs=vmem(8) + [pl.BlockSpec(memory_space=pl.ANY)] * len(after),
        out_specs=vmem(2),
        out_shape=[
            jax.ShapeDtypeStruct((length, rank), BF),
            jax.ShapeDtypeStruct((length, rank), F32),
        ],
        scratch_shapes=[
            pltpu.VMEM((stack, HD), BF),
            pltpu.VMEM((length, HD), BF),
            pltpu.VMEM((length, 2 * HD), BF),
            pltpu.VMEM((stack, length), F32),
            pltpu.VMEM((stack, length), BF),
            pltpu.VMEM((stack, 2 * HD), F32),
            pltpu.VMEM((length, ne), BF),
        ],
        compiler_params=pltpu.CompilerParams(vmem_limit_bytes=VMEM_BYTES),
        cost_estimate=cost(10**4, 10**3),
        name="attention_forward",
    )(new, sent, basis, m2, o2, g3, cosine, sine, *after)


def write_split(ref, value):
    high, low = split(value, 2)
    both = jnp.concatenate([high.astype(F32), low.astype(F32)], axis=0)
    ref[ref.shape[0] - 16 :, :] = both.astype(BF)


def read_split(ref):
    both = ref[ref.shape[0] - 16 :, :].astype(F32)
    return both[:8] + both[8:]


def gain_kernel(
    u_ref, wq_ref, narrow_ref, inner_ref, got_ref, x_ref, after,
    pair_ref, out_ref, turned, rows_f32,
):
    nq = wq_ref.shape[1]
    rows = u_ref.shape[0] // 2
    rank = u_ref.shape[1]
    half = inner_ref.shape[0] // 2
    core = lax.axis_index("dp") & 1
    mine = add_wide(inner_ref[:half, :], got_ref[half:, :]).astype(BF)
    theirs = add_wide(inner_ref[half:, :], got_ref[:half, :]).astype(BF)
    pair_ref[...] = mine
    out_ref[: x_ref.shape[0], :] = x_ref[...]
    turned[:, pl.ds(pl.multiple_of(core * half, half), half)] = mine.T
    turned[:, pl.ds(pl.multiple_of((1 - core) * half, half), half)] = theirs.T
    for at in range(0, rows, CHUNK):
        place = pl.ds(pl.multiple_of(core * rows + at, CHUNK), CHUNK)
        against = nn(wq_ref[place, :], turned[:nq, :])
        against += nn(narrow_ref[place, :], turned[nq:, :])
        terms = against * u_ref[place, :].astype(F32)
        folded = sum(terms[:, side : side + HD] for side in range(0, terms.shape[1], HD))
        line = jnp.sum(folded.T, axis=0, keepdims=True)
        for side in range(0, CHUNK, rank):
            row = (at + side) // rank
            rows_f32[row : row + 1, :] = line[:, side : side + rank]
    write_split(out_ref, rows_f32[...])


def gain_part(basis, wq, narrow, inner, got, x, after):
    wide, rank = basis.shape
    assert wide // 2 == 8 * rank
    held = tuple(pltpu.with_memory_space_constraint(a, pltpu.VMEM) for a in (basis, wq, narrow))
    return pl.pallas_call(
        gain_kernel,
        in_specs=vmem(6) + [pl.BlockSpec(memory_space=pl.ANY)],
        out_specs=vmem(2),
        out_shape=[
            jax.ShapeDtypeStruct((rank // 2, inner.shape[1]), BF),
            jax.ShapeDtypeStruct((x.shape[0] + 16, rank), BF),
        ],
        scratch_shapes=[
            pltpu.VMEM((inner.shape[1], rank), BF),
            pltpu.VMEM((8, rank), F32),
        ],
        compiler_params=pltpu.CompilerParams(vmem_limit_bytes=VMEM_BYTES),
        cost_estimate=cost(10**4, 10**3),
        name="pair_sum_and_gain_gradient",
    )(*held, inner, got, x, after)


def merge_kernel(a_ref, b_ref, after, out_ref):
    rest = out_ref.shape[0] - 16
    out_ref[:rest, :] = add_wide(a_ref[:rest, :], b_ref[:rest, :]).astype(BF)
    write_split(out_ref, read_split(a_ref) + read_split(b_ref))


def total_kernel(a_ref, b_ref, after, out_ref):
    out_ref[...] = read_split(a_ref) + read_split(b_ref)


def own_kernel(a_ref, b_ref, after, *out_refs):
    at = 0
    for ref in out_refs:
        size = ref.shape[1]
        ref[...] = add_wide(a_ref[:, at : at + size], b_ref[:, at : at + size]).astype(BF)
        at += size


def small_kernel(kernel, name, out_shape, a, b, after):
    return pl.pallas_call(
        kernel,
        in_specs=vmem(2) + [pl.BlockSpec(memory_space=pl.ANY)],
        out_specs=jax.tree.map(lambda _: pl.BlockSpec(memory_space=pltpu.VMEM), out_shape),
        out_shape=out_shape,
        compiler_params=pltpu.CompilerParams(vmem_limit_bytes=VMEM_BYTES // 2),
        cost_estimate=cost(10**4, 10**3),
        name=name,
    )(a, b, after)


def merge(a, b, after):
    return small_kernel(merge_kernel, "sum_with_gain", jax.ShapeDtypeStruct(a.shape, BF), a, b, after)


def gain_total(a, b, after):
    shape = jax.ShapeDtypeStruct((8, a.shape[1]), F32)
    return small_kernel(total_kernel, "gain_total", shape, a, b, after)


def own_pieces(a, b, sizes, after):
    shapes = [jax.ShapeDtypeStruct((a.shape[0], n), BF) for n in sizes]
    return small_kernel(own_kernel, "sum_over_y", shapes, a, b, after)


def add_kernel(a_ref, b_ref, after, out_ref):
    out_ref[...] = add_wide(a_ref[...], b_ref[...]).astype(out_ref.dtype)


def add_after(a, b, after):
    return small_kernel(add_kernel, "pair_sum", jax.ShapeDtypeStruct(a.shape, a.dtype), a, b, after)


def gather_halves(own_refs, other_refs, whole):
    half = whole.shape[0] // 2
    core = lax.axis_index("dp") & 1
    at = 0
    for own_ref, other_ref in zip(own_refs, other_refs):
        columns = pl.ds(at, own_ref.shape[1])
        whole[pl.ds(pl.multiple_of(core * half, half), half), columns] = own_ref[...]
        whole[pl.ds(pl.multiple_of((1 - core) * half, half), half), columns] = other_ref[...]
        at += own_ref.shape[1]


def inward_kernel(pieces, u_ref, gain_ref, *refs):
    own_refs, other_refs = refs[:pieces], refs[pieces : 2 * pieces]
    q_ref, k_ref, v_ref, inner = refs[-4:]
    nq, nk = q_ref.shape[1], k_ref.shape[1]
    block = q_ref.shape[0]

    @pl.when(pl.program_id(0) == 0)
    def _():
        gather_halves(own_refs, other_refs, inner)

    step = lax.axis_index("dp") * pl.num_programs(0) + pl.program_id(0)
    rows = pl.ds(pl.multiple_of(step * block, block), block)
    gain = jnp.broadcast_to(gain_ref[:, rows], (HD, block)).T[:, :1]
    grad = nn(u_ref[rows, :], inner[...]) * gain
    q_ref[...] = grad[:, :nq].astype(BF)
    k_ref[...] = grad[:, nq : nq + nk].astype(BF)
    v_ref[...] = grad[:, nq + nk :].astype(BF)


def outward_kernel(u_ref, own_ref, other_ref, after, o_ref, inner):
    @pl.when(pl.program_id(0) == 0)
    def _():
        gather_halves([own_ref], [other_ref], inner)

    block, rows = o_ref.shape
    at = pl.multiple_of(pl.program_id(0) * block, block)
    basis = u_ref[pl.ds(pl.multiple_of(lax.axis_index("dp") * rows, rows), rows), :]
    o_ref[...] = nt(inner[:, pl.ds(at, block)].T, basis).astype(BF)


STEPS = 2


def inward_grads(basis, gain, own, other, sizes, after):
    wide, rank = basis.shape
    rows = wide // lax.axis_size("dp")
    block = rows // STEPS
    return pl.pallas_call(
        functools.partial(inward_kernel, len(own)),
        grid=(STEPS,),
        in_specs=vmem(2 + 2 * len(own)) + [pl.BlockSpec(memory_space=pl.ANY)],
        out_specs=[pl.BlockSpec((block, n), lambda i: (i, 0)) for n in sizes],
        scratch_shapes=[pltpu.VMEM((rank, sum(sizes)), BF)],
        out_shape=[jax.ShapeDtypeStruct((rows, n), BF) for n in sizes],
        compiler_params=pltpu.CompilerParams(vmem_limit_bytes=VMEM_BYTES),
        cost_estimate=cost(10**4, 10**3),
        name="inward_weight_gradients",
    )(basis, gain, *own, *other, after)


def outward_grad(basis, own, other, after):
    wide, rank = basis.shape
    rows = wide // lax.axis_size("dp")
    ne = own.shape[1]
    return pl.pallas_call(
        outward_kernel,
        grid=(STEPS,),
        in_specs=vmem(3) + [pl.BlockSpec(memory_space=pl.ANY)],
        out_specs=pl.BlockSpec((ne // STEPS, rows), lambda i: (i, 0)),
        scratch_shapes=[pltpu.VMEM((rank, ne), BF)],
        out_shape=jax.ShapeDtypeStruct((ne, rows), BF),
        compiler_params=pltpu.CompilerParams(vmem_limit_bytes=VMEM_BYTES),
        cost_estimate=cost(10**4, 10**3),
        name="output_weight_gradient",
    )(basis, own, other, after)


def results_kernel(
    wide, fbase_ref, y_ref, ygot_ref, base_ref, unit_ref, x_ref, xgot_ref, back_ref, inv_ref,
    gain_ref, gain_other_ref, after,
    f_ref, b_ref, gain_out_ref,
):
    f_ref[...] = (fbase_ref[...] + add_wide(y_ref[...], ygot_ref[...])).astype(BF)
    length = back_ref.shape[0]
    x = add_wide(x_ref[:length, :], xgot_ref[:length, :])
    inv = inv_ref[:, :1]
    along = jnp.sum(x * back_ref[...].astype(F32), axis=1, keepdims=True)
    middle = along * inv * (1.0 / wide)
    b_ref[...] = (base_ref[...] + (x - unit_ref[...] * middle) * inv).astype(BF)
    core = lax.axis_index("dp") & 1
    half = wide // 2
    rank = gain_ref.shape[1]
    for row in range(half // rank):
        mine = pl.ds(pl.multiple_of(core * half + row * rank, rank), rank)
        theirs = pl.ds(pl.multiple_of((1 - core) * half + row * rank, rank), rank)
        gain_out_ref[:, mine] = gain_ref[row : row + 1, :]
        gain_out_ref[:, theirs] = gain_other_ref[row : row + 1, :]


def results(wide, after, *operands):
    shape = operands[0].shape
    held = tuple(pltpu.with_memory_space_constraint(a, pltpu.VMEM) for a in operands)
    return pl.pallas_call(
        functools.partial(results_kernel, wide),
        in_specs=vmem(len(operands)) + [pl.BlockSpec(memory_space=pl.ANY)],
        out_specs=vmem(3),
        out_shape=[jax.ShapeDtypeStruct(shape, BF)] * 2 + [jax.ShapeDtypeStruct((1, wide), F32)],
        compiler_params=pltpu.CompilerParams(vmem_limit_bytes=VMEM_BYTES // 2),
        cost_estimate=cost(10**4, 10**3),
        name="section_results",
    )(*held, *in_hbm((after,)))


def body(
    new_coeffs,
    loss_grad,
    sent_forward,
    sent_backward,
    stashed,
    subspace,
    norm_gain,
    w_query,
    w_key,
    w_value,
    w_output,
):
    wide = subspace.shape[0]
    wq, wk, wv, wo = w_query[0], w_key[0], w_value[0], w_output[0]
    nq, nk, nv = wq.shape[1], wk.shape[1], wv.shape[1]
    back = stashed[0]
    arrived, returned = cross_pipe(sent_forward[0], sent_backward[0])
    cosine, sine = rope_tables(back.shape[0])

    m2, o2, g3, inv, basis, wq, narrow = project(back, norm_gain, subspace, wq, wk, wv, wo)
    inner, out_give, out_keep, x, base, unit = backward(
        back, loss_grad, returned, m2, o2, g3, inv, cosine, sine
    )
    out_got = swap(out_give, "dp", 1)
    inner_got = swap(inner, "dp", 1)
    out_pair = add_wide(out_keep, out_got).astype(BF)
    out_got = swap(out_pair, "dp", 2)
    pair, x = gain_part(basis, wq, narrow, inner, inner_got, x, out_pair)
    pair_got = swap(pair, "dp", 2)
    x_got = swap(x, "tensor", 1)
    y, fbase = forward(new_coeffs, arrived, basis, m2, o2, g3, cosine, sine, pair)
    y_got = swap(y, "tensor", 1)
    x = merge(x, x_got, y)
    x_got = swap(x, "tensor", 2)
    out_own = add_after(out_pair, out_got, x)
    grad_o = outward_grad(basis, out_own, swap(out_own, "dp", 1), x)
    y = add_after(y, y_got, *in_hbm((grad_o,)))
    y_got = swap(y, "tensor", 2)
    own = own_pieces(pair, pair_got, (nq // 2, nq - nq // 2, nk + nv), y)
    other = [swap(piece, "dp", 1) for piece in own]
    gain = gain_total(x, x_got, own[0])
    gain_got = swap(gain, "dp", 2)
    grad_q, grad_k, grad_v = inward_grads(basis, norm_gain, own, other, (nq, nk, nv), gain)
    gain = add_after(gain, gain_got, *in_hbm((grad_v,)))
    gain_other = swap(gain, "dp", 1)
    forward_out, backward_out, grad_gain = results(
        wide, grad_v, fbase, y, y_got, base, unit, x, x_got, back, inv, gain, gain_other
    )
    return (
        forward_out[None],
        backward_out[None],
        grad_q[None],
        grad_k[None],
        grad_v[None],
        grad_o[None],
        grad_gain,
    )


def solution(mesh):
    return jax.shard_map(
        body,
        mesh=mesh,
        in_specs=(
            P("dp", None),
            P("dp", None),
            P("pipe", "dp", None),
            P("pipe", "dp", None),
            P("pipe", "dp", None),
            P(),
            P("pipe", None),
            P("pipe", None, "tensor"),
            P("pipe", None, "tensor"),
            P("pipe", None, "tensor"),
            P("pipe", "tensor", None),
        ),
        out_specs=(
            P("pipe", "dp", None),
            P("pipe", "dp", None),
            P("pipe", "dp", "tensor"),
            P("pipe", "dp", "tensor"),
            P("pipe", "dp", "tensor"),
            P("pipe", "tensor", "dp"),
            P("pipe", None),
        ),
        check_vma=False,
    )
```

```python
import functools
import math

import jax
import jax.numpy as jnp
import numpy as np
from jax import lax
from jax.experimental import pallas as pl
from jax.experimental.pallas import tpu as pltpu
from jax.sharding import PartitionSpec as P

HD = 128
EPSILON = 1e-05
ROPE_BASE = 500000.0
BF = jnp.bfloat16
F32 = jnp.float32
VMEM_BYTES = 24 * 1024 * 1024
CHUNK = 512
PIECE = 1024
AHEAD = 3
LOG2E = 1.4426950408889634


def shifted(x, axis, by):
    devices = lax.axis_size(axis)
    pairs = [(i, i + by) for i in range(devices) if 0 <= i + by < devices]
    return lax.ppermute(x, axis, pairs)


def swap(x, axis, bit):
    devices = lax.axis_size(axis)
    return lax.ppermute(x, axis, [(i, i ^ bit) for i in range(devices)])


def cross_pipe(sent_forward, sent_backward):
    if lax.axis_size("pipe") != 2:
        return shifted(sent_forward, "pipe", 1), shifted(sent_backward, "pipe", -1)
    first = lax.axis_index("pipe") == 0
    got = swap(jnp.where(first, sent_forward, sent_backward), "pipe", 1)
    return got, got


def add_wide(a, b):
    return a.astype(F32) + b.astype(F32)


def nt(a, b):
    return lax.dot_general(a, b, (((1,), (1,)), ((), ())), preferred_element_type=F32)


def nn(a, b):
    return jnp.dot(a, b, preferred_element_type=F32)


def split(x, parts):
    out = []
    for _ in range(parts):
        piece = x.astype(BF)
        out.append(piece)
        x = x - piece.astype(F32)
    return out


def rope_tables(length):
    half = HD // 2
    frequency = np.float32(ROPE_BASE) ** (-2.0 * np.arange(half, dtype=np.float32) / HD)
    angles = np.arange(length, dtype=np.float32)[:, None] * frequency.astype(np.float32)
    cosine, sine = np.cos(angles), np.sin(angles)
    tables = (np.concatenate([cosine, cosine], 1), np.concatenate([-sine, sine], 1))
    return tuple(jnp.asarray(t, dtype=F32) for t in tables)


def rope(x, cosine, sine):
    return x * cosine + pltpu.roll(x, HD // 2, 1) * sine


def unrope(x, cosine, sine):
    return x * cosine - pltpu.roll(x, HD // 2, 1) * sine


def inverse_root(square_sum, width):
    return 1.0 / jnp.sqrt(square_sum / width + EPSILON)


def vmem(count):
    return [pl.BlockSpec(memory_space=pltpu.VMEM)] * count


def in_hbm(arrays):
    return tuple(pltpu.with_memory_space_constraint(a, pltpu.HBM) for a in arrays)


def cost(flops, num_bytes, exps=0):
    return pl.CostEstimate(flops=flops, bytes_accessed=num_bytes, transcendentals=exps)


def project_kernel(
    back_hbm, gain_hbm, u_hbm, wq_hbm, wk_hbm, wv_hbm, wo_hbm,
    m_ref, o_ref, inv_ref, u, wq, narrow, turned,
    back, gain, wo, scaled, m_acc, o_acc, sems,
):
    wide, rank = u.shape
    nq = wq.shape[1]
    nk = wk_hbm.shape[1]
    parts = wide // PIECE
    pieces = [pl.ds(i * PIECE, PIECE) for i in range(parts)]
    pairs = [(back_hbm, back), (gain_hbm, gain)]
    pairs += [(u_hbm.at[at, :], u.at[at, :]) for at in pieces]
    pairs += [(wq_hbm.at[at, :], wq.at[at, :]) for at in pieces[:2]]
    pairs += [(wk_hbm, narrow.at[:, pl.ds(0, nk)])]
    pairs += [(wv_hbm, narrow.at[:, pl.ds(nk, narrow.shape[1] - nk)])]
    pairs += [(wq_hbm.at[at, :], wq.at[at, :]) for at in pieces[2:]]
    pairs += [(wo_hbm.at[:, at], wo.at[:, at]) for at in pieces]
    copies = [
        pltpu.make_async_copy(source, target, sems.at[n])
        for n, (source, target) in enumerate(pairs)
    ]
    started = 0

    def start_to(count):
        nonlocal started
        for copy in copies[started:count]:
            copy.start()
        started = max(started, min(count, len(copies)))

    def wait(n):
        start_to(n + 1 + AHEAD)
        copies[n].wait()

    start_to(2 + parts + AHEAD)
    copies[0].wait()
    copies[1].wait()
    square = jnp.zeros((back.shape[0], HD), F32)
    for i, at in enumerate(pieces):
        copies[2 + i].wait()
        turned[:, at] = u[at, :].T
        scaled[:, at] = (turned[:, at].astype(F32) * gain[:, at]).astype(BF)
        decoded = nn(back[...], turned[:, at])
        for side in range(0, PIECE, HD):
            part = decoded[:, side : side + HD]
            square = square + part * part
    inv_ref[...] = jnp.broadcast_to(
        inverse_root(jnp.sum(square, axis=1, keepdims=True), wide), inv_ref.shape
    )
    place = 2 + parts
    for i, at in enumerate(pieces):
        if i == 2:
            wait(place)
            wait(place + 1)
            place += 2
            for p, piece in enumerate(split(nn(scaled[...], narrow[...]), 2)):
                m_ref[p * rank : (p + 1) * rank, nq:] = piece
        wait(place)
        place += 1
        part = nn(scaled[:, at], wq[at, :])
        if i == 0:
            m_acc[...] = part
        else:
            m_acc[...] += part
    for p, piece in enumerate(split(m_acc[...], 2)):
        m_ref[p * rank : (p + 1) * rank, :nq] = piece
    for i, at in enumerate(pieces):
        wait(place)
        place += 1
        part = nn(wo[:, at], u[at, :])
        if i == 0:
            o_acc[...] = part
        else:
            o_acc[...] += part
    o_ref[...] = o_acc[...].astype(BF)


def project(back, gain, basis, wq, wk, wv, wo):
    wide, rank = basis.shape
    length = back.shape[0]
    ne = wo.shape[0]
    nq = wq.shape[1]
    rest = wk.shape[1] + wv.shape[1]
    operands = in_hbm((back, gain, basis, wq, wk, wv, wo))
    return pl.pallas_call(
        project_kernel,
        in_specs=[pl.BlockSpec(memory_space=pltpu.HBM)] * len(operands),
        out_specs=vmem(7),
        out_shape=[
            jax.ShapeDtypeStruct((2 * rank, nq + rest), BF),
            jax.ShapeDtypeStruct((ne, rank), BF),
            jax.ShapeDtypeStruct((length, HD), F32),
            jax.ShapeDtypeStruct(basis.shape, BF),
            jax.ShapeDtypeStruct(wq.shape, BF),
            jax.ShapeDtypeStruct((wide, rest), BF),
            jax.ShapeDtypeStruct((rank, wide), BF),
        ],
        scratch_shapes=[
            pltpu.VMEM(back.shape, BF),
            pltpu.VMEM(gain.shape, F32),
            pltpu.VMEM(wo.shape, BF),
            pltpu.VMEM((rank, wide), BF),
            pltpu.VMEM((rank, nq), F32),
            pltpu.VMEM((ne, rank), F32),
            pltpu.SemaphoreType.DMA((4 + 3 * (wide // PIECE),)),
        ],
        compiler_params=pltpu.CompilerParams(vmem_limit_bytes=VMEM_BYTES * 3 // 2),
        cost_estimate=cost(6 * 10**9, 20 * 10**6),
        name="project_weights",
    )(*operands)


def project_heads(coeffs, inv, m_ref, cosine, sine, q, k, v1):
    length = coeffs.shape[0]
    heads = q.shape[0] // length
    twice = jnp.concatenate([coeffs, coeffs], axis=1)
    for h in range(heads):
        part = nn(twice, m_ref[:, h * HD : (h + 1) * HD]) * inv
        q[h * length : (h + 1) * length, :] = rope(part, cosine, sine).astype(BF)
    part = nn(twice, m_ref[:, heads * HD :]) * inv
    k[...] = rope(part[:, :HD], cosine, sine).astype(BF)
    v1[:, :HD] = part[:, HD:].astype(BF)
    v1[:, HD:] = jnp.ones_like(v1[:, HD:])


def exps_of(scores, exps, low, length):
    row = lax.broadcasted_iota(jnp.int32, (length, length), 0)
    column = lax.broadcasted_iota(jnp.int32, (length, length), 1)
    causal = row >= column

    def one(h, _):
        at = pl.ds(pl.multiple_of(h * length, length), length)
        s = jnp.where(causal, scores[at, :], -jnp.inf)
        top = jnp.max(s, axis=1, keepdims=True)
        e = jnp.exp2((s - top) * (LOG2E / math.sqrt(HD)))
        if exps is not None:
            exps[at, :] = e
        low[at, :] = e.astype(BF)
        return 0

    lax.fori_loop(0, scores.shape[0] // length, one, 0, unroll=2)


def backward_kernel(
    back_ref, loss_ref, sent_ref, m_ref, o_ref, inv_ref, cos_ref, sin_ref,
    inner_ref, out_give_ref, out_keep_ref, x_ref,
    q, k, v1, gh, ghs, scores, low, mixed, gp, ds, dq, heads, grads, inner, out_inner,
):
    length, rank = back_ref.shape
    ne = o_ref.shape[0]
    count = ne // HD
    scale = 1.0 / math.sqrt(HD)
    last = lax.axis_size("pipe") - 1
    is_last = lax.axis_index("pipe") == last
    back = back_ref[...]
    up = jnp.where(is_last, loss_ref[...], sent_ref[...])
    cosine, sine = cos_ref[...], sin_ref[...]
    inv = inv_ref[...]
    project_heads(back, inv[:, :1], m_ref, cosine, sine, q, k, v1)
    scores[...] = nt(q[...], k[...])
    for h in range(count):
        gh[h * length : (h + 1) * length, :] = nt(up, o_ref[h * HD : (h + 1) * HD, :]).astype(BF)
    exps_of(scores, scores, low, length)
    mixed[...] = nn(low[...], v1[...])
    gp[...] = nt(gh[...], v1[:, :HD])

    for h in range(count):
        at = slice(h * length, (h + 1) * length)
        inverse = 1.0 / mixed[at, HD:]
        out = mixed[at, :HD] * inverse
        heads[:, h * HD : (h + 1) * HD] = out.astype(BF)
        grad = gh[at, :].astype(F32)
        ghs[at, :] = (grad * inverse).astype(BF)
        delta = jnp.sum(grad * out, axis=1, keepdims=True)
        factor = inverse * scale
        for side in range(0, length, HD):
            part = scores[at, side : side + HD] * factor
            ds[at, side : side + HD] = (part * (gp[at, side : side + HD] - delta)).astype(BF)

    dq[...] = nn(ds[...], k[...])
    for h in range(count):
        part = dq[h * length : (h + 1) * length, :]
        grads[:, h * HD : (h + 1) * HD] = unrope(part, cosine, sine).astype(BF)
    dk = nn(q[...].T, ds[...]).T
    grads[:, ne : ne + HD] = unrope(dk, cosine, sine).astype(BF)
    grads[:, ne + HD :] = nn(ghs[...].T, low[...]).T.astype(BF)
    unit = (back.astype(F32) * inv[:, :1]).astype(BF)
    half = rank // 2
    core = lax.axis_index("dp") & 1
    mine = pl.ds(pl.multiple_of(core * half, half), half)
    theirs = pl.ds(pl.multiple_of((1 - core) * half, half), half)
    inner[...] = nn(unit.T, grads[...]).astype(BF)
    inner_ref[:half, :] = inner[mine, :]
    inner_ref[half:, :] = inner[theirs, :]
    out_inner[...] = nn(up.T, heads[...]).astype(BF)
    out_keep_ref[...] = out_inner[mine, :]
    out_give_ref[...] = out_inner[theirs, :]
    x_ref[...] = nt(grads[...], m_ref[:rank, :]).astype(BF)


def backward(back, loss, sent, m2, o2, inv, cosine, sine):
    length, rank = back.shape
    ne = o2.shape[0]
    total = m2.shape[1]
    assert total == ne + 2 * HD
    stack = ne // HD * length
    return pl.pallas_call(
        backward_kernel,
        in_specs=vmem(8),
        out_specs=vmem(4),
        out_shape=[
            jax.ShapeDtypeStruct((rank, total), BF),
            jax.ShapeDtypeStruct((rank // 2, ne), BF),
            jax.ShapeDtypeStruct((rank // 2, ne), BF),
            jax.ShapeDtypeStruct((length, rank), BF),
        ],
        scratch_shapes=[
            pltpu.VMEM((stack, HD), BF),
            pltpu.VMEM((length, HD), BF),
            pltpu.VMEM((length, 2 * HD), BF),
            pltpu.VMEM((stack, HD), BF),
            pltpu.VMEM((stack, HD), BF),
            pltpu.VMEM((stack, length), F32),
            pltpu.VMEM((stack, length), BF),
            pltpu.VMEM((stack, 2 * HD), F32),
            pltpu.VMEM((stack, length), F32),
            pltpu.VMEM((stack, length), BF),
            pltpu.VMEM((stack, HD), F32),
            pltpu.VMEM((length, ne), BF),
            pltpu.VMEM((length, total), BF),
            pltpu.VMEM((rank, total), BF),
            pltpu.VMEM((rank, ne), BF),
        ],
        compiler_params=pltpu.CompilerParams(vmem_limit_bytes=VMEM_BYTES),
        cost_estimate=cost(10**4, 10**3),
        name="attention_backward",
    )(back, loss, sent, m2, o2, inv, cosine, sine)


def bases_kernel(
    back_ref, loss_ref, returned_ref, new_ref, arrived_ref, u_ref, turned_ref, inv_ref, after,
    base_ref, unit_ref, fbase_ref, g_ref,
):
    rank = u_ref.shape[1]
    for i, piece in enumerate(split(nn(turned_ref[...], u_ref[...]), 3)):
        g_ref[i * rank : (i + 1) * rank, :] = piece
    is_last = lax.axis_index("pipe") == lax.axis_size("pipe") - 1
    is_first = lax.axis_index("pipe") == 0
    up = jnp.where(is_last, loss_ref[...], returned_ref[...])
    coeffs = jnp.where(is_first, new_ref[...], arrived_ref[...])
    base_ref[...] = nn(jnp.concatenate([up] * 3, axis=1), g_ref[...])
    fbase_ref[...] = nn(jnp.concatenate([coeffs] * 3, axis=1), g_ref[...])
    unit_ref[...] = nn(jnp.concatenate([back_ref[...]] * 3, axis=1), g_ref[...]) * inv_ref[:, :1]


def bases(back, loss, returned, new, arrived, basis, turned, inv, after):
    length, rank = back.shape
    return pl.pallas_call(
        bases_kernel,
        in_specs=vmem(8) + [pl.BlockSpec(memory_space=pl.ANY)],
        out_specs=vmem(3),
        out_shape=[jax.ShapeDtypeStruct((length, rank), F32)] * 3,
        scratch_shapes=[pltpu.VMEM((3 * rank, rank), BF)],
        compiler_params=pltpu.CompilerParams(vmem_limit_bytes=VMEM_BYTES // 2),
        cost_estimate=cost(10**4, 10**3),
        name="encoded_again",
    )(back, loss, returned, new, arrived, basis, turned, inv, after)


def forward_kernel(
    new_ref, sent_ref, turned_ref, m_ref, o_ref, cos_ref, sin_ref, after,
    y_ref, q, k, v1, scores, low, mixed, heads,
):
    length, rank = new_ref.shape
    wide = turned_ref.shape[1]
    is_first = lax.axis_index("pipe") == 0
    coeffs = jnp.where(is_first, new_ref[...], sent_ref[...])
    square = jnp.zeros((length, HD), F32)
    for at in range(0, wide, PIECE):
        decoded = nn(coeffs, turned_ref[:, at : at + PIECE])
        for side in range(0, PIECE, HD):
            part = decoded[:, side : side + HD]
            square = square + part * part
    inv = inverse_root(jnp.sum(square, axis=1, keepdims=True), wide)
    project_heads(coeffs, inv, m_ref, cos_ref[...], sin_ref[...], q, k, v1)
    scores[...] = nt(q[...], k[...])
    exps_of(scores, None, low, length)
    mixed[...] = nn(low[...], v1[...])
    for h in range(heads.shape[1] // HD):
        at = slice(h * length, (h + 1) * length)
        heads[:, h * HD : (h + 1) * HD] = (mixed[at, :HD] / mixed[at, HD:]).astype(BF)
    y_ref[...] = nn(heads[...], o_ref[...]).astype(BF)


def forward(new, sent, turned, m2, o2, cosine, sine, after):
    length, rank = new.shape
    ne = o2.shape[0]
    stack = ne // HD * length
    return pl.pallas_call(
        forward_kernel,
        in_specs=vmem(7) + [pl.BlockSpec(memory_space=pl.ANY)],
        out_specs=pl.BlockSpec(memory_space=pltpu.VMEM),
        out_shape=jax.ShapeDtypeStruct((length, rank), BF),
        scratch_shapes=[
            pltpu.VMEM((stack, HD), BF),
            pltpu.VMEM((length, HD), BF),
            pltpu.VMEM((length, 2 * HD), BF),
            pltpu.VMEM((stack, length), F32),
            pltpu.VMEM((stack, length), BF),
            pltpu.VMEM((stack, 2 * HD), F32),
            pltpu.VMEM((length, ne), BF),
        ],
        compiler_params=pltpu.CompilerParams(vmem_limit_bytes=VMEM_BYTES),
        cost_estimate=cost(10**4, 10**3),
        name="attention_forward",
    )(new, sent, turned, m2, o2, cosine, sine, after)


def write_split(ref, value):
    high, low = split(value, 2)
    both = jnp.concatenate([high.astype(F32), low.astype(F32)], axis=0)
    ref[ref.shape[0] - 16 :, :] = both.astype(BF)


def read_split(ref):
    both = ref[ref.shape[0] - 16 :, :].astype(F32)
    return both[:8] + both[8:]


def gain_kernel(
    u_ref, wq_ref, narrow_ref, inner_ref, got_ref, x_ref, after,
    pair_ref, out_ref, turned, rows_f32,
):
    nq = wq_ref.shape[1]
    rows = u_ref.shape[0] // 2
    rank = u_ref.shape[1]
    half = inner_ref.shape[0] // 2
    core = lax.axis_index("dp") & 1
    mine = add_wide(inner_ref[:half, :], got_ref[half:, :]).astype(BF)
    theirs = add_wide(inner_ref[half:, :], got_ref[:half, :]).astype(BF)
    pair_ref[...] = mine
    out_ref[: x_ref.shape[0], :] = x_ref[...]
    turned[:, pl.ds(pl.multiple_of(core * half, half), half)] = mine.T
    turned[:, pl.ds(pl.multiple_of((1 - core) * half, half), half)] = theirs.T
    for at in range(0, rows, CHUNK):
        place = pl.ds(pl.multiple_of(core * rows + at, CHUNK), CHUNK)
        against = nn(wq_ref[place, :], turned[:nq, :])
        against += nn(narrow_ref[place, :], turned[nq:, :])
        terms = against * u_ref[place, :].astype(F32)
        folded = sum(terms[:, side : side + HD] for side in range(0, terms.shape[1], HD))
        line = jnp.sum(folded.T, axis=0, keepdims=True)
        for side in range(0, CHUNK, rank):
            row = (at + side) // rank
            rows_f32[row : row + 1, :] = line[:, side : side + rank]
    write_split(out_ref, rows_f32[...])


def gain_part(basis, wq, narrow, inner, got, x, after):
    wide, rank = basis.shape
    assert wide // 2 == 8 * rank
    held = tuple(pltpu.with_memory_space_constraint(a, pltpu.VMEM) for a in (basis, wq, narrow))
    return pl.pallas_call(
        gain_kernel,
        in_specs=vmem(6) + [pl.BlockSpec(memory_space=pl.ANY)],
        out_specs=vmem(2),
        out_shape=[
            jax.ShapeDtypeStruct((rank // 2, inner.shape[1]), BF),
            jax.ShapeDtypeStruct((x.shape[0] + 16, rank), BF),
        ],
        scratch_shapes=[
            pltpu.VMEM((inner.shape[1], rank), BF),
            pltpu.VMEM((8, rank), F32),
        ],
        compiler_params=pltpu.CompilerParams(vmem_limit_bytes=VMEM_BYTES),
        cost_estimate=cost(10**4, 10**3),
        name="pair_sum_and_gain_gradient",
    )(*held, inner, got, x, after)


def merge_kernel(a_ref, b_ref, after, out_ref):
    rest = out_ref.shape[0] - 16
    out_ref[:rest, :] = add_wide(a_ref[:rest, :], b_ref[:rest, :]).astype(BF)
    write_split(out_ref, read_split(a_ref) + read_split(b_ref))


def total_kernel(a_ref, b_ref, after, out_ref):
    out_ref[...] = read_split(a_ref) + read_split(b_ref)


def own_kernel(a_ref, b_ref, after, *out_refs):
    at = 0
    for ref in out_refs:
        size = ref.shape[1]
        ref[...] = add_wide(a_ref[:, at : at + size], b_ref[:, at : at + size]).astype(BF)
        at += size


def small_kernel(kernel, name, out_shape, a, b, after):
    return pl.pallas_call(
        kernel,
        in_specs=vmem(2) + [pl.BlockSpec(memory_space=pl.ANY)],
        out_specs=jax.tree.map(lambda _: pl.BlockSpec(memory_space=pltpu.VMEM), out_shape),
        out_shape=out_shape,
        compiler_params=pltpu.CompilerParams(vmem_limit_bytes=VMEM_BYTES // 2),
        cost_estimate=cost(10**4, 10**3),
        name=name,
    )(a, b, after)


def merge(a, b, after):
    return small_kernel(merge_kernel, "sum_with_gain", jax.ShapeDtypeStruct(a.shape, BF), a, b, after)


def gain_total(a, b, after):
    shape = jax.ShapeDtypeStruct((8, a.shape[1]), F32)
    return small_kernel(total_kernel, "gain_total", shape, a, b, after)


def own_pieces(a, b, sizes, after):
    shapes = [jax.ShapeDtypeStruct((a.shape[0], n), BF) for n in sizes]
    return small_kernel(own_kernel, "sum_over_y", shapes, a, b, after)


def add_kernel(a_ref, b_ref, after, out_ref):
    out_ref[...] = add_wide(a_ref[...], b_ref[...]).astype(out_ref.dtype)


def add_after(a, b, after):
    return small_kernel(add_kernel, "pair_sum", jax.ShapeDtypeStruct(a.shape, a.dtype), a, b, after)


def gather_halves(own_refs, other_refs, whole):
    half = whole.shape[0] // 2
    core = lax.axis_index("dp") & 1
    at = 0
    for own_ref, other_ref in zip(own_refs, other_refs):
        columns = pl.ds(at, own_ref.shape[1])
        whole[pl.ds(pl.multiple_of(core * half, half), half), columns] = own_ref[...]
        whole[pl.ds(pl.multiple_of((1 - core) * half, half), half), columns] = other_ref[...]
        at += own_ref.shape[1]


def inward_kernel(pieces, u_ref, gain_ref, *refs):
    own_refs, other_refs = refs[:pieces], refs[pieces : 2 * pieces]
    q_ref, k_ref, v_ref, inner = refs[-4:]
    nq, nk = q_ref.shape[1], k_ref.shape[1]
    block = q_ref.shape[0]

    @pl.when(pl.program_id(0) == 0)
    def _():
        gather_halves(own_refs, other_refs, inner)

    step = lax.axis_index("dp") * pl.num_programs(0) + pl.program_id(0)
    rows = pl.ds(pl.multiple_of(step * block, block), block)
    gain = jnp.broadcast_to(gain_ref[:, rows], (HD, block)).T[:, :1]
    grad = nn(u_ref[rows, :], inner[...]) * gain
    q_ref[...] = grad[:, :nq].astype(BF)
    k_ref[...] = grad[:, nq : nq + nk].astype(BF)
    v_ref[...] = grad[:, nq + nk :].astype(BF)


def outward_kernel(pieces, u_ref, *refs):
    own_refs, other_refs = refs[:pieces], refs[pieces : 2 * pieces]
    o_ref, inner = refs[-2:]

    @pl.when(pl.program_id(0) == 0)
    def _():
        gather_halves(own_refs, other_refs, inner)

    block, rows = o_ref.shape
    at = pl.multiple_of(pl.program_id(0) * block, block)
    basis = u_ref[pl.ds(pl.multiple_of(lax.axis_index("dp") * rows, rows), rows), :]
    o_ref[...] = nt(inner[:, pl.ds(at, block)].T, basis).astype(BF)


STEPS = 2


def inward_grads(basis, gain, own, other, sizes, after):
    wide, rank = basis.shape
    rows = wide // lax.axis_size("dp")
    block = rows // STEPS
    return pl.pallas_call(
        functools.partial(inward_kernel, len(own)),
        grid=(STEPS,),
        in_specs=vmem(2 + 2 * len(own)) + [pl.BlockSpec(memory_space=pl.ANY)],
        out_specs=[pl.BlockSpec((block, n), lambda i: (i, 0)) for n in sizes],
        scratch_shapes=[pltpu.VMEM((rank, sum(sizes)), BF)],
        out_shape=[jax.ShapeDtypeStruct((rows, n), BF) for n in sizes],
        compiler_params=pltpu.CompilerParams(vmem_limit_bytes=VMEM_BYTES),
        cost_estimate=cost(10**4, 10**3),
        name="inward_weight_gradients",
    )(basis, gain, *own, *other, after)


def outward_grad(basis, own, other, after):
    wide, rank = basis.shape
    rows = wide // lax.axis_size("dp")
    ne = sum(piece.shape[1] for piece in own)
    return pl.pallas_call(
        functools.partial(outward_kernel, len(own)),
        grid=(STEPS,),
        in_specs=vmem(1 + 2 * len(own)) + [pl.BlockSpec(memory_space=pl.ANY)],
        out_specs=pl.BlockSpec((ne // STEPS, rows), lambda i: (i, 0)),
        scratch_shapes=[pltpu.VMEM((rank, ne), BF)],
        out_shape=jax.ShapeDtypeStruct((ne, rows), BF),
        compiler_params=pltpu.CompilerParams(vmem_limit_bytes=VMEM_BYTES),
        cost_estimate=cost(10**4, 10**3),
        name="output_weight_gradient",
    )(basis, *own, *other, after)


def results_kernel(
    wide, fbase_ref, y_ref, ygot_ref, base_ref, unit_ref, x_ref, xgot_ref, back_ref, inv_ref,
    gain_ref, gain_other_ref, after,
    f_ref, b_ref, gain_out_ref,
):
    f_ref[...] = (fbase_ref[...] + add_wide(y_ref[...], ygot_ref[...])).astype(BF)
    length = back_ref.shape[0]
    x = add_wide(x_ref[:length, :], xgot_ref[:length, :])
    inv = inv_ref[:, :1]
    along = jnp.sum(x * back_ref[...].astype(F32), axis=1, keepdims=True)
    middle = along * inv * (1.0 / wide)
    b_ref[...] = (base_ref[...] + (x - unit_ref[...] * middle) * inv).astype(BF)
    core = lax.axis_index("dp") & 1
    half = wide // 2
    rank = gain_ref.shape[1]
    for row in range(half // rank):
        mine = pl.ds(pl.multiple_of(core * half + row * rank, rank), rank)
        theirs = pl.ds(pl.multiple_of((1 - core) * half + row * rank, rank), rank)
        gain_out_ref[:, mine] = gain_ref[row : row + 1, :]
        gain_out_ref[:, theirs] = gain_other_ref[row : row + 1, :]


def results(wide, after, *operands):
    shape = operands[0].shape
    held = tuple(pltpu.with_memory_space_constraint(a, pltpu.VMEM) for a in operands)
    return pl.pallas_call(
        functools.partial(results_kernel, wide),
        in_specs=vmem(len(operands)) + [pl.BlockSpec(memory_space=pl.ANY)],
        out_specs=vmem(3),
        out_shape=[jax.ShapeDtypeStruct(shape, BF)] * 2 + [jax.ShapeDtypeStruct((1, wide), F32)],
        compiler_params=pltpu.CompilerParams(vmem_limit_bytes=VMEM_BYTES // 2),
        cost_estimate=cost(10**4, 10**3),
        name="section_results",
    )(*held, *in_hbm((after,)))


def body(
    new_coeffs,
    loss_grad,
    sent_forward,
    sent_backward,
    stashed,
    subspace,
    norm_gain,
    w_query,
    w_key,
    w_value,
    w_output,
):
    wide = subspace.shape[0]
    wq, wk, wv, wo = w_query[0], w_key[0], w_value[0], w_output[0]
    nq, nk, nv = wq.shape[1], wk.shape[1], wv.shape[1]
    back = stashed[0]
    arrived, returned = cross_pipe(sent_forward[0], sent_backward[0])
    cosine, sine = rope_tables(back.shape[0])

    m2, o2, inv, basis, wq, narrow, turned = project(
        back, norm_gain, subspace, wq, wk, wv, wo
    )
    inner, out_give, out_keep, x = backward(
        back, loss_grad, returned, m2, o2, inv, cosine, sine
    )
    out_got = swap(out_give, "dp", 1)
    inner_got = swap(inner, "dp", 1)
    base, unit, fbase = bases(
        back, loss_grad, returned, new_coeffs, arrived, basis, turned, inv, out_keep
    )
    out_pair = add_after(out_keep, out_got, fbase)
    out_got = swap(out_pair, "dp", 2)
    pair, x = gain_part(basis, wq, narrow, inner, inner_got, x, out_pair)
    pair_got = swap(pair, "dp", 2)
    x_got = swap(x, "tensor", 2)
    y = forward(new_coeffs, arrived, turned, m2, o2, cosine, sine, pair)
    y_got = swap(y, "tensor", 1)
    ne = wo.shape[0]
    out_own = own_pieces(out_pair, out_got, (ne // 2, ne - ne // 2), y)
    x = merge(x, x_got, out_own[0])
    x_got = swap(x, "tensor", 1)
    out_other = [swap(piece, "dp", 1) for piece in out_own]
    grad_o = outward_grad(basis, out_own, out_other, x)
    y = add_after(y, y_got, *in_hbm((grad_o,)))
    y_got = swap(y, "tensor", 2)
    own = own_pieces(pair, pair_got, (nq // 2, nq - nq // 2, nk + nv), y)
    other = [swap(piece, "dp", 1) for piece in own]
    gain = gain_total(x, x_got, own[0])
    gain_got = swap(gain, "dp", 2)
    grad_q, grad_k, grad_v = inward_grads(basis, norm_gain, own, other, (nq, nk, nv), gain)
    gain = add_after(gain, gain_got, *in_hbm((grad_v,)))
    gain_other = swap(gain, "dp", 1)
    forward_out, backward_out, grad_gain = results(
        wide, grad_v, fbase, y, y_got, base, unit, x, x_got, back, inv, gain, gain_other
    )
    return (
        forward_out[None],
        backward_out[None],
        grad_q[None],
        grad_k[None],
        grad_v[None],
        grad_o[None],
        grad_gain,
    )


def solution(mesh):
    return jax.shard_map(
        body,
        mesh=mesh,
        in_specs=(
            P("dp", None),
            P("dp", None),
            P("pipe", "dp", None),
            P("pipe", "dp", None),
            P("pipe", "dp", None),
            P(),
            P("pipe", None),
            P("pipe", None, "tensor"),
            P("pipe", None, "tensor"),
            P("pipe", None, "tensor"),
            P("pipe", "tensor", None),
        ),
        out_specs=(
            P("pipe", "dp", None),
            P("pipe", "dp", None),
            P("pipe", "dp", "tensor"),
            P("pipe", "dp", "tensor"),
            P("pipe", "dp", "tensor"),
            P("pipe", "tensor", "dp"),
            P("pipe", None),
        ),
        check_vma=False,
    )
```

```python
import functools
import math

import jax
import jax.numpy as jnp
import numpy as np
from jax import lax
from jax.experimental import pallas as pl
from jax.experimental.pallas import tpu as pltpu
from jax.sharding import PartitionSpec as P

HD = 128
EPSILON = 1e-05
ROPE_BASE = 500000.0
BF = jnp.bfloat16
F32 = jnp.float32
VMEM_BYTES = 24 * 1024 * 1024
CHUNK = 512
PIECE = 1024
AHEAD = 3
LOG2E = 1.4426950408889634


def shifted(x, axis, by):
    devices = lax.axis_size(axis)
    pairs = [(i, i + by) for i in range(devices) if 0 <= i + by < devices]
    return lax.ppermute(x, axis, pairs)


def swap(x, axis, bit):
    devices = lax.axis_size(axis)
    return lax.ppermute(x, axis, [(i, i ^ bit) for i in range(devices)])


def cross_pipe(sent_forward, sent_backward):
    if lax.axis_size("pipe") != 2:
        return shifted(sent_forward, "pipe", 1), shifted(sent_backward, "pipe", -1)
    first = lax.axis_index("pipe") == 0
    got = swap(jnp.where(first, sent_forward, sent_backward), "pipe", 1)
    return got, got


def add_wide(a, b):
    return a.astype(F32) + b.astype(F32)


def nt(a, b):
    return lax.dot_general(a, b, (((1,), (1,)), ((), ())), preferred_element_type=F32)


def nn(a, b):
    return jnp.dot(a, b, preferred_element_type=F32)


def split(x, parts):
    out = []
    for _ in range(parts):
        piece = x.astype(BF)
        out.append(piece)
        x = x - piece.astype(F32)
    return out


def rope_tables(length):
    half = HD // 2
    frequency = np.float32(ROPE_BASE) ** (-2.0 * np.arange(half, dtype=np.float32) / HD)
    angles = np.arange(length, dtype=np.float32)[:, None] * frequency.astype(np.float32)
    cosine, sine = np.cos(angles), np.sin(angles)
    tables = (np.concatenate([cosine, cosine], 1), np.concatenate([-sine, sine], 1))
    return tuple(jnp.asarray(t, dtype=F32) for t in tables)


def rope(x, cosine, sine):
    return x * cosine + pltpu.roll(x, HD // 2, 1) * sine


def unrope(x, cosine, sine):
    return x * cosine - pltpu.roll(x, HD // 2, 1) * sine


def inverse_root(square_sum, width):
    return 1.0 / jnp.sqrt(square_sum / width + EPSILON)


def vmem(count):
    return [pl.BlockSpec(memory_space=pltpu.VMEM)] * count


def in_hbm(arrays):
    return tuple(pltpu.with_memory_space_constraint(a, pltpu.HBM) for a in arrays)


def cost(flops, num_bytes, exps=0):
    return pl.CostEstimate(flops=flops, bytes_accessed=num_bytes, transcendentals=exps)


def project_kernel(
    back_hbm, gain_hbm, u_hbm, wq_hbm, wk_hbm, wv_hbm, wo_hbm,
    m_ref, o_ref, inv_ref, u, wq, narrow, turned,
    back, gain, wo, scaled, m_acc, o_acc, sems,
):
    wide, rank = u.shape
    nq = wq.shape[1]
    nk = wk_hbm.shape[1]
    parts = wide // PIECE
    pieces = [pl.ds(i * PIECE, PIECE) for i in range(parts)]
    pairs = [(back_hbm, back), (gain_hbm, gain)]
    pairs += [(u_hbm.at[at, :], u.at[at, :]) for at in pieces]
    pairs += [(wq_hbm.at[at, :], wq.at[at, :]) for at in pieces[:2]]
    pairs += [(wk_hbm, narrow.at[:, pl.ds(0, nk)])]
    pairs += [(wv_hbm, narrow.at[:, pl.ds(nk, narrow.shape[1] - nk)])]
    pairs += [(wq_hbm.at[at, :], wq.at[at, :]) for at in pieces[2:]]
    pairs += [(wo_hbm.at[:, at], wo.at[:, at]) for at in pieces]
    copies = [
        pltpu.make_async_copy(source, target, sems.at[n])
        for n, (source, target) in enumerate(pairs)
    ]
    started = 0

    def start_to(count):
        nonlocal started
        for copy in copies[started:count]:
            copy.start()
        started = max(started, min(count, len(copies)))

    def wait(n):
        start_to(n + 1 + AHEAD)
        copies[n].wait()

    start_to(2 + parts + AHEAD)
    copies[0].wait()
    copies[1].wait()
    square = jnp.zeros((back.shape[0], HD), F32)
    for i, at in enumerate(pieces):
        copies[2 + i].wait()
        turned[:, at] = u[at, :].T
        scaled[:, at] = (turned[:, at].astype(F32) * gain[:, at]).astype(BF)
        decoded = nn(back[...], turned[:, at])
        for side in range(0, PIECE, HD):
            part = decoded[:, side : side + HD]
            square = square + part * part
    inv_ref[...] = jnp.broadcast_to(
        inverse_root(jnp.sum(square, axis=1, keepdims=True), wide), inv_ref.shape
    )
    place = 2 + parts
    for i, at in enumerate(pieces):
        if i == 2:
            wait(place)
            wait(place + 1)
            place += 2
            for p, piece in enumerate(split(nn(scaled[...], narrow[...]), 2)):
                m_ref[p * rank : (p + 1) * rank, nq:] = piece
        wait(place)
        place += 1
        part = nn(scaled[:, at], wq[at, :])
        if i == 0:
            m_acc[...] = part
        else:
            m_acc[...] += part
    for p, piece in enumerate(split(m_acc[...], 2)):
        m_ref[p * rank : (p + 1) * rank, :nq] = piece
    for i, at in enumerate(pieces):
        wait(place)
        place += 1
        part = nn(wo[:, at], u[at, :])
        if i == 0:
            o_acc[...] = part
        else:
            o_acc[...] += part
    o_ref[...] = o_acc[...].astype(BF)


def project(back, gain, basis, wq, wk, wv, wo):
    wide, rank = basis.shape
    length = back.shape[0]
    ne = wo.shape[0]
    nq = wq.shape[1]
    rest = wk.shape[1] + wv.shape[1]
    operands = in_hbm((back, gain, basis, wq, wk, wv, wo))
    return pl.pallas_call(
        project_kernel,
        in_specs=[pl.BlockSpec(memory_space=pltpu.HBM)] * len(operands),
        out_specs=vmem(7),
        out_shape=[
            jax.ShapeDtypeStruct((2 * rank, nq + rest), BF),
            jax.ShapeDtypeStruct((ne, rank), BF),
            jax.ShapeDtypeStruct((length, HD), F32),
            jax.ShapeDtypeStruct(basis.shape, BF),
            jax.ShapeDtypeStruct(wq.shape, BF),
            jax.ShapeDtypeStruct((wide, rest), BF),
            jax.ShapeDtypeStruct((rank, wide), BF),
        ],
        scratch_shapes=[
            pltpu.VMEM(back.shape, BF),
            pltpu.VMEM(gain.shape, F32),
            pltpu.VMEM(wo.shape, BF),
            pltpu.VMEM((rank, wide), BF),
            pltpu.VMEM((rank, nq), F32),
            pltpu.VMEM((ne, rank), F32),
            pltpu.SemaphoreType.DMA((4 + 3 * (wide // PIECE),)),
        ],
        compiler_params=pltpu.CompilerParams(vmem_limit_bytes=VMEM_BYTES * 3 // 2),
        cost_estimate=cost(6 * 10**9, 20 * 10**6),
        name="project_weights",
    )(*operands)


def project_heads(coeffs, inv, m_ref, cosine, sine, q, k, v1):
    length = coeffs.shape[0]
    heads = q.shape[0] // length
    twice = jnp.concatenate([coeffs, coeffs], axis=1)
    for h in range(heads):
        part = nn(twice, m_ref[:, h * HD : (h + 1) * HD]) * inv
        q[h * length : (h + 1) * length, :] = rope(part, cosine, sine).astype(BF)
    part = nn(twice, m_ref[:, heads * HD :]) * inv
    k[...] = rope(part[:, :HD], cosine, sine).astype(BF)
    v1[:, :HD] = part[:, HD:].astype(BF)
    v1[:, HD:] = jnp.ones_like(v1[:, HD:])


def exps_of(scores, exps, low, length):
    row = lax.broadcasted_iota(jnp.int32, (length, length), 0)
    column = lax.broadcasted_iota(jnp.int32, (length, length), 1)
    causal = row >= column

    def one(h, _):
        at = pl.ds(pl.multiple_of(h * length, length), length)
        s = jnp.where(causal, scores[at, :], -jnp.inf)
        top = jnp.max(s, axis=1, keepdims=True)
        e = jnp.exp2((s - top) * (LOG2E / math.sqrt(HD)))
        if exps is not None:
            exps[at, :] = e
        low[at, :] = e.astype(BF)
        return 0

    lax.fori_loop(0, scores.shape[0] // length, one, 0, unroll=2)


def backward_kernel(
    back_ref, loss_ref, sent_ref, m_ref, o_ref, inv_ref, cos_ref, sin_ref,
    inner_ref, give_a_ref, give_b_ref, keep_a_ref, keep_b_ref, x_ref,
    q, k, v1, gh, ghs, scores, low, mixed, gp, ds, dq, heads, grads, inner, out_inner,
):
    length, rank = back_ref.shape
    ne = o_ref.shape[0]
    count = ne // HD
    scale = 1.0 / math.sqrt(HD)
    last = lax.axis_size("pipe") - 1
    is_last = lax.axis_index("pipe") == last
    back = back_ref[...]
    up = jnp.where(is_last, loss_ref[...], sent_ref[...])
    cosine, sine = cos_ref[...], sin_ref[...]
    inv = inv_ref[...]
    project_heads(back, inv[:, :1], m_ref, cosine, sine, q, k, v1)
    scores[...] = nt(q[...], k[...])
    for h in range(count):
        gh[h * length : (h + 1) * length, :] = nt(up, o_ref[h * HD : (h + 1) * HD, :]).astype(BF)
    exps_of(scores, scores, low, length)
    mixed[...] = nn(low[...], v1[...])
    gp[...] = nt(gh[...], v1[:, :HD])

    for h in range(count):
        at = slice(h * length, (h + 1) * length)
        inverse = 1.0 / mixed[at, HD:]
        out = mixed[at, :HD] * inverse
        heads[:, h * HD : (h + 1) * HD] = out.astype(BF)
        grad = gh[at, :].astype(F32)
        ghs[at, :] = (grad * inverse).astype(BF)
        delta = jnp.sum(grad * out, axis=1, keepdims=True)
        factor = inverse * scale
        for side in range(0, length, HD):
            part = scores[at, side : side + HD] * factor
            ds[at, side : side + HD] = (part * (gp[at, side : side + HD] - delta)).astype(BF)

    dq[...] = nn(ds[...], k[...])
    for h in range(count):
        part = dq[h * length : (h + 1) * length, :]
        grads[:, h * HD : (h + 1) * HD] = unrope(part, cosine, sine).astype(BF)
    dk = nn(q[...].T, ds[...]).T
    grads[:, ne : ne + HD] = unrope(dk, cosine, sine).astype(BF)
    grads[:, ne + HD :] = nn(ghs[...].T, low[...]).T.astype(BF)
    unit = (back.astype(F32) * inv[:, :1]).astype(BF)
    half = rank // 2
    core = lax.axis_index("dp") & 1
    mine = pl.ds(pl.multiple_of(core * half, half), half)
    theirs = pl.ds(pl.multiple_of((1 - core) * half, half), half)
    inner[...] = nn(unit.T, grads[...]).astype(BF)
    inner_ref[:half, :] = inner[mine, :]
    inner_ref[half:, :] = inner[theirs, :]
    out_inner[...] = nn(up.T, heads[...]).astype(BF)
    middle = ne // 2
    give_a_ref[...] = out_inner[theirs, :middle]
    give_b_ref[...] = out_inner[theirs, middle:]
    keep_a_ref[...] = out_inner[mine, :middle]
    keep_b_ref[...] = out_inner[mine, middle:]
    x_ref[:length, :] = nt(grads[...], m_ref[:rank, :]).astype(BF)
    x_ref[length:, :] = jnp.zeros_like(x_ref[length:, :])


def backward(back, loss, sent, m2, o2, inv, cosine, sine):
    length, rank = back.shape
    ne = o2.shape[0]
    total = m2.shape[1]
    assert total == ne + 2 * HD
    stack = ne // HD * length
    return pl.pallas_call(
        backward_kernel,
        in_specs=vmem(8),
        out_specs=vmem(6),
        out_shape=[
            jax.ShapeDtypeStruct((rank, total), BF),
            jax.ShapeDtypeStruct((rank // 2, ne // 2), BF),
            jax.ShapeDtypeStruct((rank // 2, ne // 2), BF),
            jax.ShapeDtypeStruct((rank // 2, ne // 2), BF),
            jax.ShapeDtypeStruct((rank // 2, ne // 2), BF),
            jax.ShapeDtypeStruct((length + 16, rank), BF),
        ],
        scratch_shapes=[
            pltpu.VMEM((stack, HD), BF),
            pltpu.VMEM((length, HD), BF),
            pltpu.VMEM((length, 2 * HD), BF),
            pltpu.VMEM((stack, HD), BF),
            pltpu.VMEM((stack, HD), BF),
            pltpu.VMEM((stack, length), F32),
            pltpu.VMEM((stack, length), BF),
            pltpu.VMEM((stack, 2 * HD), F32),
            pltpu.VMEM((stack, length), F32),
            pltpu.VMEM((stack, length), BF),
            pltpu.VMEM((stack, HD), F32),
            pltpu.VMEM((length, ne), BF),
            pltpu.VMEM((length, total), BF),
            pltpu.VMEM((rank, total), BF),
            pltpu.VMEM((rank, ne), BF),
        ],
        compiler_params=pltpu.CompilerParams(vmem_limit_bytes=VMEM_BYTES),
        cost_estimate=cost(10**4, 10**3),
        name="attention_backward",
    )(back, loss, sent, m2, o2, inv, cosine, sine)


def bases_kernel(
    back_ref, loss_ref, returned_ref, new_ref, arrived_ref, u_ref, turned_ref, inv_ref, after,
    base_ref, unit_ref, fbase_ref, g_ref,
):
    rank = u_ref.shape[1]
    for i, piece in enumerate(split(nn(turned_ref[...], u_ref[...]), 3)):
        g_ref[i * rank : (i + 1) * rank, :] = piece
    is_last = lax.axis_index("pipe") == lax.axis_size("pipe") - 1
    is_first = lax.axis_index("pipe") == 0
    up = jnp.where(is_last, loss_ref[...], returned_ref[...])
    coeffs = jnp.where(is_first, new_ref[...], arrived_ref[...])
    base_ref[...] = nn(jnp.concatenate([up] * 3, axis=1), g_ref[...])
    fbase_ref[...] = nn(jnp.concatenate([coeffs] * 3, axis=1), g_ref[...])
    unit_ref[...] = nn(jnp.concatenate([back_ref[...]] * 3, axis=1), g_ref[...]) * inv_ref[:, :1]


def bases(back, loss, returned, new, arrived, basis, turned, inv, after):
    length, rank = back.shape
    return pl.pallas_call(
        bases_kernel,
        in_specs=vmem(8) + [pl.BlockSpec(memory_space=pl.ANY)],
        out_specs=vmem(3),
        out_shape=[jax.ShapeDtypeStruct((length, rank), F32)] * 3,
        scratch_shapes=[pltpu.VMEM((3 * rank, rank), BF)],
        compiler_params=pltpu.CompilerParams(vmem_limit_bytes=VMEM_BYTES // 2),
        cost_estimate=cost(10**4, 10**3),
        name="encoded_again",
    )(back, loss, returned, new, arrived, basis, turned, inv, after)


def forward_kernel(
    new_ref, sent_ref, turned_ref, m_ref, o_ref, cos_ref, sin_ref, gain_ref,
    y_ref, q, k, v1, scores, low, mixed, heads,
):
    length, rank = new_ref.shape
    wide = turned_ref.shape[1]
    is_first = lax.axis_index("pipe") == 0
    coeffs = jnp.where(is_first, new_ref[...], sent_ref[...])
    square = jnp.zeros((length, HD), F32)
    for at in range(0, wide, PIECE):
        decoded = nn(coeffs, turned_ref[:, at : at + PIECE])
        for side in range(0, PIECE, HD):
            part = decoded[:, side : side + HD]
            square = square + part * part
    inv = inverse_root(jnp.sum(square, axis=1, keepdims=True), wide)
    project_heads(coeffs, inv, m_ref, cos_ref[...], sin_ref[...], q, k, v1)
    scores[...] = nt(q[...], k[...])
    exps_of(scores, None, low, length)
    mixed[...] = nn(low[...], v1[...])
    for h in range(heads.shape[1] // HD):
        at = slice(h * length, (h + 1) * length)
        heads[:, h * HD : (h + 1) * HD] = (mixed[at, :HD] / mixed[at, HD:]).astype(BF)
    y_ref[:length, :] = nn(heads[...], o_ref[...]).astype(BF)
    y_ref[length:, :] = gain_ref[...]


def forward(new, sent, turned, m2, o2, cosine, sine, gain):
    length, rank = new.shape
    ne = o2.shape[0]
    stack = ne // HD * length
    return pl.pallas_call(
        forward_kernel,
        in_specs=vmem(8),
        out_specs=pl.BlockSpec(memory_space=pltpu.VMEM),
        out_shape=jax.ShapeDtypeStruct((length + 16, rank), BF),
        scratch_shapes=[
            pltpu.VMEM((stack, HD), BF),
            pltpu.VMEM((length, HD), BF),
            pltpu.VMEM((length, 2 * HD), BF),
            pltpu.VMEM((stack, length), F32),
            pltpu.VMEM((stack, length), BF),
            pltpu.VMEM((stack, 2 * HD), F32),
            pltpu.VMEM((length, ne), BF),
        ],
        compiler_params=pltpu.CompilerParams(vmem_limit_bytes=VMEM_BYTES),
        cost_estimate=cost(10**4, 10**3),
        name="attention_forward",
    )(new, sent, turned, m2, o2, cosine, sine, gain)


def write_split(ref, value):
    high, low = split(value, 2)
    both = jnp.concatenate([high.astype(F32), low.astype(F32)], axis=0)
    ref[ref.shape[0] - 16 :, :] = both.astype(BF)


def read_split(ref):
    both = ref[ref.shape[0] - 16 :, :].astype(F32)
    return both[:8] + both[8:]


def gain_kernel(
    u_ref, wq_ref, narrow_ref, inner_ref, got_ref, after,
    pair_a_ref, pair_b_ref, out_ref, turned, rows_f32,
):
    nq = wq_ref.shape[1]
    rows = u_ref.shape[0] // 2
    rank = u_ref.shape[1]
    half = inner_ref.shape[0] // 2
    core = lax.axis_index("dp") & 1
    mine = add_wide(inner_ref[:half, :], got_ref[half:, :]).astype(BF)
    theirs = add_wide(inner_ref[half:, :], got_ref[:half, :]).astype(BF)
    middle = pair_a_ref.shape[1]
    pair_a_ref[...] = mine[:, :middle]
    pair_b_ref[...] = mine[:, middle:]
    turned[:, pl.ds(pl.multiple_of(core * half, half), half)] = mine.T
    turned[:, pl.ds(pl.multiple_of((1 - core) * half, half), half)] = theirs.T
    for at in range(0, rows, CHUNK):
        place = pl.ds(pl.multiple_of(core * rows + at, CHUNK), CHUNK)
        against = nn(wq_ref[place, :], turned[:nq, :])
        against += nn(narrow_ref[place, :], turned[nq:, :])
        terms = against * u_ref[place, :].astype(F32)
        folded = sum(terms[:, side : side + HD] for side in range(0, terms.shape[1], HD))
        line = jnp.sum(folded.T, axis=0, keepdims=True)
        for side in range(0, CHUNK, rank):
            row = (at + side) // rank
            rows_f32[row : row + 1, :] = line[:, side : side + rank]
    write_split(out_ref, rows_f32[...])


def gain_part(basis, wq, narrow, inner, got, after):
    wide, rank = basis.shape
    assert wide // 2 == 8 * rank
    held = tuple(pltpu.with_memory_space_constraint(a, pltpu.VMEM) for a in (basis, wq, narrow))
    return pl.pallas_call(
        gain_kernel,
        in_specs=vmem(5) + [pl.BlockSpec(memory_space=pl.ANY)],
        out_specs=vmem(3),
        out_shape=[
            jax.ShapeDtypeStruct((rank // 2, inner.shape[1] // 2), BF),
            jax.ShapeDtypeStruct((rank // 2, inner.shape[1] // 2), BF),
            jax.ShapeDtypeStruct((16, rank), BF),
        ],
        scratch_shapes=[
            pltpu.VMEM((inner.shape[1], rank), BF),
            pltpu.VMEM((8, rank), F32),
        ],
        compiler_params=pltpu.CompilerParams(vmem_limit_bytes=VMEM_BYTES),
        cost_estimate=cost(10**4, 10**3),
        name="pair_sum_and_gain_gradient",
    )(*held, inner, got, after)


def merge_kernel(a_ref, b_ref, after, out_ref, gain_ref):
    rest = out_ref.shape[0]
    out_ref[...] = add_wide(a_ref[:rest, :], b_ref[:rest, :]).astype(BF)
    gain_ref[...] = read_split(a_ref) + read_split(b_ref)


def own_kernel(a_ref, b_ref, after, *out_refs):
    at = 0
    for ref in out_refs:
        size = ref.shape[1]
        ref[...] = add_wide(a_ref[:, at : at + size], b_ref[:, at : at + size]).astype(BF)
        at += size


def small_kernel(kernel, name, out_shape, a, b, after):
    return pl.pallas_call(
        kernel,
        in_specs=vmem(2) + [pl.BlockSpec(memory_space=pl.ANY)],
        out_specs=jax.tree.map(lambda _: pl.BlockSpec(memory_space=pltpu.VMEM), out_shape),
        out_shape=out_shape,
        compiler_params=pltpu.CompilerParams(vmem_limit_bytes=VMEM_BYTES // 2),
        cost_estimate=cost(10**4, 10**3),
        name=name,
    )(a, b, after)


def merge(a, b, after):
    rows, width = a.shape
    shapes = [jax.ShapeDtypeStruct((rows - 16, width), BF), jax.ShapeDtypeStruct((8, width), F32)]
    return small_kernel(merge_kernel, "sum_with_gain", shapes, a, b, after)


def own_pieces(a, b, sizes, after):
    shapes = [jax.ShapeDtypeStruct((a.shape[0], n), BF) for n in sizes]
    return small_kernel(own_kernel, "sum_over_y", shapes, a, b, after)


def add_kernel(a_ref, b_ref, after, out_ref):
    out_ref[...] = add_wide(a_ref[...], b_ref[...]).astype(out_ref.dtype)


def add_after(a, b, after):
    return small_kernel(add_kernel, "pair_sum", jax.ShapeDtypeStruct(a.shape, a.dtype), a, b, after)


def gather_halves(own_refs, other_refs, whole):
    half = whole.shape[0] // 2
    core = lax.axis_index("dp") & 1
    at = 0
    for own_ref, other_ref in zip(own_refs, other_refs):
        columns = pl.ds(at, own_ref.shape[1])
        whole[pl.ds(pl.multiple_of(core * half, half), half), columns] = own_ref[...]
        whole[pl.ds(pl.multiple_of((1 - core) * half, half), half), columns] = other_ref[...]
        at += own_ref.shape[1]


def inward_kernel(pieces, u_ref, gain_ref, *refs):
    own_refs, other_refs = refs[:pieces], refs[pieces : 2 * pieces]
    q_ref, k_ref, v_ref, inner = refs[-4:]
    nq, nk = q_ref.shape[1], k_ref.shape[1]
    block = q_ref.shape[0]

    @pl.when(pl.program_id(0) == 0)
    def _():
        gather_halves(own_refs, other_refs, inner)

    step = lax.axis_index("dp") * pl.num_programs(0) + pl.program_id(0)
    rows = pl.ds(pl.multiple_of(step * block, block), block)
    gain = jnp.broadcast_to(gain_ref[:, rows], (HD, block)).T[:, :1]
    grad = nn(u_ref[rows, :], inner[...]) * gain
    q_ref[...] = grad[:, :nq].astype(BF)
    k_ref[...] = grad[:, nq : nq + nk].astype(BF)
    v_ref[...] = grad[:, nq + nk :].astype(BF)


def outward_kernel(pieces, u_ref, *refs):
    own_refs, other_refs = refs[:pieces], refs[pieces : 2 * pieces]
    o_ref, inner = refs[-2:]

    @pl.when(pl.program_id(0) == 0)
    def _():
        gather_halves(own_refs, other_refs, inner)

    block, rows = o_ref.shape
    at = pl.multiple_of(pl.program_id(0) * block, block)
    basis = u_ref[pl.ds(pl.multiple_of(lax.axis_index("dp") * rows, rows), rows), :]
    o_ref[...] = nt(inner[:, pl.ds(at, block)].T, basis).astype(BF)


STEPS = 2


def inward_grads(basis, gain, own, other, sizes, after):
    wide, rank = basis.shape
    rows = wide // lax.axis_size("dp")
    block = rows // STEPS
    return pl.pallas_call(
        functools.partial(inward_kernel, len(own)),
        grid=(STEPS,),
        in_specs=vmem(2 + 2 * len(own)) + [pl.BlockSpec(memory_space=pl.ANY)],
        out_specs=[pl.BlockSpec((block, n), lambda i: (i, 0)) for n in sizes],
        scratch_shapes=[pltpu.VMEM((rank, sum(sizes)), BF)],
        out_shape=[jax.ShapeDtypeStruct((rows, n), BF) for n in sizes],
        compiler_params=pltpu.CompilerParams(vmem_limit_bytes=VMEM_BYTES),
        cost_estimate=cost(10**4, 10**3),
        name="inward_weight_gradients",
    )(basis, gain, *own, *other, after)


def outward_grad(basis, own, other, after):
    wide, rank = basis.shape
    rows = wide // lax.axis_size("dp")
    ne = sum(piece.shape[1] for piece in own)
    return pl.pallas_call(
        functools.partial(outward_kernel, len(own)),
        grid=(STEPS,),
        in_specs=vmem(1 + 2 * len(own)) + [pl.BlockSpec(memory_space=pl.ANY)],
        out_specs=pl.BlockSpec((ne // STEPS, rows), lambda i: (i, 0)),
        scratch_shapes=[pltpu.VMEM((rank, ne), BF)],
        out_shape=jax.ShapeDtypeStruct((ne, rows), BF),
        compiler_params=pltpu.CompilerParams(vmem_limit_bytes=VMEM_BYTES),
        cost_estimate=cost(10**4, 10**3),
        name="output_weight_gradient",
    )(basis, *own, *other, after)


def results_kernel(
    wide, fbase_ref, y_ref, ygot_ref, base_ref, unit_ref, x_ref, xgot_ref, back_ref, inv_ref,
    gain_ref, gain_other_ref, after,
    f_ref, b_ref, gain_out_ref,
):
    f_ref[...] = (fbase_ref[...] + add_wide(y_ref[...], ygot_ref[...])).astype(BF)
    length = back_ref.shape[0]
    x = add_wide(x_ref[:length, :], xgot_ref[:length, :])
    inv = inv_ref[:, :1]
    along = jnp.sum(x * back_ref[...].astype(F32), axis=1, keepdims=True)
    middle = along * inv * (1.0 / wide)
    b_ref[...] = (base_ref[...] + (x - unit_ref[...] * middle) * inv).astype(BF)
    core = lax.axis_index("dp") & 1
    half = wide // 2
    rank = gain_ref.shape[1]
    for row in range(half // rank):
        mine = pl.ds(pl.multiple_of(core * half + row * rank, rank), rank)
        theirs = pl.ds(pl.multiple_of((1 - core) * half + row * rank, rank), rank)
        gain_out_ref[:, mine] = gain_ref[row : row + 1, :]
        gain_out_ref[:, theirs] = gain_other_ref[row : row + 1, :]


def results(wide, after, *operands):
    shape = operands[0].shape
    held = tuple(pltpu.with_memory_space_constraint(a, pltpu.VMEM) for a in operands)
    return pl.pallas_call(
        functools.partial(results_kernel, wide),
        in_specs=vmem(len(operands)) + [pl.BlockSpec(memory_space=pl.ANY)],
        out_specs=vmem(3),
        out_shape=[jax.ShapeDtypeStruct(shape, BF)] * 2 + [jax.ShapeDtypeStruct((1, wide), F32)],
        compiler_params=pltpu.CompilerParams(vmem_limit_bytes=VMEM_BYTES // 2),
        cost_estimate=cost(10**4, 10**3),
        name="section_results",
    )(*held, *in_hbm((after,)))


def body(
    new_coeffs,
    loss_grad,
    sent_forward,
    sent_backward,
    stashed,
    subspace,
    norm_gain,
    w_query,
    w_key,
    w_value,
    w_output,
):
    wide = subspace.shape[0]
    wq, wk, wv, wo = w_query[0], w_key[0], w_value[0], w_output[0]
    nq, nk, nv = wq.shape[1], wk.shape[1], wv.shape[1]
    back = stashed[0]
    arrived, returned = cross_pipe(sent_forward[0], sent_backward[0])
    cosine, sine = rope_tables(back.shape[0])

    m2, o2, inv, basis, wq, narrow, turned = project(
        back, norm_gain, subspace, wq, wk, wv, wo
    )
    inner, give_a, give_b, keep_a, keep_b, x = backward(
        back, loss_grad, returned, m2, o2, inv, cosine, sine
    )
    out_got = [swap(piece, "dp", 1) for piece in (give_a, give_b)]
    inner_got = swap(inner, "dp", 1)
    x_got = swap(x, "tensor", 2)
    out_pair = [add_wide(keep, got).astype(BF) for keep, got in zip((keep_a, keep_b), out_got)]
    out_got = [swap(piece, "dp", 2) for piece in out_pair]
    *pair, gain = gain_part(basis, wq, narrow, inner, inner_got, x)
    pair_got = [swap(piece, "dp", 2) for piece in pair]
    y = forward(new_coeffs, arrived, turned, m2, o2, cosine, sine, gain)
    y_got = swap(y, "tensor", 1)
    x = add_after(x, x_got, y)
    x_got = swap(x, "tensor", 1)
    out_own = [add_after(piece, got, x) for piece, got in zip(out_pair, out_got)]
    out_other = [swap(piece, "dp", 1) for piece in out_own]
    grad_o = outward_grad(basis, out_own, out_other, x)
    y, gain = merge(y, y_got, *in_hbm((grad_o,)))
    gain_got = swap(gain, "tensor", 2)
    y_got = swap(y, "tensor", 2)
    own = [add_after(piece, got, y) for piece, got in zip(pair, pair_got)]
    other = [swap(piece, "dp", 1) for piece in own]
    base, unit, fbase = bases(
        back, loss_grad, returned, new_coeffs, arrived, basis, turned, inv, own[0]
    )
    gain = add_after(gain, gain_got, base)
    gain_got = swap(gain, "dp", 2)
    grad_q, grad_k, grad_v = inward_grads(basis, norm_gain, own, other, (nq, nk, nv), gain)
    gain = add_after(gain, gain_got, *in_hbm((grad_v,)))
    gain_other = swap(gain, "dp", 1)
    forward_out, backward_out, grad_gain = results(
        wide, grad_v, fbase, y, y_got, base, unit, x, x_got, back, inv, gain, gain_other
    )
    return (
        forward_out[None],
        backward_out[None],
        grad_q[None],
        grad_k[None],
        grad_v[None],
        grad_o[None],
        grad_gain,
    )


def solution(mesh):
    return jax.shard_map(
        body,
        mesh=mesh,
        in_specs=(
            P("dp", None),
            P("dp", None),
            P("pipe", "dp", None),
            P("pipe", "dp", None),
            P("pipe", "dp", None),
            P(),
            P("pipe", None),
            P("pipe", None, "tensor"),
            P("pipe", None, "tensor"),
            P("pipe", None, "tensor"),
            P("pipe", "tensor", None),
        ),
        out_specs=(
            P("pipe", "dp", None),
            P("pipe", "dp", None),
            P("pipe", "dp", "tensor"),
            P("pipe", "dp", "tensor"),
            P("pipe", "dp", "tensor"),
            P("pipe", "tensor", "dp"),
            P("pipe", None),
        ),
        check_vma=False,
    )
```

```python
import functools
import math

import jax
import jax.numpy as jnp
import numpy as np
from jax import lax
from jax.experimental import pallas as pl
from jax.experimental.pallas import tpu as pltpu
from jax.sharding import PartitionSpec as P

HD = 128
EPSILON = 1e-05
ROPE_BASE = 500000.0
BF = jnp.bfloat16
F32 = jnp.float32
VMEM_BYTES = 24 * 1024 * 1024
CHUNK = 512
PIECE = 1024
AHEAD = 3
LOG2E = 1.4426950408889634


def shifted(x, axis, by):
    devices = lax.axis_size(axis)
    pairs = [(i, i + by) for i in range(devices) if 0 <= i + by < devices]
    return lax.ppermute(x, axis, pairs)


def swap(x, axis, bit):
    devices = lax.axis_size(axis)
    return lax.ppermute(x, axis, [(i, i ^ bit) for i in range(devices)])


def cross_pipe(sent_forward, sent_backward):
    if lax.axis_size("pipe") != 2:
        return shifted(sent_forward, "pipe", 1), shifted(sent_backward, "pipe", -1)
    first = lax.axis_index("pipe") == 0
    got = swap(jnp.where(first, sent_forward, sent_backward), "pipe", 1)
    return got, got


def add_wide(a, b):
    return a.astype(F32) + b.astype(F32)


def nt(a, b):
    return lax.dot_general(a, b, (((1,), (1,)), ((), ())), preferred_element_type=F32)


def nn(a, b):
    return jnp.dot(a, b, preferred_element_type=F32)


def split(x, parts):
    out = []
    for _ in range(parts):
        piece = x.astype(BF)
        out.append(piece)
        x = x - piece.astype(F32)
    return out


def rope_tables(length):
    half = HD // 2
    frequency = np.float32(ROPE_BASE) ** (-2.0 * np.arange(half, dtype=np.float32) / HD)
    angles = np.arange(length, dtype=np.float32)[:, None] * frequency.astype(np.float32)
    cosine, sine = np.cos(angles), np.sin(angles)
    tables = (np.concatenate([cosine, cosine], 1), np.concatenate([-sine, sine], 1))
    return tuple(jnp.asarray(t, dtype=F32) for t in tables)


def rope(x, cosine, sine):
    return x * cosine + pltpu.roll(x, HD // 2, 1) * sine


def unrope(x, cosine, sine):
    return x * cosine - pltpu.roll(x, HD // 2, 1) * sine


def inverse_root(square_sum, width):
    return 1.0 / jnp.sqrt(square_sum / width + EPSILON)


def vmem(count):
    return [pl.BlockSpec(memory_space=pltpu.VMEM)] * count


def in_hbm(arrays):
    return tuple(pltpu.with_memory_space_constraint(a, pltpu.HBM) for a in arrays)


def cost(flops, num_bytes, exps=0):
    return pl.CostEstimate(flops=flops, bytes_accessed=num_bytes, transcendentals=exps)


def project_kernel(
    back_hbm, gain_hbm, u_hbm, wq_hbm, wk_hbm, wv_hbm, wo_hbm,
    m_ref, o_ref, inv_ref, u, wq, narrow, turned,
    back, gain, wo, scaled, m_acc, o_acc, sems,
):
    wide, rank = u.shape
    nq = wq.shape[1]
    nk = wk_hbm.shape[1]
    parts = wide // PIECE
    pieces = [pl.ds(i * PIECE, PIECE) for i in range(parts)]
    pairs = [(back_hbm, back), (gain_hbm, gain)]
    pairs += [(u_hbm.at[at, :], u.at[at, :]) for at in pieces]
    pairs += [(wq_hbm.at[at, :], wq.at[at, :]) for at in pieces[:2]]
    pairs += [(wk_hbm, narrow.at[:, pl.ds(0, nk)])]
    pairs += [(wv_hbm, narrow.at[:, pl.ds(nk, narrow.shape[1] - nk)])]
    pairs += [(wq_hbm.at[at, :], wq.at[at, :]) for at in pieces[2:]]
    pairs += [(wo_hbm.at[:, at], wo.at[:, at]) for at in pieces]
    copies = [
        pltpu.make_async_copy(source, target, sems.at[n])
        for n, (source, target) in enumerate(pairs)
    ]
    started = 0

    def start_to(count):
        nonlocal started
        for copy in copies[started:count]:
            copy.start()
        started = max(started, min(count, len(copies)))

    def wait(n):
        start_to(n + 1 + AHEAD)
        copies[n].wait()

    start_to(2 + parts + AHEAD)
    copies[0].wait()
    copies[1].wait()
    square = jnp.zeros((back.shape[0], HD), F32)
    for i, at in enumerate(pieces):
        copies[2 + i].wait()
        turned[:, at] = u[at, :].T
        scaled[:, at] = (turned[:, at].astype(F32) * gain[:, at]).astype(BF)
        decoded = nn(back[...], turned[:, at])
        for side in range(0, PIECE, HD):
            part = decoded[:, side : side + HD]
            square = square + part * part
    inv_ref[...] = jnp.broadcast_to(
        inverse_root(jnp.sum(square, axis=1, keepdims=True), wide), inv_ref.shape
    )
    place = 2 + parts
    for i, at in enumerate(pieces):
        if i == 2:
            wait(place)
            wait(place + 1)
            place += 2
            for p, piece in enumerate(split(nn(scaled[...], narrow[...]), 2)):
                m_ref[p * rank : (p + 1) * rank, nq:] = piece
        wait(place)
        place += 1
        part = nn(scaled[:, at], wq[at, :])
        if i == 0:
            m_acc[...] = part
        else:
            m_acc[...] += part
    for p, piece in enumerate(split(m_acc[...], 2)):
        m_ref[p * rank : (p + 1) * rank, :nq] = piece
    for i, at in enumerate(pieces):
        wait(place)
        place += 1
        part = nn(wo[:, at], u[at, :])
        if i == 0:
            o_acc[...] = part
        else:
            o_acc[...] += part
    o_ref[...] = o_acc[...].astype(BF)


def project(back, gain, basis, wq, wk, wv, wo):
    wide, rank = basis.shape
    length = back.shape[0]
    ne = wo.shape[0]
    nq = wq.shape[1]
    rest = wk.shape[1] + wv.shape[1]
    operands = in_hbm((back, gain, basis, wq, wk, wv, wo))
    return pl.pallas_call(
        project_kernel,
        in_specs=[pl.BlockSpec(memory_space=pltpu.HBM)] * len(operands),
        out_specs=vmem(7),
        out_shape=[
            jax.ShapeDtypeStruct((2 * rank, nq + rest), BF),
            jax.ShapeDtypeStruct((ne, rank), BF),
            jax.ShapeDtypeStruct((length, HD), F32),
            jax.ShapeDtypeStruct(basis.shape, BF),
            jax.ShapeDtypeStruct(wq.shape, BF),
            jax.ShapeDtypeStruct((wide, rest), BF),
            jax.ShapeDtypeStruct((rank, wide), BF),
        ],
        scratch_shapes=[
            pltpu.VMEM(back.shape, BF),
            pltpu.VMEM(gain.shape, F32),
            pltpu.VMEM(wo.shape, BF),
            pltpu.VMEM((rank, wide), BF),
            pltpu.VMEM((rank, nq), F32),
            pltpu.VMEM((ne, rank), F32),
            pltpu.SemaphoreType.DMA((4 + 3 * (wide // PIECE),)),
        ],
        compiler_params=pltpu.CompilerParams(vmem_limit_bytes=VMEM_BYTES * 3 // 2),
        cost_estimate=cost(6 * 10**9, 20 * 10**6),
        name="project_weights",
    )(*operands)


def project_heads(coeffs, inv, m_ref, cosine, sine, q, k, v1):
    length = coeffs.shape[0]
    heads = q.shape[0] // length
    twice = jnp.concatenate([coeffs, coeffs], axis=1)
    for h in range(heads):
        part = nn(twice, m_ref[:, h * HD : (h + 1) * HD]) * inv
        q[h * length : (h + 1) * length, :] = rope(part, cosine, sine).astype(BF)
    part = nn(twice, m_ref[:, heads * HD :]) * inv
    k[...] = rope(part[:, :HD], cosine, sine).astype(BF)
    v1[:, :HD] = part[:, HD:].astype(BF)
    v1[:, HD:] = jnp.ones_like(v1[:, HD:])


def exps_of(scores, exps, low, length):
    row = lax.broadcasted_iota(jnp.int32, (length, length), 0)
    column = lax.broadcasted_iota(jnp.int32, (length, length), 1)
    causal = row >= column

    def one(h, _):
        at = pl.ds(pl.multiple_of(h * length, length), length)
        s = jnp.where(causal, scores[at, :], -jnp.inf)
        top = jnp.max(s, axis=1, keepdims=True)
        e = jnp.exp2((s - top) * (LOG2E / math.sqrt(HD)))
        if exps is not None:
            exps[at, :] = e
        low[at, :] = e.astype(BF)
        return 0

    lax.fori_loop(0, scores.shape[0] // length, one, 0, unroll=2)


def backward_kernel(
    back_ref, loss_ref, sent_ref, m_ref, o_ref, inv_ref, cos_ref, sin_ref,
    inner_ref, out_give_ref, out_keep_ref, x_ref,
    q, k, v1, gh, ghs, scores, low, mixed, gp, ds, dq, heads, grads, inner, out_inner,
):
    length, rank = back_ref.shape
    ne = o_ref.shape[0]
    count = ne // HD
    scale = 1.0 / math.sqrt(HD)
    last = lax.axis_size("pipe") - 1
    is_last = lax.axis_index("pipe") == last
    back = back_ref[...]
    up = jnp.where(is_last, loss_ref[...], sent_ref[...])
    cosine, sine = cos_ref[...], sin_ref[...]
    inv = inv_ref[...]
    project_heads(back, inv[:, :1], m_ref, cosine, sine, q, k, v1)
    scores[...] = nt(q[...], k[...])
    for h in range(count):
        gh[h * length : (h + 1) * length, :] = nt(up, o_ref[h * HD : (h + 1) * HD, :]).astype(BF)
    exps_of(scores, scores, low, length)
    mixed[...] = nn(low[...], v1[...])
    gp[...] = nt(gh[...], v1[:, :HD])

    for h in range(count):
        at = slice(h * length, (h + 1) * length)
        inverse = 1.0 / mixed[at, HD:]
        out = mixed[at, :HD] * inverse
        heads[:, h * HD : (h + 1) * HD] = out.astype(BF)
        grad = gh[at, :].astype(F32)
        ghs[at, :] = (grad * inverse).astype(BF)
        delta = jnp.sum(grad * out, axis=1, keepdims=True)
        factor = inverse * scale
        for side in range(0, length, HD):
            part = scores[at, side : side + HD] * factor
            ds[at, side : side + HD] = (part * (gp[at, side : side + HD] - delta)).astype(BF)

    dq[...] = nn(ds[...], k[...])
    for h in range(count):
        part = dq[h * length : (h + 1) * length, :]
        grads[:, h * HD : (h + 1) * HD] = unrope(part, cosine, sine).astype(BF)
    dk = nn(q[...].T, ds[...]).T
    grads[:, ne : ne + HD] = unrope(dk, cosine, sine).astype(BF)
    grads[:, ne + HD :] = nn(ghs[...].T, low[...]).T.astype(BF)
    unit = (back.astype(F32) * inv[:, :1]).astype(BF)
    half = rank // 2
    core = lax.axis_index("dp") & 1
    mine = pl.ds(pl.multiple_of(core * half, half), half)
    theirs = pl.ds(pl.multiple_of((1 - core) * half, half), half)
    inner[...] = nn(unit.T, grads[...]).astype(BF)
    inner_ref[:half, :] = inner[mine, :]
    inner_ref[half:, :] = inner[theirs, :]
    out_inner[...] = nn(up.T, heads[...]).astype(BF)
    out_keep_ref[...] = out_inner[mine, :]
    out_give_ref[...] = out_inner[theirs, :]
    x_ref[...] = nt(grads[...], m_ref[:rank, :]).astype(BF)


def backward(back, loss, sent, m2, o2, inv, cosine, sine):
    length, rank = back.shape
    ne = o2.shape[0]
    total = m2.shape[1]
    assert total == ne + 2 * HD
    stack = ne // HD * length
    return pl.pallas_call(
        backward_kernel,
        in_specs=vmem(8),
        out_specs=vmem(4),
        out_shape=[
            jax.ShapeDtypeStruct((rank, total), BF),
            jax.ShapeDtypeStruct((rank // 2, ne), BF),
            jax.ShapeDtypeStruct((rank // 2, ne), BF),
            jax.ShapeDtypeStruct((length, rank), BF),
        ],
        scratch_shapes=[
            pltpu.VMEM((stack, HD), BF),
            pltpu.VMEM((length, HD), BF),
            pltpu.VMEM((length, 2 * HD), BF),
            pltpu.VMEM((stack, HD), BF),
            pltpu.VMEM((stack, HD), BF),
            pltpu.VMEM((stack, length), F32),
            pltpu.VMEM((stack, length), BF),
            pltpu.VMEM((stack, 2 * HD), F32),
            pltpu.VMEM((stack, length), F32),
            pltpu.VMEM((stack, length), BF),
            pltpu.VMEM((stack, HD), F32),
            pltpu.VMEM((length, ne), BF),
            pltpu.VMEM((length, total), BF),
            pltpu.VMEM((rank, total), BF),
            pltpu.VMEM((rank, ne), BF),
        ],
        compiler_params=pltpu.CompilerParams(vmem_limit_bytes=VMEM_BYTES),
        cost_estimate=cost(10**4, 10**3),
        name="attention_backward",
    )(back, loss, sent, m2, o2, inv, cosine, sine)


def bases_kernel(
    back_ref, loss_ref, returned_ref, new_ref, arrived_ref, u_ref, turned_ref, inv_ref, after,
    base_ref, unit_ref, fbase_ref, g_ref,
):
    rank = u_ref.shape[1]
    for i, piece in enumerate(split(nn(turned_ref[...], u_ref[...]), 3)):
        g_ref[i * rank : (i + 1) * rank, :] = piece
    is_last = lax.axis_index("pipe") == lax.axis_size("pipe") - 1
    is_first = lax.axis_index("pipe") == 0
    up = jnp.where(is_last, loss_ref[...], returned_ref[...])
    coeffs = jnp.where(is_first, new_ref[...], arrived_ref[...])
    base_ref[...] = nn(jnp.concatenate([up] * 3, axis=1), g_ref[...])
    fbase_ref[...] = nn(jnp.concatenate([coeffs] * 3, axis=1), g_ref[...])
    unit_ref[...] = nn(jnp.concatenate([back_ref[...]] * 3, axis=1), g_ref[...]) * inv_ref[:, :1]


def bases(back, loss, returned, new, arrived, basis, turned, inv, after):
    length, rank = back.shape
    return pl.pallas_call(
        bases_kernel,
        in_specs=vmem(8) + [pl.BlockSpec(memory_space=pl.ANY)],
        out_specs=vmem(3),
        out_shape=[jax.ShapeDtypeStruct((length, rank), F32)] * 3,
        scratch_shapes=[pltpu.VMEM((3 * rank, rank), BF)],
        compiler_params=pltpu.CompilerParams(vmem_limit_bytes=VMEM_BYTES // 2),
        cost_estimate=cost(10**4, 10**3),
        name="encoded_again",
    )(back, loss, returned, new, arrived, basis, turned, inv, after)


def forward_kernel(
    new_ref, sent_ref, turned_ref, m_ref, o_ref, cos_ref, sin_ref, after,
    y_ref, q, k, v1, scores, low, mixed, heads,
):
    length, rank = new_ref.shape
    wide = turned_ref.shape[1]
    is_first = lax.axis_index("pipe") == 0
    coeffs = jnp.where(is_first, new_ref[...], sent_ref[...])
    square = jnp.zeros((length, HD), F32)
    for at in range(0, wide, PIECE):
        decoded = nn(coeffs, turned_ref[:, at : at + PIECE])
        for side in range(0, PIECE, HD):
            part = decoded[:, side : side + HD]
            square = square + part * part
    inv = inverse_root(jnp.sum(square, axis=1, keepdims=True), wide)
    project_heads(coeffs, inv, m_ref, cos_ref[...], sin_ref[...], q, k, v1)
    scores[...] = nt(q[...], k[...])
    exps_of(scores, None, low, length)
    mixed[...] = nn(low[...], v1[...])
    for h in range(heads.shape[1] // HD):
        at = slice(h * length, (h + 1) * length)
        heads[:, h * HD : (h + 1) * HD] = (mixed[at, :HD] / mixed[at, HD:]).astype(BF)
    y_ref[:length, :] = nn(heads[...], o_ref[...]).astype(BF)
    y_ref[length:, :] = jnp.zeros_like(y_ref[length:, :])


def forward(new, sent, turned, m2, o2, cosine, sine, after):
    length, rank = new.shape
    ne = o2.shape[0]
    stack = ne // HD * length
    return pl.pallas_call(
        forward_kernel,
        in_specs=vmem(7) + [pl.BlockSpec(memory_space=pl.ANY)],
        out_specs=pl.BlockSpec(memory_space=pltpu.VMEM),
        out_shape=jax.ShapeDtypeStruct((length + 32, rank), BF),
        scratch_shapes=[
            pltpu.VMEM((stack, HD), BF),
            pltpu.VMEM((length, HD), BF),
            pltpu.VMEM((length, 2 * HD), BF),
            pltpu.VMEM((stack, length), F32),
            pltpu.VMEM((stack, length), BF),
            pltpu.VMEM((stack, 2 * HD), F32),
            pltpu.VMEM((length, ne), BF),
        ],
        compiler_params=pltpu.CompilerParams(vmem_limit_bytes=VMEM_BYTES),
        cost_estimate=cost(10**4, 10**3),
        name="attention_forward",
    )(new, sent, turned, m2, o2, cosine, sine, after)


def write_split(ref, value):
    high, low = split(value, 2)
    both = jnp.concatenate([high.astype(F32), low.astype(F32)], axis=0)
    ref[ref.shape[0] - 16 :, :] = both.astype(BF)


def read_split(ref):
    both = ref[ref.shape[0] - 16 :, :].astype(F32)
    return both[:8] + both[8:]


def gain_kernel(
    u_ref, wq_ref, narrow_ref, inner_ref, got_ref, x_ref, after,
    pair_ref, out_ref, turned, rows_f32,
):
    nq = wq_ref.shape[1]
    rows = u_ref.shape[0] // 2
    rank = u_ref.shape[1]
    half = inner_ref.shape[0] // 2
    core = lax.axis_index("dp") & 1
    mine = add_wide(inner_ref[:half, :], got_ref[half:, :]).astype(BF)
    theirs = add_wide(inner_ref[half:, :], got_ref[:half, :]).astype(BF)
    pair_ref[...] = mine
    out_ref[: x_ref.shape[0], :] = x_ref[...]
    turned[:, pl.ds(pl.multiple_of(core * half, half), half)] = mine.T
    turned[:, pl.ds(pl.multiple_of((1 - core) * half, half), half)] = theirs.T
    for at in range(0, rows, CHUNK):
        place = pl.ds(pl.multiple_of(core * rows + at, CHUNK), CHUNK)
        against = nn(wq_ref[place, :], turned[:nq, :])
        against += nn(narrow_ref[place, :], turned[nq:, :])
        terms = against * u_ref[place, :].astype(F32)
        folded = sum(terms[:, side : side + HD] for side in range(0, terms.shape[1], HD))
        line = jnp.sum(folded.T, axis=0, keepdims=True)
        for side in range(0, CHUNK, rank):
            row = (at + side) // rank
            rows_f32[row : row + 1, :] = line[:, side : side + rank]
    write_split(out_ref, rows_f32[...])


def gain_part(basis, wq, narrow, inner, got, x, after):
    wide, rank = basis.shape
    assert wide // 2 == 8 * rank
    held = tuple(pltpu.with_memory_space_constraint(a, pltpu.VMEM) for a in (basis, wq, narrow))
    return pl.pallas_call(
        gain_kernel,
        in_specs=vmem(6) + [pl.BlockSpec(memory_space=pl.ANY)],
        out_specs=vmem(2),
        out_shape=[
            jax.ShapeDtypeStruct((rank // 2, inner.shape[1]), BF),
            jax.ShapeDtypeStruct((x.shape[0] + 16, rank), BF),
        ],
        scratch_shapes=[
            pltpu.VMEM((inner.shape[1], rank), BF),
            pltpu.VMEM((8, rank), F32),
        ],
        compiler_params=pltpu.CompilerParams(vmem_limit_bytes=VMEM_BYTES),
        cost_estimate=cost(10**4, 10**3),
        name="pair_sum_and_gain_gradient",
    )(*held, inner, got, x, after)


def merge_kernel(a_ref, b_ref, after, out_ref):
    rest = out_ref.shape[0] - 16
    out_ref[:rest, :] = add_wide(a_ref[:rest, :], b_ref[:rest, :]).astype(BF)
    write_split(out_ref, read_split(a_ref) + read_split(b_ref))


def total_kernel(a_ref, b_ref, after, out_ref):
    out_ref[...] = read_split(a_ref) + read_split(b_ref)


def own_kernel(a_ref, b_ref, after, *out_refs):
    at = 0
    for ref in out_refs:
        size = ref.shape[1]
        ref[...] = add_wide(a_ref[:, at : at + size], b_ref[:, at : at + size]).astype(BF)
        at += size


def small_kernel(kernel, name, out_shape, a, b, after):
    return pl.pallas_call(
        kernel,
        in_specs=vmem(2) + [pl.BlockSpec(memory_space=pl.ANY)],
        out_specs=jax.tree.map(lambda _: pl.BlockSpec(memory_space=pltpu.VMEM), out_shape),
        out_shape=out_shape,
        compiler_params=pltpu.CompilerParams(vmem_limit_bytes=VMEM_BYTES // 2),
        cost_estimate=cost(10**4, 10**3),
        name=name,
    )(a, b, after)


def merge(a, b, after):
    return small_kernel(merge_kernel, "sum_with_gain", jax.ShapeDtypeStruct(a.shape, BF), a, b, after)


def gain_total(a, b, after):
    shape = jax.ShapeDtypeStruct((8, a.shape[1]), F32)
    return small_kernel(total_kernel, "gain_total", shape, a, b, after)


def own_pieces(a, b, sizes, after):
    shapes = [jax.ShapeDtypeStruct((a.shape[0], n), BF) for n in sizes]
    return small_kernel(own_kernel, "sum_over_y", shapes, a, b, after)


def add_kernel(a_ref, b_ref, after, out_ref):
    rows = out_ref.shape[0]
    out_ref[...] = add_wide(a_ref[:rows, :], b_ref[:rows, :]).astype(out_ref.dtype)


def add_after(a, b, after, rows=None):
    shape = jax.ShapeDtypeStruct((rows or a.shape[0], a.shape[1]), a.dtype)
    return small_kernel(add_kernel, "pair_sum", shape, a, b, after)


def gather_halves(own_refs, other_refs, whole):
    half = whole.shape[0] // 2
    core = lax.axis_index("dp") & 1
    at = 0
    for own_ref, other_ref in zip(own_refs, other_refs):
        columns = pl.ds(at, own_ref.shape[1])
        whole[pl.ds(pl.multiple_of(core * half, half), half), columns] = own_ref[...]
        whole[pl.ds(pl.multiple_of((1 - core) * half, half), half), columns] = other_ref[...]
        at += own_ref.shape[1]


def inward_kernel(pieces, u_ref, gain_ref, *refs):
    own_refs, other_refs = refs[:pieces], refs[pieces : 2 * pieces]
    q_ref, k_ref, v_ref, inner = refs[-4:]
    nq, nk = q_ref.shape[1], k_ref.shape[1]
    block = q_ref.shape[0]

    @pl.when(pl.program_id(0) == 0)
    def _():
        gather_halves(own_refs, other_refs, inner)

    step = lax.axis_index("dp") * pl.num_programs(0) + pl.program_id(0)
    rows = pl.ds(pl.multiple_of(step * block, block), block)
    gain = jnp.broadcast_to(gain_ref[:, rows], (HD, block)).T[:, :1]
    grad = nn(u_ref[rows, :], inner[...]) * gain
    q_ref[...] = grad[:, :nq].astype(BF)
    k_ref[...] = grad[:, nq : nq + nk].astype(BF)
    v_ref[...] = grad[:, nq + nk :].astype(BF)


def outward_kernel(pieces, u_ref, *refs):
    own_refs, other_refs = refs[:pieces], refs[pieces : 2 * pieces]
    o_ref, inner = refs[-2:]

    @pl.when(pl.program_id(0) == 0)
    def _():
        gather_halves(own_refs, other_refs, inner)

    block, rows = o_ref.shape
    at = pl.multiple_of(pl.program_id(0) * block, block)
    basis = u_ref[pl.ds(pl.multiple_of(lax.axis_index("dp") * rows, rows), rows), :]
    o_ref[...] = nt(inner[:, pl.ds(at, block)].T, basis).astype(BF)


STEPS = 2


def inward_grads(basis, gain, own, other, sizes, after):
    wide, rank = basis.shape
    rows = wide // lax.axis_size("dp")
    block = rows // STEPS
    return pl.pallas_call(
        functools.partial(inward_kernel, len(own)),
        grid=(STEPS,),
        in_specs=vmem(2 + 2 * len(own)) + [pl.BlockSpec(memory_space=pl.ANY)],
        out_specs=[pl.BlockSpec((block, n), lambda i: (i, 0)) for n in sizes],
        scratch_shapes=[pltpu.VMEM((rank, sum(sizes)), BF)],
        out_shape=[jax.ShapeDtypeStruct((rows, n), BF) for n in sizes],
        compiler_params=pltpu.CompilerParams(vmem_limit_bytes=VMEM_BYTES),
        cost_estimate=cost(10**4, 10**3),
        name="inward_weight_gradients",
    )(basis, gain, *own, *other, after)


def outward_grad(basis, own, other, after):
    wide, rank = basis.shape
    rows = wide // lax.axis_size("dp")
    ne = sum(piece.shape[1] for piece in own)
    return pl.pallas_call(
        functools.partial(outward_kernel, len(own)),
        grid=(STEPS,),
        in_specs=vmem(1 + 2 * len(own)) + [pl.BlockSpec(memory_space=pl.ANY)],
        out_specs=pl.BlockSpec((ne // STEPS, rows), lambda i: (i, 0)),
        scratch_shapes=[pltpu.VMEM((rank, ne), BF)],
        out_shape=jax.ShapeDtypeStruct((ne, rows), BF),
        compiler_params=pltpu.CompilerParams(vmem_limit_bytes=VMEM_BYTES),
        cost_estimate=cost(10**4, 10**3),
        name="output_weight_gradient",
    )(basis, *own, *other, after)


def results_kernel(
    wide, fbase_ref, y_ref, ygot_ref, base_ref, unit_ref, x_ref, xgot_ref, back_ref, inv_ref,
    gain_ref, gain_other_ref, after,
    f_ref, b_ref, gain_out_ref,
):
    f_ref[...] = (fbase_ref[...] + add_wide(y_ref[...], ygot_ref[...])).astype(BF)
    length = back_ref.shape[0]
    x = add_wide(x_ref[:length, :], xgot_ref[:length, :])
    inv = inv_ref[:, :1]
    along = jnp.sum(x * back_ref[...].astype(F32), axis=1, keepdims=True)
    middle = along * inv * (1.0 / wide)
    b_ref[...] = (base_ref[...] + (x - unit_ref[...] * middle) * inv).astype(BF)
    core = lax.axis_index("dp") & 1
    half = wide // 2
    rank = gain_ref.shape[1]
    for row in range(half // rank):
        mine = pl.ds(pl.multiple_of(core * half + row * rank, rank), rank)
        theirs = pl.ds(pl.multiple_of((1 - core) * half + row * rank, rank), rank)
        gain_out_ref[:, mine] = gain_ref[row : row + 1, :]
        gain_out_ref[:, theirs] = gain_other_ref[row : row + 1, :]


def results(wide, after, *operands):
    shape = operands[0].shape
    held = tuple(pltpu.with_memory_space_constraint(a, pltpu.VMEM) for a in operands)
    return pl.pallas_call(
        functools.partial(results_kernel, wide),
        in_specs=vmem(len(operands)) + [pl.BlockSpec(memory_space=pl.ANY)],
        out_specs=vmem(3),
        out_shape=[jax.ShapeDtypeStruct(shape, BF)] * 2 + [jax.ShapeDtypeStruct((1, wide), F32)],
        compiler_params=pltpu.CompilerParams(vmem_limit_bytes=VMEM_BYTES // 2),
        cost_estimate=cost(10**4, 10**3),
        name="section_results",
    )(*held, *in_hbm((after,)))


def body(
    new_coeffs,
    loss_grad,
    sent_forward,
    sent_backward,
    stashed,
    subspace,
    norm_gain,
    w_query,
    w_key,
    w_value,
    w_output,
):
    wide = subspace.shape[0]
    wq, wk, wv, wo = w_query[0], w_key[0], w_value[0], w_output[0]
    nq, nk, nv = wq.shape[1], wk.shape[1], wv.shape[1]
    back = stashed[0]
    arrived, returned = cross_pipe(sent_forward[0], sent_backward[0])
    cosine, sine = rope_tables(back.shape[0])

    m2, o2, inv, basis, wq, narrow, turned = project(
        back, norm_gain, subspace, wq, wk, wv, wo
    )
    inner, out_give, out_keep, x = backward(
        back, loss_grad, returned, m2, o2, inv, cosine, sine
    )
    out_got = swap(out_give, "dp", 1)
    inner_got = swap(inner, "dp", 1)
    base, unit, fbase = bases(
        back, loss_grad, returned, new_coeffs, arrived, basis, turned, inv, out_keep
    )
    out_pair = add_after(out_keep, out_got, fbase)
    out_got = swap(out_pair, "dp", 2)
    pair, x = gain_part(basis, wq, narrow, inner, inner_got, x, out_pair)
    pair_got = swap(pair, "dp", 2)
    x_got = swap(x, "tensor", 2)
    y = forward(new_coeffs, arrived, turned, m2, o2, cosine, sine, pair)
    y_got = swap(y, "tensor", 2)
    out_own = add_after(out_pair, out_got, y)
    out_other = swap(out_own, "dp", 1)
    x = merge(x, x_got, out_own)
    x_got = swap(x, "tensor", 1)
    grad_o = outward_grad(basis, [out_own], [out_other], x)
    sizes = (nq // 2, nq - nq // 2, nk + nv)
    own = own_pieces(pair, pair_got, sizes, *in_hbm((grad_o,)))
    other = [swap(piece, "dp", 1) for piece in own]
    gain = gain_total(x, x_got, own[0])
    gain_got = swap(gain, "dp", 2)
    y = add_after(y, y_got, gain, rows=back.shape[0])
    y_got = swap(y, "tensor", 1)
    grad_q, grad_k, grad_v = inward_grads(basis, norm_gain, own, other, (nq, nk, nv), y)
    gain = add_after(gain, gain_got, *in_hbm((grad_v,)))
    gain_other = swap(gain, "dp", 1)
    forward_out, backward_out, grad_gain = results(
        wide, grad_v, fbase, y, y_got, base, unit, x, x_got, back, inv, gain, gain_other
    )
    return (
        forward_out[None],
        backward_out[None],
        grad_q[None],
        grad_k[None],
        grad_v[None],
        grad_o[None],
        grad_gain,
    )


def solution(mesh):
    return jax.shard_map(
        body,
        mesh=mesh,
        in_specs=(
            P("dp", None),
            P("dp", None),
            P("pipe", "dp", None),
            P("pipe", "dp", None),
            P("pipe", "dp", None),
            P(),
            P("pipe", None),
            P("pipe", None, "tensor"),
            P("pipe", None, "tensor"),
            P("pipe", None, "tensor"),
            P("pipe", "tensor", None),
        ),
        out_specs=(
            P("pipe", "dp", None),
            P("pipe", "dp", None),
            P("pipe", "dp", "tensor"),
            P("pipe", "dp", "tensor"),
            P("pipe", "dp", "tensor"),
            P("pipe", "tensor", "dp"),
            P("pipe", None),
        ),
        check_vma=False,
    )
```

```python
import functools
import math

import jax
import jax.numpy as jnp
import numpy as np
from jax import lax
from jax.experimental import pallas as pl
from jax.experimental.pallas import tpu as pltpu
from jax.sharding import PartitionSpec as P

HD = 128
EPSILON = 1e-05
ROPE_BASE = 500000.0
BF = jnp.bfloat16
F32 = jnp.float32
VMEM_BYTES = 24 * 1024 * 1024
CHUNK = 512
PIECE = 1024
AHEAD = 3
LOG2E = 1.4426950408889634


def shifted(x, axis, by):
    devices = lax.axis_size(axis)
    pairs = [(i, i + by) for i in range(devices) if 0 <= i + by < devices]
    return lax.ppermute(x, axis, pairs)


def swap(x, axis, bit):
    devices = lax.axis_size(axis)
    return lax.ppermute(x, axis, [(i, i ^ bit) for i in range(devices)])


def cross_pipe(sent_forward, sent_backward):
    if lax.axis_size("pipe") != 2:
        return shifted(sent_forward, "pipe", 1), shifted(sent_backward, "pipe", -1)
    first = lax.axis_index("pipe") == 0
    got = swap(jnp.where(first, sent_forward, sent_backward), "pipe", 1)
    return got, got


def add_wide(a, b):
    return a.astype(F32) + b.astype(F32)


def nt(a, b):
    return lax.dot_general(a, b, (((1,), (1,)), ((), ())), preferred_element_type=F32)


def nn(a, b):
    return jnp.dot(a, b, preferred_element_type=F32)


def split(x, parts):
    out = []
    for _ in range(parts):
        piece = x.astype(BF)
        out.append(piece)
        x = x - piece.astype(F32)
    return out


def rope_tables(length):
    half = HD // 2
    frequency = np.float32(ROPE_BASE) ** (-2.0 * np.arange(half, dtype=np.float32) / HD)
    angles = np.arange(length, dtype=np.float32)[:, None] * frequency.astype(np.float32)
    cosine, sine = np.cos(angles), np.sin(angles)
    tables = (np.concatenate([cosine, cosine], 1), np.concatenate([-sine, sine], 1))
    return tuple(jnp.asarray(t, dtype=F32) for t in tables)


def rope(x, cosine, sine):
    return x * cosine + pltpu.roll(x, HD // 2, 1) * sine


def unrope(x, cosine, sine):
    return x * cosine - pltpu.roll(x, HD // 2, 1) * sine


def inverse_root(square_sum, width):
    return 1.0 / jnp.sqrt(square_sum / width + EPSILON)


def vmem(count):
    return [pl.BlockSpec(memory_space=pltpu.VMEM)] * count


def in_hbm(arrays):
    return tuple(pltpu.with_memory_space_constraint(a, pltpu.HBM) for a in arrays)


def cost(flops, num_bytes, exps=0):
    return pl.CostEstimate(flops=flops, bytes_accessed=num_bytes, transcendentals=exps)


def project_kernel(
    back_hbm, gain_hbm, u_hbm, wq_hbm, wk_hbm, wv_hbm, wo_hbm,
    m_ref, o_ref, inv_ref, u, wq, narrow, turned,
    back, gain, wo, scaled, m_acc, o_acc, sems,
):
    wide, rank = u.shape
    nq = wq.shape[1]
    nk = wk_hbm.shape[1]
    parts = wide // PIECE
    pieces = [pl.ds(i * PIECE, PIECE) for i in range(parts)]
    pairs = [(back_hbm, back), (gain_hbm, gain)]
    pairs += [(u_hbm.at[at, :], u.at[at, :]) for at in pieces]
    pairs += [(wq_hbm.at[at, :], wq.at[at, :]) for at in pieces[:2]]
    pairs += [(wk_hbm, narrow.at[:, pl.ds(0, nk)])]
    pairs += [(wv_hbm, narrow.at[:, pl.ds(nk, narrow.shape[1] - nk)])]
    pairs += [(wq_hbm.at[at, :], wq.at[at, :]) for at in pieces[2:]]
    pairs += [(wo_hbm.at[:, at], wo.at[:, at]) for at in pieces]
    copies = [
        pltpu.make_async_copy(source, target, sems.at[n])
        for n, (source, target) in enumerate(pairs)
    ]
    started = 0

    def start_to(count):
        nonlocal started
        for copy in copies[started:count]:
            copy.start()
        started = max(started, min(count, len(copies)))

    def wait(n):
        start_to(n + 1 + AHEAD)
        copies[n].wait()

    start_to(2 + parts + AHEAD)
    copies[0].wait()
    copies[1].wait()
    square = jnp.zeros((back.shape[0], HD), F32)
    for i, at in enumerate(pieces):
        copies[2 + i].wait()
        turned[:, at] = u[at, :].T
        scaled[:, at] = (turned[:, at].astype(F32) * gain[:, at]).astype(BF)
        decoded = nn(back[...], turned[:, at])
        for side in range(0, PIECE, HD):
            part = decoded[:, side : side + HD]
            square = square + part * part
    inv_ref[...] = jnp.broadcast_to(
        inverse_root(jnp.sum(square, axis=1, keepdims=True), wide), inv_ref.shape
    )
    place = 2 + parts
    for i, at in enumerate(pieces):
        if i == 2:
            wait(place)
            wait(place + 1)
            place += 2
            for p, piece in enumerate(split(nn(scaled[...], narrow[...]), 2)):
                m_ref[p * rank : (p + 1) * rank, nq:] = piece
        wait(place)
        place += 1
        part = nn(scaled[:, at], wq[at, :])
        if i == 0:
            m_acc[...] = part
        else:
            m_acc[...] += part
    for p, piece in enumerate(split(m_acc[...], 2)):
        m_ref[p * rank : (p + 1) * rank, :nq] = piece
    for i, at in enumerate(pieces):
        wait(place)
        place += 1
        part = nn(wo[:, at], u[at, :])
        if i == 0:
            o_acc[...] = part
        else:
            o_acc[...] += part
    o_ref[...] = o_acc[...].astype(BF)


def project(back, gain, basis, wq, wk, wv, wo):
    wide, rank = basis.shape
    length = back.shape[0]
    ne = wo.shape[0]
    nq = wq.shape[1]
    rest = wk.shape[1] + wv.shape[1]
    operands = in_hbm((back, gain, basis, wq, wk, wv, wo))
    return pl.pallas_call(
        project_kernel,
        in_specs=[pl.BlockSpec(memory_space=pltpu.HBM)] * len(operands),
        out_specs=vmem(7),
        out_shape=[
            jax.ShapeDtypeStruct((2 * rank, nq + rest), BF),
            jax.ShapeDtypeStruct((ne, rank), BF),
            jax.ShapeDtypeStruct((length, HD), F32),
            jax.ShapeDtypeStruct(basis.shape, BF),
            jax.ShapeDtypeStruct(wq.shape, BF),
            jax.ShapeDtypeStruct((wide, rest), BF),
            jax.ShapeDtypeStruct((rank, wide), BF),
        ],
        scratch_shapes=[
            pltpu.VMEM(back.shape, BF),
            pltpu.VMEM(gain.shape, F32),
            pltpu.VMEM(wo.shape, BF),
            pltpu.VMEM((rank, wide), BF),
            pltpu.VMEM((rank, nq), F32),
            pltpu.VMEM((ne, rank), F32),
            pltpu.SemaphoreType.DMA((4 + 3 * (wide // PIECE),)),
        ],
        compiler_params=pltpu.CompilerParams(vmem_limit_bytes=VMEM_BYTES * 3 // 2),
        cost_estimate=cost(6 * 10**9, 20 * 10**6),
        name="project_weights",
    )(*operands)


def project_heads(coeffs, inv, m_ref, cosine, sine, q, k, v1):
    length = coeffs.shape[0]
    heads = q.shape[0] // length
    twice = jnp.concatenate([coeffs, coeffs], axis=1)
    for h in range(heads):
        part = nn(twice, m_ref[:, h * HD : (h + 1) * HD]) * inv
        q[h * length : (h + 1) * length, :] = rope(part, cosine, sine).astype(BF)
    part = nn(twice, m_ref[:, heads * HD :]) * inv
    k[...] = rope(part[:, :HD], cosine, sine).astype(BF)
    v1[:, :HD] = part[:, HD:].astype(BF)
    v1[:, HD:] = jnp.ones_like(v1[:, HD:])


def exps_of(scores, exps, low, length):
    row = lax.broadcasted_iota(jnp.int32, (length, length), 0)
    column = lax.broadcasted_iota(jnp.int32, (length, length), 1)
    causal = row >= column

    def one(h, _):
        at = pl.ds(pl.multiple_of(h * length, length), length)
        s = jnp.where(causal, scores[at, :], -jnp.inf)
        top = jnp.max(s, axis=1, keepdims=True)
        e = jnp.exp2((s - top) * (LOG2E / math.sqrt(HD)))
        if exps is not None:
            exps[at, :] = e
        low[at, :] = e.astype(BF)
        return 0

    lax.fori_loop(0, scores.shape[0] // length, one, 0, unroll=2)


def backward_kernel(
    back_ref, loss_ref, sent_ref, m_ref, o_ref, inv_ref, cos_ref, sin_ref,
    inner_ref, out_give_ref, out_keep_ref, x_ref,
    q, k, v1, gh, ghs, scores, low, mixed, gp, ds, dq, heads, grads, inner, out_inner,
):
    length, rank = back_ref.shape
    ne = o_ref.shape[0]
    count = ne // HD
    scale = 1.0 / math.sqrt(HD)
    last = lax.axis_size("pipe") - 1
    is_last = lax.axis_index("pipe") == last
    back = back_ref[...]
    up = jnp.where(is_last, loss_ref[...], sent_ref[...])
    cosine, sine = cos_ref[...], sin_ref[...]
    inv = inv_ref[...]
    project_heads(back, inv[:, :1], m_ref, cosine, sine, q, k, v1)
    scores[...] = nt(q[...], k[...])
    for h in range(count):
        gh[h * length : (h + 1) * length, :] = nt(up, o_ref[h * HD : (h + 1) * HD, :]).astype(BF)
    exps_of(scores, scores, low, length)
    mixed[...] = nn(low[...], v1[...])
    gp[...] = nt(gh[...], v1[:, :HD])

    for h in range(count):
        at = slice(h * length, (h + 1) * length)
        inverse = 1.0 / mixed[at, HD:]
        out = mixed[at, :HD] * inverse
        heads[:, h * HD : (h + 1) * HD] = out.astype(BF)
        grad = gh[at, :].astype(F32)
        ghs[at, :] = (grad * inverse).astype(BF)
        delta = jnp.sum(grad * out, axis=1, keepdims=True)
        factor = inverse * scale
        for side in range(0, length, HD):
            part = scores[at, side : side + HD] * factor
            ds[at, side : side + HD] = (part * (gp[at, side : side + HD] - delta)).astype(BF)

    dq[...] = nn(ds[...], k[...])
    for h in range(count):
        part = dq[h * length : (h + 1) * length, :]
        grads[:, h * HD : (h + 1) * HD] = unrope(part, cosine, sine).astype(BF)
    dk = nn(q[...].T, ds[...]).T
    grads[:, ne : ne + HD] = unrope(dk, cosine, sine).astype(BF)
    grads[:, ne + HD :] = nn(ghs[...].T, low[...]).T.astype(BF)
    unit = (back.astype(F32) * inv[:, :1]).astype(BF)
    half = rank // 2
    core = lax.axis_index("dp") & 1
    mine = pl.ds(pl.multiple_of(core * half, half), half)
    theirs = pl.ds(pl.multiple_of((1 - core) * half, half), half)
    inner[...] = nn(unit.T, grads[...]).astype(BF)
    inner_ref[:half, :] = inner[mine, :]
    inner_ref[half:, :] = inner[theirs, :]
    out_inner[...] = nn(up.T, heads[...]).astype(BF)
    out_keep_ref[...] = out_inner[mine, :]
    out_give_ref[...] = out_inner[theirs, :]
    x_ref[...] = nt(grads[...], m_ref[:rank, :]).astype(BF)


def backward(back, loss, sent, m2, o2, inv, cosine, sine):
    length, rank = back.shape
    ne = o2.shape[0]
    total = m2.shape[1]
    assert total == ne + 2 * HD
    stack = ne // HD * length
    return pl.pallas_call(
        backward_kernel,
        in_specs=vmem(8),
        out_specs=vmem(4),
        out_shape=[
            jax.ShapeDtypeStruct((rank, total), BF),
            jax.ShapeDtypeStruct((rank // 2, ne), BF),
            jax.ShapeDtypeStruct((rank // 2, ne), BF),
            jax.ShapeDtypeStruct((length, rank), BF),
        ],
        scratch_shapes=[
            pltpu.VMEM((stack, HD), BF),
            pltpu.VMEM((length, HD), BF),
            pltpu.VMEM((length, 2 * HD), BF),
            pltpu.VMEM((stack, HD), BF),
            pltpu.VMEM((stack, HD), BF),
            pltpu.VMEM((stack, length), F32),
            pltpu.VMEM((stack, length), BF),
            pltpu.VMEM((stack, 2 * HD), F32),
            pltpu.VMEM((stack, length), F32),
            pltpu.VMEM((stack, length), BF),
            pltpu.VMEM((stack, HD), F32),
            pltpu.VMEM((length, ne), BF),
            pltpu.VMEM((length, total), BF),
            pltpu.VMEM((rank, total), BF),
            pltpu.VMEM((rank, ne), BF),
        ],
        compiler_params=pltpu.CompilerParams(vmem_limit_bytes=VMEM_BYTES),
        cost_estimate=cost(10**4, 10**3),
        name="attention_backward",
    )(back, loss, sent, m2, o2, inv, cosine, sine)


def bases_kernel(
    back_ref, loss_ref, returned_ref, new_ref, arrived_ref, u_ref, turned_ref, inv_ref, after,
    base_ref, unit_ref, fbase_ref, g_ref,
):
    rank = u_ref.shape[1]
    for i, piece in enumerate(split(nn(turned_ref[...], u_ref[...]), 3)):
        g_ref[i * rank : (i + 1) * rank, :] = piece
    is_last = lax.axis_index("pipe") == lax.axis_size("pipe") - 1
    is_first = lax.axis_index("pipe") == 0
    up = jnp.where(is_last, loss_ref[...], returned_ref[...])
    coeffs = jnp.where(is_first, new_ref[...], arrived_ref[...])
    base_ref[...] = nn(jnp.concatenate([up] * 3, axis=1), g_ref[...])
    fbase_ref[...] = nn(jnp.concatenate([coeffs] * 3, axis=1), g_ref[...])
    unit_ref[...] = nn(jnp.concatenate([back_ref[...]] * 3, axis=1), g_ref[...]) * inv_ref[:, :1]


def bases(back, loss, returned, new, arrived, basis, turned, inv, after):
    length, rank = back.shape
    return pl.pallas_call(
        bases_kernel,
        in_specs=vmem(8) + [pl.BlockSpec(memory_space=pl.ANY)],
        out_specs=vmem(3),
        out_shape=[jax.ShapeDtypeStruct((length, rank), F32)] * 3,
        scratch_shapes=[pltpu.VMEM((3 * rank, rank), BF)],
        compiler_params=pltpu.CompilerParams(vmem_limit_bytes=VMEM_BYTES // 2),
        cost_estimate=cost(10**4, 10**3),
        name="encoded_again",
    )(back, loss, returned, new, arrived, basis, turned, inv, after)


def scores_kernel(
    new_ref, sent_ref, turned_ref, m_ref, cos_ref, sin_ref, after,
    low_ref, v1_ref, q, k, scores,
):
    length, rank = new_ref.shape
    wide = turned_ref.shape[1]
    is_first = lax.axis_index("pipe") == 0
    coeffs = jnp.where(is_first, new_ref[...], sent_ref[...])
    square = jnp.zeros((length, HD), F32)
    for at in range(0, wide, PIECE):
        decoded = nn(coeffs, turned_ref[:, at : at + PIECE])
        for side in range(0, PIECE, HD):
            part = decoded[:, side : side + HD]
            square = square + part * part
    inv = inverse_root(jnp.sum(square, axis=1, keepdims=True), wide)
    project_heads(coeffs, inv, m_ref, cos_ref[...], sin_ref[...], q, k, v1_ref)
    scores[...] = nt(q[...], k[...])
    exps_of(scores, None, low_ref, length)


def forward_scores(new, sent, turned, m2, cosine, sine, count, after):
    length, rank = new.shape
    stack = count * length
    return pl.pallas_call(
        scores_kernel,
        in_specs=vmem(6) + [pl.BlockSpec(memory_space=pl.ANY)],
        out_specs=vmem(2),
        out_shape=[
            jax.ShapeDtypeStruct((stack, length), BF),
            jax.ShapeDtypeStruct((length, 2 * HD), BF),
        ],
        scratch_shapes=[
            pltpu.VMEM((stack, HD), BF),
            pltpu.VMEM((length, HD), BF),
            pltpu.VMEM((stack, length), F32),
        ],
        compiler_params=pltpu.CompilerParams(vmem_limit_bytes=VMEM_BYTES),
        cost_estimate=cost(10**4, 10**3),
        name="forward_scores",
    )(new, sent, turned, m2, cosine, sine, after)


def output_kernel(low_ref, v1_ref, o_ref, after, y_ref, mixed, heads):
    length = v1_ref.shape[0]
    mixed[...] = nn(low_ref[...], v1_ref[...])
    for h in range(heads.shape[1] // HD):
        at = slice(h * length, (h + 1) * length)
        heads[:, h * HD : (h + 1) * HD] = (mixed[at, :HD] / mixed[at, HD:]).astype(BF)
    y_ref[:length, :] = nn(heads[...], o_ref[...]).astype(BF)
    y_ref[length:, :] = jnp.zeros_like(y_ref[length:, :])


def forward_output(low, v1, o2, after):
    length = v1.shape[0]
    ne, rank = o2.shape
    return pl.pallas_call(
        output_kernel,
        in_specs=vmem(3) + [pl.BlockSpec(memory_space=pl.ANY)],
        out_specs=pl.BlockSpec(memory_space=pltpu.VMEM),
        out_shape=jax.ShapeDtypeStruct((length + 32, rank), BF),
        scratch_shapes=[
            pltpu.VMEM((low.shape[0], 2 * HD), F32),
            pltpu.VMEM((length, ne), BF),
        ],
        compiler_params=pltpu.CompilerParams(vmem_limit_bytes=VMEM_BYTES),
        cost_estimate=cost(10**4, 10**3),
        name="forward_output",
    )(low, v1, o2, after)


def write_split(ref, value):
    high, low = split(value, 2)
    both = jnp.concatenate([high.astype(F32), low.astype(F32)], axis=0)
    ref[ref.shape[0] - 16 :, :] = both.astype(BF)


def read_split(ref):
    both = ref[ref.shape[0] - 16 :, :].astype(F32)
    return both[:8] + both[8:]


def gain_kernel(
    u_ref, wq_ref, narrow_ref, inner_ref, got_ref, x_ref, after,
    pair_ref, out_ref, turned, rows_f32,
):
    nq = wq_ref.shape[1]
    rows = u_ref.shape[0] // 2
    rank = u_ref.shape[1]
    half = inner_ref.shape[0] // 2
    core = lax.axis_index("dp") & 1
    mine = add_wide(inner_ref[:half, :], got_ref[half:, :]).astype(BF)
    theirs = add_wide(inner_ref[half:, :], got_ref[:half, :]).astype(BF)
    pair_ref[...] = mine
    out_ref[: x_ref.shape[0], :] = x_ref[...]
    turned[:, pl.ds(pl.multiple_of(core * half, half), half)] = mine.T
    turned[:, pl.ds(pl.multiple_of((1 - core) * half, half), half)] = theirs.T
    for at in range(0, rows, CHUNK):
        place = pl.ds(pl.multiple_of(core * rows + at, CHUNK), CHUNK)
        against = nn(wq_ref[place, :], turned[:nq, :])
        against += nn(narrow_ref[place, :], turned[nq:, :])
        terms = against * u_ref[place, :].astype(F32)
        folded = sum(terms[:, side : side + HD] for side in range(0, terms.shape[1], HD))
        line = jnp.sum(folded.T, axis=0, keepdims=True)
        for side in range(0, CHUNK, rank):
            row = (at + side) // rank
            rows_f32[row : row + 1, :] = line[:, side : side + rank]
    write_split(out_ref, rows_f32[...])


def gain_part(basis, wq, narrow, inner, got, x, after):
    wide, rank = basis.shape
    assert wide // 2 == 8 * rank
    held = tuple(pltpu.with_memory_space_constraint(a, pltpu.VMEM) for a in (basis, wq, narrow))
    return pl.pallas_call(
        gain_kernel,
        in_specs=vmem(6) + [pl.BlockSpec(memory_space=pl.ANY)],
        out_specs=vmem(2),
        out_shape=[
            jax.ShapeDtypeStruct((rank // 2, inner.shape[1]), BF),
            jax.ShapeDtypeStruct((x.shape[0] + 16, rank), BF),
        ],
        scratch_shapes=[
            pltpu.VMEM((inner.shape[1], rank), BF),
            pltpu.VMEM((8, rank), F32),
        ],
        compiler_params=pltpu.CompilerParams(vmem_limit_bytes=VMEM_BYTES),
        cost_estimate=cost(10**4, 10**3),
        name="pair_sum_and_gain_gradient",
    )(*held, inner, got, x, after)


def merge_kernel(a_ref, b_ref, after, out_ref):
    rest = out_ref.shape[0] - 16
    out_ref[:rest, :] = add_wide(a_ref[:rest, :], b_ref[:rest, :]).astype(BF)
    write_split(out_ref, read_split(a_ref) + read_split(b_ref))


def total_kernel(a_ref, b_ref, after, out_ref):
    out_ref[...] = read_split(a_ref) + read_split(b_ref)


def own_kernel(a_ref, b_ref, after, *out_refs):
    at = 0
    for ref in out_refs:
        size = ref.shape[1]
        ref[...] = add_wide(a_ref[:, at : at + size], b_ref[:, at : at + size]).astype(BF)
        at += size


def small_kernel(kernel, name, out_shape, a, b, after):
    return pl.pallas_call(
        kernel,
        in_specs=vmem(2) + [pl.BlockSpec(memory_space=pl.ANY)],
        out_specs=jax.tree.map(lambda _: pl.BlockSpec(memory_space=pltpu.VMEM), out_shape),
        out_shape=out_shape,
        compiler_params=pltpu.CompilerParams(vmem_limit_bytes=VMEM_BYTES // 2),
        cost_estimate=cost(10**4, 10**3),
        name=name,
    )(a, b, after)


def merge(a, b, after):
    return small_kernel(merge_kernel, "sum_with_gain", jax.ShapeDtypeStruct(a.shape, BF), a, b, after)


def gain_total(a, b, after):
    shape = jax.ShapeDtypeStruct((8, a.shape[1]), F32)
    return small_kernel(total_kernel, "gain_total", shape, a, b, after)


def own_pieces(a, b, sizes, after):
    shapes = [jax.ShapeDtypeStruct((a.shape[0], n), BF) for n in sizes]
    return small_kernel(own_kernel, "sum_over_y", shapes, a, b, after)


def add_kernel(a_ref, b_ref, after, out_ref):
    rows = out_ref.shape[0]
    out_ref[...] = add_wide(a_ref[:rows, :], b_ref[:rows, :]).astype(out_ref.dtype)


def add_after(a, b, after, rows=None):
    shape = jax.ShapeDtypeStruct((rows or a.shape[0], a.shape[1]), a.dtype)
    return small_kernel(add_kernel, "pair_sum", shape, a, b, after)


def gather_halves(own_refs, other_refs, whole):
    half = whole.shape[0] // 2
    core = lax.axis_index("dp") & 1
    at = 0
    for own_ref, other_ref in zip(own_refs, other_refs):
        columns = pl.ds(at, own_ref.shape[1])
        whole[pl.ds(pl.multiple_of(core * half, half), half), columns] = own_ref[...]
        whole[pl.ds(pl.multiple_of((1 - core) * half, half), half), columns] = other_ref[...]
        at += own_ref.shape[1]


def inward_kernel(pieces, u_ref, gain_ref, *refs):
    own_refs, other_refs = refs[:pieces], refs[pieces : 2 * pieces]
    q_ref, k_ref, v_ref, inner = refs[-4:]
    nq, nk = q_ref.shape[1], k_ref.shape[1]
    block = q_ref.shape[0]

    @pl.when(pl.program_id(0) == 0)
    def _():
        gather_halves(own_refs, other_refs, inner)

    step = lax.axis_index("dp") * pl.num_programs(0) + pl.program_id(0)
    rows = pl.ds(pl.multiple_of(step * block, block), block)
    gain = jnp.broadcast_to(gain_ref[:, rows], (HD, block)).T[:, :1]
    grad = nn(u_ref[rows, :], inner[...]) * gain
    q_ref[...] = grad[:, :nq].astype(BF)
    k_ref[...] = grad[:, nq : nq + nk].astype(BF)
    v_ref[...] = grad[:, nq + nk :].astype(BF)


def outward_kernel(pieces, u_ref, *refs):
    own_refs, other_refs = refs[:pieces], refs[pieces : 2 * pieces]
    o_ref, inner = refs[-2:]

    @pl.when(pl.program_id(0) == 0)
    def _():
        gather_halves(own_refs, other_refs, inner)

    block, rows = o_ref.shape
    at = pl.multiple_of(pl.program_id(0) * block, block)
    basis = u_ref[pl.ds(pl.multiple_of(lax.axis_index("dp") * rows, rows), rows), :]
    o_ref[...] = nt(inner[:, pl.ds(at, block)].T, basis).astype(BF)


STEPS = 2


def inward_grads(basis, gain, own, other, sizes, after):
    wide, rank = basis.shape
    rows = wide // lax.axis_size("dp")
    block = rows // STEPS
    return pl.pallas_call(
        functools.partial(inward_kernel, len(own)),
        grid=(STEPS,),
        in_specs=vmem(2 + 2 * len(own)) + [pl.BlockSpec(memory_space=pl.ANY)],
        out_specs=[pl.BlockSpec((block, n), lambda i: (i, 0)) for n in sizes],
        scratch_shapes=[pltpu.VMEM((rank, sum(sizes)), BF)],
        out_shape=[jax.ShapeDtypeStruct((rows, n), BF) for n in sizes],
        compiler_params=pltpu.CompilerParams(vmem_limit_bytes=VMEM_BYTES),
        cost_estimate=cost(10**4, 10**3),
        name="inward_weight_gradients",
    )(basis, gain, *own, *other, after)


def outward_grad(basis, own, other, after):
    wide, rank = basis.shape
    rows = wide // lax.axis_size("dp")
    ne = sum(piece.shape[1] for piece in own)
    return pl.pallas_call(
        functools.partial(outward_kernel, len(own)),
        grid=(STEPS,),
        in_specs=vmem(1 + 2 * len(own)) + [pl.BlockSpec(memory_space=pl.ANY)],
        out_specs=pl.BlockSpec((ne // STEPS, rows), lambda i: (i, 0)),
        scratch_shapes=[pltpu.VMEM((rank, ne), BF)],
        out_shape=jax.ShapeDtypeStruct((ne, rows), BF),
        compiler_params=pltpu.CompilerParams(vmem_limit_bytes=VMEM_BYTES),
        cost_estimate=cost(10**4, 10**3),
        name="output_weight_gradient",
    )(basis, *own, *other, after)


def results_kernel(
    wide, fbase_ref, y_ref, ygot_ref, base_ref, unit_ref, x_ref, xgot_ref, back_ref, inv_ref,
    gain_ref, gain_other_ref, after,
    f_ref, b_ref, gain_out_ref,
):
    f_ref[...] = (fbase_ref[...] + add_wide(y_ref[...], ygot_ref[...])).astype(BF)
    length = back_ref.shape[0]
    x = add_wide(x_ref[:length, :], xgot_ref[:length, :])
    inv = inv_ref[:, :1]
    along = jnp.sum(x * back_ref[...].astype(F32), axis=1, keepdims=True)
    middle = along * inv * (1.0 / wide)
    b_ref[...] = (base_ref[...] + (x - unit_ref[...] * middle) * inv).astype(BF)
    core = lax.axis_index("dp") & 1
    half = wide // 2
    rank = gain_ref.shape[1]
    for row in range(half // rank):
        mine = pl.ds(pl.multiple_of(core * half + row * rank, rank), rank)
        theirs = pl.ds(pl.multiple_of((1 - core) * half + row * rank, rank), rank)
        gain_out_ref[:, mine] = gain_ref[row : row + 1, :]
        gain_out_ref[:, theirs] = gain_other_ref[row : row + 1, :]


def results(wide, after, *operands):
    shape = operands[0].shape
    held = tuple(pltpu.with_memory_space_constraint(a, pltpu.VMEM) for a in operands)
    return pl.pallas_call(
        functools.partial(results_kernel, wide),
        in_specs=vmem(len(operands)) + [pl.BlockSpec(memory_space=pl.ANY)],
        out_specs=vmem(3),
        out_shape=[jax.ShapeDtypeStruct(shape, BF)] * 2 + [jax.ShapeDtypeStruct((1, wide), F32)],
        compiler_params=pltpu.CompilerParams(vmem_limit_bytes=VMEM_BYTES // 2),
        cost_estimate=cost(10**4, 10**3),
        name="section_results",
    )(*held, *in_hbm((after,)))


def body(
    new_coeffs,
    loss_grad,
    sent_forward,
    sent_backward,
    stashed,
    subspace,
    norm_gain,
    w_query,
    w_key,
    w_value,
    w_output,
):
    wide = subspace.shape[0]
    wq, wk, wv, wo = w_query[0], w_key[0], w_value[0], w_output[0]
    nq, nk, nv = wq.shape[1], wk.shape[1], wv.shape[1]
    back = stashed[0]
    arrived, returned = cross_pipe(sent_forward[0], sent_backward[0])
    cosine, sine = rope_tables(back.shape[0])

    m2, o2, inv, basis, wq, narrow, turned = project(
        back, norm_gain, subspace, wq, wk, wv, wo
    )
    inner, out_give, out_keep, x = backward(
        back, loss_grad, returned, m2, o2, inv, cosine, sine
    )
    out_got = swap(out_give, "dp", 1)
    inner_got = swap(inner, "dp", 1)
    low, values = forward_scores(
        new_coeffs, arrived, turned, m2, cosine, sine, wo.shape[0] // HD, out_keep
    )
    out_pair = add_after(out_keep, out_got, values)
    out_got = swap(out_pair, "dp", 2)
    pair, x = gain_part(basis, wq, narrow, inner, inner_got, x, out_pair)
    pair_got = swap(pair, "dp", 2)
    x_got = swap(x, "tensor", 2)
    y = forward_output(low, values, o2, pair)
    y_got = swap(y, "tensor", 2)
    ne = wo.shape[0]
    out_own = own_pieces(out_pair, out_got, (ne // 2, ne - ne // 2), y)
    out_other = [swap(piece, "dp", 1) for piece in out_own]
    grad_o = outward_grad(basis, out_own, out_other, y)
    x = merge(x, x_got, *in_hbm((grad_o,)))
    x_got = swap(x, "tensor", 1)
    own = own_pieces(pair, pair_got, (nq // 2, nq - nq // 2, nk + nv), x)
    other = [swap(piece, "dp", 1) for piece in own]
    base, unit, fbase = bases(
        back, loss_grad, returned, new_coeffs, arrived, basis, turned, inv, own[0]
    )
    gain = gain_total(x, x_got, base)
    gain_got = swap(gain, "dp", 2)
    y = add_after(y, y_got, gain, rows=back.shape[0])
    y_got = swap(y, "tensor", 1)
    grad_q, grad_k, grad_v = inward_grads(basis, norm_gain, own, other, (nq, nk, nv), y)
    gain = add_after(gain, gain_got, *in_hbm((grad_v,)))
    gain_other = swap(gain, "dp", 1)
    forward_out, backward_out, grad_gain = results(
        wide, grad_v, fbase, y, y_got, base, unit, x, x_got, back, inv, gain, gain_other
    )
    return (
        forward_out[None],
        backward_out[None],
        grad_q[None],
        grad_k[None],
        grad_v[None],
        grad_o[None],
        grad_gain,
    )


def solution(mesh):
    return jax.shard_map(
        body,
        mesh=mesh,
        in_specs=(
            P("dp", None),
            P("dp", None),
            P("pipe", "dp", None),
            P("pipe", "dp", None),
            P("pipe", "dp", None),
            P(),
            P("pipe", None),
            P("pipe", None, "tensor"),
            P("pipe", None, "tensor"),
            P("pipe", None, "tensor"),
            P("pipe", "tensor", None),
        ),
        out_specs=(
            P("pipe", "dp", None),
            P("pipe", "dp", None),
            P("pipe", "dp", "tensor"),
            P("pipe", "dp", "tensor"),
            P("pipe", "dp", "tensor"),
            P("pipe", "tensor", "dp"),
            P("pipe", None),
        ),
        check_vma=False,
    )
```

```python
import functools
import math

import jax
import jax.numpy as jnp
import numpy as np
from jax import lax
from jax.experimental import pallas as pl
from jax.experimental.pallas import tpu as pltpu
from jax.sharding import PartitionSpec as P

HD = 128
EPSILON = 1e-05
ROPE_BASE = 500000.0
BF = jnp.bfloat16
F32 = jnp.float32
VMEM_BYTES = 24 * 1024 * 1024
CHUNK = 512
PIECE = 1024
AHEAD = 3
LOG2E = 1.4426950408889634


def shifted(x, axis, by):
    devices = lax.axis_size(axis)
    pairs = [(i, i + by) for i in range(devices) if 0 <= i + by < devices]
    return lax.ppermute(x, axis, pairs)


def swap(x, axis, bit):
    devices = lax.axis_size(axis)
    return lax.ppermute(x, axis, [(i, i ^ bit) for i in range(devices)])


def cross_pipe(sent_forward, sent_backward):
    if lax.axis_size("pipe") != 2:
        return shifted(sent_forward, "pipe", 1), shifted(sent_backward, "pipe", -1)
    first = lax.axis_index("pipe") == 0
    got = swap(jnp.where(first, sent_forward, sent_backward), "pipe", 1)
    return got, got


def add_wide(a, b):
    return a.astype(F32) + b.astype(F32)


def nt(a, b):
    return lax.dot_general(a, b, (((1,), (1,)), ((), ())), preferred_element_type=F32)


def nn(a, b):
    return jnp.dot(a, b, preferred_element_type=F32)


def split(x, parts):
    out = []
    for _ in range(parts):
        piece = x.astype(BF)
        out.append(piece)
        x = x - piece.astype(F32)
    return out


def rope_tables(length):
    half = HD // 2
    frequency = np.float32(ROPE_BASE) ** (-2.0 * np.arange(half, dtype=np.float32) / HD)
    angles = np.arange(length, dtype=np.float32)[:, None] * frequency.astype(np.float32)
    cosine, sine = np.cos(angles), np.sin(angles)
    tables = (np.concatenate([cosine, cosine], 1), np.concatenate([-sine, sine], 1))
    return tuple(jnp.asarray(t, dtype=F32) for t in tables)


def rope(x, cosine, sine):
    return x * cosine + pltpu.roll(x, HD // 2, 1) * sine


def unrope(x, cosine, sine):
    return x * cosine - pltpu.roll(x, HD // 2, 1) * sine


def inverse_root(square_sum, width):
    return 1.0 / jnp.sqrt(square_sum / width + EPSILON)


def vmem(count):
    return [pl.BlockSpec(memory_space=pltpu.VMEM)] * count


def in_hbm(arrays):
    return tuple(pltpu.with_memory_space_constraint(a, pltpu.HBM) for a in arrays)


def cost(flops, num_bytes, exps=0):
    return pl.CostEstimate(flops=flops, bytes_accessed=num_bytes, transcendentals=exps)


def project_kernel(
    back_hbm, gain_hbm, u_hbm, wq_hbm, wk_hbm, wv_hbm, wo_hbm,
    m_ref, o_ref, inv_ref, u, wq, narrow, turned,
    back, gain, wo, scaled, m_acc, o_acc, sems,
):
    wide, rank = u.shape
    nq = wq.shape[1]
    nk = wk_hbm.shape[1]
    parts = wide // PIECE
    pieces = [pl.ds(i * PIECE, PIECE) for i in range(parts)]
    pairs = [(back_hbm, back), (gain_hbm, gain)]
    pairs += [(u_hbm.at[at, :], u.at[at, :]) for at in pieces]
    pairs += [(wo_hbm.at[:, at], wo.at[:, at]) for at in pieces]
    pairs += [(wq_hbm.at[at, :], wq.at[at, :]) for at in pieces[:2]]
    pairs += [(wk_hbm, narrow.at[:, pl.ds(0, nk)])]
    pairs += [(wv_hbm, narrow.at[:, pl.ds(nk, narrow.shape[1] - nk)])]
    pairs += [(wq_hbm.at[at, :], wq.at[at, :]) for at in pieces[2:]]
    copies = [
        pltpu.make_async_copy(source, target, sems.at[n])
        for n, (source, target) in enumerate(pairs)
    ]
    started = 0

    def start_to(count):
        nonlocal started
        for copy in copies[started:count]:
            copy.start()
        started = max(started, min(count, len(copies)))

    def wait(n):
        start_to(n + 1 + AHEAD)
        copies[n].wait()

    start_to(2 + parts + AHEAD)
    copies[0].wait()
    copies[1].wait()
    squares = [jnp.zeros((back.shape[0], HD), F32)]

    def decode(i):
        at = pieces[i]
        copies[2 + i].wait()
        turned[:, at] = u[at, :].T
        scaled[:, at] = (turned[:, at].astype(F32) * gain[:, at]).astype(BF)
        decoded = nn(back[...], turned[:, at])
        for side in range(0, PIECE, HD):
            part = decoded[:, side : side + HD]
            squares[0] = squares[0] + part * part

    decode(0)
    place = 2 + parts
    for i, at in enumerate(pieces):
        wait(place)
        place += 1
        if i + 1 < parts:
            decode(i + 1)
        part = nn(wo[:, at], u[at, :])
        if i == 0:
            o_acc[...] = part
        elif i + 1 < parts:
            o_acc[...] += part
        else:
            o_ref[...] = (o_acc[...] + part).astype(BF)
    inv_ref[...] = jnp.broadcast_to(
        inverse_root(jnp.sum(squares[0], axis=1, keepdims=True), wide), inv_ref.shape
    )
    for i, at in enumerate(pieces):
        if i == 2:
            wait(place)
            wait(place + 1)
            place += 2
            for p, piece in enumerate(split(nn(scaled[...], narrow[...]), 2)):
                m_ref[p * rank : (p + 1) * rank, nq:] = piece
        wait(place)
        place += 1
        part = nn(scaled[:, at], wq[at, :])
        if i == 0:
            m_acc[...] = part
        elif i + 1 < parts:
            m_acc[...] += part
        else:
            for p, piece in enumerate(split(m_acc[...] + part, 2)):
                m_ref[p * rank : (p + 1) * rank, :nq] = piece


def project(back, gain, basis, wq, wk, wv, wo):
    wide, rank = basis.shape
    length = back.shape[0]
    ne = wo.shape[0]
    nq = wq.shape[1]
    rest = wk.shape[1] + wv.shape[1]
    operands = in_hbm((back, gain, basis, wq, wk, wv, wo))
    return pl.pallas_call(
        project_kernel,
        in_specs=[pl.BlockSpec(memory_space=pltpu.HBM)] * len(operands),
        out_specs=vmem(7),
        out_shape=[
            jax.ShapeDtypeStruct((2 * rank, nq + rest), BF),
            jax.ShapeDtypeStruct((ne, rank), BF),
            jax.ShapeDtypeStruct((length, HD), F32),
            jax.ShapeDtypeStruct(basis.shape, BF),
            jax.ShapeDtypeStruct(wq.shape, BF),
            jax.ShapeDtypeStruct((wide, rest), BF),
            jax.ShapeDtypeStruct((rank, wide), BF),
        ],
        scratch_shapes=[
            pltpu.VMEM(back.shape, BF),
            pltpu.VMEM(gain.shape, F32),
            pltpu.VMEM(wo.shape, BF),
            pltpu.VMEM((rank, wide), BF),
            pltpu.VMEM((rank, nq), F32),
            pltpu.VMEM((ne, rank), F32),
            pltpu.SemaphoreType.DMA((4 + 3 * (wide // PIECE),)),
        ],
        compiler_params=pltpu.CompilerParams(vmem_limit_bytes=VMEM_BYTES * 3 // 2),
        cost_estimate=cost(6 * 10**9, 20 * 10**6),
        name="project_weights",
    )(*operands)


def project_heads(coeffs, inv, m_ref, cosine, sine, q, k, v1):
    length = coeffs.shape[0]
    heads = q.shape[0] // length
    twice = jnp.concatenate([coeffs, coeffs], axis=1)
    for h in range(0, heads, 2):
        both = nn(twice, m_ref[:, h * HD : (h + 2) * HD]) * inv
        for part, at in ((both[:, :HD], h * length), (both[:, HD:], (h + 1) * length)):
            q[at : at + length, :] = rope(part, cosine, sine).astype(BF)
    part = nn(twice, m_ref[:, heads * HD :]) * inv
    k[...] = rope(part[:, :HD], cosine, sine).astype(BF)
    v1[:, :HD] = part[:, HD:].astype(BF)
    v1[:, HD:] = jnp.ones_like(v1[:, HD:])


def exps_of(scores, exps, low, length):
    row = lax.broadcasted_iota(jnp.int32, (length, length), 0)
    column = lax.broadcasted_iota(jnp.int32, (length, length), 1)
    causal = row >= column

    def one(h, _):
        at = pl.ds(pl.multiple_of(h * length, length), length)
        s = jnp.where(causal, scores[at, :], -jnp.inf)
        top = jnp.max(s, axis=1, keepdims=True)
        e = jnp.exp2((s - top) * (LOG2E / math.sqrt(HD)))
        if exps is not None:
            exps[at, :] = e
        low[at, :] = e.astype(BF)
        return 0

    lax.fori_loop(0, scores.shape[0] // length, one, 0, unroll=2)


def backward_kernel(
    back_ref, loss_ref, sent_ref, m_ref, o_ref, inv_ref, cos_ref, sin_ref,
    inner_ref, out_give_ref, out_keep_ref, x_ref,
    q, k, v1, gh, ghs, scores, low, mixed, gp, ds, dq, heads, grads, inner, out_inner,
):
    length, rank = back_ref.shape
    ne = o_ref.shape[0]
    count = ne // HD
    scale = 1.0 / math.sqrt(HD)
    last = lax.axis_size("pipe") - 1
    is_last = lax.axis_index("pipe") == last
    back = back_ref[...]
    up = jnp.where(is_last, loss_ref[...], sent_ref[...])
    cosine, sine = cos_ref[...], sin_ref[...]
    inv = inv_ref[...]
    project_heads(back, inv[:, :1], m_ref, cosine, sine, q, k, v1)
    scores[...] = nt(q[...], k[...])
    for h in range(0, count, 2):
        both = nt(up, o_ref[h * HD : (h + 2) * HD, :]).astype(BF)
        gh[h * length : (h + 1) * length, :] = both[:, :HD]
        gh[(h + 1) * length : (h + 2) * length, :] = both[:, HD:]
    exps_of(scores, scores, low, length)
    mixed[...] = nn(low[...], v1[...])
    gp[...] = nt(gh[...], v1[:, :HD])

    for h in range(count):
        at = slice(h * length, (h + 1) * length)
        inverse = 1.0 / mixed[at, HD:]
        out = mixed[at, :HD] * inverse
        heads[:, h * HD : (h + 1) * HD] = out.astype(BF)
        grad = gh[at, :].astype(F32)
        ghs[at, :] = (grad * inverse).astype(BF)
        delta = jnp.sum(grad * out, axis=1, keepdims=True)
        factor = inverse * scale
        for side in range(0, length, HD):
            part = scores[at, side : side + HD] * factor
            ds[at, side : side + HD] = (part * (gp[at, side : side + HD] - delta)).astype(BF)

    dq[...] = nn(ds[...], k[...])
    for h in range(count):
        part = dq[h * length : (h + 1) * length, :]
        grads[:, h * HD : (h + 1) * HD] = unrope(part, cosine, sine).astype(BF)
    dk = nn(q[...].T, ds[...]).T
    grads[:, ne : ne + HD] = unrope(dk, cosine, sine).astype(BF)
    grads[:, ne + HD :] = nn(ghs[...].T, low[...]).T.astype(BF)
    unit = (back.astype(F32) * inv[:, :1]).astype(BF)
    half = rank // 2
    core = lax.axis_index("dp") & 1
    mine = pl.ds(pl.multiple_of(core * half, half), half)
    theirs = pl.ds(pl.multiple_of((1 - core) * half, half), half)
    inner[...] = nn(unit.T, grads[...]).astype(BF)
    inner_ref[:half, :] = inner[mine, :]
    inner_ref[half:, :] = inner[theirs, :]
    out_inner[...] = nn(up.T, heads[...]).astype(BF)
    out_keep_ref[...] = out_inner[mine, :]
    out_give_ref[...] = out_inner[theirs, :]
    x_ref[...] = nt(grads[...], m_ref[:rank, :]).astype(BF)


def backward(back, loss, sent, m2, o2, inv, cosine, sine):
    length, rank = back.shape
    ne = o2.shape[0]
    total = m2.shape[1]
    assert total == ne + 2 * HD
    stack = ne // HD * length
    return pl.pallas_call(
        backward_kernel,
        in_specs=vmem(8),
        out_specs=vmem(4),
        out_shape=[
            jax.ShapeDtypeStruct((rank, total), BF),
            jax.ShapeDtypeStruct((rank // 2, ne), BF),
            jax.ShapeDtypeStruct((rank // 2, ne), BF),
            jax.ShapeDtypeStruct((length, rank), BF),
        ],
        scratch_shapes=[
            pltpu.VMEM((stack, HD), BF),
            pltpu.VMEM((length, HD), BF),
            pltpu.VMEM((length, 2 * HD), BF),
            pltpu.VMEM((stack, HD), BF),
            pltpu.VMEM((stack, HD), BF),
            pltpu.VMEM((stack, length), F32),
            pltpu.VMEM((stack, length), BF),
            pltpu.VMEM((stack, 2 * HD), F32),
            pltpu.VMEM((stack, length), F32),
            pltpu.VMEM((stack, length), BF),
            pltpu.VMEM((stack, HD), F32),
            pltpu.VMEM((length, ne), BF),
            pltpu.VMEM((length, total), BF),
            pltpu.VMEM((rank, total), BF),
            pltpu.VMEM((rank, ne), BF),
        ],
        compiler_params=pltpu.CompilerParams(vmem_limit_bytes=VMEM_BYTES),
        cost_estimate=cost(10**4, 10**3),
        name="attention_backward",
    )(back, loss, sent, m2, o2, inv, cosine, sine)


def bases_kernel(
    back_ref, loss_ref, returned_ref, new_ref, arrived_ref, u_ref, turned_ref, inv_ref, after,
    base_ref, unit_ref, fbase_ref, g_ref,
):
    rank = u_ref.shape[1]
    for i, piece in enumerate(split(nn(turned_ref[...], u_ref[...]), 3)):
        g_ref[i * rank : (i + 1) * rank, :] = piece
    is_last = lax.axis_index("pipe") == lax.axis_size("pipe") - 1
    is_first = lax.axis_index("pipe") == 0
    up = jnp.where(is_last, loss_ref[...], returned_ref[...])
    coeffs = jnp.where(is_first, new_ref[...], arrived_ref[...])
    base_ref[...] = nn(jnp.concatenate([up] * 3, axis=1), g_ref[...])
    fbase_ref[...] = nn(jnp.concatenate([coeffs] * 3, axis=1), g_ref[...])
    unit_ref[...] = nn(jnp.concatenate([back_ref[...]] * 3, axis=1), g_ref[...]) * inv_ref[:, :1]


def bases(back, loss, returned, new, arrived, basis, turned, inv, after):
    length, rank = back.shape
    return pl.pallas_call(
        bases_kernel,
        in_specs=vmem(8) + [pl.BlockSpec(memory_space=pl.ANY)],
        out_specs=vmem(3),
        out_shape=[jax.ShapeDtypeStruct((length, rank), F32)] * 3,
        scratch_shapes=[pltpu.VMEM((3 * rank, rank), BF)],
        compiler_params=pltpu.CompilerParams(vmem_limit_bytes=VMEM_BYTES // 2),
        cost_estimate=cost(10**4, 10**3),
        name="encoded_again",
    )(back, loss, returned, new, arrived, basis, turned, inv, after)


def forward_kernel(
    new_ref, sent_ref, turned_ref, m_ref, o_ref, cos_ref, sin_ref, after,
    y_ref, q, k, v1, scores, low, mixed, heads,
):
    length, rank = new_ref.shape
    wide = turned_ref.shape[1]
    is_first = lax.axis_index("pipe") == 0
    coeffs = jnp.where(is_first, new_ref[...], sent_ref[...])
    square = jnp.zeros((length, HD), F32)
    for at in range(0, wide, PIECE):
        decoded = nn(coeffs, turned_ref[:, at : at + PIECE])
        for side in range(0, PIECE, HD):
            part = decoded[:, side : side + HD]
            square = square + part * part
    inv = inverse_root(jnp.sum(square, axis=1, keepdims=True), wide)
    project_heads(coeffs, inv, m_ref, cos_ref[...], sin_ref[...], q, k, v1)
    scores[...] = nt(q[...], k[...])
    exps_of(scores, None, low, length)
    mixed[...] = nn(low[...], v1[...])
    for h in range(heads.shape[1] // HD):
        at = slice(h * length, (h + 1) * length)
        heads[:, h * HD : (h + 1) * HD] = (mixed[at, :HD] / mixed[at, HD:]).astype(BF)
    y_ref[:length, :] = nn(heads[...], o_ref[...]).astype(BF)
    y_ref[length:, :] = jnp.zeros_like(y_ref[length:, :])


def forward(new, sent, turned, m2, o2, cosine, sine, after):
    length, rank = new.shape
    ne = o2.shape[0]
    stack = ne // HD * length
    return pl.pallas_call(
        forward_kernel,
        in_specs=vmem(7) + [pl.BlockSpec(memory_space=pl.ANY)],
        out_specs=pl.BlockSpec(memory_space=pltpu.VMEM),
        out_shape=jax.ShapeDtypeStruct((length + 32, rank), BF),
        scratch_shapes=[
            pltpu.VMEM((stack, HD), BF),
            pltpu.VMEM((length, HD), BF),
            pltpu.VMEM((length, 2 * HD), BF),
            pltpu.VMEM((stack, length), F32),
            pltpu.VMEM((stack, length), BF),
            pltpu.VMEM((stack, 2 * HD), F32),
            pltpu.VMEM((length, ne), BF),
        ],
        compiler_params=pltpu.CompilerParams(vmem_limit_bytes=VMEM_BYTES),
        cost_estimate=cost(10**4, 10**3),
        name="attention_forward",
    )(new, sent, turned, m2, o2, cosine, sine, after)


def write_split(ref, value):
    high, low = split(value, 2)
    both = jnp.concatenate([high.astype(F32), low.astype(F32)], axis=0)
    ref[ref.shape[0] - 16 :, :] = both.astype(BF)


def read_split(ref):
    both = ref[ref.shape[0] - 16 :, :].astype(F32)
    return both[:8] + both[8:]


def gain_kernel(
    u_ref, wq_ref, narrow_ref, inner_ref, got_ref, x_ref, after,
    pair_ref, out_ref, turned, rows_f32,
):
    nq = wq_ref.shape[1]
    rows = u_ref.shape[0] // 2
    rank = u_ref.shape[1]
    half = inner_ref.shape[0] // 2
    core = lax.axis_index("dp") & 1
    mine = add_wide(inner_ref[:half, :], got_ref[half:, :]).astype(BF)
    theirs = add_wide(inner_ref[half:, :], got_ref[:half, :]).astype(BF)
    pair_ref[...] = mine
    out_ref[: x_ref.shape[0], :] = x_ref[...]
    turned[:, pl.ds(pl.multiple_of(core * half, half), half)] = mine.T
    turned[:, pl.ds(pl.multiple_of((1 - core) * half, half), half)] = theirs.T
    for at in range(0, rows, CHUNK):
        place = pl.ds(pl.multiple_of(core * rows + at, CHUNK), CHUNK)
        against = nn(wq_ref[place, :], turned[:nq, :])
        against += nn(narrow_ref[place, :], turned[nq:, :])
        terms = against * u_ref[place, :].astype(F32)
        folded = sum(terms[:, side : side + HD] for side in range(0, terms.shape[1], HD))
        line = jnp.sum(folded.T, axis=0, keepdims=True)
        for side in range(0, CHUNK, rank):
            row = (at + side) // rank
            rows_f32[row : row + 1, :] = line[:, side : side + rank]
    write_split(out_ref, rows_f32[...])


def gain_part(basis, wq, narrow, inner, got, x, after):
    wide, rank = basis.shape
    assert wide // 2 == 8 * rank
    held = tuple(pltpu.with_memory_space_constraint(a, pltpu.VMEM) for a in (basis, wq, narrow))
    return pl.pallas_call(
        gain_kernel,
        in_specs=vmem(6) + [pl.BlockSpec(memory_space=pl.ANY)],
        out_specs=vmem(2),
        out_shape=[
            jax.ShapeDtypeStruct((rank // 2, inner.shape[1]), BF),
            jax.ShapeDtypeStruct((x.shape[0] + 16, rank), BF),
        ],
        scratch_shapes=[
            pltpu.VMEM((inner.shape[1], rank), BF),
            pltpu.VMEM((8, rank), F32),
        ],
        compiler_params=pltpu.CompilerParams(vmem_limit_bytes=VMEM_BYTES),
        cost_estimate=cost(10**4, 10**3),
        name="pair_sum_and_gain_gradient",
    )(*held, inner, got, x, after)


def merge_kernel(a_ref, b_ref, after, out_ref):
    rest = out_ref.shape[0] - 16
    out_ref[:rest, :] = add_wide(a_ref[:rest, :], b_ref[:rest, :]).astype(BF)
    write_split(out_ref, read_split(a_ref) + read_split(b_ref))


def total_kernel(a_ref, b_ref, after, out_ref):
    out_ref[...] = read_split(a_ref) + read_split(b_ref)


def own_kernel(a_ref, b_ref, after, *out_refs):
    at = 0
    for ref in out_refs:
        size = ref.shape[1]
        ref[...] = add_wide(a_ref[:, at : at + size], b_ref[:, at : at + size]).astype(BF)
        at += size


def small_kernel(kernel, name, out_shape, a, b, after):
    return pl.pallas_call(
        kernel,
        in_specs=vmem(2) + [pl.BlockSpec(memory_space=pl.ANY)],
        out_specs=jax.tree.map(lambda _: pl.BlockSpec(memory_space=pltpu.VMEM), out_shape),
        out_shape=out_shape,
        compiler_params=pltpu.CompilerParams(vmem_limit_bytes=VMEM_BYTES // 2),
        cost_estimate=cost(10**4, 10**3),
        name=name,
    )(a, b, after)


def merge(a, b, after):
    return small_kernel(merge_kernel, "sum_with_gain", jax.ShapeDtypeStruct(a.shape, BF), a, b, after)


def gain_total(a, b, after):
    shape = jax.ShapeDtypeStruct((8, a.shape[1]), F32)
    return small_kernel(total_kernel, "gain_total", shape, a, b, after)


def own_pieces(a, b, sizes, after):
    shapes = [jax.ShapeDtypeStruct((a.shape[0], n), BF) for n in sizes]
    return small_kernel(own_kernel, "sum_over_y", shapes, a, b, after)


def add_kernel(a_ref, b_ref, after, out_ref):
    rows = out_ref.shape[0]
    out_ref[...] = add_wide(a_ref[:rows, :], b_ref[:rows, :]).astype(out_ref.dtype)


def add_after(a, b, after, rows=None):
    shape = jax.ShapeDtypeStruct((rows or a.shape[0], a.shape[1]), a.dtype)
    return small_kernel(add_kernel, "pair_sum", shape, a, b, after)


def gather_halves(own_refs, other_refs, whole):
    half = whole.shape[0] // 2
    core = lax.axis_index("dp") & 1
    at = 0
    for own_ref, other_ref in zip(own_refs, other_refs):
        columns = pl.ds(at, own_ref.shape[1])
        whole[pl.ds(pl.multiple_of(core * half, half), half), columns] = own_ref[...]
        whole[pl.ds(pl.multiple_of((1 - core) * half, half), half), columns] = other_ref[...]
        at += own_ref.shape[1]


def inward_kernel(pieces, u_ref, gain_ref, *refs):
    own_refs, other_refs = refs[:pieces], refs[pieces : 2 * pieces]
    q_ref, k_ref, v_ref, inner = refs[-4:]
    nq, nk = q_ref.shape[1], k_ref.shape[1]
    block = q_ref.shape[0]

    @pl.when(pl.program_id(0) == 0)
    def _():
        gather_halves(own_refs, other_refs, inner)

    step = lax.axis_index("dp") * pl.num_programs(0) + pl.program_id(0)
    rows = pl.ds(pl.multiple_of(step * block, block), block)
    gain = jnp.broadcast_to(gain_ref[:, rows], (HD, block)).T[:, :1]
    grad = nn(u_ref[rows, :], inner[...]) * gain
    q_ref[...] = grad[:, :nq].astype(BF)
    k_ref[...] = grad[:, nq : nq + nk].astype(BF)
    v_ref[...] = grad[:, nq + nk :].astype(BF)


def outward_kernel(pieces, u_ref, *refs):
    own_refs, other_refs = refs[:pieces], refs[pieces : 2 * pieces]
    o_ref, inner = refs[-2:]

    @pl.when(pl.program_id(0) == 0)
    def _():
        gather_halves(own_refs, other_refs, inner)

    block, rows = o_ref.shape
    at = pl.multiple_of(pl.program_id(0) * block, block)
    basis = u_ref[pl.ds(pl.multiple_of(lax.axis_index("dp") * rows, rows), rows), :]
    o_ref[...] = nt(inner[:, pl.ds(at, block)].T, basis).astype(BF)


STEPS = 2


def inward_grads(basis, gain, own, other, sizes, after):
    wide, rank = basis.shape
    rows = wide // lax.axis_size("dp")
    block = rows // STEPS
    return pl.pallas_call(
        functools.partial(inward_kernel, len(own)),
        grid=(STEPS,),
        in_specs=vmem(2 + 2 * len(own)) + [pl.BlockSpec(memory_space=pl.ANY)],
        out_specs=[pl.BlockSpec((block, n), lambda i: (i, 0)) for n in sizes],
        scratch_shapes=[pltpu.VMEM((rank, sum(sizes)), BF)],
        out_shape=[jax.ShapeDtypeStruct((rows, n), BF) for n in sizes],
        compiler_params=pltpu.CompilerParams(vmem_limit_bytes=VMEM_BYTES),
        cost_estimate=cost(10**4, 10**3),
        name="inward_weight_gradients",
    )(basis, gain, *own, *other, after)


def outward_grad(basis, own, other, after):
    wide, rank = basis.shape
    rows = wide // lax.axis_size("dp")
    ne = sum(piece.shape[1] for piece in own)
    return pl.pallas_call(
        functools.partial(outward_kernel, len(own)),
        grid=(STEPS,),
        in_specs=vmem(1 + 2 * len(own)) + [pl.BlockSpec(memory_space=pl.ANY)],
        out_specs=pl.BlockSpec((ne // STEPS, rows), lambda i: (i, 0)),
        scratch_shapes=[pltpu.VMEM((rank, ne), BF)],
        out_shape=jax.ShapeDtypeStruct((ne, rows), BF),
        compiler_params=pltpu.CompilerParams(vmem_limit_bytes=VMEM_BYTES),
        cost_estimate=cost(10**4, 10**3),
        name="output_weight_gradient",
    )(basis, *own, *other, after)


def results_kernel(
    wide, fbase_ref, y_ref, ygot_ref, base_ref, unit_ref, x_ref, xgot_ref, back_ref, inv_ref,
    gain_ref, gain_other_ref, after,
    f_ref, b_ref, gain_out_ref,
):
    f_ref[...] = (fbase_ref[...] + add_wide(y_ref[...], ygot_ref[...])).astype(BF)
    length = back_ref.shape[0]
    x = add_wide(x_ref[:length, :], xgot_ref[:length, :])
    inv = inv_ref[:, :1]
    along = jnp.sum(x * back_ref[...].astype(F32), axis=1, keepdims=True)
    middle = along * inv * (1.0 / wide)
    b_ref[...] = (base_ref[...] + (x - unit_ref[...] * middle) * inv).astype(BF)
    core = lax.axis_index("dp") & 1
    half = wide // 2
    rank = gain_ref.shape[1]
    for row in range(half // rank):
        mine = pl.ds(pl.multiple_of(core * half + row * rank, rank), rank)
        theirs = pl.ds(pl.multiple_of((1 - core) * half + row * rank, rank), rank)
        gain_out_ref[:, mine] = gain_ref[row : row + 1, :]
        gain_out_ref[:, theirs] = gain_other_ref[row : row + 1, :]


def results(wide, after, *operands):
    shape = operands[0].shape
    held = tuple(pltpu.with_memory_space_constraint(a, pltpu.VMEM) for a in operands)
    return pl.pallas_call(
        functools.partial(results_kernel, wide),
        in_specs=vmem(len(operands)) + [pl.BlockSpec(memory_space=pl.ANY)],
        out_specs=vmem(3),
        out_shape=[jax.ShapeDtypeStruct(shape, BF)] * 2 + [jax.ShapeDtypeStruct((1, wide), F32)],
        compiler_params=pltpu.CompilerParams(vmem_limit_bytes=VMEM_BYTES // 2),
        cost_estimate=cost(10**4, 10**3),
        name="section_results",
    )(*held, *in_hbm((after,)))


def body(
    new_coeffs,
    loss_grad,
    sent_forward,
    sent_backward,
    stashed,
    subspace,
    norm_gain,
    w_query,
    w_key,
    w_value,
    w_output,
):
    wide = subspace.shape[0]
    wq, wk, wv, wo = w_query[0], w_key[0], w_value[0], w_output[0]
    nq, nk, nv = wq.shape[1], wk.shape[1], wv.shape[1]
    back = stashed[0]
    arrived, returned = cross_pipe(sent_forward[0], sent_backward[0])
    cosine, sine = rope_tables(back.shape[0])

    m2, o2, inv, basis, wq, narrow, turned = project(
        back, norm_gain, subspace, wq, wk, wv, wo
    )
    inner, out_give, out_keep, x = backward(
        back, loss_grad, returned, m2, o2, inv, cosine, sine
    )
    out_got = swap(out_give, "dp", 1)
    inner_got = swap(inner, "dp", 1)
    base, unit, fbase = bases(
        back, loss_grad, returned, new_coeffs, arrived, basis, turned, inv, out_keep
    )
    out_pair = add_after(out_keep, out_got, fbase)
    out_got = swap(out_pair, "dp", 2)
    pair, x = gain_part(basis, wq, narrow, inner, inner_got, x, out_pair)
    pair_got = swap(pair, "dp", 2)
    x_got = swap(x, "tensor", 2)
    y = forward(new_coeffs, arrived, turned, m2, o2, cosine, sine, pair)
    y_got = swap(y, "tensor", 2)
    out_own = add_after(out_pair, out_got, y)
    out_other = swap(out_own, "dp", 1)
    x = merge(x, x_got, out_own)
    x_got = swap(x, "tensor", 1)
    grad_o = outward_grad(basis, [out_own], [out_other], x)
    sizes = (nq // 2, nq - nq // 2, nk + nv)
    own = own_pieces(pair, pair_got, sizes, *in_hbm((grad_o,)))
    other = [swap(piece, "dp", 1) for piece in own]
    gain = gain_total(x, x_got, own[0])
    gain_got = swap(gain, "dp", 2)
    y = add_after(y, y_got, gain, rows=back.shape[0])
    y_got = swap(y, "tensor", 1)
    grad_q, grad_k, grad_v = inward_grads(basis, norm_gain, own, other, (nq, nk, nv), y)
    gain = add_after(gain, gain_got, *in_hbm((grad_v,)))
    gain_other = swap(gain, "dp", 1)
    forward_out, backward_out, grad_gain = results(
        wide, grad_v, fbase, y, y_got, base, unit, x, x_got, back, inv, gain, gain_other
    )
    return (
        forward_out[None],
        backward_out[None],
        grad_q[None],
        grad_k[None],
        grad_v[None],
        grad_o[None],
        grad_gain,
    )


def solution(mesh):
    return jax.shard_map(
        body,
        mesh=mesh,
        in_specs=(
            P("dp", None),
            P("dp", None),
            P("pipe", "dp", None),
            P("pipe", "dp", None),
            P("pipe", "dp", None),
            P(),
            P("pipe", None),
            P("pipe", None, "tensor"),
            P("pipe", None, "tensor"),
            P("pipe", None, "tensor"),
            P("pipe", "tensor", None),
        ),
        out_specs=(
            P("pipe", "dp", None),
            P("pipe", "dp", None),
            P("pipe", "dp", "tensor"),
            P("pipe", "dp", "tensor"),
            P("pipe", "dp", "tensor"),
            P("pipe", "tensor", "dp"),
            P("pipe", None),
        ),
        check_vma=False,
    )
```

```python
import functools
import math

import jax
import jax.numpy as jnp
import numpy as np
from jax import lax
from jax.experimental import pallas as pl
from jax.experimental.pallas import tpu as pltpu
from jax.sharding import PartitionSpec as P

HD = 128
EPSILON = 1e-05
ROPE_BASE = 500000.0
BF = jnp.bfloat16
F32 = jnp.float32
VMEM_BYTES = 24 * 1024 * 1024
CHUNK = 512
PIECE = 1024
AHEAD = 5
LOG2E = 1.4426950408889634


def shifted(x, axis, by):
    devices = lax.axis_size(axis)
    pairs = [(i, i + by) for i in range(devices) if 0 <= i + by < devices]
    return lax.ppermute(x, axis, pairs)


def swap(x, axis, bit):
    devices = lax.axis_size(axis)
    return lax.ppermute(x, axis, [(i, i ^ bit) for i in range(devices)])


def cross_pipe(sent_forward, sent_backward):
    if lax.axis_size("pipe") != 2:
        return shifted(sent_forward, "pipe", 1), shifted(sent_backward, "pipe", -1)
    first = lax.axis_index("pipe") == 0
    got = swap(jnp.where(first, sent_forward, sent_backward), "pipe", 1)
    return got, got


def add_wide(a, b):
    return a.astype(F32) + b.astype(F32)


def nt(a, b):
    return lax.dot_general(a, b, (((1,), (1,)), ((), ())), preferred_element_type=F32)


def nn(a, b):
    return jnp.dot(a, b, preferred_element_type=F32)


def split(x, parts):
    out = []
    for _ in range(parts):
        piece = x.astype(BF)
        out.append(piece)
        x = x - piece.astype(F32)
    return out


def rope_tables(length):
    half = HD // 2
    frequency = np.float32(ROPE_BASE) ** (-2.0 * np.arange(half, dtype=np.float32) / HD)
    angles = np.arange(length, dtype=np.float32)[:, None] * frequency.astype(np.float32)
    cosine, sine = np.cos(angles), np.sin(angles)
    tables = (np.concatenate([cosine, cosine], 1), np.concatenate([-sine, sine], 1))
    return tuple(jnp.asarray(t, dtype=F32) for t in tables)


def rope(x, cosine, sine):
    return x * cosine + pltpu.roll(x, HD // 2, 1) * sine


def unrope(x, cosine, sine):
    return x * cosine - pltpu.roll(x, HD // 2, 1) * sine


def inverse_root(square_sum, width):
    return 1.0 / jnp.sqrt(square_sum / width + EPSILON)


def vmem(count):
    return [pl.BlockSpec(memory_space=pltpu.VMEM)] * count


def in_hbm(arrays):
    return tuple(pltpu.with_memory_space_constraint(a, pltpu.HBM) for a in arrays)


def cost(flops, num_bytes, exps=0):
    return pl.CostEstimate(flops=flops, bytes_accessed=num_bytes, transcendentals=exps)


def project_kernel(
    back_hbm, gain_hbm, u_hbm, wq_hbm, wk_hbm, wv_hbm, wo_hbm,
    m_ref, o_ref, inv_ref, u, wq, narrow, turned,
    back, gain, wo, scaled, m_acc, sems,
):
    wide, rank = u.shape
    nq = wq.shape[1]
    nk = wk_hbm.shape[1]
    parts = wide // PIECE
    pieces = [pl.ds(i * PIECE, PIECE) for i in range(parts)]
    pairs = [(back_hbm, back), (gain_hbm, gain)]
    pairs += [(u_hbm.at[at, :], u.at[at, :]) for at in pieces]
    pairs += [(wq_hbm.at[at, :], wq.at[at, :]) for at in pieces]
    pairs += [(wk_hbm, narrow.at[:, pl.ds(0, nk)])]
    pairs += [(wv_hbm, narrow.at[:, pl.ds(nk, narrow.shape[1] - nk)])]
    block = wo.shape[0] // parts
    blocks = [pl.ds(i * block, block) for i in range(parts)]
    pairs += [(wo_hbm.at[at, :], wo.at[at, :]) for at in blocks]
    copies = [
        pltpu.make_async_copy(source, target, sems.at[n])
        for n, (source, target) in enumerate(pairs)
    ]
    started = 0

    def start_to(count):
        nonlocal started
        for copy in copies[started:count]:
            copy.start()
        started = max(started, min(count, len(copies)))

    def wait(n):
        start_to(n + 1 + AHEAD)
        copies[n].wait()

    start_to(2 + parts + AHEAD)
    copies[0].wait()
    copies[1].wait()
    squares = [jnp.zeros((back.shape[0], HD), F32)]

    def decode(i):
        at = pieces[i]
        copies[2 + i].wait()
        turned[:, at] = u[at, :].T
        scaled[:, at] = (turned[:, at].astype(F32) * gain[:, at]).astype(BF)
        decoded = nn(back[...], turned[:, at])
        for side in range(0, PIECE, HD):
            part = decoded[:, side : side + HD]
            squares[0] = squares[0] + part * part

    decode(0)
    place = 2 + parts
    for i, at in enumerate(pieces):
        wait(place)
        place += 1
        if i + 1 < parts:
            decode(i + 1)
        part = nn(scaled[:, at], wq[at, :])
        if i == 0:
            m_acc[...] = part
        elif i + 1 < parts:
            m_acc[...] += part
        else:
            for p, piece in enumerate(split(m_acc[...] + part, 2)):
                m_ref[p * rank : (p + 1) * rank, :nq] = piece
    inv_ref[...] = jnp.broadcast_to(
        inverse_root(jnp.sum(squares[0], axis=1, keepdims=True), wide), inv_ref.shape
    )
    wait(place)
    wait(place + 1)
    place += 2
    for p, piece in enumerate(split(nn(scaled[...], narrow[...]), 2)):
        m_ref[p * rank : (p + 1) * rank, nq:] = piece
    for at in blocks:
        wait(place)
        place += 1
        o_ref[at, :] = nn(wo[at, :], u[...]).astype(BF)


def project(back, gain, basis, wq, wk, wv, wo):
    wide, rank = basis.shape
    length = back.shape[0]
    ne = wo.shape[0]
    nq = wq.shape[1]
    rest = wk.shape[1] + wv.shape[1]
    operands = in_hbm((back, gain, basis, wq, wk, wv, wo))
    return pl.pallas_call(
        project_kernel,
        in_specs=[pl.BlockSpec(memory_space=pltpu.HBM)] * len(operands),
        out_specs=vmem(7),
        out_shape=[
            jax.ShapeDtypeStruct((2 * rank, nq + rest), BF),
            jax.ShapeDtypeStruct((ne, rank), BF),
            jax.ShapeDtypeStruct((length, HD), F32),
            jax.ShapeDtypeStruct(basis.shape, BF),
            jax.ShapeDtypeStruct(wq.shape, BF),
            jax.ShapeDtypeStruct((wide, rest), BF),
            jax.ShapeDtypeStruct((rank, wide), BF),
        ],
        scratch_shapes=[
            pltpu.VMEM(back.shape, BF),
            pltpu.VMEM(gain.shape, F32),
            pltpu.VMEM(wo.shape, BF),
            pltpu.VMEM((rank, wide), BF),
            pltpu.VMEM((rank, nq), F32),
            pltpu.SemaphoreType.DMA((4 + 3 * (wide // PIECE),)),
        ],
        compiler_params=pltpu.CompilerParams(vmem_limit_bytes=VMEM_BYTES * 3 // 2),
        cost_estimate=cost(6 * 10**9, 20 * 10**6),
        name="project_weights",
    )(*operands)


def project_heads(coeffs, inv, m_ref, cosine, sine, q, k, v1):
    length = coeffs.shape[0]
    heads = q.shape[0] // length
    twice = jnp.concatenate([coeffs, coeffs], axis=1)
    for h in range(0, heads, 2):
        both = nn(twice, m_ref[:, h * HD : (h + 2) * HD]) * inv
        for part, at in ((both[:, :HD], h * length), (both[:, HD:], (h + 1) * length)):
            q[at : at + length, :] = rope(part, cosine, sine).astype(BF)
    part = nn(twice, m_ref[:, heads * HD :]) * inv
    k[...] = rope(part[:, :HD], cosine, sine).astype(BF)
    v1[:, :HD] = part[:, HD:].astype(BF)
    v1[:, HD:] = jnp.ones_like(v1[:, HD:])


def exps_of(scores, exps, low, length):
    row = lax.broadcasted_iota(jnp.int32, (length, length), 0)
    column = lax.broadcasted_iota(jnp.int32, (length, length), 1)
    causal = row >= column

    def one(h, _):
        at = pl.ds(pl.multiple_of(h * length, length), length)
        s = jnp.where(causal, scores[at, :], -jnp.inf)
        top = jnp.max(s, axis=1, keepdims=True)
        e = jnp.exp2((s - top) * (LOG2E / math.sqrt(HD)))
        if exps is not None:
            exps[at, :] = e
        low[at, :] = e.astype(BF)
        return 0

    lax.fori_loop(0, scores.shape[0] // length, one, 0, unroll=2)


def backward_kernel(
    back_ref, loss_ref, sent_ref, m_ref, o_ref, inv_ref, cos_ref, sin_ref,
    inner_ref, out_give_ref, out_keep_ref, x_ref,
    q, k, v1, gh, ghs, scores, low, mixed, gp, ds, dq, heads, grads, inner, out_inner,
):
    length, rank = back_ref.shape
    ne = o_ref.shape[0]
    count = ne // HD
    scale = 1.0 / math.sqrt(HD)
    last = lax.axis_size("pipe") - 1
    is_last = lax.axis_index("pipe") == last
    back = back_ref[...]
    up = jnp.where(is_last, loss_ref[...], sent_ref[...])
    cosine, sine = cos_ref[...], sin_ref[...]
    inv = inv_ref[...]
    project_heads(back, inv[:, :1], m_ref, cosine, sine, q, k, v1)
    scores[...] = nt(q[...], k[...])
    for h in range(0, count, 2):
        both = nt(up, o_ref[h * HD : (h + 2) * HD, :]).astype(BF)
        gh[h * length : (h + 1) * length, :] = both[:, :HD]
        gh[(h + 1) * length : (h + 2) * length, :] = both[:, HD:]
    exps_of(scores, scores, low, length)
    mixed[...] = nn(low[...], v1[...])
    gp[...] = nt(gh[...], v1[:, :HD])

    for h in range(count):
        at = slice(h * length, (h + 1) * length)
        inverse = 1.0 / mixed[at, HD:]
        out = mixed[at, :HD] * inverse
        heads[:, h * HD : (h + 1) * HD] = out.astype(BF)
        grad = gh[at, :].astype(F32)
        ghs[at, :] = (grad * inverse).astype(BF)
        delta = jnp.sum(grad * out, axis=1, keepdims=True)
        factor = inverse * scale
        for side in range(0, length, HD):
            part = scores[at, side : side + HD] * factor
            ds[at, side : side + HD] = (part * (gp[at, side : side + HD] - delta)).astype(BF)

    dq[...] = nn(ds[...], k[...])
    for h in range(count):
        part = dq[h * length : (h + 1) * length, :]
        grads[:, h * HD : (h + 1) * HD] = unrope(part, cosine, sine).astype(BF)
    dk = nn(q[...].T, ds[...]).T
    grads[:, ne : ne + HD] = unrope(dk, cosine, sine).astype(BF)
    grads[:, ne + HD :] = nn(ghs[...].T, low[...]).T.astype(BF)
    unit = (back.astype(F32) * inv[:, :1]).astype(BF)
    half = rank // 2
    core = lax.axis_index("dp") & 1
    mine = pl.ds(pl.multiple_of(core * half, half), half)
    theirs = pl.ds(pl.multiple_of((1 - core) * half, half), half)
    inner[...] = nn(unit.T, grads[...]).astype(BF)
    inner_ref[:half, :] = inner[mine, :]
    inner_ref[half:, :] = inner[theirs, :]
    out_inner[...] = nn(up.T, heads[...]).astype(BF)
    out_keep_ref[...] = out_inner[mine, :]
    out_give_ref[...] = out_inner[theirs, :]
    x_ref[...] = nt(grads[...], m_ref[:rank, :]).astype(BF)


def backward(back, loss, sent, m2, o2, inv, cosine, sine):
    length, rank = back.shape
    ne = o2.shape[0]
    total = m2.shape[1]
    assert total == ne + 2 * HD
    stack = ne // HD * length
    return pl.pallas_call(
        backward_kernel,
        in_specs=vmem(8),
        out_specs=vmem(4),
        out_shape=[
            jax.ShapeDtypeStruct((rank, total), BF),
            jax.ShapeDtypeStruct((rank // 2, ne), BF),
            jax.ShapeDtypeStruct((rank // 2, ne), BF),
            jax.ShapeDtypeStruct((length, rank), BF),
        ],
        scratch_shapes=[
            pltpu.VMEM((stack, HD), BF),
            pltpu.VMEM((length, HD), BF),
            pltpu.VMEM((length, 2 * HD), BF),
            pltpu.VMEM((stack, HD), BF),
            pltpu.VMEM((stack, HD), BF),
            pltpu.VMEM((stack, length), F32),
            pltpu.VMEM((stack, length), BF),
            pltpu.VMEM((stack, 2 * HD), F32),
            pltpu.VMEM((stack, length), F32),
            pltpu.VMEM((stack, length), BF),
            pltpu.VMEM((stack, HD), F32),
            pltpu.VMEM((length, ne), BF),
            pltpu.VMEM((length, total), BF),
            pltpu.VMEM((rank, total), BF),
            pltpu.VMEM((rank, ne), BF),
        ],
        compiler_params=pltpu.CompilerParams(vmem_limit_bytes=VMEM_BYTES),
        cost_estimate=cost(10**4, 10**3),
        name="attention_backward",
    )(back, loss, sent, m2, o2, inv, cosine, sine)


def bases_kernel(
    back_ref, loss_ref, returned_ref, new_ref, arrived_ref, u_ref, turned_ref, inv_ref, after,
    base_ref, unit_ref, fbase_ref, g_ref,
):
    rank = u_ref.shape[1]
    for i, piece in enumerate(split(nn(turned_ref[...], u_ref[...]), 3)):
        g_ref[i * rank : (i + 1) * rank, :] = piece
    is_last = lax.axis_index("pipe") == lax.axis_size("pipe") - 1
    is_first = lax.axis_index("pipe") == 0
    up = jnp.where(is_last, loss_ref[...], returned_ref[...])
    coeffs = jnp.where(is_first, new_ref[...], arrived_ref[...])
    base_ref[...] = nn(jnp.concatenate([up] * 3, axis=1), g_ref[...])
    fbase_ref[...] = nn(jnp.concatenate([coeffs] * 3, axis=1), g_ref[...])
    unit_ref[...] = nn(jnp.concatenate([back_ref[...]] * 3, axis=1), g_ref[...]) * inv_ref[:, :1]


def bases(back, loss, returned, new, arrived, basis, turned, inv, after):
    length, rank = back.shape
    return pl.pallas_call(
        bases_kernel,
        in_specs=vmem(8) + [pl.BlockSpec(memory_space=pl.ANY)],
        out_specs=vmem(3),
        out_shape=[jax.ShapeDtypeStruct((length, rank), F32)] * 3,
        scratch_shapes=[pltpu.VMEM((3 * rank, rank), BF)],
        compiler_params=pltpu.CompilerParams(vmem_limit_bytes=VMEM_BYTES // 2),
        cost_estimate=cost(10**4, 10**3),
        name="encoded_again",
    )(back, loss, returned, new, arrived, basis, turned, inv, after)


def forward_kernel(
    new_ref, sent_ref, turned_ref, m_ref, o_ref, cos_ref, sin_ref, after,
    y_ref, q, k, v1, scores, low, mixed, heads,
):
    length, rank = new_ref.shape
    wide = turned_ref.shape[1]
    is_first = lax.axis_index("pipe") == 0
    coeffs = jnp.where(is_first, new_ref[...], sent_ref[...])
    square = jnp.zeros((length, HD), F32)
    for at in range(0, wide, PIECE):
        decoded = nn(coeffs, turned_ref[:, at : at + PIECE])
        for side in range(0, PIECE, HD):
            part = decoded[:, side : side + HD]
            square = square + part * part
    inv = inverse_root(jnp.sum(square, axis=1, keepdims=True), wide)
    project_heads(coeffs, inv, m_ref, cos_ref[...], sin_ref[...], q, k, v1)
    scores[...] = nt(q[...], k[...])
    exps_of(scores, None, low, length)
    mixed[...] = nn(low[...], v1[...])
    for h in range(heads.shape[1] // HD):
        at = slice(h * length, (h + 1) * length)
        heads[:, h * HD : (h + 1) * HD] = (mixed[at, :HD] / mixed[at, HD:]).astype(BF)
    y_ref[:length, :] = nn(heads[...], o_ref[...]).astype(BF)
    y_ref[length:, :] = jnp.zeros_like(y_ref[length:, :])


def forward(new, sent, turned, m2, o2, cosine, sine, after):
    length, rank = new.shape
    ne = o2.shape[0]
    stack = ne // HD * length
    return pl.pallas_call(
        forward_kernel,
        in_specs=vmem(7) + [pl.BlockSpec(memory_space=pl.ANY)],
        out_specs=pl.BlockSpec(memory_space=pltpu.VMEM),
        out_shape=jax.ShapeDtypeStruct((length + 32, rank), BF),
        scratch_shapes=[
            pltpu.VMEM((stack, HD), BF),
            pltpu.VMEM((length, HD), BF),
            pltpu.VMEM((length, 2 * HD), BF),
            pltpu.VMEM((stack, length), F32),
            pltpu.VMEM((stack, length), BF),
            pltpu.VMEM((stack, 2 * HD), F32),
            pltpu.VMEM((length, ne), BF),
        ],
        compiler_params=pltpu.CompilerParams(vmem_limit_bytes=VMEM_BYTES),
        cost_estimate=cost(10**4, 10**3),
        name="attention_forward",
    )(new, sent, turned, m2, o2, cosine, sine, after)


def write_split(ref, value):
    high, low = split(value, 2)
    both = jnp.concatenate([high.astype(F32), low.astype(F32)], axis=0)
    ref[ref.shape[0] - 16 :, :] = both.astype(BF)


def read_split(ref):
    both = ref[ref.shape[0] - 16 :, :].astype(F32)
    return both[:8] + both[8:]


def gain_kernel(
    u_ref, wq_ref, narrow_ref, inner_ref, got_ref, x_ref, after,
    pair_ref, out_ref, turned, rows_f32,
):
    nq = wq_ref.shape[1]
    rows = u_ref.shape[0] // 2
    rank = u_ref.shape[1]
    half = inner_ref.shape[0] // 2
    core = lax.axis_index("dp") & 1
    mine = add_wide(inner_ref[:half, :], got_ref[half:, :]).astype(BF)
    theirs = add_wide(inner_ref[half:, :], got_ref[:half, :]).astype(BF)
    pair_ref[...] = mine
    out_ref[: x_ref.shape[0], :] = x_ref[...]
    turned[:, pl.ds(pl.multiple_of(core * half, half), half)] = mine.T
    turned[:, pl.ds(pl.multiple_of((1 - core) * half, half), half)] = theirs.T
    for at in range(0, rows, CHUNK):
        place = pl.ds(pl.multiple_of(core * rows + at, CHUNK), CHUNK)
        against = nn(wq_ref[place, :], turned[:nq, :])
        against += nn(narrow_ref[place, :], turned[nq:, :])
        terms = against * u_ref[place, :].astype(F32)
        folded = sum(terms[:, side : side + HD] for side in range(0, terms.shape[1], HD))
        line = jnp.sum(folded.T, axis=0, keepdims=True)
        for side in range(0, CHUNK, rank):
            row = (at + side) // rank
            rows_f32[row : row + 1, :] = line[:, side : side + rank]
    write_split(out_ref, rows_f32[...])


def gain_part(basis, wq, narrow, inner, got, x, after):
    wide, rank = basis.shape
    assert wide // 2 == 8 * rank
    held = tuple(pltpu.with_memory_space_constraint(a, pltpu.VMEM) for a in (basis, wq, narrow))
    return pl.pallas_call(
        gain_kernel,
        in_specs=vmem(6) + [pl.BlockSpec(memory_space=pl.ANY)],
        out_specs=vmem(2),
        out_shape=[
            jax.ShapeDtypeStruct((rank // 2, inner.shape[1]), BF),
            jax.ShapeDtypeStruct((x.shape[0] + 16, rank), BF),
        ],
        scratch_shapes=[
            pltpu.VMEM((inner.shape[1], rank), BF),
            pltpu.VMEM((8, rank), F32),
        ],
        compiler_params=pltpu.CompilerParams(vmem_limit_bytes=VMEM_BYTES),
        cost_estimate=cost(10**4, 10**3),
        name="pair_sum_and_gain_gradient",
    )(*held, inner, got, x, after)


def merge_kernel(a_ref, b_ref, after, out_ref):
    rest = out_ref.shape[0] - 16
    out_ref[:rest, :] = add_wide(a_ref[:rest, :], b_ref[:rest, :]).astype(BF)
    write_split(out_ref, read_split(a_ref) + read_split(b_ref))


def total_kernel(a_ref, b_ref, after, out_ref):
    out_ref[...] = read_split(a_ref) + read_split(b_ref)


def own_kernel(a_ref, b_ref, after, *out_refs):
    at = 0
    for ref in out_refs:
        size = ref.shape[1]
        ref[...] = add_wide(a_ref[:, at : at + size], b_ref[:, at : at + size]).astype(BF)
        at += size


def small_kernel(kernel, name, out_shape, a, b, after):
    return pl.pallas_call(
        kernel,
        in_specs=vmem(2) + [pl.BlockSpec(memory_space=pl.ANY)],
        out_specs=jax.tree.map(lambda _: pl.BlockSpec(memory_space=pltpu.VMEM), out_shape),
        out_shape=out_shape,
        compiler_params=pltpu.CompilerParams(vmem_limit_bytes=VMEM_BYTES // 2),
        cost_estimate=cost(10**4, 10**3),
        name=name,
    )(a, b, after)


def merge(a, b, after):
    return small_kernel(merge_kernel, "sum_with_gain", jax.ShapeDtypeStruct(a.shape, BF), a, b, after)


def gain_total(a, b, after):
    shape = jax.ShapeDtypeStruct((8, a.shape[1]), F32)
    return small_kernel(total_kernel, "gain_total", shape, a, b, after)


def own_pieces(a, b, sizes, after):
    shapes = [jax.ShapeDtypeStruct((a.shape[0], n), BF) for n in sizes]
    return small_kernel(own_kernel, "sum_over_y", shapes, a, b, after)


def add_kernel(a_ref, b_ref, after, out_ref):
    rows = out_ref.shape[0]
    out_ref[...] = add_wide(a_ref[:rows, :], b_ref[:rows, :]).astype(out_ref.dtype)


def add_after(a, b, after, rows=None):
    shape = jax.ShapeDtypeStruct((rows or a.shape[0], a.shape[1]), a.dtype)
    return small_kernel(add_kernel, "pair_sum", shape, a, b, after)


def gather_halves(own_refs, other_refs, whole):
    half = whole.shape[0] // 2
    core = lax.axis_index("dp") & 1
    at = 0
    for own_ref, other_ref in zip(own_refs, other_refs):
        columns = pl.ds(at, own_ref.shape[1])
        whole[pl.ds(pl.multiple_of(core * half, half), half), columns] = own_ref[...]
        whole[pl.ds(pl.multiple_of((1 - core) * half, half), half), columns] = other_ref[...]
        at += own_ref.shape[1]


def inward_kernel(pieces, u_ref, gain_ref, *refs):
    own_refs, other_refs = refs[:pieces], refs[pieces : 2 * pieces]
    q_ref, k_ref, v_ref, inner = refs[-4:]
    nq, nk = q_ref.shape[1], k_ref.shape[1]
    block = q_ref.shape[0]

    @pl.when(pl.program_id(0) == 0)
    def _():
        gather_halves(own_refs, other_refs, inner)

    step = lax.axis_index("dp") * pl.num_programs(0) + pl.program_id(0)
    rows = pl.ds(pl.multiple_of(step * block, block), block)
    gain = jnp.broadcast_to(gain_ref[:, rows], (HD, block)).T[:, :1]
    grad = nn(u_ref[rows, :], inner[...]) * gain
    q_ref[...] = grad[:, :nq].astype(BF)
    k_ref[...] = grad[:, nq : nq + nk].astype(BF)
    v_ref[...] = grad[:, nq + nk :].astype(BF)


def outward_kernel(pieces, u_ref, *refs):
    own_refs, other_refs = refs[:pieces], refs[pieces : 2 * pieces]
    o_ref, inner = refs[-2:]

    @pl.when(pl.program_id(0) == 0)
    def _():
        gather_halves(own_refs, other_refs, inner)

    block, rows = o_ref.shape
    at = pl.multiple_of(pl.program_id(0) * block, block)
    basis = u_ref[pl.ds(pl.multiple_of(lax.axis_index("dp") * rows, rows), rows), :]
    o_ref[...] = nt(inner[:, pl.ds(at, block)].T, basis).astype(BF)


STEPS = 2


def inward_grads(basis, gain, own, other, sizes, after):
    wide, rank = basis.shape
    rows = wide // lax.axis_size("dp")
    block = rows // STEPS
    return pl.pallas_call(
        functools.partial(inward_kernel, len(own)),
        grid=(STEPS,),
        in_specs=vmem(2 + 2 * len(own)) + [pl.BlockSpec(memory_space=pl.ANY)],
        out_specs=[pl.BlockSpec((block, n), lambda i: (i, 0)) for n in sizes],
        scratch_shapes=[pltpu.VMEM((rank, sum(sizes)), BF)],
        out_shape=[jax.ShapeDtypeStruct((rows, n), BF) for n in sizes],
        compiler_params=pltpu.CompilerParams(vmem_limit_bytes=VMEM_BYTES),
        cost_estimate=cost(10**4, 10**3),
        name="inward_weight_gradients",
    )(basis, gain, *own, *other, after)


def outward_grad(basis, own, other, after):
    wide, rank = basis.shape
    rows = wide // lax.axis_size("dp")
    ne = sum(piece.shape[1] for piece in own)
    return pl.pallas_call(
        functools.partial(outward_kernel, len(own)),
        grid=(STEPS,),
        in_specs=vmem(1 + 2 * len(own)) + [pl.BlockSpec(memory_space=pl.ANY)],
        out_specs=pl.BlockSpec((ne // STEPS, rows), lambda i: (i, 0)),
        scratch_shapes=[pltpu.VMEM((rank, ne), BF)],
        out_shape=jax.ShapeDtypeStruct((ne, rows), BF),
        compiler_params=pltpu.CompilerParams(vmem_limit_bytes=VMEM_BYTES),
        cost_estimate=cost(10**4, 10**3),
        name="output_weight_gradient",
    )(basis, *own, *other, after)


def results_kernel(
    wide, fbase_ref, y_ref, ygot_ref, base_ref, unit_ref, x_ref, xgot_ref, back_ref, inv_ref,
    gain_ref, gain_other_ref, after,
    f_ref, b_ref, gain_out_ref,
):
    f_ref[...] = (fbase_ref[...] + add_wide(y_ref[...], ygot_ref[...])).astype(BF)
    length = back_ref.shape[0]
    x = add_wide(x_ref[:length, :], xgot_ref[:length, :])
    inv = inv_ref[:, :1]
    along = jnp.sum(x * back_ref[...].astype(F32), axis=1, keepdims=True)
    middle = along * inv * (1.0 / wide)
    b_ref[...] = (base_ref[...] + (x - unit_ref[...] * middle) * inv).astype(BF)
    core = lax.axis_index("dp") & 1
    half = wide // 2
    rank = gain_ref.shape[1]
    for row in range(half // rank):
        mine = pl.ds(pl.multiple_of(core * half + row * rank, rank), rank)
        theirs = pl.ds(pl.multiple_of((1 - core) * half + row * rank, rank), rank)
        gain_out_ref[:, mine] = gain_ref[row : row + 1, :]
        gain_out_ref[:, theirs] = gain_other_ref[row : row + 1, :]


def results(wide, after, *operands):
    shape = operands[0].shape
    held = tuple(pltpu.with_memory_space_constraint(a, pltpu.VMEM) for a in operands)
    return pl.pallas_call(
        functools.partial(results_kernel, wide),
        in_specs=vmem(len(operands)) + [pl.BlockSpec(memory_space=pl.ANY)],
        out_specs=vmem(3),
        out_shape=[jax.ShapeDtypeStruct(shape, BF)] * 2 + [jax.ShapeDtypeStruct((1, wide), F32)],
        compiler_params=pltpu.CompilerParams(vmem_limit_bytes=VMEM_BYTES // 2),
        cost_estimate=cost(10**4, 10**3),
        name="section_results",
    )(*held, *in_hbm((after,)))


def body(
    new_coeffs,
    loss_grad,
    sent_forward,
    sent_backward,
    stashed,
    subspace,
    norm_gain,
    w_query,
    w_key,
    w_value,
    w_output,
):
    wide = subspace.shape[0]
    wq, wk, wv, wo = w_query[0], w_key[0], w_value[0], w_output[0]
    nq, nk, nv = wq.shape[1], wk.shape[1], wv.shape[1]
    back = stashed[0]
    arrived, returned = cross_pipe(sent_forward[0], sent_backward[0])
    cosine, sine = rope_tables(back.shape[0])

    m2, o2, inv, basis, wq, narrow, turned = project(
        back, norm_gain, subspace, wq, wk, wv, wo
    )
    inner, out_give, out_keep, x = backward(
        back, loss_grad, returned, m2, o2, inv, cosine, sine
    )
    out_got = swap(out_give, "dp", 1)
    inner_got = swap(inner, "dp", 1)
    base, unit, fbase = bases(
        back, loss_grad, returned, new_coeffs, arrived, basis, turned, inv, out_keep
    )
    out_pair = add_after(out_keep, out_got, fbase)
    out_got = swap(out_pair, "dp", 2)
    pair, x = gain_part(basis, wq, narrow, inner, inner_got, x, out_pair)
    pair_got = swap(pair, "dp", 2)
    x_got = swap(x, "tensor", 2)
    y = forward(new_coeffs, arrived, turned, m2, o2, cosine, sine, pair)
    y_got = swap(y, "tensor", 2)
    out_own = add_after(out_pair, out_got, y)
    out_other = swap(out_own, "dp", 1)
    x = merge(x, x_got, out_own)
    x_got = swap(x, "tensor", 1)
    grad_o = outward_grad(basis, [out_own], [out_other], x)
    sizes = (nq // 2, nq - nq // 2, nk + nv)
    own = own_pieces(pair, pair_got, sizes, *in_hbm((grad_o,)))
    other = [swap(piece, "dp", 1) for piece in own]
    gain = gain_total(x, x_got, own[0])
    gain_got = swap(gain, "dp", 2)
    y = add_after(y, y_got, gain, rows=back.shape[0])
    y_got = swap(y, "tensor", 1)
    grad_q, grad_k, grad_v = inward_grads(basis, norm_gain, own, other, (nq, nk, nv), y)
    gain = add_after(gain, gain_got, *in_hbm((grad_v,)))
    gain_other = swap(gain, "dp", 1)
    forward_out, backward_out, grad_gain = results(
        wide, grad_v, fbase, y, y_got, base, unit, x, x_got, back, inv, gain, gain_other
    )
    return (
        forward_out[None],
        backward_out[None],
        grad_q[None],
        grad_k[None],
        grad_v[None],
        grad_o[None],
        grad_gain,
    )


def solution(mesh):
    return jax.shard_map(
        body,
        mesh=mesh,
        in_specs=(
            P("dp", None),
            P("dp", None),
            P("pipe", "dp", None),
            P("pipe", "dp", None),
            P("pipe", "dp", None),
            P(),
            P("pipe", None),
            P("pipe", None, "tensor"),
            P("pipe", None, "tensor"),
            P("pipe", None, "tensor"),
            P("pipe", "tensor", None),
        ),
        out_specs=(
            P("pipe", "dp", None),
            P("pipe", "dp", None),
            P("pipe", "dp", "tensor"),
            P("pipe", "dp", "tensor"),
            P("pipe", "dp", "tensor"),
            P("pipe", "tensor", "dp"),
            P("pipe", None),
        ),
        check_vma=False,
    )
```

```python
import functools
import math

import jax
import jax.numpy as jnp
import numpy as np
from jax import lax
from jax.experimental import pallas as pl
from jax.experimental.pallas import tpu as pltpu
from jax.sharding import PartitionSpec as P

HD = 128
EPSILON = 1e-05
ROPE_BASE = 500000.0
BF = jnp.bfloat16
F32 = jnp.float32
VMEM_BYTES = 24 * 1024 * 1024
CHUNK = 512
PIECE = 1024
AHEAD = 4
LOG2E = 1.4426950408889634


def shifted(x, axis, by):
    devices = lax.axis_size(axis)
    pairs = [(i, i + by) for i in range(devices) if 0 <= i + by < devices]
    return lax.ppermute(x, axis, pairs)


def swap(x, axis, bit):
    devices = lax.axis_size(axis)
    return lax.ppermute(x, axis, [(i, i ^ bit) for i in range(devices)])


def cross_pipe(sent_forward, sent_backward):
    if lax.axis_size("pipe") != 2:
        return shifted(sent_forward, "pipe", 1), shifted(sent_backward, "pipe", -1)
    first = lax.axis_index("pipe") == 0
    got = swap(jnp.where(first, sent_forward, sent_backward), "pipe", 1)
    return got, got


def add_wide(a, b):
    return a.astype(F32) + b.astype(F32)


def nt(a, b):
    return lax.dot_general(a, b, (((1,), (1,)), ((), ())), preferred_element_type=F32)


def nn(a, b):
    return jnp.dot(a, b, preferred_element_type=F32)


def split(x, parts):
    out = []
    for _ in range(parts):
        piece = x.astype(BF)
        out.append(piece)
        x = x - piece.astype(F32)
    return out


def rope_tables(length):
    half = HD // 2
    frequency = np.float32(ROPE_BASE) ** (-2.0 * np.arange(half, dtype=np.float32) / HD)
    angles = np.arange(length, dtype=np.float32)[:, None] * frequency.astype(np.float32)
    cosine, sine = np.cos(angles), np.sin(angles)
    tables = (np.concatenate([cosine, cosine], 1), np.concatenate([-sine, sine], 1))
    return tuple(jnp.asarray(t, dtype=F32) for t in tables)


def rope(x, cosine, sine):
    return x * cosine + pltpu.roll(x, HD // 2, 1) * sine


def unrope(x, cosine, sine):
    return x * cosine - pltpu.roll(x, HD // 2, 1) * sine


def inverse_root(square_sum, width):
    return 1.0 / jnp.sqrt(square_sum / width + EPSILON)


def vmem(count):
    return [pl.BlockSpec(memory_space=pltpu.VMEM)] * count


def in_hbm(arrays):
    return tuple(pltpu.with_memory_space_constraint(a, pltpu.HBM) for a in arrays)


def cost(flops, num_bytes, exps=0):
    return pl.CostEstimate(flops=flops, bytes_accessed=num_bytes, transcendentals=exps)


def project_kernel(
    back_hbm, gain_hbm, u_hbm, wq_hbm, wk_hbm, wv_hbm, wo_hbm,
    m_ref, o_ref, inv_ref, u, wq, narrow, turned,
    back, gain, wo, scaled, m_acc, sems,
):
    wide, rank = u.shape
    nq = wq.shape[1]
    nk = wk_hbm.shape[1]
    parts = wide // PIECE
    pieces = [pl.ds(i * PIECE, PIECE) for i in range(parts)]
    pairs = [(back_hbm, back), (gain_hbm, gain)]
    pairs += [(u_hbm.at[at, :], u.at[at, :]) for at in pieces]
    pairs += [(wq_hbm.at[at, :], wq.at[at, :]) for at in pieces[:2]]
    pairs += [(wk_hbm, narrow.at[:, pl.ds(0, nk)])]
    pairs += [(wv_hbm, narrow.at[:, pl.ds(nk, narrow.shape[1] - nk)])]
    pairs += [(wq_hbm.at[at, :], wq.at[at, :]) for at in pieces[2:]]
    block = wo.shape[0] // parts
    blocks = [pl.ds(i * block, block) for i in range(parts)]
    pairs += [(wo_hbm.at[at, :], wo.at[at, :]) for at in blocks]
    copies = [
        pltpu.make_async_copy(source, target, sems.at[n])
        for n, (source, target) in enumerate(pairs)
    ]
    started = 0

    def start_to(count):
        nonlocal started
        for copy in copies[started:count]:
            copy.start()
        started = max(started, min(count, len(copies)))

    def wait(n):
        start_to(n + 1 + AHEAD)
        copies[n].wait()

    start_to(2 + parts + AHEAD)
    copies[0].wait()
    copies[1].wait()
    square = jnp.zeros((back.shape[0], HD), F32)
    for i, at in enumerate(pieces):
        copies[2 + i].wait()
        turned[:, at] = u[at, :].T
        scaled[:, at] = (turned[:, at].astype(F32) * gain[:, at]).astype(BF)
        decoded = nn(back[...], turned[:, at])
        for side in range(0, PIECE, HD):
            part = decoded[:, side : side + HD]
            square = square + part * part
    inv_ref[...] = jnp.broadcast_to(
        inverse_root(jnp.sum(square, axis=1, keepdims=True), wide), inv_ref.shape
    )
    place = 2 + parts
    for i, at in enumerate(pieces):
        if i == 2:
            wait(place)
            wait(place + 1)
            place += 2
            for p, piece in enumerate(split(nn(scaled[...], narrow[...]), 2)):
                m_ref[p * rank : (p + 1) * rank, nq:] = piece
        wait(place)
        place += 1
        part = nn(scaled[:, at], wq[at, :])
        if i == 0:
            m_acc[...] = part
        else:
            m_acc[...] += part
    for p, piece in enumerate(split(m_acc[...], 2)):
        m_ref[p * rank : (p + 1) * rank, :nq] = piece
    for _ in blocks:
        wait(place)
        place += 1
    o_ref[...] = nn(wo[...], u[...]).astype(BF)


def project(back, gain, basis, wq, wk, wv, wo):
    wide, rank = basis.shape
    length = back.shape[0]
    ne = wo.shape[0]
    nq = wq.shape[1]
    rest = wk.shape[1] + wv.shape[1]
    operands = in_hbm((back, gain, basis, wq, wk, wv, wo))
    return pl.pallas_call(
        project_kernel,
        in_specs=[pl.BlockSpec(memory_space=pltpu.HBM)] * len(operands),
        out_specs=vmem(7),
        out_shape=[
            jax.ShapeDtypeStruct((2 * rank, nq + rest), BF),
            jax.ShapeDtypeStruct((ne, rank), BF),
            jax.ShapeDtypeStruct((length, HD), F32),
            jax.ShapeDtypeStruct(basis.shape, BF),
            jax.ShapeDtypeStruct(wq.shape, BF),
            jax.ShapeDtypeStruct((wide, rest), BF),
            jax.ShapeDtypeStruct((rank, wide), BF),
        ],
        scratch_shapes=[
            pltpu.VMEM(back.shape, BF),
            pltpu.VMEM(gain.shape, F32),
            pltpu.VMEM(wo.shape, BF),
            pltpu.VMEM((rank, wide), BF),
            pltpu.VMEM((rank, nq), F32),
            pltpu.SemaphoreType.DMA((4 + 3 * (wide // PIECE),)),
        ],
        compiler_params=pltpu.CompilerParams(vmem_limit_bytes=VMEM_BYTES * 3 // 2),
        cost_estimate=cost(6 * 10**9, 20 * 10**6),
        name="project_weights",
    )(*operands)


def project_heads(coeffs, inv, m_ref, cosine, sine, q, k, v1):
    length = coeffs.shape[0]
    heads = q.shape[0] // length
    twice = jnp.concatenate([coeffs, coeffs], axis=1)
    for h in range(0, heads, 2):
        both = nn(twice, m_ref[:, h * HD : (h + 2) * HD]) * inv
        for part, at in ((both[:, :HD], h * length), (both[:, HD:], (h + 1) * length)):
            q[at : at + length, :] = rope(part, cosine, sine).astype(BF)
    part = nn(twice, m_ref[:, heads * HD :]) * inv
    k[...] = rope(part[:, :HD], cosine, sine).astype(BF)
    v1[:, :HD] = part[:, HD:].astype(BF)
    v1[:, HD:] = jnp.ones_like(v1[:, HD:])


def exps_of(scores, exps, low, length):
    row = lax.broadcasted_iota(jnp.int32, (length, length), 0)
    column = lax.broadcasted_iota(jnp.int32, (length, length), 1)
    causal = row >= column

    def one(h, _):
        at = pl.ds(pl.multiple_of(h * length, length), length)
        s = jnp.where(causal, scores[at, :], -jnp.inf)
        top = jnp.max(s, axis=1, keepdims=True)
        e = jnp.exp2((s - top) * (LOG2E / math.sqrt(HD)))
        if exps is not None:
            exps[at, :] = e
        low[at, :] = e.astype(BF)
        return 0

    lax.fori_loop(0, scores.shape[0] // length, one, 0, unroll=2)


def backward_kernel(
    back_ref, loss_ref, sent_ref, m_ref, o_ref, inv_ref, cos_ref, sin_ref,
    inner_ref, out_give_ref, out_keep_ref, x_ref,
    q, k, v1, gh, ghs, scores, low, mixed, gp, ds, dq, heads, grads, inner, out_inner,
):
    length, rank = back_ref.shape
    ne = o_ref.shape[0]
    count = ne // HD
    scale = 1.0 / math.sqrt(HD)
    last = lax.axis_size("pipe") - 1
    is_last = lax.axis_index("pipe") == last
    back = back_ref[...]
    up = jnp.where(is_last, loss_ref[...], sent_ref[...])
    cosine, sine = cos_ref[...], sin_ref[...]
    inv = inv_ref[...]
    project_heads(back, inv[:, :1], m_ref, cosine, sine, q, k, v1)
    scores[...] = nt(q[...], k[...])
    for h in range(0, count, 2):
        both = nt(up, o_ref[h * HD : (h + 2) * HD, :]).astype(BF)
        gh[h * length : (h + 1) * length, :] = both[:, :HD]
        gh[(h + 1) * length : (h + 2) * length, :] = both[:, HD:]
    exps_of(scores, scores, low, length)
    mixed[...] = nn(low[...], v1[...])
    gp[...] = nt(gh[...], v1[:, :HD])

    for h in range(count):
        at = slice(h * length, (h + 1) * length)
        inverse = 1.0 / mixed[at, HD:]
        out = mixed[at, :HD] * inverse
        heads[:, h * HD : (h + 1) * HD] = out.astype(BF)
        grad = gh[at, :].astype(F32)
        ghs[at, :] = (grad * inverse).astype(BF)
        delta = jnp.sum(grad * out, axis=1, keepdims=True)
        factor = inverse * scale
        for side in range(0, length, HD):
            part = scores[at, side : side + HD] * factor
            ds[at, side : side + HD] = (part * (gp[at, side : side + HD] - delta)).astype(BF)

    dq[...] = nn(ds[...], k[...])
    for h in range(count):
        part = dq[h * length : (h + 1) * length, :]
        grads[:, h * HD : (h + 1) * HD] = unrope(part, cosine, sine).astype(BF)
    dk = nn(q[...].T, ds[...]).T
    grads[:, ne : ne + HD] = unrope(dk, cosine, sine).astype(BF)
    grads[:, ne + HD :] = nn(ghs[...].T, low[...]).T.astype(BF)
    unit = (back.astype(F32) * inv[:, :1]).astype(BF)
    half = rank // 2
    core = lax.axis_index("dp") & 1
    mine = pl.ds(pl.multiple_of(core * half, half), half)
    theirs = pl.ds(pl.multiple_of((1 - core) * half, half), half)
    inner[...] = nn(unit.T, grads[...]).astype(BF)
    inner_ref[:half, :] = inner[mine, :]
    inner_ref[half:, :] = inner[theirs, :]
    out_inner[...] = nn(up.T, heads[...]).astype(BF)
    out_keep_ref[...] = out_inner[mine, :]
    out_give_ref[...] = out_inner[theirs, :]
    x_ref[...] = nt(grads[...], m_ref[:rank, :]).astype(BF)


def backward(back, loss, sent, m2, o2, inv, cosine, sine):
    length, rank = back.shape
    ne = o2.shape[0]
    total = m2.shape[1]
    assert total == ne + 2 * HD
    stack = ne // HD * length
    return pl.pallas_call(
        backward_kernel,
        in_specs=vmem(8),
        out_specs=vmem(4),
        out_shape=[
            jax.ShapeDtypeStruct((rank, total), BF),
            jax.ShapeDtypeStruct((rank // 2, ne), BF),
            jax.ShapeDtypeStruct((rank // 2, ne), BF),
            jax.ShapeDtypeStruct((length, rank), BF),
        ],
        scratch_shapes=[
            pltpu.VMEM((stack, HD), BF),
            pltpu.VMEM((length, HD), BF),
            pltpu.VMEM((length, 2 * HD), BF),
            pltpu.VMEM((stack, HD), BF),
            pltpu.VMEM((stack, HD), BF),
            pltpu.VMEM((stack, length), F32),
            pltpu.VMEM((stack, length), BF),
            pltpu.VMEM((stack, 2 * HD), F32),
            pltpu.VMEM((stack, length), F32),
            pltpu.VMEM((stack, length), BF),
            pltpu.VMEM((stack, HD), F32),
            pltpu.VMEM((length, ne), BF),
            pltpu.VMEM((length, total), BF),
            pltpu.VMEM((rank, total), BF),
            pltpu.VMEM((rank, ne), BF),
        ],
        compiler_params=pltpu.CompilerParams(vmem_limit_bytes=VMEM_BYTES),
        cost_estimate=cost(10**4, 10**3),
        name="attention_backward",
    )(back, loss, sent, m2, o2, inv, cosine, sine)


def bases_kernel(
    back_ref, loss_ref, returned_ref, new_ref, arrived_ref, u_ref, turned_ref, inv_ref, after,
    base_ref, unit_ref, fbase_ref, g_ref,
):
    rank = u_ref.shape[1]
    for i, piece in enumerate(split(nn(turned_ref[...], u_ref[...]), 3)):
        g_ref[i * rank : (i + 1) * rank, :] = piece
    is_last = lax.axis_index("pipe") == lax.axis_size("pipe") - 1
    is_first = lax.axis_index("pipe") == 0
    up = jnp.where(is_last, loss_ref[...], returned_ref[...])
    coeffs = jnp.where(is_first, new_ref[...], arrived_ref[...])
    base_ref[...] = nn(jnp.concatenate([up] * 3, axis=1), g_ref[...])
    fbase_ref[...] = nn(jnp.concatenate([coeffs] * 3, axis=1), g_ref[...])
    unit_ref[...] = nn(jnp.concatenate([back_ref[...]] * 3, axis=1), g_ref[...]) * inv_ref[:, :1]


def bases(back, loss, returned, new, arrived, basis, turned, inv, after):
    length, rank = back.shape
    return pl.pallas_call(
        bases_kernel,
        in_specs=vmem(8) + [pl.BlockSpec(memory_space=pl.ANY)],
        out_specs=vmem(3),
        out_shape=[jax.ShapeDtypeStruct((length, rank), F32)] * 3,
        scratch_shapes=[pltpu.VMEM((3 * rank, rank), BF)],
        compiler_params=pltpu.CompilerParams(vmem_limit_bytes=VMEM_BYTES // 2),
        cost_estimate=cost(10**4, 10**3),
        name="encoded_again",
    )(back, loss, returned, new, arrived, basis, turned, inv, after)


def forward_kernel(
    new_ref, sent_ref, turned_ref, m_ref, o_ref, cos_ref, sin_ref, after,
    y_ref, q, k, v1, scores, low, mixed, heads,
):
    length, rank = new_ref.shape
    wide = turned_ref.shape[1]
    is_first = lax.axis_index("pipe") == 0
    coeffs = jnp.where(is_first, new_ref[...], sent_ref[...])
    square = jnp.zeros((length, HD), F32)
    for at in range(0, wide, PIECE):
        decoded = nn(coeffs, turned_ref[:, at : at + PIECE])
        for side in range(0, PIECE, HD):
            part = decoded[:, side : side + HD]
            square = square + part * part
    inv = inverse_root(jnp.sum(square, axis=1, keepdims=True), wide)
    project_heads(coeffs, inv, m_ref, cos_ref[...], sin_ref[...], q, k, v1)
    scores[...] = nt(q[...], k[...])
    exps_of(scores, None, low, length)
    mixed[...] = nn(low[...], v1[...])
    for h in range(heads.shape[1] // HD):
        at = slice(h * length, (h + 1) * length)
        heads[:, h * HD : (h + 1) * HD] = (mixed[at, :HD] / mixed[at, HD:]).astype(BF)
    y_ref[:length, :] = nn(heads[...], o_ref[...]).astype(BF)
    y_ref[length:, :] = jnp.zeros_like(y_ref[length:, :])


def forward(new, sent, turned, m2, o2, cosine, sine, after):
    length, rank = new.shape
    ne = o2.shape[0]
    stack = ne // HD * length
    return pl.pallas_call(
        forward_kernel,
        in_specs=vmem(7) + [pl.BlockSpec(memory_space=pl.ANY)],
        out_specs=pl.BlockSpec(memory_space=pltpu.VMEM),
        out_shape=jax.ShapeDtypeStruct((length + 32, rank), BF),
        scratch_shapes=[
            pltpu.VMEM((stack, HD), BF),
            pltpu.VMEM((length, HD), BF),
            pltpu.VMEM((length, 2 * HD), BF),
            pltpu.VMEM((stack, length), F32),
            pltpu.VMEM((stack, length), BF),
            pltpu.VMEM((stack, 2 * HD), F32),
            pltpu.VMEM((length, ne), BF),
        ],
        compiler_params=pltpu.CompilerParams(vmem_limit_bytes=VMEM_BYTES),
        cost_estimate=cost(10**4, 10**3),
        name="attention_forward",
    )(new, sent, turned, m2, o2, cosine, sine, after)


def write_split(ref, value):
    high, low = split(value, 2)
    both = jnp.concatenate([high.astype(F32), low.astype(F32)], axis=0)
    ref[ref.shape[0] - 16 :, :] = both.astype(BF)


def read_split(ref):
    both = ref[ref.shape[0] - 16 :, :].astype(F32)
    return both[:8] + both[8:]


def gain_kernel(
    u_ref, wq_ref, narrow_ref, inner_ref, got_ref, x_ref, after,
    pair_ref, out_ref, turned, rows_f32,
):
    nq = wq_ref.shape[1]
    rows = u_ref.shape[0] // 2
    rank = u_ref.shape[1]
    half = inner_ref.shape[0] // 2
    core = lax.axis_index("dp") & 1
    mine = add_wide(inner_ref[:half, :], got_ref[half:, :]).astype(BF)
    theirs = add_wide(inner_ref[half:, :], got_ref[:half, :]).astype(BF)
    pair_ref[...] = mine
    out_ref[: x_ref.shape[0], :] = x_ref[...]
    turned[:, pl.ds(pl.multiple_of(core * half, half), half)] = mine.T
    turned[:, pl.ds(pl.multiple_of((1 - core) * half, half), half)] = theirs.T
    for at in range(0, rows, CHUNK):
        place = pl.ds(pl.multiple_of(core * rows + at, CHUNK), CHUNK)
        against = nn(wq_ref[place, :], turned[:nq, :])
        against += nn(narrow_ref[place, :], turned[nq:, :])
        terms = against * u_ref[place, :].astype(F32)
        folded = sum(terms[:, side : side + HD] for side in range(0, terms.shape[1], HD))
        line = jnp.sum(folded.T, axis=0, keepdims=True)
        for side in range(0, CHUNK, rank):
            row = (at + side) // rank
            rows_f32[row : row + 1, :] = line[:, side : side + rank]
    write_split(out_ref, rows_f32[...])


def gain_part(basis, wq, narrow, inner, got, x, after):
    wide, rank = basis.shape
    assert wide // 2 == 8 * rank
    held = tuple(pltpu.with_memory_space_constraint(a, pltpu.VMEM) for a in (basis, wq, narrow))
    return pl.pallas_call(
        gain_kernel,
        in_specs=vmem(6) + [pl.BlockSpec(memory_space=pl.ANY)],
        out_specs=vmem(2),
        out_shape=[
            jax.ShapeDtypeStruct((rank // 2, inner.shape[1]), BF),
            jax.ShapeDtypeStruct((x.shape[0] + 16, rank), BF),
        ],
        scratch_shapes=[
            pltpu.VMEM((inner.shape[1], rank), BF),
            pltpu.VMEM((8, rank), F32),
        ],
        compiler_params=pltpu.CompilerParams(vmem_limit_bytes=VMEM_BYTES),
        cost_estimate=cost(10**4, 10**3),
        name="pair_sum_and_gain_gradient",
    )(*held, inner, got, x, after)


def merge_kernel(a_ref, b_ref, after, out_ref):
    rest = out_ref.shape[0] - 16
    out_ref[:rest, :] = add_wide(a_ref[:rest, :], b_ref[:rest, :]).astype(BF)
    write_split(out_ref, read_split(a_ref) + read_split(b_ref))


def total_kernel(a_ref, b_ref, after, out_ref):
    out_ref[...] = read_split(a_ref) + read_split(b_ref)


def own_kernel(a_ref, b_ref, after, *out_refs):
    at = 0
    for ref in out_refs:
        size = ref.shape[1]
        ref[...] = add_wide(a_ref[:, at : at + size], b_ref[:, at : at + size]).astype(BF)
        at += size


def small_kernel(kernel, name, out_shape, a, b, after):
    return pl.pallas_call(
        kernel,
        in_specs=vmem(2) + [pl.BlockSpec(memory_space=pl.ANY)],
        out_specs=jax.tree.map(lambda _: pl.BlockSpec(memory_space=pltpu.VMEM), out_shape),
        out_shape=out_shape,
        compiler_params=pltpu.CompilerParams(vmem_limit_bytes=VMEM_BYTES // 2),
        cost_estimate=cost(10**4, 10**3),
        name=name,
    )(a, b, after)


def merge(a, b, after):
    return small_kernel(merge_kernel, "sum_with_gain", jax.ShapeDtypeStruct(a.shape, BF), a, b, after)


def gain_total(a, b, after):
    shape = jax.ShapeDtypeStruct((8, a.shape[1]), F32)
    return small_kernel(total_kernel, "gain_total", shape, a, b, after)


def own_pieces(a, b, sizes, after):
    shapes = [jax.ShapeDtypeStruct((a.shape[0], n), BF) for n in sizes]
    return small_kernel(own_kernel, "sum_over_y", shapes, a, b, after)


def add_kernel(a_ref, b_ref, after, out_ref):
    rows = out_ref.shape[0]
    out_ref[...] = add_wide(a_ref[:rows, :], b_ref[:rows, :]).astype(out_ref.dtype)


def add_after(a, b, after, rows=None):
    shape = jax.ShapeDtypeStruct((rows or a.shape[0], a.shape[1]), a.dtype)
    return small_kernel(add_kernel, "pair_sum", shape, a, b, after)


def gather_halves(own_refs, other_refs, whole):
    half = whole.shape[0] // 2
    core = lax.axis_index("dp") & 1
    at = 0
    for own_ref, other_ref in zip(own_refs, other_refs):
        columns = pl.ds(at, own_ref.shape[1])
        whole[pl.ds(pl.multiple_of(core * half, half), half), columns] = own_ref[...]
        whole[pl.ds(pl.multiple_of((1 - core) * half, half), half), columns] = other_ref[...]
        at += own_ref.shape[1]


def inward_kernel(pieces, u_ref, gain_ref, *refs):
    own_refs, other_refs = refs[:pieces], refs[pieces : 2 * pieces]
    q_ref, k_ref, v_ref, inner = refs[-4:]
    nq, nk = q_ref.shape[1], k_ref.shape[1]
    block = q_ref.shape[0]

    @pl.when(pl.program_id(0) == 0)
    def _():
        gather_halves(own_refs, other_refs, inner)

    step = lax.axis_index("dp") * pl.num_programs(0) + pl.program_id(0)
    rows = pl.ds(pl.multiple_of(step * block, block), block)
    gain = jnp.broadcast_to(gain_ref[:, rows], (HD, block)).T[:, :1]
    grad = nn(u_ref[rows, :], inner[...]) * gain
    q_ref[...] = grad[:, :nq].astype(BF)
    k_ref[...] = grad[:, nq : nq + nk].astype(BF)
    v_ref[...] = grad[:, nq + nk :].astype(BF)


def outward_kernel(pieces, u_ref, *refs):
    own_refs, other_refs = refs[:pieces], refs[pieces : 2 * pieces]
    o_ref, inner = refs[-2:]

    @pl.when(pl.program_id(0) == 0)
    def _():
        gather_halves(own_refs, other_refs, inner)

    block, rows = o_ref.shape
    at = pl.multiple_of(pl.program_id(0) * block, block)
    basis = u_ref[pl.ds(pl.multiple_of(lax.axis_index("dp") * rows, rows), rows), :]
    o_ref[...] = nt(inner[:, pl.ds(at, block)].T, basis).astype(BF)


STEPS = 2


def inward_grads(basis, gain, own, other, sizes, after):
    wide, rank = basis.shape
    rows = wide // lax.axis_size("dp")
    block = rows // STEPS
    return pl.pallas_call(
        functools.partial(inward_kernel, len(own)),
        grid=(STEPS,),
        in_specs=vmem(2 + 2 * len(own)) + [pl.BlockSpec(memory_space=pl.ANY)],
        out_specs=[pl.BlockSpec((block, n), lambda i: (i, 0)) for n in sizes],
        scratch_shapes=[pltpu.VMEM((rank, sum(sizes)), BF)],
        out_shape=[jax.ShapeDtypeStruct((rows, n), BF) for n in sizes],
        compiler_params=pltpu.CompilerParams(vmem_limit_bytes=VMEM_BYTES),
        cost_estimate=cost(10**4, 10**3),
        name="inward_weight_gradients",
    )(basis, gain, *own, *other, after)


def outward_grad(basis, own, other, after):
    wide, rank = basis.shape
    rows = wide // lax.axis_size("dp")
    ne = sum(piece.shape[1] for piece in own)
    return pl.pallas_call(
        functools.partial(outward_kernel, len(own)),
        grid=(STEPS,),
        in_specs=vmem(1 + 2 * len(own)) + [pl.BlockSpec(memory_space=pl.ANY)],
        out_specs=pl.BlockSpec((ne // STEPS, rows), lambda i: (i, 0)),
        scratch_shapes=[pltpu.VMEM((rank, ne), BF)],
        out_shape=jax.ShapeDtypeStruct((ne, rows), BF),
        compiler_params=pltpu.CompilerParams(vmem_limit_bytes=VMEM_BYTES),
        cost_estimate=cost(10**4, 10**3),
        name="output_weight_gradient",
    )(basis, *own, *other, after)


def results_kernel(
    wide, fbase_ref, y_ref, ygot_ref, base_ref, unit_ref, x_ref, xgot_ref, back_ref, inv_ref,
    gain_ref, gain_other_ref, after,
    f_ref, b_ref, gain_out_ref,
):
    f_ref[...] = (fbase_ref[...] + add_wide(y_ref[...], ygot_ref[...])).astype(BF)
    length = back_ref.shape[0]
    x = add_wide(x_ref[:length, :], xgot_ref[:length, :])
    inv = inv_ref[:, :1]
    along = jnp.sum(x * back_ref[...].astype(F32), axis=1, keepdims=True)
    middle = along * inv * (1.0 / wide)
    b_ref[...] = (base_ref[...] + (x - unit_ref[...] * middle) * inv).astype(BF)
    core = lax.axis_index("dp") & 1
    half = wide // 2
    rank = gain_ref.shape[1]
    for row in range(half // rank):
        mine = pl.ds(pl.multiple_of(core * half + row * rank, rank), rank)
        theirs = pl.ds(pl.multiple_of((1 - core) * half + row * rank, rank), rank)
        gain_out_ref[:, mine] = gain_ref[row : row + 1, :]
        gain_out_ref[:, theirs] = gain_other_ref[row : row + 1, :]


def results(wide, after, *operands):
    shape = operands[0].shape
    held = tuple(pltpu.with_memory_space_constraint(a, pltpu.VMEM) for a in operands)
    return pl.pallas_call(
        functools.partial(results_kernel, wide),
        in_specs=vmem(len(operands)) + [pl.BlockSpec(memory_space=pl.ANY)],
        out_specs=vmem(3),
        out_shape=[jax.ShapeDtypeStruct(shape, BF)] * 2 + [jax.ShapeDtypeStruct((1, wide), F32)],
        compiler_params=pltpu.CompilerParams(vmem_limit_bytes=VMEM_BYTES // 2),
        cost_estimate=cost(10**4, 10**3),
        name="section_results",
    )(*held, *in_hbm((after,)))


def body(
    new_coeffs,
    loss_grad,
    sent_forward,
    sent_backward,
    stashed,
    subspace,
    norm_gain,
    w_query,
    w_key,
    w_value,
    w_output,
):
    wide = subspace.shape[0]
    wq, wk, wv, wo = w_query[0], w_key[0], w_value[0], w_output[0]
    nq, nk, nv = wq.shape[1], wk.shape[1], wv.shape[1]
    back = stashed[0]
    arrived, returned = cross_pipe(sent_forward[0], sent_backward[0])
    cosine, sine = rope_tables(back.shape[0])

    m2, o2, inv, basis, wq, narrow, turned = project(
        back, norm_gain, subspace, wq, wk, wv, wo
    )
    inner, out_give, out_keep, x = backward(
        back, loss_grad, returned, m2, o2, inv, cosine, sine
    )
    out_got = swap(out_give, "dp", 1)
    inner_got = swap(inner, "dp", 1)
    base, unit, fbase = bases(
        back, loss_grad, returned, new_coeffs, arrived, basis, turned, inv, out_keep
    )
    out_pair = add_after(out_keep, out_got, fbase)
    out_got = swap(out_pair, "dp", 2)
    pair, x = gain_part(basis, wq, narrow, inner, inner_got, x, out_pair)
    pair_got = swap(pair, "dp", 2)
    x_got = swap(x, "tensor", 2)
    y = forward(new_coeffs, arrived, turned, m2, o2, cosine, sine, pair)
    y_got = swap(y, "tensor", 2)
    out_own = add_after(out_pair, out_got, y)
    out_other = swap(out_own, "dp", 1)
    x = merge(x, x_got, out_own)
    x_got = swap(x, "tensor", 1)
    grad_o = outward_grad(basis, [out_own], [out_other], x)
    sizes = (nq // 2, nq - nq // 2, nk + nv)
    own = own_pieces(pair, pair_got, sizes, *in_hbm((grad_o,)))
    other = [swap(piece, "dp", 1) for piece in own]
    gain = gain_total(x, x_got, own[0])
    gain_got = swap(gain, "dp", 2)
    y = add_after(y, y_got, gain, rows=back.shape[0])
    y_got = swap(y, "tensor", 1)
    grad_q, grad_k, grad_v = inward_grads(basis, norm_gain, own, other, (nq, nk, nv), y)
    gain = add_after(gain, gain_got, *in_hbm((grad_v,)))
    gain_other = swap(gain, "dp", 1)
    forward_out, backward_out, grad_gain = results(
        wide, grad_v, fbase, y, y_got, base, unit, x, x_got, back, inv, gain, gain_other
    )
    return (
        forward_out[None],
        backward_out[None],
        grad_q[None],
        grad_k[None],
        grad_v[None],
        grad_o[None],
        grad_gain,
    )


def solution(mesh):
    return jax.shard_map(
        body,
        mesh=mesh,
        in_specs=(
            P("dp", None),
            P("dp", None),
            P("pipe", "dp", None),
            P("pipe", "dp", None),
            P("pipe", "dp", None),
            P(),
            P("pipe", None),
            P("pipe", None, "tensor"),
            P("pipe", None, "tensor"),
            P("pipe", None, "tensor"),
            P("pipe", "tensor", None),
        ),
        out_specs=(
            P("pipe", "dp", None),
            P("pipe", "dp", None),
            P("pipe", "dp", "tensor"),
            P("pipe", "dp", "tensor"),
            P("pipe", "dp", "tensor"),
            P("pipe", "tensor", "dp"),
            P("pipe", None),
        ),
        check_vma=False,
    )
```

```python
import functools
import math

import jax
import jax.numpy as jnp
import numpy as np
from jax import lax
from jax.experimental import pallas as pl
from jax.experimental.pallas import tpu as pltpu
from jax.sharding import PartitionSpec as P

HD = 128
EPSILON = 1e-05
ROPE_BASE = 500000.0
BF = jnp.bfloat16
F32 = jnp.float32
VMEM_BYTES = 24 * 1024 * 1024
CHUNK = 512
PIECE = 1024
AHEAD = 4
LOG2E = 1.4426950408889634


def shifted(x, axis, by):
    devices = lax.axis_size(axis)
    pairs = [(i, i + by) for i in range(devices) if 0 <= i + by < devices]
    return lax.ppermute(x, axis, pairs)


def swap(x, axis, bit):
    devices = lax.axis_size(axis)
    return lax.ppermute(x, axis, [(i, i ^ bit) for i in range(devices)])


def cross_pipe(sent_forward, sent_backward):
    if lax.axis_size("pipe") != 2:
        return shifted(sent_forward, "pipe", 1), shifted(sent_backward, "pipe", -1)
    first = lax.axis_index("pipe") == 0
    got = swap(jnp.where(first, sent_forward, sent_backward), "pipe", 1)
    return got, got


def add_wide(a, b):
    return a.astype(F32) + b.astype(F32)


def nt(a, b):
    return lax.dot_general(a, b, (((1,), (1,)), ((), ())), preferred_element_type=F32)


def nn(a, b):
    return jnp.dot(a, b, preferred_element_type=F32)


def split(x, parts):
    out = []
    for _ in range(parts):
        piece = x.astype(BF)
        out.append(piece)
        x = x - piece.astype(F32)
    return out


def rope_tables(length):
    half = HD // 2
    frequency = np.float32(ROPE_BASE) ** (-2.0 * np.arange(half, dtype=np.float32) / HD)
    angles = np.arange(length, dtype=np.float32)[:, None] * frequency.astype(np.float32)
    cosine, sine = np.cos(angles), np.sin(angles)
    tables = (np.concatenate([cosine, cosine], 1), np.concatenate([-sine, sine], 1))
    return tuple(jnp.asarray(t, dtype=F32) for t in tables)


def rope(x, cosine, sine):
    return x * cosine + pltpu.roll(x, HD // 2, 1) * sine


def unrope(x, cosine, sine):
    return x * cosine - pltpu.roll(x, HD // 2, 1) * sine


def inverse_root(square_sum, width):
    return 1.0 / jnp.sqrt(square_sum / width + EPSILON)


def vmem(count):
    return [pl.BlockSpec(memory_space=pltpu.VMEM)] * count


def in_hbm(arrays):
    return tuple(pltpu.with_memory_space_constraint(a, pltpu.HBM) for a in arrays)


def cost(flops, num_bytes, exps=0):
    return pl.CostEstimate(flops=flops, bytes_accessed=num_bytes, transcendentals=exps)


def project_kernel(
    back_hbm, gain_hbm, u_hbm, wq_hbm, wk_hbm, wv_hbm, wo_hbm,
    m_ref, o_ref, inv_ref, u, wq, narrow, turned,
    back, gain, wo, scaled, m_acc, sems,
):
    wide, rank = u.shape
    nq = wq.shape[1]
    nk = wk_hbm.shape[1]
    parts = wide // PIECE
    pieces = [pl.ds(i * PIECE, PIECE) for i in range(parts)]
    pairs = [(back_hbm, back), (gain_hbm, gain)]
    pairs += [(u_hbm.at[at, :], u.at[at, :]) for at in pieces]
    pairs += [(wq_hbm.at[at, :], wq.at[at, :]) for at in pieces[:2]]
    pairs += [(wk_hbm, narrow.at[:, pl.ds(0, nk)])]
    pairs += [(wv_hbm, narrow.at[:, pl.ds(nk, narrow.shape[1] - nk)])]
    pairs += [(wq_hbm.at[at, :], wq.at[at, :]) for at in pieces[2:]]
    block = wo.shape[0] // parts
    blocks = [pl.ds(i * block, block) for i in range(parts)]
    pairs += [(wo_hbm.at[at, :], wo.at[at, :]) for at in blocks]
    copies = [
        pltpu.make_async_copy(source, target, sems.at[n])
        for n, (source, target) in enumerate(pairs)
    ]
    started = 0

    def start_to(count):
        nonlocal started
        for copy in copies[started:count]:
            copy.start()
        started = max(started, min(count, len(copies)))

    def wait(n):
        start_to(n + 1 + AHEAD)
        copies[n].wait()

    start_to(2 + parts + AHEAD)
    copies[0].wait()
    copies[1].wait()
    square = jnp.zeros((back.shape[0], HD), F32)
    for i, at in enumerate(pieces):
        copies[2 + i].wait()
        turned[:, at] = u[at, :].T
        scaled[:, at] = (turned[:, at].astype(F32) * gain[:, at]).astype(BF)
        decoded = nn(back[...], turned[:, at])
        for side in range(0, PIECE, HD):
            part = decoded[:, side : side + HD]
            square = square + part * part
    inv_ref[...] = jnp.broadcast_to(
        inverse_root(jnp.sum(square, axis=1, keepdims=True), wide), inv_ref.shape
    )
    place = 2 + parts
    for i, at in enumerate(pieces):
        if i == 2:
            wait(place)
            wait(place + 1)
            place += 2
            for p, piece in enumerate(split(nn(scaled[...], narrow[...]), 2)):
                m_ref[p * rank : (p + 1) * rank, nq:] = piece
        wait(place)
        place += 1
        part = nn(scaled[:, at], wq[at, :])
        if i == 0:
            m_acc[...] = part
        else:
            m_acc[...] += part
    for p, piece in enumerate(split(m_acc[...], 2)):
        m_ref[p * rank : (p + 1) * rank, :nq] = piece
    for _ in blocks:
        wait(place)
        place += 1
    o_ref[...] = nn(wo[...], u[...]).astype(BF)


def project(back, gain, basis, wq, wk, wv, wo):
    wide, rank = basis.shape
    length = back.shape[0]
    ne = wo.shape[0]
    nq = wq.shape[1]
    rest = wk.shape[1] + wv.shape[1]
    operands = in_hbm((back, gain, basis, wq, wk, wv, wo))
    return pl.pallas_call(
        project_kernel,
        in_specs=[pl.BlockSpec(memory_space=pltpu.HBM)] * len(operands),
        out_specs=vmem(7),
        out_shape=[
            jax.ShapeDtypeStruct((2 * rank, nq + rest), BF),
            jax.ShapeDtypeStruct((ne, rank), BF),
            jax.ShapeDtypeStruct((length, HD), F32),
            jax.ShapeDtypeStruct(basis.shape, BF),
            jax.ShapeDtypeStruct(wq.shape, BF),
            jax.ShapeDtypeStruct((wide, rest), BF),
            jax.ShapeDtypeStruct((rank, wide), BF),
        ],
        scratch_shapes=[
            pltpu.VMEM(back.shape, BF),
            pltpu.VMEM(gain.shape, F32),
            pltpu.VMEM(wo.shape, BF),
            pltpu.VMEM((rank, wide), BF),
            pltpu.VMEM((rank, nq), F32),
            pltpu.SemaphoreType.DMA((4 + 3 * (wide // PIECE),)),
        ],
        compiler_params=pltpu.CompilerParams(vmem_limit_bytes=VMEM_BYTES * 3 // 2),
        cost_estimate=cost(6 * 10**9, 20 * 10**6),
        name="project_weights",
    )(*operands)


def project_heads(coeffs, inv, m_ref, cosine, sine, q, k, v1):
    length = coeffs.shape[0]
    heads = q.shape[0] // length
    twice = jnp.concatenate([coeffs, coeffs], axis=1)
    for h in range(0, heads, 2):
        both = nn(twice, m_ref[:, h * HD : (h + 2) * HD]) * inv
        for part, at in ((both[:, :HD], h * length), (both[:, HD:], (h + 1) * length)):
            q[at : at + length, :] = rope(part, cosine, sine).astype(BF)
    part = nn(twice, m_ref[:, heads * HD :]) * inv
    k[...] = rope(part[:, :HD], cosine, sine).astype(BF)
    v1[:, :HD] = part[:, HD:].astype(BF)
    v1[:, HD:] = jnp.ones_like(v1[:, HD:])


def exps_of(scores, exps, low, length):
    row = lax.broadcasted_iota(jnp.int32, (length, length), 0)
    column = lax.broadcasted_iota(jnp.int32, (length, length), 1)
    causal = row >= column

    def one(h, _):
        at = pl.ds(pl.multiple_of(h * length, length), length)
        s = jnp.where(causal, scores[at, :], -jnp.inf)
        top = jnp.max(s, axis=1, keepdims=True)
        e = jnp.exp2((s - top) * (LOG2E / math.sqrt(HD)))
        if exps is not None:
            exps[at, :] = e
        low[at, :] = e.astype(BF)
        return 0

    lax.fori_loop(0, scores.shape[0] // length, one, 0, unroll=2)


def backward_kernel(
    back_ref, loss_ref, sent_ref, m_ref, o_ref, inv_ref, cos_ref, sin_ref,
    inner_ref, out_give_ref, out_keep_ref, x_ref,
    q, k, v1, gh, ghs, scores, low, mixed, gp, ds, dq, heads, grads, inner, out_inner,
):
    length, rank = back_ref.shape
    ne = o_ref.shape[0]
    count = ne // HD
    scale = 1.0 / math.sqrt(HD)
    last = lax.axis_size("pipe") - 1
    is_last = lax.axis_index("pipe") == last
    back = back_ref[...]
    up = jnp.where(is_last, loss_ref[...], sent_ref[...])
    cosine, sine = cos_ref[...], sin_ref[...]
    inv = inv_ref[...]
    project_heads(back, inv[:, :1], m_ref, cosine, sine, q, k, v1)
    scores[...] = nt(q[...], k[...])
    for h in range(0, count, 2):
        both = nt(up, o_ref[h * HD : (h + 2) * HD, :]).astype(BF)
        gh[h * length : (h + 1) * length, :] = both[:, :HD]
        gh[(h + 1) * length : (h + 2) * length, :] = both[:, HD:]
    exps_of(scores, scores, low, length)
    mixed[...] = nn(low[...], v1[...])
    gp[...] = nt(gh[...], v1[:, :HD])

    for h in range(count):
        at = slice(h * length, (h + 1) * length)
        inverse = 1.0 / mixed[at, HD:]
        out = mixed[at, :HD] * inverse
        heads[:, h * HD : (h + 1) * HD] = out.astype(BF)
        grad = gh[at, :].astype(F32)
        ghs[at, :] = (grad * inverse).astype(BF)
        delta = jnp.sum(grad * out, axis=1, keepdims=True)
        factor = inverse * scale
        for side in range(0, length, HD):
            part = scores[at, side : side + HD] * factor
            ds[at, side : side + HD] = (part * (gp[at, side : side + HD] - delta)).astype(BF)

    dq[...] = nn(ds[...], k[...])
    for h in range(count):
        part = dq[h * length : (h + 1) * length, :]
        grads[:, h * HD : (h + 1) * HD] = unrope(part, cosine, sine).astype(BF)
    dk = nn(q[...].T, ds[...]).T
    grads[:, ne : ne + HD] = unrope(dk, cosine, sine).astype(BF)
    grads[:, ne + HD :] = nn(ghs[...].T, low[...]).T.astype(BF)
    unit = (back.astype(F32) * inv[:, :1]).astype(BF)
    half = rank // 2
    core = lax.axis_index("dp") & 1
    mine = pl.ds(pl.multiple_of(core * half, half), half)
    theirs = pl.ds(pl.multiple_of((1 - core) * half, half), half)
    inner[...] = nn(unit.T, grads[...]).astype(BF)
    inner_ref[:half, :] = inner[mine, :]
    inner_ref[half:, :] = inner[theirs, :]
    out_inner[...] = nn(up.T, heads[...]).astype(BF)
    out_keep_ref[...] = out_inner[mine, :]
    out_give_ref[...] = out_inner[theirs, :]
    x_ref[...] = nt(grads[...], m_ref[:rank, :]).astype(BF)


def backward(back, loss, sent, m2, o2, inv, cosine, sine):
    length, rank = back.shape
    ne = o2.shape[0]
    total = m2.shape[1]
    assert total == ne + 2 * HD
    stack = ne // HD * length
    return pl.pallas_call(
        backward_kernel,
        in_specs=vmem(8),
        out_specs=vmem(4),
        out_shape=[
            jax.ShapeDtypeStruct((rank, total), BF),
            jax.ShapeDtypeStruct((rank // 2, ne), BF),
            jax.ShapeDtypeStruct((rank // 2, ne), BF),
            jax.ShapeDtypeStruct((length, rank), BF),
        ],
        scratch_shapes=[
            pltpu.VMEM((stack, HD), BF),
            pltpu.VMEM((length, HD), BF),
            pltpu.VMEM((length, 2 * HD), BF),
            pltpu.VMEM((stack, HD), BF),
            pltpu.VMEM((stack, HD), BF),
            pltpu.VMEM((stack, length), F32),
            pltpu.VMEM((stack, length), BF),
            pltpu.VMEM((stack, 2 * HD), F32),
            pltpu.VMEM((stack, length), F32),
            pltpu.VMEM((stack, length), BF),
            pltpu.VMEM((stack, HD), F32),
            pltpu.VMEM((length, ne), BF),
            pltpu.VMEM((length, total), BF),
            pltpu.VMEM((rank, total), BF),
            pltpu.VMEM((rank, ne), BF),
        ],
        compiler_params=pltpu.CompilerParams(vmem_limit_bytes=VMEM_BYTES),
        cost_estimate=cost(10**4, 10**3),
        name="attention_backward",
    )(back, loss, sent, m2, o2, inv, cosine, sine)


def bases_kernel(
    back_ref, loss_ref, returned_ref, new_ref, arrived_ref, u_ref, turned_ref, inv_ref, after,
    base_ref, unit_ref, fbase_ref, g_ref,
):
    rank = u_ref.shape[1]
    for i, piece in enumerate(split(nn(turned_ref[...], u_ref[...]), 3)):
        g_ref[i * rank : (i + 1) * rank, :] = piece
    is_last = lax.axis_index("pipe") == lax.axis_size("pipe") - 1
    is_first = lax.axis_index("pipe") == 0
    up = jnp.where(is_last, loss_ref[...], returned_ref[...])
    coeffs = jnp.where(is_first, new_ref[...], arrived_ref[...])
    base_ref[...] = nn(jnp.concatenate([up] * 3, axis=1), g_ref[...])
    fbase_ref[...] = nn(jnp.concatenate([coeffs] * 3, axis=1), g_ref[...])
    unit_ref[...] = nn(jnp.concatenate([back_ref[...]] * 3, axis=1), g_ref[...]) * inv_ref[:, :1]


def bases(back, loss, returned, new, arrived, basis, turned, inv, after):
    length, rank = back.shape
    return pl.pallas_call(
        bases_kernel,
        in_specs=vmem(8) + [pl.BlockSpec(memory_space=pl.ANY)],
        out_specs=vmem(3),
        out_shape=[jax.ShapeDtypeStruct((length, rank), F32)] * 3,
        scratch_shapes=[pltpu.VMEM((3 * rank, rank), BF)],
        compiler_params=pltpu.CompilerParams(vmem_limit_bytes=VMEM_BYTES // 2),
        cost_estimate=cost(10**4, 10**3),
        name="encoded_again",
    )(back, loss, returned, new, arrived, basis, turned, inv, after)


def forward_kernel(
    new_ref, sent_ref, turned_ref, m_ref, o_ref, cos_ref, sin_ref, after,
    y_ref, q, k, v1, scores, low, mixed, heads,
):
    length, rank = new_ref.shape
    wide = turned_ref.shape[1]
    is_first = lax.axis_index("pipe") == 0
    coeffs = jnp.where(is_first, new_ref[...], sent_ref[...])
    square = jnp.zeros((length, HD), F32)
    for at in range(0, wide, PIECE):
        decoded = nn(coeffs, turned_ref[:, at : at + PIECE])
        for side in range(0, PIECE, HD):
            part = decoded[:, side : side + HD]
            square = square + part * part
    inv = inverse_root(jnp.sum(square, axis=1, keepdims=True), wide)
    project_heads(coeffs, inv, m_ref, cos_ref[...], sin_ref[...], q, k, v1)
    scores[...] = nt(q[...], k[...])
    exps_of(scores, None, low, length)
    mixed[...] = nn(low[...], v1[...])
    for h in range(heads.shape[1] // HD):
        at = slice(h * length, (h + 1) * length)
        heads[:, h * HD : (h + 1) * HD] = (mixed[at, :HD] / mixed[at, HD:]).astype(BF)
    y_ref[...] = nn(heads[...], o_ref[...]).astype(BF)


def forward(new, sent, turned, m2, o2, cosine, sine, after):
    length, rank = new.shape
    ne = o2.shape[0]
    stack = ne // HD * length
    return pl.pallas_call(
        forward_kernel,
        in_specs=vmem(7) + [pl.BlockSpec(memory_space=pl.ANY)],
        out_specs=pl.BlockSpec(memory_space=pltpu.VMEM),
        out_shape=jax.ShapeDtypeStruct((length, rank), BF),
        scratch_shapes=[
            pltpu.VMEM((stack, HD), BF),
            pltpu.VMEM((length, HD), BF),
            pltpu.VMEM((length, 2 * HD), BF),
            pltpu.VMEM((stack, length), F32),
            pltpu.VMEM((stack, length), BF),
            pltpu.VMEM((stack, 2 * HD), F32),
            pltpu.VMEM((length, ne), BF),
        ],
        compiler_params=pltpu.CompilerParams(vmem_limit_bytes=VMEM_BYTES),
        cost_estimate=cost(10**4, 10**3),
        name="attention_forward",
    )(new, sent, turned, m2, o2, cosine, sine, after)


def write_split(ref, value):
    high, low = split(value, 2)
    both = jnp.concatenate([high.astype(F32), low.astype(F32)], axis=0)
    ref[ref.shape[0] - 16 :, :] = both.astype(BF)


def read_split(ref):
    both = ref[ref.shape[0] - 16 :, :].astype(F32)
    return both[:8] + both[8:]


def gain_kernel(
    u_ref, wq_ref, narrow_ref, inner_ref, got_ref, x_ref, after,
    pair_ref, out_ref, turned, rows_f32,
):
    nq = wq_ref.shape[1]
    rows = u_ref.shape[0] // 2
    rank = u_ref.shape[1]
    half = inner_ref.shape[0] // 2
    core = lax.axis_index("dp") & 1
    mine = add_wide(inner_ref[:half, :], got_ref[half:, :]).astype(BF)
    theirs = add_wide(inner_ref[half:, :], got_ref[:half, :]).astype(BF)
    pair_ref[...] = mine
    out_ref[: x_ref.shape[0], :] = x_ref[...]
    turned[:, pl.ds(pl.multiple_of(core * half, half), half)] = mine.T
    turned[:, pl.ds(pl.multiple_of((1 - core) * half, half), half)] = theirs.T
    for at in range(0, rows, CHUNK):
        place = pl.ds(pl.multiple_of(core * rows + at, CHUNK), CHUNK)
        against = nn(wq_ref[place, :], turned[:nq, :])
        against += nn(narrow_ref[place, :], turned[nq:, :])
        terms = against * u_ref[place, :].astype(F32)
        folded = sum(terms[:, side : side + HD] for side in range(0, terms.shape[1], HD))
        line = jnp.sum(folded.T, axis=0, keepdims=True)
        for side in range(0, CHUNK, rank):
            row = (at + side) // rank
            rows_f32[row : row + 1, :] = line[:, side : side + rank]
    write_split(out_ref, rows_f32[...])


def gain_part(basis, wq, narrow, inner, got, x, after):
    wide, rank = basis.shape
    assert wide // 2 == 8 * rank
    held = tuple(pltpu.with_memory_space_constraint(a, pltpu.VMEM) for a in (basis, wq, narrow))
    return pl.pallas_call(
        gain_kernel,
        in_specs=vmem(6) + [pl.BlockSpec(memory_space=pl.ANY)],
        out_specs=vmem(2),
        out_shape=[
            jax.ShapeDtypeStruct((rank // 2, inner.shape[1]), BF),
            jax.ShapeDtypeStruct((x.shape[0] + 16, rank), BF),
        ],
        scratch_shapes=[
            pltpu.VMEM((inner.shape[1], rank), BF),
            pltpu.VMEM((8, rank), F32),
        ],
        compiler_params=pltpu.CompilerParams(vmem_limit_bytes=VMEM_BYTES),
        cost_estimate=cost(10**4, 10**3),
        name="pair_sum_and_gain_gradient",
    )(*held, inner, got, x, after)


def merge_kernel(a_ref, b_ref, after, out_ref):
    rest = out_ref.shape[0] - 16
    out_ref[:rest, :] = add_wide(a_ref[:rest, :], b_ref[:rest, :]).astype(BF)
    write_split(out_ref, read_split(a_ref) + read_split(b_ref))


def total_kernel(a_ref, b_ref, after, out_ref):
    out_ref[...] = read_split(a_ref) + read_split(b_ref)


def own_kernel(a_ref, b_ref, after, *out_refs):
    at = 0
    for ref in out_refs:
        size = ref.shape[1]
        ref[...] = add_wide(a_ref[:, at : at + size], b_ref[:, at : at + size]).astype(BF)
        at += size


def small_kernel(kernel, name, out_shape, a, b, after):
    return pl.pallas_call(
        kernel,
        in_specs=vmem(2) + [pl.BlockSpec(memory_space=pl.ANY)],
        out_specs=jax.tree.map(lambda _: pl.BlockSpec(memory_space=pltpu.VMEM), out_shape),
        out_shape=out_shape,
        compiler_params=pltpu.CompilerParams(vmem_limit_bytes=VMEM_BYTES // 2),
        cost_estimate=cost(10**4, 10**3),
        name=name,
    )(a, b, after)


def merge(a, b, after):
    return small_kernel(merge_kernel, "sum_with_gain", jax.ShapeDtypeStruct(a.shape, BF), a, b, after)


def gain_total(a, b, after):
    shape = jax.ShapeDtypeStruct((8, a.shape[1]), F32)
    return small_kernel(total_kernel, "gain_total", shape, a, b, after)


def own_pieces(a, b, sizes, after):
    shapes = [jax.ShapeDtypeStruct((a.shape[0], n), BF) for n in sizes]
    return small_kernel(own_kernel, "sum_over_y", shapes, a, b, after)


def add_kernel(a_ref, b_ref, after, out_ref):
    rows = out_ref.shape[0]
    out_ref[...] = add_wide(a_ref[:rows, :], b_ref[:rows, :]).astype(out_ref.dtype)


def add_after(a, b, after, rows=None):
    shape = jax.ShapeDtypeStruct((rows or a.shape[0], a.shape[1]), a.dtype)
    return small_kernel(add_kernel, "pair_sum", shape, a, b, after)


def gather_halves(own_refs, other_refs, whole):
    half = whole.shape[0] // 2
    core = lax.axis_index("dp") & 1
    at = 0
    for own_ref, other_ref in zip(own_refs, other_refs):
        columns = pl.ds(at, own_ref.shape[1])
        whole[pl.ds(pl.multiple_of(core * half, half), half), columns] = own_ref[...]
        whole[pl.ds(pl.multiple_of((1 - core) * half, half), half), columns] = other_ref[...]
        at += own_ref.shape[1]


def inward_kernel(pieces, u_ref, gain_ref, *refs):
    own_refs, other_refs = refs[:pieces], refs[pieces : 2 * pieces]
    q_ref, k_ref, v_ref, inner = refs[-4:]
    nq, nk = q_ref.shape[1], k_ref.shape[1]
    block = q_ref.shape[0]

    @pl.when(pl.program_id(0) == 0)
    def _():
        gather_halves(own_refs, other_refs, inner)

    step = lax.axis_index("dp") * pl.num_programs(0) + pl.program_id(0)
    rows = pl.ds(pl.multiple_of(step * block, block), block)
    gain = jnp.broadcast_to(gain_ref[:, rows], (HD, block)).T[:, :1]
    grad = nn(u_ref[rows, :], inner[...]) * gain
    q_ref[...] = grad[:, :nq].astype(BF)
    k_ref[...] = grad[:, nq : nq + nk].astype(BF)
    v_ref[...] = grad[:, nq + nk :].astype(BF)


def outward_kernel(pieces, u_ref, *refs):
    own_refs, other_refs = refs[:pieces], refs[pieces : 2 * pieces]
    o_ref, inner = refs[-2:]

    @pl.when(pl.program_id(0) == 0)
    def _():
        gather_halves(own_refs, other_refs, inner)

    block, rows = o_ref.shape
    at = pl.multiple_of(pl.program_id(0) * block, block)
    basis = u_ref[pl.ds(pl.multiple_of(lax.axis_index("dp") * rows, rows), rows), :]
    o_ref[...] = nt(inner[:, pl.ds(at, block)].T, basis).astype(BF)


STEPS = 2


def inward_grads(basis, gain, own, other, sizes, after):
    wide, rank = basis.shape
    rows = wide // lax.axis_size("dp")
    block = rows // STEPS
    return pl.pallas_call(
        functools.partial(inward_kernel, len(own)),
        grid=(STEPS,),
        in_specs=vmem(2 + 2 * len(own)) + [pl.BlockSpec(memory_space=pl.ANY)],
        out_specs=[pl.BlockSpec((block, n), lambda i: (i, 0)) for n in sizes],
        scratch_shapes=[pltpu.VMEM((rank, sum(sizes)), BF)],
        out_shape=[jax.ShapeDtypeStruct((rows, n), BF) for n in sizes],
        compiler_params=pltpu.CompilerParams(vmem_limit_bytes=VMEM_BYTES),
        cost_estimate=cost(10**4, 10**3),
        name="inward_weight_gradients",
    )(basis, gain, *own, *other, after)


def outward_grad(basis, own, other, after):
    wide, rank = basis.shape
    rows = wide // lax.axis_size("dp")
    ne = sum(piece.shape[1] for piece in own)
    return pl.pallas_call(
        functools.partial(outward_kernel, len(own)),
        grid=(STEPS,),
        in_specs=vmem(1 + 2 * len(own)) + [pl.BlockSpec(memory_space=pl.ANY)],
        out_specs=pl.BlockSpec((ne // STEPS, rows), lambda i: (i, 0)),
        scratch_shapes=[pltpu.VMEM((rank, ne), BF)],
        out_shape=jax.ShapeDtypeStruct((ne, rows), BF),
        compiler_params=pltpu.CompilerParams(vmem_limit_bytes=VMEM_BYTES),
        cost_estimate=cost(10**4, 10**3),
        name="output_weight_gradient",
    )(basis, *own, *other, after)


def results_kernel(
    wide, fbase_ref, y_ref, ygot_ref, base_ref, unit_ref, x_ref, xgot_ref, back_ref, inv_ref,
    gain_ref, gain_other_ref, after,
    f_ref, b_ref, gain_out_ref,
):
    f_ref[...] = (fbase_ref[...] + add_wide(y_ref[...], ygot_ref[...])).astype(BF)
    length = back_ref.shape[0]
    x = add_wide(x_ref[:length, :], xgot_ref[:length, :])
    inv = inv_ref[:, :1]
    along = jnp.sum(x * back_ref[...].astype(F32), axis=1, keepdims=True)
    middle = along * inv * (1.0 / wide)
    b_ref[...] = (base_ref[...] + (x - unit_ref[...] * middle) * inv).astype(BF)
    core = lax.axis_index("dp") & 1
    half = wide // 2
    rank = gain_ref.shape[1]
    for row in range(half // rank):
        mine = pl.ds(pl.multiple_of(core * half + row * rank, rank), rank)
        theirs = pl.ds(pl.multiple_of((1 - core) * half + row * rank, rank), rank)
        gain_out_ref[:, mine] = gain_ref[row : row + 1, :]
        gain_out_ref[:, theirs] = gain_other_ref[row : row + 1, :]


def results(wide, after, *operands):
    shape = operands[0].shape
    held = tuple(pltpu.with_memory_space_constraint(a, pltpu.VMEM) for a in operands)
    return pl.pallas_call(
        functools.partial(results_kernel, wide),
        in_specs=vmem(len(operands)) + [pl.BlockSpec(memory_space=pl.ANY)],
        out_specs=vmem(3),
        out_shape=[jax.ShapeDtypeStruct(shape, BF)] * 2 + [jax.ShapeDtypeStruct((1, wide), F32)],
        compiler_params=pltpu.CompilerParams(vmem_limit_bytes=VMEM_BYTES // 2),
        cost_estimate=cost(10**4, 10**3),
        name="section_results",
    )(*held, *in_hbm((after,)))


def body(
    new_coeffs,
    loss_grad,
    sent_forward,
    sent_backward,
    stashed,
    subspace,
    norm_gain,
    w_query,
    w_key,
    w_value,
    w_output,
):
    wide = subspace.shape[0]
    wq, wk, wv, wo = w_query[0], w_key[0], w_value[0], w_output[0]
    nq, nk, nv = wq.shape[1], wk.shape[1], wv.shape[1]
    back = stashed[0]
    arrived, returned = cross_pipe(sent_forward[0], sent_backward[0])
    cosine, sine = rope_tables(back.shape[0])

    m2, o2, inv, basis, wq, narrow, turned = project(
        back, norm_gain, subspace, wq, wk, wv, wo
    )
    inner, out_give, out_keep, x = backward(
        back, loss_grad, returned, m2, o2, inv, cosine, sine
    )
    out_got = swap(out_give, "dp", 1)
    inner_got = swap(inner, "dp", 1)
    base, unit, fbase = bases(
        back, loss_grad, returned, new_coeffs, arrived, basis, turned, inv, out_keep
    )
    out_pair = add_after(out_keep, out_got, fbase)
    out_got = swap(out_pair, "dp", 2)
    pair, x = gain_part(basis, wq, narrow, inner, inner_got, x, out_pair)
    pair_got = swap(pair, "dp", 2)
    x_got = swap(x, "tensor", 2)
    y = forward(new_coeffs, arrived, turned, m2, o2, cosine, sine, pair)
    y_got = swap(y, "tensor", 2)
    ne = wo.shape[0]
    out_own = own_pieces(out_pair, out_got, (ne // 2, ne - ne // 2), y)
    out_other = [swap(piece, "dp", 1) for piece in out_own]
    x = merge(x, x_got, out_own[0])
    x_got = swap(x, "tensor", 1)
    grad_o = outward_grad(basis, out_own, out_other, x)
    sizes = (nq // 2, nq - nq // 2, nk + nv)
    own = own_pieces(pair, pair_got, sizes, *in_hbm((grad_o,)))
    other = [swap(piece, "dp", 1) for piece in own]
    y = add_after(y, y_got, own[0])
    y_got = swap(y, "tensor", 1)
    gain = gain_total(x, x_got, y)
    gain_got = swap(gain, "dp", 2)
    grad_q, grad_k, grad_v = inward_grads(basis, norm_gain, own, other, (nq, nk, nv), gain)
    gain = add_after(gain, gain_got, *in_hbm((grad_v,)))
    gain_other = swap(gain, "dp", 1)
    forward_out, backward_out, grad_gain = results(
        wide, grad_v, fbase, y, y_got, base, unit, x, x_got, back, inv, gain, gain_other
    )
    return (
        forward_out[None],
        backward_out[None],
        grad_q[None],
        grad_k[None],
        grad_v[None],
        grad_o[None],
        grad_gain,
    )


def solution(mesh):
    return jax.shard_map(
        body,
        mesh=mesh,
        in_specs=(
            P("dp", None),
            P("dp", None),
            P("pipe", "dp", None),
            P("pipe", "dp", None),
            P("pipe", "dp", None),
            P(),
            P("pipe", None),
            P("pipe", None, "tensor"),
            P("pipe", None, "tensor"),
            P("pipe", None, "tensor"),
            P("pipe", "tensor", None),
        ),
        out_specs=(
            P("pipe", "dp", None),
            P("pipe", "dp", None),
            P("pipe", "dp", "tensor"),
            P("pipe", "dp", "tensor"),
            P("pipe", "dp", "tensor"),
            P("pipe", "tensor", "dp"),
            P("pipe", None),
        ),
        check_vma=False,
    )
```

```python
import functools
import math

import jax
import jax.numpy as jnp
import numpy as np
from jax import lax
from jax.experimental import pallas as pl
from jax.experimental.pallas import tpu as pltpu
from jax.sharding import PartitionSpec as P

HD = 128
EPSILON = 1e-05
ROPE_BASE = 500000.0
BF = jnp.bfloat16
F32 = jnp.float32
VMEM_BYTES = 24 * 1024 * 1024
CHUNK = 512
PIECE = 1024
AHEAD = 4
LOG2E = 1.4426950408889634


def shifted(x, axis, by):
    devices = lax.axis_size(axis)
    pairs = [(i, i + by) for i in range(devices) if 0 <= i + by < devices]
    return lax.ppermute(x, axis, pairs)


def swap(x, axis, bit):
    devices = lax.axis_size(axis)
    return lax.ppermute(x, axis, [(i, i ^ bit) for i in range(devices)])


def cross_pipe(sent_forward, sent_backward):
    if lax.axis_size("pipe") != 2:
        return shifted(sent_forward, "pipe", 1), shifted(sent_backward, "pipe", -1)
    first = lax.axis_index("pipe") == 0
    got = swap(jnp.where(first, sent_forward, sent_backward), "pipe", 1)
    return got, got


def add_wide(a, b):
    return a.astype(F32) + b.astype(F32)


def nt(a, b):
    return lax.dot_general(a, b, (((1,), (1,)), ((), ())), preferred_element_type=F32)


def nn(a, b):
    return jnp.dot(a, b, preferred_element_type=F32)


def split(x, parts):
    out = []
    for _ in range(parts):
        piece = x.astype(BF)
        out.append(piece)
        x = x - piece.astype(F32)
    return out


def rope_tables(length):
    half = HD // 2
    frequency = np.float32(ROPE_BASE) ** (-2.0 * np.arange(half, dtype=np.float32) / HD)
    angles = np.arange(length, dtype=np.float32)[:, None] * frequency.astype(np.float32)
    cosine, sine = np.cos(angles), np.sin(angles)
    tables = (np.concatenate([cosine, cosine], 1), np.concatenate([-sine, sine], 1))
    return tuple(jnp.asarray(t, dtype=F32) for t in tables)


def rope(x, cosine, sine):
    return x * cosine + pltpu.roll(x, HD // 2, 1) * sine


def unrope(x, cosine, sine):
    return x * cosine - pltpu.roll(x, HD // 2, 1) * sine


def inverse_root(square_sum, width):
    return 1.0 / jnp.sqrt(square_sum / width + EPSILON)


def vmem(count):
    return [pl.BlockSpec(memory_space=pltpu.VMEM)] * count


def in_hbm(arrays):
    return tuple(pltpu.with_memory_space_constraint(a, pltpu.HBM) for a in arrays)


def cost(flops, num_bytes, exps=0):
    return pl.CostEstimate(flops=flops, bytes_accessed=num_bytes, transcendentals=exps)


def project_kernel(
    back_hbm, gain_hbm, u_hbm, wq_hbm, wk_hbm, wv_hbm, wo_hbm,
    m_ref, o_ref, inv_ref, u, wq, narrow, turned,
    back, gain, wo, scaled, m_acc, sems,
):
    wide, rank = u.shape
    nq = wq.shape[1]
    nk = wk_hbm.shape[1]
    parts = wide // PIECE
    pieces = [pl.ds(i * PIECE, PIECE) for i in range(parts)]
    pairs = [(back_hbm, back), (gain_hbm, gain)]
    pairs += [(u_hbm.at[at, :], u.at[at, :]) for at in pieces]
    pairs += [(wq_hbm.at[at, :], wq.at[at, :]) for at in pieces[:2]]
    pairs += [(wk_hbm, narrow.at[:, pl.ds(0, nk)])]
    pairs += [(wv_hbm, narrow.at[:, pl.ds(nk, narrow.shape[1] - nk)])]
    pairs += [(wq_hbm.at[at, :], wq.at[at, :]) for at in pieces[2:]]
    block = wo.shape[0] // parts
    blocks = [pl.ds(i * block, block) for i in range(parts)]
    pairs += [(wo_hbm.at[at, :], wo.at[at, :]) for at in blocks]
    copies = [
        pltpu.make_async_copy(source, target, sems.at[n])
        for n, (source, target) in enumerate(pairs)
    ]
    started = 0

    def start_to(count):
        nonlocal started
        for copy in copies[started:count]:
            copy.start()
        started = max(started, min(count, len(copies)))

    def wait(n):
        start_to(n + 1 + AHEAD)
        copies[n].wait()

    start_to(2 + parts + AHEAD)
    copies[0].wait()
    copies[1].wait()
    square = jnp.zeros((back.shape[0], HD), F32)
    for i, at in enumerate(pieces):
        copies[2 + i].wait()
        turned[:, at] = u[at, :].T
        scaled[:, at] = (turned[:, at].astype(F32) * gain[:, at]).astype(BF)
        decoded = nn(back[...], turned[:, at])
        for side in range(0, PIECE, HD):
            part = decoded[:, side : side + HD]
            square = square + part * part
    inv_ref[...] = jnp.broadcast_to(
        inverse_root(jnp.sum(square, axis=1, keepdims=True), wide), inv_ref.shape
    )
    place = 2 + parts
    for i, at in enumerate(pieces):
        if i == 2:
            wait(place)
            wait(place + 1)
            place += 2
            for p, piece in enumerate(split(nn(scaled[...], narrow[...]), 2)):
                m_ref[p * rank : (p + 1) * rank, nq:] = piece
        wait(place)
        place += 1
        part = nn(scaled[:, at], wq[at, :])
        if i == 0:
            m_acc[...] = part
        else:
            m_acc[...] += part
    for p, piece in enumerate(split(m_acc[...], 2)):
        m_ref[p * rank : (p + 1) * rank, :nq] = piece
    for _ in blocks:
        wait(place)
        place += 1
    o_ref[...] = nn(wo[...], u[...]).astype(BF)


def project(back, gain, basis, wq, wk, wv, wo):
    wide, rank = basis.shape
    length = back.shape[0]
    ne = wo.shape[0]
    nq = wq.shape[1]
    rest = wk.shape[1] + wv.shape[1]
    operands = in_hbm((back, gain, basis, wq, wk, wv, wo))
    return pl.pallas_call(
        project_kernel,
        in_specs=[pl.BlockSpec(memory_space=pltpu.HBM)] * len(operands),
        out_specs=vmem(7),
        out_shape=[
            jax.ShapeDtypeStruct((2 * rank, nq + rest), BF),
            jax.ShapeDtypeStruct((ne, rank), BF),
            jax.ShapeDtypeStruct((length, HD), F32),
            jax.ShapeDtypeStruct(basis.shape, BF),
            jax.ShapeDtypeStruct(wq.shape, BF),
            jax.ShapeDtypeStruct((wide, rest), BF),
            jax.ShapeDtypeStruct((rank, wide), BF),
        ],
        scratch_shapes=[
            pltpu.VMEM(back.shape, BF),
            pltpu.VMEM(gain.shape, F32),
            pltpu.VMEM(wo.shape, BF),
            pltpu.VMEM((rank, wide), BF),
            pltpu.VMEM((rank, nq), F32),
            pltpu.SemaphoreType.DMA((4 + 3 * (wide // PIECE),)),
        ],
        compiler_params=pltpu.CompilerParams(vmem_limit_bytes=VMEM_BYTES * 3 // 2),
        cost_estimate=cost(6 * 10**9, 20 * 10**6),
        name="project_weights",
    )(*operands)


def project_heads(coeffs, inv, m_ref, cosine, sine, q, k, v1):
    length = coeffs.shape[0]
    heads = q.shape[0] // length
    twice = jnp.concatenate([coeffs, coeffs], axis=1)
    for h in range(0, heads, 2):
        both = nn(twice, m_ref[:, h * HD : (h + 2) * HD]) * inv
        for part, at in ((both[:, :HD], h * length), (both[:, HD:], (h + 1) * length)):
            q[at : at + length, :] = rope(part, cosine, sine).astype(BF)
    part = nn(twice, m_ref[:, heads * HD :]) * inv
    k[...] = rope(part[:, :HD], cosine, sine).astype(BF)
    v1[:, :HD] = part[:, HD:].astype(BF)
    v1[:, HD:] = jnp.ones_like(v1[:, HD:])


def exps_of(scores, exps, low, length):
    row = lax.broadcasted_iota(jnp.int32, (length, length), 0)
    column = lax.broadcasted_iota(jnp.int32, (length, length), 1)
    causal = row >= column

    def one(h, _):
        at = pl.ds(pl.multiple_of(h * length, length), length)
        s = jnp.where(causal, scores[at, :], -jnp.inf)
        top = jnp.max(s, axis=1, keepdims=True)
        e = jnp.exp2((s - top) * (LOG2E / math.sqrt(HD)))
        if exps is not None:
            exps[at, :] = e
        low[at, :] = e.astype(BF)
        return 0

    lax.fori_loop(0, scores.shape[0] // length, one, 0, unroll=2)


def backward_kernel(
    back_ref, loss_ref, sent_ref, m_ref, o_ref, inv_ref, cos_ref, sin_ref,
    inner_ref, out_give_ref, out_keep_ref, x_ref,
    q, k, v1, gh, ghs, scores, low, mixed, gp, ds, dq, heads, grads, inner, out_inner,
):
    length, rank = back_ref.shape
    ne = o_ref.shape[0]
    count = ne // HD
    scale = 1.0 / math.sqrt(HD)
    last = lax.axis_size("pipe") - 1
    is_last = lax.axis_index("pipe") == last
    back = back_ref[...]
    up = jnp.where(is_last, loss_ref[...], sent_ref[...])
    cosine, sine = cos_ref[...], sin_ref[...]
    inv = inv_ref[...]
    project_heads(back, inv[:, :1], m_ref, cosine, sine, q, k, v1)
    scores[...] = nt(q[...], k[...])
    for h in range(0, count, 2):
        both = nt(up, o_ref[h * HD : (h + 2) * HD, :]).astype(BF)
        gh[h * length : (h + 1) * length, :] = both[:, :HD]
        gh[(h + 1) * length : (h + 2) * length, :] = both[:, HD:]
    exps_of(scores, scores, low, length)
    mixed[...] = nn(low[...], v1[...])
    gp[...] = nt(gh[...], v1[:, :HD])

    for h in range(count):
        at = slice(h * length, (h + 1) * length)
        inverse = 1.0 / mixed[at, HD:]
        out = mixed[at, :HD] * inverse
        heads[:, h * HD : (h + 1) * HD] = out.astype(BF)
        grad = gh[at, :].astype(F32)
        ghs[at, :] = (grad * inverse).astype(BF)
        delta = jnp.sum(grad * out, axis=1, keepdims=True)
        factor = inverse * scale
        for side in range(0, length, HD):
            part = scores[at, side : side + HD] * factor
            ds[at, side : side + HD] = (part * (gp[at, side : side + HD] - delta)).astype(BF)

    dq[...] = nn(ds[...], k[...])
    for h in range(count):
        part = dq[h * length : (h + 1) * length, :]
        grads[:, h * HD : (h + 1) * HD] = unrope(part, cosine, sine).astype(BF)
    dk = nn(q[...].T, ds[...]).T
    grads[:, ne : ne + HD] = unrope(dk, cosine, sine).astype(BF)
    grads[:, ne + HD :] = nn(ghs[...].T, low[...]).T.astype(BF)
    unit = (back.astype(F32) * inv[:, :1]).astype(BF)
    half = rank // 2
    core = lax.axis_index("dp") & 1
    mine = pl.ds(pl.multiple_of(core * half, half), half)
    theirs = pl.ds(pl.multiple_of((1 - core) * half, half), half)
    inner[...] = nn(unit.T, grads[...]).astype(BF)
    inner_ref[:half, :] = inner[mine, :]
    inner_ref[half:, :] = inner[theirs, :]
    out_inner[...] = nn(up.T, heads[...]).astype(BF)
    out_keep_ref[...] = out_inner[mine, :]
    out_give_ref[...] = out_inner[theirs, :]
    x_ref[...] = nt(grads[...], m_ref[:rank, :]).astype(BF)


def backward(back, loss, sent, m2, o2, inv, cosine, sine):
    length, rank = back.shape
    ne = o2.shape[0]
    total = m2.shape[1]
    assert total == ne + 2 * HD
    stack = ne // HD * length
    return pl.pallas_call(
        backward_kernel,
        in_specs=vmem(8),
        out_specs=vmem(4),
        out_shape=[
            jax.ShapeDtypeStruct((rank, total), BF),
            jax.ShapeDtypeStruct((rank // 2, ne), BF),
            jax.ShapeDtypeStruct((rank // 2, ne), BF),
            jax.ShapeDtypeStruct((length, rank), BF),
        ],
        scratch_shapes=[
            pltpu.VMEM((stack, HD), BF),
            pltpu.VMEM((length, HD), BF),
            pltpu.VMEM((length, 2 * HD), BF),
            pltpu.VMEM((stack, HD), BF),
            pltpu.VMEM((stack, HD), BF),
            pltpu.VMEM((stack, length), F32),
            pltpu.VMEM((stack, length), BF),
            pltpu.VMEM((stack, 2 * HD), F32),
            pltpu.VMEM((stack, length), F32),
            pltpu.VMEM((stack, length), BF),
            pltpu.VMEM((stack, HD), F32),
            pltpu.VMEM((length, ne), BF),
            pltpu.VMEM((length, total), BF),
            pltpu.VMEM((rank, total), BF),
            pltpu.VMEM((rank, ne), BF),
        ],
        compiler_params=pltpu.CompilerParams(vmem_limit_bytes=VMEM_BYTES),
        cost_estimate=cost(10**4, 10**3),
        name="attention_backward",
    )(back, loss, sent, m2, o2, inv, cosine, sine)


def bases_kernel(
    back_ref, loss_ref, returned_ref, new_ref, arrived_ref, u_ref, turned_ref, inv_ref, after,
    base_ref, unit_ref, fbase_ref, g_ref,
):
    rank = u_ref.shape[1]
    for i, piece in enumerate(split(nn(turned_ref[...], u_ref[...]), 3)):
        g_ref[i * rank : (i + 1) * rank, :] = piece
    is_last = lax.axis_index("pipe") == lax.axis_size("pipe") - 1
    is_first = lax.axis_index("pipe") == 0
    up = jnp.where(is_last, loss_ref[...], returned_ref[...])
    coeffs = jnp.where(is_first, new_ref[...], arrived_ref[...])
    base_ref[...] = nn(jnp.concatenate([up] * 3, axis=1), g_ref[...])
    fbase_ref[...] = nn(jnp.concatenate([coeffs] * 3, axis=1), g_ref[...])
    unit_ref[...] = nn(jnp.concatenate([back_ref[...]] * 3, axis=1), g_ref[...]) * inv_ref[:, :1]


def bases(back, loss, returned, new, arrived, basis, turned, inv, after):
    length, rank = back.shape
    return pl.pallas_call(
        bases_kernel,
        in_specs=vmem(8) + [pl.BlockSpec(memory_space=pl.ANY)],
        out_specs=vmem(3),
        out_shape=[jax.ShapeDtypeStruct((length, rank), F32)] * 3,
        scratch_shapes=[pltpu.VMEM((3 * rank, rank), BF)],
        compiler_params=pltpu.CompilerParams(vmem_limit_bytes=VMEM_BYTES // 2),
        cost_estimate=cost(10**4, 10**3),
        name="encoded_again",
    )(back, loss, returned, new, arrived, basis, turned, inv, after)


def forward_kernel(
    new_ref, sent_ref, turned_ref, m_ref, o_ref, cos_ref, sin_ref, after,
    y_ref, q, k, v1, scores, low, mixed, heads,
):
    length, rank = new_ref.shape
    wide = turned_ref.shape[1]
    is_first = lax.axis_index("pipe") == 0
    coeffs = jnp.where(is_first, new_ref[...], sent_ref[...])
    square = jnp.zeros((length, HD), F32)
    for at in range(0, wide, PIECE):
        decoded = nn(coeffs, turned_ref[:, at : at + PIECE])
        for side in range(0, PIECE, HD):
            part = decoded[:, side : side + HD]
            square = square + part * part
    inv = inverse_root(jnp.sum(square, axis=1, keepdims=True), wide)
    project_heads(coeffs, inv, m_ref, cos_ref[...], sin_ref[...], q, k, v1)
    scores[...] = nt(q[...], k[...])
    exps_of(scores, None, low, length)
    mixed[...] = nn(low[...], v1[...])
    for h in range(heads.shape[1] // HD):
        at = slice(h * length, (h + 1) * length)
        heads[:, h * HD : (h + 1) * HD] = (mixed[at, :HD] / mixed[at, HD:]).astype(BF)
    y_ref[...] = nn(heads[...], o_ref[...]).astype(BF)


def forward(new, sent, turned, m2, o2, cosine, sine, after):
    length, rank = new.shape
    ne = o2.shape[0]
    stack = ne // HD * length
    return pl.pallas_call(
        forward_kernel,
        in_specs=vmem(7) + [pl.BlockSpec(memory_space=pl.ANY)],
        out_specs=pl.BlockSpec(memory_space=pltpu.VMEM),
        out_shape=jax.ShapeDtypeStruct((length, rank), BF),
        scratch_shapes=[
            pltpu.VMEM((stack, HD), BF),
            pltpu.VMEM((length, HD), BF),
            pltpu.VMEM((length, 2 * HD), BF),
            pltpu.VMEM((stack, length), F32),
            pltpu.VMEM((stack, length), BF),
            pltpu.VMEM((stack, 2 * HD), F32),
            pltpu.VMEM((length, ne), BF),
        ],
        compiler_params=pltpu.CompilerParams(vmem_limit_bytes=VMEM_BYTES),
        cost_estimate=cost(10**4, 10**3),
        name="attention_forward",
    )(new, sent, turned, m2, o2, cosine, sine, after)


def write_split(ref, value):
    high, low = split(value, 2)
    both = jnp.concatenate([high.astype(F32), low.astype(F32)], axis=0)
    ref[ref.shape[0] - 16 :, :] = both.astype(BF)


def read_split(ref):
    both = ref[ref.shape[0] - 16 :, :].astype(F32)
    return both[:8] + both[8:]


def gain_kernel(
    u_ref, wq_ref, narrow_ref, inner_ref, got_ref, x_ref, after,
    pair_ref, out_ref, turned, rows_f32,
):
    nq = wq_ref.shape[1]
    rows = u_ref.shape[0] // 2
    rank = u_ref.shape[1]
    half = inner_ref.shape[0] // 2
    core = lax.axis_index("dp") & 1
    mine = add_wide(inner_ref[:half, :], got_ref[half:, :]).astype(BF)
    theirs = add_wide(inner_ref[half:, :], got_ref[:half, :]).astype(BF)
    pair_ref[...] = mine
    out_ref[: x_ref.shape[0], :] = x_ref[...]
    turned[:, pl.ds(pl.multiple_of(core * half, half), half)] = mine.T
    turned[:, pl.ds(pl.multiple_of((1 - core) * half, half), half)] = theirs.T
    for at in range(0, rows, CHUNK):
        place = pl.ds(pl.multiple_of(core * rows + at, CHUNK), CHUNK)
        against = nn(wq_ref[place, :], turned[:nq, :])
        against += nn(narrow_ref[place, :], turned[nq:, :])
        terms = against * u_ref[place, :].astype(F32)
        folded = sum(terms[:, side : side + HD] for side in range(0, terms.shape[1], HD))
        line = jnp.sum(folded.T, axis=0, keepdims=True)
        for side in range(0, CHUNK, rank):
            row = (at + side) // rank
            rows_f32[row : row + 1, :] = line[:, side : side + rank]
    write_split(out_ref, rows_f32[...])


def gain_part(basis, wq, narrow, inner, got, x, after):
    wide, rank = basis.shape
    assert wide // 2 == 8 * rank
    held = tuple(pltpu.with_memory_space_constraint(a, pltpu.VMEM) for a in (basis, wq, narrow))
    return pl.pallas_call(
        gain_kernel,
        in_specs=vmem(6) + [pl.BlockSpec(memory_space=pl.ANY)],
        out_specs=vmem(2),
        out_shape=[
            jax.ShapeDtypeStruct((rank // 2, inner.shape[1]), BF),
            jax.ShapeDtypeStruct((x.shape[0] + 16, rank), BF),
        ],
        scratch_shapes=[
            pltpu.VMEM((inner.shape[1], rank), BF),
            pltpu.VMEM((8, rank), F32),
        ],
        compiler_params=pltpu.CompilerParams(vmem_limit_bytes=VMEM_BYTES),
        cost_estimate=cost(10**4, 10**3),
        name="pair_sum_and_gain_gradient",
    )(*held, inner, got, x, after)


def merge_kernel(a_ref, b_ref, after, out_ref):
    rest = out_ref.shape[0] - 16
    out_ref[:rest, :] = add_wide(a_ref[:rest, :], b_ref[:rest, :]).astype(BF)
    write_split(out_ref, read_split(a_ref) + read_split(b_ref))


def total_kernel(a_ref, b_ref, after, out_ref):
    out_ref[...] = read_split(a_ref) + read_split(b_ref)


def own_kernel(a_ref, b_ref, after, *out_refs):
    at = 0
    for ref in out_refs:
        size = ref.shape[1]
        ref[...] = add_wide(a_ref[:, at : at + size], b_ref[:, at : at + size]).astype(BF)
        at += size


def small_kernel(kernel, name, out_shape, a, b, after):
    return pl.pallas_call(
        kernel,
        in_specs=vmem(2) + [pl.BlockSpec(memory_space=pl.ANY)],
        out_specs=jax.tree.map(lambda _: pl.BlockSpec(memory_space=pltpu.VMEM), out_shape),
        out_shape=out_shape,
        compiler_params=pltpu.CompilerParams(vmem_limit_bytes=VMEM_BYTES // 2),
        cost_estimate=cost(10**4, 10**3),
        name=name,
    )(a, b, after)


def merge(a, b, after):
    return small_kernel(merge_kernel, "sum_with_gain", jax.ShapeDtypeStruct(a.shape, BF), a, b, after)


def gain_total(a, b, after):
    shape = jax.ShapeDtypeStruct((8, a.shape[1]), F32)
    return small_kernel(total_kernel, "gain_total", shape, a, b, after)


def own_pieces(a, b, sizes, after):
    shapes = [jax.ShapeDtypeStruct((a.shape[0], n), BF) for n in sizes]
    return small_kernel(own_kernel, "sum_over_y", shapes, a, b, after)


def add_kernel(a_ref, b_ref, after, out_ref):
    rows = out_ref.shape[0]
    out_ref[...] = add_wide(a_ref[:rows, :], b_ref[:rows, :]).astype(out_ref.dtype)


def add_after(a, b, after, rows=None):
    shape = jax.ShapeDtypeStruct((rows or a.shape[0], a.shape[1]), a.dtype)
    return small_kernel(add_kernel, "pair_sum", shape, a, b, after)


def gather_halves(own_refs, other_refs, whole):
    half = whole.shape[0] // 2
    core = lax.axis_index("dp") & 1
    at = 0
    for own_ref, other_ref in zip(own_refs, other_refs):
        columns = pl.ds(at, own_ref.shape[1])
        whole[pl.ds(pl.multiple_of(core * half, half), half), columns] = own_ref[...]
        whole[pl.ds(pl.multiple_of((1 - core) * half, half), half), columns] = other_ref[...]
        at += own_ref.shape[1]


def inward_kernel(pieces, u_ref, gain_ref, *refs):
    own_refs, other_refs = refs[:pieces], refs[pieces : 2 * pieces]
    q_ref, k_ref, v_ref, inner = refs[-4:]
    nq, nk = q_ref.shape[1], k_ref.shape[1]
    block = q_ref.shape[0]

    @pl.when(pl.program_id(0) == 0)
    def _():
        gather_halves(own_refs, other_refs, inner)

    step = lax.axis_index("dp") * pl.num_programs(0) + pl.program_id(0)
    rows = pl.ds(pl.multiple_of(step * block, block), block)
    gain = jnp.broadcast_to(gain_ref[:, rows], (HD, block)).T[:, :1]
    grad = nn(u_ref[rows, :], inner[...]) * gain
    q_ref[...] = grad[:, :nq].astype(BF)
    k_ref[...] = grad[:, nq : nq + nk].astype(BF)
    v_ref[...] = grad[:, nq + nk :].astype(BF)


def outward_kernel(pieces, u_ref, *refs):
    own_refs, other_refs = refs[:pieces], refs[pieces : 2 * pieces]
    o_ref, inner = refs[-2:]

    @pl.when(pl.program_id(0) == 0)
    def _():
        gather_halves(own_refs, other_refs, inner)

    block, rows = o_ref.shape
    at = pl.multiple_of(pl.program_id(0) * block, block)
    basis = u_ref[pl.ds(pl.multiple_of(lax.axis_index("dp") * rows, rows), rows), :]
    o_ref[...] = nt(inner[:, pl.ds(at, block)].T, basis).astype(BF)


STEPS = 2


def inward_grads(basis, gain, own, other, sizes, after):
    wide, rank = basis.shape
    rows = wide // lax.axis_size("dp")
    block = rows // STEPS
    return pl.pallas_call(
        functools.partial(inward_kernel, len(own)),
        grid=(STEPS,),
        in_specs=vmem(2 + 2 * len(own)) + [pl.BlockSpec(memory_space=pl.ANY)],
        out_specs=[pl.BlockSpec((block, n), lambda i: (i, 0)) for n in sizes],
        scratch_shapes=[pltpu.VMEM((rank, sum(sizes)), BF)],
        out_shape=[jax.ShapeDtypeStruct((rows, n), BF) for n in sizes],
        compiler_params=pltpu.CompilerParams(vmem_limit_bytes=VMEM_BYTES),
        cost_estimate=cost(10**4, 10**3),
        name="inward_weight_gradients",
    )(basis, gain, *own, *other, after)


def outward_grad(basis, own, other, after):
    wide, rank = basis.shape
    rows = wide // lax.axis_size("dp")
    ne = sum(piece.shape[1] for piece in own)
    return pl.pallas_call(
        functools.partial(outward_kernel, len(own)),
        grid=(STEPS,),
        in_specs=vmem(1 + 2 * len(own)) + [pl.BlockSpec(memory_space=pl.ANY)],
        out_specs=pl.BlockSpec((ne // STEPS, rows), lambda i: (i, 0)),
        scratch_shapes=[pltpu.VMEM((rank, ne), BF)],
        out_shape=jax.ShapeDtypeStruct((ne, rows), BF),
        compiler_params=pltpu.CompilerParams(vmem_limit_bytes=VMEM_BYTES),
        cost_estimate=cost(10**4, 10**3),
        name="output_weight_gradient",
    )(basis, *own, *other, after)


def results_kernel(
    wide, fbase_ref, y_ref, ygot_ref, base_ref, unit_ref, x_ref, xgot_ref, back_ref, inv_ref,
    gain_ref, gain_other_ref, after,
    f_ref, b_ref, gain_out_ref,
):
    f_ref[...] = (fbase_ref[...] + add_wide(y_ref[...], ygot_ref[...])).astype(BF)
    length = back_ref.shape[0]
    x = add_wide(x_ref[:length, :], xgot_ref[:length, :])
    inv = inv_ref[:, :1]
    along = jnp.sum(x * back_ref[...].astype(F32), axis=1, keepdims=True)
    middle = along * inv * (1.0 / wide)
    b_ref[...] = (base_ref[...] + (x - unit_ref[...] * middle) * inv).astype(BF)
    core = lax.axis_index("dp") & 1
    half = wide // 2
    rank = gain_ref.shape[1]
    for row in range(half // rank):
        mine = pl.ds(pl.multiple_of(core * half + row * rank, rank), rank)
        theirs = pl.ds(pl.multiple_of((1 - core) * half + row * rank, rank), rank)
        gain_out_ref[:, mine] = gain_ref[row : row + 1, :]
        gain_out_ref[:, theirs] = gain_other_ref[row : row + 1, :]


def results(wide, after, *operands):
    shape = operands[0].shape
    held = tuple(pltpu.with_memory_space_constraint(a, pltpu.VMEM) for a in operands)
    return pl.pallas_call(
        functools.partial(results_kernel, wide),
        in_specs=vmem(len(operands)) + [pl.BlockSpec(memory_space=pl.ANY)],
        out_specs=vmem(3),
        out_shape=[jax.ShapeDtypeStruct(shape, BF)] * 2 + [jax.ShapeDtypeStruct((1, wide), F32)],
        compiler_params=pltpu.CompilerParams(vmem_limit_bytes=VMEM_BYTES // 2),
        cost_estimate=cost(10**4, 10**3),
        name="section_results",
    )(*held, *in_hbm((after,)))


def body(
    new_coeffs,
    loss_grad,
    sent_forward,
    sent_backward,
    stashed,
    subspace,
    norm_gain,
    w_query,
    w_key,
    w_value,
    w_output,
):
    wide = subspace.shape[0]
    wq, wk, wv, wo = w_query[0], w_key[0], w_value[0], w_output[0]
    nq, nk, nv = wq.shape[1], wk.shape[1], wv.shape[1]
    back = stashed[0]
    arrived, returned = cross_pipe(sent_forward[0], sent_backward[0])
    cosine, sine = rope_tables(back.shape[0])

    m2, o2, inv, basis, wq, narrow, turned = project(
        back, norm_gain, subspace, wq, wk, wv, wo
    )
    inner, out_give, out_keep, x = backward(
        back, loss_grad, returned, m2, o2, inv, cosine, sine
    )
    out_got = swap(out_give, "dp", 1)
    inner_got = swap(inner, "dp", 1)
    base, unit, fbase = bases(
        back, loss_grad, returned, new_coeffs, arrived, basis, turned, inv, out_keep
    )
    out_pair = add_after(out_keep, out_got, fbase)
    out_got = swap(out_pair, "dp", 2)
    pair, x = gain_part(basis, wq, narrow, inner, inner_got, x, out_pair)
    pair_got = swap(pair, "dp", 2)
    x_got = swap(x, "tensor", 2)
    y = forward(new_coeffs, arrived, turned, m2, o2, cosine, sine, pair)
    y_got = swap(y, "tensor", 2)
    ne = wo.shape[0]
    out_own = own_pieces(out_pair, out_got, (ne // 4,) * 4, y)
    out_other = [swap(piece, "dp", 1) for piece in out_own]
    x = merge(x, x_got, out_own[0])
    x_got = swap(x, "tensor", 1)
    grad_o = outward_grad(basis, out_own, out_other, x)
    sizes = (nq // 2, nq - nq // 2, nk + nv)
    own = own_pieces(pair, pair_got, sizes, *in_hbm((grad_o,)))
    other = [swap(piece, "dp", 1) for piece in own]
    y = add_after(y, y_got, own[0])
    y_got = swap(y, "tensor", 1)
    gain = gain_total(x, x_got, y)
    gain_got = swap(gain, "dp", 2)
    grad_q, grad_k, grad_v = inward_grads(basis, norm_gain, own, other, (nq, nk, nv), gain)
    gain = add_after(gain, gain_got, *in_hbm((grad_v,)))
    gain_other = swap(gain, "dp", 1)
    forward_out, backward_out, grad_gain = results(
        wide, grad_v, fbase, y, y_got, base, unit, x, x_got, back, inv, gain, gain_other
    )
    return (
        forward_out[None],
        backward_out[None],
        grad_q[None],
        grad_k[None],
        grad_v[None],
        grad_o[None],
        grad_gain,
    )


def solution(mesh):
    return jax.shard_map(
        body,
        mesh=mesh,
        in_specs=(
            P("dp", None),
            P("dp", None),
            P("pipe", "dp", None),
            P("pipe", "dp", None),
            P("pipe", "dp", None),
            P(),
            P("pipe", None),
            P("pipe", None, "tensor"),
            P("pipe", None, "tensor"),
            P("pipe", None, "tensor"),
            P("pipe", "tensor", None),
        ),
        out_specs=(
            P("pipe", "dp", None),
            P("pipe", "dp", None),
            P("pipe", "dp", "tensor"),
            P("pipe", "dp", "tensor"),
            P("pipe", "dp", "tensor"),
            P("pipe", "tensor", "dp"),
            P("pipe", None),
        ),
        check_vma=False,
    )
```

```python
import functools
import math

import jax
import jax.numpy as jnp
import numpy as np
from jax import lax
from jax.experimental import pallas as pl
from jax.experimental.pallas import tpu as pltpu
from jax.sharding import PartitionSpec as P

HD = 128
EPSILON = 1e-05
ROPE_BASE = 500000.0
BF = jnp.bfloat16
F32 = jnp.float32
VMEM_BYTES = 24 * 1024 * 1024
CHUNK = 512
PIECE = 1024
AHEAD = 4
LOG2E = 1.4426950408889634


def shifted(x, axis, by):
    devices = lax.axis_size(axis)
    pairs = [(i, i + by) for i in range(devices) if 0 <= i + by < devices]
    return lax.ppermute(x, axis, pairs)


def swap(x, axis, bit):
    devices = lax.axis_size(axis)
    return lax.ppermute(x, axis, [(i, i ^ bit) for i in range(devices)])


def cross_pipe(sent_forward, sent_backward):
    if lax.axis_size("pipe") != 2:
        return shifted(sent_forward, "pipe", 1), shifted(sent_backward, "pipe", -1)
    first = lax.axis_index("pipe") == 0
    got = swap(jnp.where(first, sent_forward, sent_backward), "pipe", 1)
    return got, got


def add_wide(a, b):
    return a.astype(F32) + b.astype(F32)


def nt(a, b):
    return lax.dot_general(a, b, (((1,), (1,)), ((), ())), preferred_element_type=F32)


def nn(a, b):
    return jnp.dot(a, b, preferred_element_type=F32)


def split(x, parts):
    out = []
    for _ in range(parts):
        piece = x.astype(BF)
        out.append(piece)
        x = x - piece.astype(F32)
    return out


def rope_tables(length):
    half = HD // 2
    frequency = np.float32(ROPE_BASE) ** (-2.0 * np.arange(half, dtype=np.float32) / HD)
    angles = np.arange(length, dtype=np.float32)[:, None] * frequency.astype(np.float32)
    cosine, sine = np.cos(angles), np.sin(angles)
    tables = (np.concatenate([cosine, cosine], 1), np.concatenate([-sine, sine], 1))
    return tuple(jnp.asarray(t, dtype=F32) for t in tables)


def rope(x, cosine, sine):
    return x * cosine + pltpu.roll(x, HD // 2, 1) * sine


def unrope(x, cosine, sine):
    return x * cosine - pltpu.roll(x, HD // 2, 1) * sine


def inverse_root(square_sum, width):
    return 1.0 / jnp.sqrt(square_sum / width + EPSILON)


def vmem(count):
    return [pl.BlockSpec(memory_space=pltpu.VMEM)] * count


def in_hbm(arrays):
    return tuple(pltpu.with_memory_space_constraint(a, pltpu.HBM) for a in arrays)


def cost(flops, num_bytes, exps=0):
    return pl.CostEstimate(flops=flops, bytes_accessed=num_bytes, transcendentals=exps)


def project_kernel(
    back_hbm, gain_hbm, u_hbm, wq_hbm, wk_hbm, wv_hbm, wo_hbm,
    m_ref, o_ref, inv_ref, u, wq, narrow, turned,
    back, gain, wo, scaled, m_acc, sems,
):
    wide, rank = u.shape
    nq = wq.shape[1]
    nk = wk_hbm.shape[1]
    parts = wide // PIECE
    pieces = [pl.ds(i * PIECE, PIECE) for i in range(parts)]
    pairs = [(back_hbm, back), (gain_hbm, gain)]
    pairs += [(u_hbm.at[at, :], u.at[at, :]) for at in pieces]
    pairs += [(wq_hbm.at[at, :], wq.at[at, :]) for at in pieces[:2]]
    pairs += [(wk_hbm, narrow.at[:, pl.ds(0, nk)])]
    pairs += [(wv_hbm, narrow.at[:, pl.ds(nk, narrow.shape[1] - nk)])]
    pairs += [(wq_hbm.at[at, :], wq.at[at, :]) for at in pieces[2:]]
    block = wo.shape[0] // parts
    blocks = [pl.ds(i * block, block) for i in range(parts)]
    pairs += [(wo_hbm.at[at, :], wo.at[at, :]) for at in blocks]
    copies = [
        pltpu.make_async_copy(source, target, sems.at[n])
        for n, (source, target) in enumerate(pairs)
    ]
    started = 0

    def start_to(count):
        nonlocal started
        for copy in copies[started:count]:
            copy.start()
        started = max(started, min(count, len(copies)))

    def wait(n):
        start_to(n + 1 + AHEAD)
        copies[n].wait()

    start_to(2 + parts + 1)
    copies[0].wait()
    copies[1].wait()
    square = jnp.zeros((back.shape[0], HD), F32)
    for i, at in enumerate(pieces):
        copies[2 + i].wait()
        start_to(2 + parts + 2 + i)
        turned[:, at] = u[at, :].T
        scaled[:, at] = (turned[:, at].astype(F32) * gain[:, at]).astype(BF)
        decoded = nn(back[...], turned[:, at])
        for side in range(0, PIECE, HD):
            part = decoded[:, side : side + HD]
            square = square + part * part
    inv_ref[...] = jnp.broadcast_to(
        inverse_root(jnp.sum(square, axis=1, keepdims=True), wide), inv_ref.shape
    )
    place = 2 + parts
    for i, at in enumerate(pieces):
        if i == 2:
            wait(place)
            wait(place + 1)
            place += 2
            for p, piece in enumerate(split(nn(scaled[...], narrow[...]), 2)):
                m_ref[p * rank : (p + 1) * rank, nq:] = piece
        wait(place)
        place += 1
        part = nn(scaled[:, at], wq[at, :])
        if i == 0:
            m_acc[...] = part
        else:
            m_acc[...] += part
    for p, piece in enumerate(split(m_acc[...], 2)):
        m_ref[p * rank : (p + 1) * rank, :nq] = piece
    for _ in blocks:
        wait(place)
        place += 1
    o_ref[...] = nn(wo[...], u[...]).astype(BF)


def project(back, gain, basis, wq, wk, wv, wo):
    wide, rank = basis.shape
    length = back.shape[0]
    ne = wo.shape[0]
    nq = wq.shape[1]
    rest = wk.shape[1] + wv.shape[1]
    operands = in_hbm((back, gain, basis, wq, wk, wv, wo))
    return pl.pallas_call(
        project_kernel,
        in_specs=[pl.BlockSpec(memory_space=pltpu.HBM)] * len(operands),
        out_specs=vmem(7),
        out_shape=[
            jax.ShapeDtypeStruct((2 * rank, nq + rest), BF),
            jax.ShapeDtypeStruct((ne, rank), BF),
            jax.ShapeDtypeStruct((length, HD), F32),
            jax.ShapeDtypeStruct(basis.shape, BF),
            jax.ShapeDtypeStruct(wq.shape, BF),
            jax.ShapeDtypeStruct((wide, rest), BF),
            jax.ShapeDtypeStruct((rank, wide), BF),
        ],
        scratch_shapes=[
            pltpu.VMEM(back.shape, BF),
            pltpu.VMEM(gain.shape, F32),
            pltpu.VMEM(wo.shape, BF),
            pltpu.VMEM((rank, wide), BF),
            pltpu.VMEM((rank, nq), F32),
            pltpu.SemaphoreType.DMA((4 + 3 * (wide // PIECE),)),
        ],
        compiler_params=pltpu.CompilerParams(vmem_limit_bytes=VMEM_BYTES * 3 // 2),
        cost_estimate=cost(6 * 10**9, 20 * 10**6),
        name="project_weights",
    )(*operands)


def project_heads(coeffs, inv, m_ref, cosine, sine, q, k, v1):
    length = coeffs.shape[0]
    heads = q.shape[0] // length
    twice = jnp.concatenate([coeffs, coeffs], axis=1)
    for h in range(0, heads, 2):
        both = nn(twice, m_ref[:, h * HD : (h + 2) * HD]) * inv
        for part, at in ((both[:, :HD], h * length), (both[:, HD:], (h + 1) * length)):
            q[at : at + length, :] = rope(part, cosine, sine).astype(BF)
    part = nn(twice, m_ref[:, heads * HD :]) * inv
    k[...] = rope(part[:, :HD], cosine, sine).astype(BF)
    v1[:, :HD] = part[:, HD:].astype(BF)
    v1[:, HD:] = jnp.ones_like(v1[:, HD:])


def exps_of(scores, exps, low, length):
    row = lax.broadcasted_iota(jnp.int32, (length, length), 0)
    column = lax.broadcasted_iota(jnp.int32, (length, length), 1)
    causal = row >= column

    def one(h, _):
        at = pl.ds(pl.multiple_of(h * length, length), length)
        s = jnp.where(causal, scores[at, :], -jnp.inf)
        top = jnp.max(s, axis=1, keepdims=True)
        e = jnp.exp2((s - top) * (LOG2E / math.sqrt(HD)))
        if exps is not None:
            exps[at, :] = e
        low[at, :] = e.astype(BF)
        return 0

    lax.fori_loop(0, scores.shape[0] // length, one, 0, unroll=2)


def backward_kernel(
    back_ref, loss_ref, sent_ref, m_ref, o_ref, inv_ref, cos_ref, sin_ref,
    inner_ref, out_give_ref, out_keep_ref, x_ref,
    q, k, v1, gh, ghs, scores, low, mixed, gp, ds, dq, heads, grads, inner, out_inner,
):
    length, rank = back_ref.shape
    ne = o_ref.shape[0]
    count = ne // HD
    scale = 1.0 / math.sqrt(HD)
    last = lax.axis_size("pipe") - 1
    is_last = lax.axis_index("pipe") == last
    back = back_ref[...]
    up = jnp.where(is_last, loss_ref[...], sent_ref[...])
    cosine, sine = cos_ref[...], sin_ref[...]
    inv = inv_ref[...]
    project_heads(back, inv[:, :1], m_ref, cosine, sine, q, k, v1)
    scores[...] = nt(q[...], k[...])
    for h in range(0, count, 2):
        both = nt(up, o_ref[h * HD : (h + 2) * HD, :]).astype(BF)
        gh[h * length : (h + 1) * length, :] = both[:, :HD]
        gh[(h + 1) * length : (h + 2) * length, :] = both[:, HD:]
    exps_of(scores, scores, low, length)
    mixed[...] = nn(low[...], v1[...])
    gp[...] = nt(gh[...], v1[:, :HD])

    for h in range(count):
        at = slice(h * length, (h + 1) * length)
        inverse = 1.0 / mixed[at, HD:]
        out = mixed[at, :HD] * inverse
        heads[:, h * HD : (h + 1) * HD] = out.astype(BF)
        grad = gh[at, :].astype(F32)
        ghs[at, :] = (grad * inverse).astype(BF)
        delta = jnp.sum(grad * out, axis=1, keepdims=True)
        factor = inverse * scale
        for side in range(0, length, HD):
            part = scores[at, side : side + HD] * factor
            ds[at, side : side + HD] = (part * (gp[at, side : side + HD] - delta)).astype(BF)

    dq[...] = nn(ds[...], k[...])
    for h in range(count):
        part = dq[h * length : (h + 1) * length, :]
        grads[:, h * HD : (h + 1) * HD] = unrope(part, cosine, sine).astype(BF)
    dk = nn(q[...].T, ds[...]).T
    grads[:, ne : ne + HD] = unrope(dk, cosine, sine).astype(BF)
    grads[:, ne + HD :] = nn(ghs[...].T, low[...]).T.astype(BF)
    unit = (back.astype(F32) * inv[:, :1]).astype(BF)
    half = rank // 2
    core = lax.axis_index("dp") & 1
    mine = pl.ds(pl.multiple_of(core * half, half), half)
    theirs = pl.ds(pl.multiple_of((1 - core) * half, half), half)
    inner[...] = nn(unit.T, grads[...]).astype(BF)
    inner_ref[:half, :] = inner[mine, :]
    inner_ref[half:, :] = inner[theirs, :]
    out_inner[...] = nn(up.T, heads[...]).astype(BF)
    out_keep_ref[...] = out_inner[mine, :]
    out_give_ref[...] = out_inner[theirs, :]
    x_ref[...] = nt(grads[...], m_ref[:rank, :]).astype(BF)


def backward(back, loss, sent, m2, o2, inv, cosine, sine):
    length, rank = back.shape
    ne = o2.shape[0]
    total = m2.shape[1]
    assert total == ne + 2 * HD
    stack = ne // HD * length
    return pl.pallas_call(
        backward_kernel,
        in_specs=vmem(8),
        out_specs=vmem(4),
        out_shape=[
            jax.ShapeDtypeStruct((rank, total), BF),
            jax.ShapeDtypeStruct((rank // 2, ne), BF),
            jax.ShapeDtypeStruct((rank // 2, ne), BF),
            jax.ShapeDtypeStruct((length, rank), BF),
        ],
        scratch_shapes=[
            pltpu.VMEM((stack, HD), BF),
            pltpu.VMEM((length, HD), BF),
            pltpu.VMEM((length, 2 * HD), BF),
            pltpu.VMEM((stack, HD), BF),
            pltpu.VMEM((stack, HD), BF),
            pltpu.VMEM((stack, length), F32),
            pltpu.VMEM((stack, length), BF),
            pltpu.VMEM((stack, 2 * HD), F32),
            pltpu.VMEM((stack, length), F32),
            pltpu.VMEM((stack, length), BF),
            pltpu.VMEM((stack, HD), F32),
            pltpu.VMEM((length, ne), BF),
            pltpu.VMEM((length, total), BF),
            pltpu.VMEM((rank, total), BF),
            pltpu.VMEM((rank, ne), BF),
        ],
        compiler_params=pltpu.CompilerParams(vmem_limit_bytes=VMEM_BYTES),
        cost_estimate=cost(10**4, 10**3),
        name="attention_backward",
    )(back, loss, sent, m2, o2, inv, cosine, sine)


def bases_kernel(
    back_ref, loss_ref, returned_ref, new_ref, arrived_ref, u_ref, turned_ref, inv_ref, after,
    base_ref, unit_ref, fbase_ref, g_ref,
):
    rank = u_ref.shape[1]
    for i, piece in enumerate(split(nn(turned_ref[...], u_ref[...]), 3)):
        g_ref[i * rank : (i + 1) * rank, :] = piece
    is_last = lax.axis_index("pipe") == lax.axis_size("pipe") - 1
    is_first = lax.axis_index("pipe") == 0
    up = jnp.where(is_last, loss_ref[...], returned_ref[...])
    coeffs = jnp.where(is_first, new_ref[...], arrived_ref[...])
    base_ref[...] = nn(jnp.concatenate([up] * 3, axis=1), g_ref[...])
    fbase_ref[...] = nn(jnp.concatenate([coeffs] * 3, axis=1), g_ref[...])
    unit_ref[...] = nn(jnp.concatenate([back_ref[...]] * 3, axis=1), g_ref[...]) * inv_ref[:, :1]


def bases(back, loss, returned, new, arrived, basis, turned, inv, after):
    length, rank = back.shape
    return pl.pallas_call(
        bases_kernel,
        in_specs=vmem(8) + [pl.BlockSpec(memory_space=pl.ANY)],
        out_specs=vmem(3),
        out_shape=[jax.ShapeDtypeStruct((length, rank), F32)] * 3,
        scratch_shapes=[pltpu.VMEM((3 * rank, rank), BF)],
        compiler_params=pltpu.CompilerParams(vmem_limit_bytes=VMEM_BYTES // 2),
        cost_estimate=cost(10**4, 10**3),
        name="encoded_again",
    )(back, loss, returned, new, arrived, basis, turned, inv, after)


def forward_kernel(
    new_ref, sent_ref, turned_ref, m_ref, o_ref, cos_ref, sin_ref, after,
    y_ref, q, k, v1, scores, low, mixed, heads,
):
    length, rank = new_ref.shape
    wide = turned_ref.shape[1]
    is_first = lax.axis_index("pipe") == 0
    coeffs = jnp.where(is_first, new_ref[...], sent_ref[...])
    square = jnp.zeros((length, HD), F32)
    for at in range(0, wide, PIECE):
        decoded = nn(coeffs, turned_ref[:, at : at + PIECE])
        for side in range(0, PIECE, HD):
            part = decoded[:, side : side + HD]
            square = square + part * part
    inv = inverse_root(jnp.sum(square, axis=1, keepdims=True), wide)
    project_heads(coeffs, inv, m_ref, cos_ref[...], sin_ref[...], q, k, v1)
    scores[...] = nt(q[...], k[...])
    exps_of(scores, None, low, length)
    mixed[...] = nn(low[...], v1[...])
    for h in range(heads.shape[1] // HD):
        at = slice(h * length, (h + 1) * length)
        heads[:, h * HD : (h + 1) * HD] = (mixed[at, :HD] / mixed[at, HD:]).astype(BF)
    y_ref[...] = nn(heads[...], o_ref[...]).astype(BF)


def forward(new, sent, turned, m2, o2, cosine, sine, after):
    length, rank = new.shape
    ne = o2.shape[0]
    stack = ne // HD * length
    return pl.pallas_call(
        forward_kernel,
        in_specs=vmem(7) + [pl.BlockSpec(memory_space=pl.ANY)],
        out_specs=pl.BlockSpec(memory_space=pltpu.VMEM),
        out_shape=jax.ShapeDtypeStruct((length, rank), BF),
        scratch_shapes=[
            pltpu.VMEM((stack, HD), BF),
            pltpu.VMEM((length, HD), BF),
            pltpu.VMEM((length, 2 * HD), BF),
            pltpu.VMEM((stack, length), F32),
            pltpu.VMEM((stack, length), BF),
            pltpu.VMEM((stack, 2 * HD), F32),
            pltpu.VMEM((length, ne), BF),
        ],
        compiler_params=pltpu.CompilerParams(vmem_limit_bytes=VMEM_BYTES),
        cost_estimate=cost(10**4, 10**3),
        name="attention_forward",
    )(new, sent, turned, m2, o2, cosine, sine, after)


def write_split(ref, value):
    high, low = split(value, 2)
    both = jnp.concatenate([high.astype(F32), low.astype(F32)], axis=0)
    ref[ref.shape[0] - 16 :, :] = both.astype(BF)


def read_split(ref):
    both = ref[ref.shape[0] - 16 :, :].astype(F32)
    return both[:8] + both[8:]


def gain_kernel(
    u_ref, wq_ref, narrow_ref, inner_ref, got_ref, x_ref, after,
    pair_ref, out_ref, turned, rows_f32,
):
    nq = wq_ref.shape[1]
    rows = u_ref.shape[0] // 2
    rank = u_ref.shape[1]
    half = inner_ref.shape[0] // 2
    core = lax.axis_index("dp") & 1
    mine = add_wide(inner_ref[:half, :], got_ref[half:, :]).astype(BF)
    theirs = add_wide(inner_ref[half:, :], got_ref[:half, :]).astype(BF)
    pair_ref[...] = mine
    out_ref[: x_ref.shape[0], :] = x_ref[...]
    turned[:, pl.ds(pl.multiple_of(core * half, half), half)] = mine.T
    turned[:, pl.ds(pl.multiple_of((1 - core) * half, half), half)] = theirs.T
    for at in range(0, rows, CHUNK):
        place = pl.ds(pl.multiple_of(core * rows + at, CHUNK), CHUNK)
        against = nn(wq_ref[place, :], turned[:nq, :])
        against += nn(narrow_ref[place, :], turned[nq:, :])
        terms = against * u_ref[place, :].astype(F32)
        folded = sum(terms[:, side : side + HD] for side in range(0, terms.shape[1], HD))
        line = jnp.sum(folded.T, axis=0, keepdims=True)
        for side in range(0, CHUNK, rank):
            row = (at + side) // rank
            rows_f32[row : row + 1, :] = line[:, side : side + rank]
    write_split(out_ref, rows_f32[...])


def gain_part(basis, wq, narrow, inner, got, x, after):
    wide, rank = basis.shape
    assert wide // 2 == 8 * rank
    held = tuple(pltpu.with_memory_space_constraint(a, pltpu.VMEM) for a in (basis, wq, narrow))
    return pl.pallas_call(
        gain_kernel,
        in_specs=vmem(6) + [pl.BlockSpec(memory_space=pl.ANY)],
        out_specs=vmem(2),
        out_shape=[
            jax.ShapeDtypeStruct((rank // 2, inner.shape[1]), BF),
            jax.ShapeDtypeStruct((x.shape[0] + 16, rank), BF),
        ],
        scratch_shapes=[
            pltpu.VMEM((inner.shape[1], rank), BF),
            pltpu.VMEM((8, rank), F32),
        ],
        compiler_params=pltpu.CompilerParams(vmem_limit_bytes=VMEM_BYTES),
        cost_estimate=cost(10**4, 10**3),
        name="pair_sum_and_gain_gradient",
    )(*held, inner, got, x, after)


def merge_kernel(a_ref, b_ref, after, out_ref):
    rest = out_ref.shape[0] - 16
    out_ref[:rest, :] = add_wide(a_ref[:rest, :], b_ref[:rest, :]).astype(BF)
    write_split(out_ref, read_split(a_ref) + read_split(b_ref))


def total_kernel(a_ref, b_ref, after, out_ref):
    out_ref[...] = read_split(a_ref) + read_split(b_ref)


def own_kernel(a_ref, b_ref, after, *out_refs):
    at = 0
    for ref in out_refs:
        size = ref.shape[1]
        ref[...] = add_wide(a_ref[:, at : at + size], b_ref[:, at : at + size]).astype(BF)
        at += size


def small_kernel(kernel, name, out_shape, a, b, after):
    return pl.pallas_call(
        kernel,
        in_specs=vmem(2) + [pl.BlockSpec(memory_space=pl.ANY)],
        out_specs=jax.tree.map(lambda _: pl.BlockSpec(memory_space=pltpu.VMEM), out_shape),
        out_shape=out_shape,
        compiler_params=pltpu.CompilerParams(vmem_limit_bytes=VMEM_BYTES // 2),
        cost_estimate=cost(10**4, 10**3),
        name=name,
    )(a, b, after)


def merge(a, b, after):
    return small_kernel(merge_kernel, "sum_with_gain", jax.ShapeDtypeStruct(a.shape, BF), a, b, after)


def gain_total(a, b, after):
    shape = jax.ShapeDtypeStruct((8, a.shape[1]), F32)
    return small_kernel(total_kernel, "gain_total", shape, a, b, after)


def own_pieces(a, b, sizes, after):
    shapes = [jax.ShapeDtypeStruct((a.shape[0], n), BF) for n in sizes]
    return small_kernel(own_kernel, "sum_over_y", shapes, a, b, after)


def add_kernel(a_ref, b_ref, after, out_ref):
    rows = out_ref.shape[0]
    out_ref[...] = add_wide(a_ref[:rows, :], b_ref[:rows, :]).astype(out_ref.dtype)


def add_after(a, b, after, rows=None):
    shape = jax.ShapeDtypeStruct((rows or a.shape[0], a.shape[1]), a.dtype)
    return small_kernel(add_kernel, "pair_sum", shape, a, b, after)


def gather_halves(own_refs, other_refs, whole):
    half = whole.shape[0] // 2
    core = lax.axis_index("dp") & 1
    at = 0
    for own_ref, other_ref in zip(own_refs, other_refs):
        columns = pl.ds(at, own_ref.shape[1])
        whole[pl.ds(pl.multiple_of(core * half, half), half), columns] = own_ref[...]
        whole[pl.ds(pl.multiple_of((1 - core) * half, half), half), columns] = other_ref[...]
        at += own_ref.shape[1]


def inward_kernel(pieces, u_ref, gain_ref, *refs):
    own_refs, other_refs = refs[:pieces], refs[pieces : 2 * pieces]
    q_ref, k_ref, v_ref, inner = refs[-4:]
    nq, nk = q_ref.shape[1], k_ref.shape[1]
    block = q_ref.shape[0]

    @pl.when(pl.program_id(0) == 0)
    def _():
        gather_halves(own_refs, other_refs, inner)

    step = lax.axis_index("dp") * pl.num_programs(0) + pl.program_id(0)
    rows = pl.ds(pl.multiple_of(step * block, block), block)
    gain = jnp.broadcast_to(gain_ref[:, rows], (HD, block)).T[:, :1]
    grad = nn(u_ref[rows, :], inner[...]) * gain
    q_ref[...] = grad[:, :nq].astype(BF)
    k_ref[...] = grad[:, nq : nq + nk].astype(BF)
    v_ref[...] = grad[:, nq + nk :].astype(BF)


def outward_kernel(pieces, u_ref, *refs):
    own_refs, other_refs = refs[:pieces], refs[pieces : 2 * pieces]
    o_ref, inner = refs[-2:]

    @pl.when(pl.program_id(0) == 0)
    def _():
        gather_halves(own_refs, other_refs, inner)

    block, rows = o_ref.shape
    at = pl.multiple_of(pl.program_id(0) * block, block)
    basis = u_ref[pl.ds(pl.multiple_of(lax.axis_index("dp") * rows, rows), rows), :]
    o_ref[...] = nt(inner[:, pl.ds(at, block)].T, basis).astype(BF)


STEPS = 2


def inward_grads(basis, gain, own, other, sizes, after):
    wide, rank = basis.shape
    rows = wide // lax.axis_size("dp")
    block = rows // STEPS
    return pl.pallas_call(
        functools.partial(inward_kernel, len(own)),
        grid=(STEPS,),
        in_specs=vmem(2 + 2 * len(own)) + [pl.BlockSpec(memory_space=pl.ANY)],
        out_specs=[pl.BlockSpec((block, n), lambda i: (i, 0)) for n in sizes],
        scratch_shapes=[pltpu.VMEM((rank, sum(sizes)), BF)],
        out_shape=[jax.ShapeDtypeStruct((rows, n), BF) for n in sizes],
        compiler_params=pltpu.CompilerParams(vmem_limit_bytes=VMEM_BYTES),
        cost_estimate=cost(10**4, 10**3),
        name="inward_weight_gradients",
    )(basis, gain, *own, *other, after)


def outward_grad(basis, own, other, after):
    wide, rank = basis.shape
    rows = wide // lax.axis_size("dp")
    ne = sum(piece.shape[1] for piece in own)
    return pl.pallas_call(
        functools.partial(outward_kernel, len(own)),
        grid=(STEPS,),
        in_specs=vmem(1 + 2 * len(own)) + [pl.BlockSpec(memory_space=pl.ANY)],
        out_specs=pl.BlockSpec((ne // STEPS, rows), lambda i: (i, 0)),
        scratch_shapes=[pltpu.VMEM((rank, ne), BF)],
        out_shape=jax.ShapeDtypeStruct((ne, rows), BF),
        compiler_params=pltpu.CompilerParams(vmem_limit_bytes=VMEM_BYTES),
        cost_estimate=cost(10**4, 10**3),
        name="output_weight_gradient",
    )(basis, *own, *other, after)


def results_kernel(
    wide, fbase_ref, y_ref, ygot_ref, base_ref, unit_ref, x_ref, xgot_ref, back_ref, inv_ref,
    gain_ref, gain_other_ref, after,
    f_ref, b_ref, gain_out_ref,
):
    f_ref[...] = (fbase_ref[...] + add_wide(y_ref[...], ygot_ref[...])).astype(BF)
    length = back_ref.shape[0]
    x = add_wide(x_ref[:length, :], xgot_ref[:length, :])
    inv = inv_ref[:, :1]
    along = jnp.sum(x * back_ref[...].astype(F32), axis=1, keepdims=True)
    middle = along * inv * (1.0 / wide)
    b_ref[...] = (base_ref[...] + (x - unit_ref[...] * middle) * inv).astype(BF)
    core = lax.axis_index("dp") & 1
    half = wide // 2
    rank = gain_ref.shape[1]
    for row in range(half // rank):
        mine = pl.ds(pl.multiple_of(core * half + row * rank, rank), rank)
        theirs = pl.ds(pl.multiple_of((1 - core) * half + row * rank, rank), rank)
        gain_out_ref[:, mine] = gain_ref[row : row + 1, :]
        gain_out_ref[:, theirs] = gain_other_ref[row : row + 1, :]


def results(wide, after, *operands):
    shape = operands[0].shape
    held = tuple(pltpu.with_memory_space_constraint(a, pltpu.VMEM) for a in operands)
    return pl.pallas_call(
        functools.partial(results_kernel, wide),
        in_specs=vmem(len(operands)) + [pl.BlockSpec(memory_space=pl.ANY)],
        out_specs=vmem(3),
        out_shape=[jax.ShapeDtypeStruct(shape, BF)] * 2 + [jax.ShapeDtypeStruct((1, wide), F32)],
        compiler_params=pltpu.CompilerParams(vmem_limit_bytes=VMEM_BYTES // 2),
        cost_estimate=cost(10**4, 10**3),
        name="section_results",
    )(*held, *in_hbm((after,)))


def body(
    new_coeffs,
    loss_grad,
    sent_forward,
    sent_backward,
    stashed,
    subspace,
    norm_gain,
    w_query,
    w_key,
    w_value,
    w_output,
):
    wide = subspace.shape[0]
    wq, wk, wv, wo = w_query[0], w_key[0], w_value[0], w_output[0]
    nq, nk, nv = wq.shape[1], wk.shape[1], wv.shape[1]
    back = stashed[0]
    arrived, returned = cross_pipe(sent_forward[0], sent_backward[0])
    cosine, sine = rope_tables(back.shape[0])

    m2, o2, inv, basis, wq, narrow, turned = project(
        back, norm_gain, subspace, wq, wk, wv, wo
    )
    inner, out_give, out_keep, x = backward(
        back, loss_grad, returned, m2, o2, inv, cosine, sine
    )
    out_got = swap(out_give, "dp", 1)
    inner_got = swap(inner, "dp", 1)
    base, unit, fbase = bases(
        back, loss_grad, returned, new_coeffs, arrived, basis, turned, inv, out_keep
    )
    out_pair = add_after(out_keep, out_got, fbase)
    out_got = swap(out_pair, "dp", 2)
    pair, x = gain_part(basis, wq, narrow, inner, inner_got, x, out_pair)
    pair_got = swap(pair, "dp", 2)
    x_got = swap(x, "tensor", 2)
    y = forward(new_coeffs, arrived, turned, m2, o2, cosine, sine, pair)
    y_got = swap(y, "tensor", 2)
    ne = wo.shape[0]
    out_own = own_pieces(out_pair, out_got, (ne // 2, ne - ne // 2), y)
    out_other = [swap(piece, "dp", 1) for piece in out_own]
    x = merge(x, x_got, out_own[0])
    x_got = swap(x, "tensor", 1)
    grad_o = outward_grad(basis, out_own, out_other, x)
    sizes = (nq // 2, nq - nq // 2, nk + nv)
    own = own_pieces(pair, pair_got, sizes, *in_hbm((grad_o,)))
    other = [swap(piece, "dp", 1) for piece in own]
    y = add_after(y, y_got, own[0])
    y_got = swap(y, "tensor", 1)
    gain = gain_total(x, x_got, y)
    gain_got = swap(gain, "dp", 2)
    grad_q, grad_k, grad_v = inward_grads(basis, norm_gain, own, other, (nq, nk, nv), gain)
    gain = add_after(gain, gain_got, *in_hbm((grad_v,)))
    gain_other = swap(gain, "dp", 1)
    forward_out, backward_out, grad_gain = results(
        wide, grad_v, fbase, y, y_got, base, unit, x, x_got, back, inv, gain, gain_other
    )
    return (
        forward_out[None],
        backward_out[None],
        grad_q[None],
        grad_k[None],
        grad_v[None],
        grad_o[None],
        grad_gain,
    )


def solution(mesh):
    return jax.shard_map(
        body,
        mesh=mesh,
        in_specs=(
            P("dp", None),
            P("dp", None),
            P("pipe", "dp", None),
            P("pipe", "dp", None),
            P("pipe", "dp", None),
            P(),
            P("pipe", None),
            P("pipe", None, "tensor"),
            P("pipe", None, "tensor"),
            P("pipe", None, "tensor"),
            P("pipe", "tensor", None),
        ),
        out_specs=(
            P("pipe", "dp", None),
            P("pipe", "dp", None),
            P("pipe", "dp", "tensor"),
            P("pipe", "dp", "tensor"),
            P("pipe", "dp", "tensor"),
            P("pipe", "tensor", "dp"),
            P("pipe", None),
        ),
        check_vma=False,
    )
```
